32 devices in a mesh: dp: 4 (over y, x), row: 4 (over z), col: 2 (over core).
Axes of the slice: x: 2, y: 2, z: 4, core: 2. Of those that a mesh axis runs over, the one named last changes fastest.
Arguments:
- x_in: bfloat16 [1024, 1536], P(('dp', 'col'), 'row'), may hold values from -6 to 6
- lengths: int32 [4, 8], replicated, may hold values from 1 to 128, 256 in all within a row
- seq_order: int32 [32], replicated, may hold values from 0 to 31, each once
- norm1_gain: float32 [1536], P('row'), may hold values from 0.5 to 1.5
- w_in_x: bfloat16 [1536, 3072], P('row', 'col'), may hold values from -0.15625 to 0.15625
- w_in_z: bfloat16 [1536, 3072], P('row', 'col'), may hold values from -0.15625 to 0.15625
- conv_w: float32 [3072, 4], P(('col', 'row')), may hold values from -0.5 to 0.5
- conv_b: float32 [3072], P(('col', 'row')), may hold values from -0.5 to 0.5
- w_xp: bfloat16 [3072, 128], P(('col', 'row')), may hold values from -0.109375 to 0.109375
- w_dt: bfloat16 [96, 3072], P(None, ('col', 'row')), may hold values from -0.625 to 0.625
- dt_bias: float32 [3072], P(('col', 'row')), may hold values from -6.9 to -2.3
- a_log: float32 [3072, 16], P(('col', 'row')), may hold values from 0 to 2.77
- skip_weight: float32 [3072], P(('col', 'row')), may hold values from 0.5 to 1.5
- w_out: bfloat16 [3072, 1536], P('col', 'row'), may hold values from -0.109375 to 0.109375
- norm2_gain: float32 [1536], P('row'), may hold values from 0.5 to 1.5
- w_gate: bfloat16 [1536, 4096], P('row', 'col'), may hold values from -0.15625 to 0.15625
- w_up: bfloat16 [1536, 4096], P('row', 'col'), may hold values from -0.15625 to 0.15625
- w_down: bfloat16 [4096, 1536], P('col', 'row'), may hold values from -0.09375 to 0.09375
- cotangent: bfloat16 [1024, 1536], P(('dp', 'col'), 'row'), may hold values from -6 to 6
Outputs:
- y_out: bfloat16 [1024, 1536], P(('dp', 'col'), 'row')
- dx_out: bfloat16 [1024, 1536], P(('dp', 'col'), 'row')
- grad_norm1_gain: float32 [1536], P('row')
- grad_w_in_x: float32 [1536, 3072], P('row', 'col')
- grad_w_in_z: float32 [1536, 3072], P('row', 'col')
- grad_conv_w: float32 [3072, 4], P(('col', 'row'))
- grad_conv_b: float32 [3072], P(('col', 'row'))
- grad_w_xp: float32 [3072, 128], P(('col', 'row'))
- grad_w_dt: float32 [96, 3072], P(None, ('col', 'row'))
- grad_dt_bias: float32 [3072], P(('col', 'row'))
- grad_a_log: float32 [3072, 16], P(('col', 'row'))
- grad_skip_weight: float32 [3072], P(('col', 'row'))
- grad_w_out: float32 [3072, 1536], P('col', 'row')
- grad_norm2_gain: float32 [1536], P('row')
- grad_w_gate: float32 [1536, 4096], P('row', 'col')
- grad_w_up: float32 [1536, 4096], P('row', 'col')
- grad_w_down: float32 [4096, 1536], P('col', 'row')
The draws below stay inside these ranges and needn't reach their ends.
Inputs may be any that keep to these rules, and one draw needn't show every extreme that they name: Each row of lengths holds the lengths of one group's 8 sequences and sums to 256. `seq_order`: A permutation of the 32 sequence numbers.
All inputs are finite; a program needn't handle non-finite values.
Results may differ from the reference program's by a relative error of at most 0.015.
Values may be sent and summed in bfloat16 or wider, within the bound.
A program may use at most 192 MiB of HBM per device.

```python
import math
import jax
import jax.numpy as jnp
import numpy as np
from jax import lax

D = 1536
E = 3072
FF = 4096
R = 96
NSTATE = 16
KCONV = 4
XP = 128
TOKENS_G = 256
TOKENS = 1024
SEQ_G = 8
MAXLEN = 128
N_DP = 4


def block_scale(own_key, extent, shards, smallest, high):
    def one(axis_at, blocks):
        draws = jax.random.uniform(jax.random.fold_in(jax.random.fold_in(own_key, 6), axis_at), (blocks,), jnp.float32, smallest / len(shards), high / len(shards))
        return jnp.repeat(jnp.exp(draws), extent[axis_at] // blocks).reshape((-1,) + (1,) * (len(extent) - axis_at - 1))

    level = one(*shards[0])
    for cut in shards[1:]:
        level = level * one(*cut)
    return level


def split_up(amount, total, limit, slope):
    portions = [(1 << 20) // math.isqrt(standing ** slope) + 1 for standing in range(2, amount + 1)]
    spare, counts = total - limit - (amount - 1), [1] * (amount - 1)
    while spare > 0:
        movable = [i for i in range(amount - 1) if counts[i] < limit]
        whole, left = sum([portions[i] for i in movable]), spare
        for i in movable:
            extra = min(limit - counts[i], max(1, left * portions[i] // whole), spare)
            counts[i] = counts[i] + extra
            spare = spare - extra
    return np.array([limit] + counts)


def ragged(rng, count, total, most, slope):
    if count == 2:
        one = jax.random.randint(rng, (), max(1, total - most), min(most, total - 1) + 1)
        return jnp.stack([one, total - one])
    sizes = jnp.asarray(split_up(count, total, most, slope), jnp.int32)
    couples = (count - 1) // 2
    giver, taker = sizes[1:1 + 2 * couples:2], sizes[2:2 + 2 * couples:2]
    slack = jnp.minimum(giver - 1, most - taker)
    moved = jax.random.randint(jax.random.fold_in(rng, 1), (couples,), 0, 1 << 20) % (slack + 1)
    sizes = sizes.at[1:1 + 2 * couples:2].set(giver - moved).at[2:2 + 2 * couples:2].set(taker + moved)
    return sizes[jax.random.permutation(jax.random.fold_in(rng, 2), count)]


def bell_draw(stream_key, shape, spread, most, split=(), held_as=jnp.bfloat16):
    entries = jax.random.normal(stream_key, shape, jnp.float32) * spread
    if len(split) > 0:
        entries = block_scale(stream_key, shape, split, -0.22, 0.18) * entries
    return jnp.clip(entries, min=-most, max=most).astype(held_as)


def setup_inputs(seed: int = 0) -> dict:
    splits = jax.random.split(jax.random.key(seed), 20)
    x_in = bell_draw(splits[0], (TOKENS, D), 1.0, 6.0, ((0, 8), (1, 4)))
    lengths = jax.vmap(lambda own: ragged(own, SEQ_G, TOKENS_G, MAXLEN, 2))(jax.random.split(splits[1], N_DP)).reshape((N_DP, SEQ_G)).astype(jnp.int32)
    seq_order = jax.random.permutation(splits[2], N_DP * SEQ_G).astype(jnp.int32)
    norm1_gain = jnp.clip(1.0 + 0.1 * jax.random.normal(splits[3], (D,), jnp.float32), 0.5, 1.5)
    w_in_x = bell_draw(splits[4], (D, E), D ** -0.5, 0.15625, ((0, 4), (1, 2)))
    w_in_z = bell_draw(splits[5], (D, E), D ** -0.5, 0.15625, ((0, 4), (1, 2)))
    conv_w = jnp.clip(jax.random.uniform(splits[6], (E, KCONV), jnp.float32, -0.5, 0.5) * block_scale(splits[6], (E, KCONV), ((0, 8),), -0.4, 0.0), -0.5, 0.5)
    conv_b = jnp.clip(jax.random.uniform(splits[7], (E,), jnp.float32, -0.5, 0.5) * block_scale(splits[7], (E,), ((0, 8),), -0.4, 0.0), -0.5, 0.5)
    w_xp = bell_draw(splits[8], (E, XP), E ** -0.5, 0.109375, ((0, 8),))
    w_dt = bell_draw(splits[9], (R, E), R ** -0.5, 0.625, ((1, 8),))
    dt_bias = jnp.clip(-6.9 + 4.6000001430511475 * jax.random.uniform(splits[10], (E,), jnp.float32) ** block_scale(splits[10], (E,), ((0, 8),), -0.2, 0.2), -6.9, -2.3)
    a_log = jnp.clip(2.77 * jax.random.uniform(splits[11], (E, NSTATE), jnp.float32) ** block_scale(splits[11], (E, NSTATE), ((0, 8),), -0.2, 0.2), 0.0, 2.77)
    skip_weight = jnp.clip(0.5 + 1.0 * jax.random.uniform(splits[12], (E,), jnp.float32) ** block_scale(splits[12], (E,), ((0, 8),), -0.2, 0.2), 0.5, 1.5)
    w_out = bell_draw(splits[13], (E, D), E ** -0.5, 0.109375, ((0, 2), (1, 4)))
    norm2_gain = jnp.clip(1.0 + 0.1 * jax.random.normal(splits[14], (D,), jnp.float32), 0.5, 1.5)
    w_gate = bell_draw(splits[15], (D, FF), D ** -0.5, 0.15625, ((0, 4), (1, 2)))
    w_up = bell_draw(splits[16], (D, FF), D ** -0.5, 0.15625, ((0, 4), (1, 2)))
    w_down = bell_draw(splits[17], (FF, D), FF ** -0.5, 0.09375, ((0, 2), (1, 4)))
    cotangent = bell_draw(splits[18], (TOKENS, D), 1.0, 6.0, ((0, 8), (1, 4)))
    return {"x_in": x_in, "lengths": lengths, "seq_order": seq_order, "norm1_gain": norm1_gain, "w_in_x": w_in_x, "w_in_z": w_in_z, "conv_w": conv_w, "conv_b": conv_b, "w_xp": w_xp, "w_dt": w_dt, "dt_bias": dt_bias, "a_log": a_log, "skip_weight": skip_weight, "w_out": w_out, "norm2_gain": norm2_gain, "w_gate": w_gate, "w_up": w_up, "w_down": w_down, "cotangent": cotangent}


epsilon = 1e-05

@jax.custom_vjp
def low(v):
    return lax.optimization_barrier(v.astype(jnp.bfloat16)).astype(jnp.float32)

@jax.custom_vjp
def low_back(v):
    return v

def low_keep(v):
    return (low(v), None)

def low_pass(kept, grad):
    return (grad,)

def back_keep(v):
    return (v, None)

def back_low(kept, grad):
    return (low(grad),)
low.defvjp(low_keep, low_pass)
low_back.defvjp(back_keep, back_low)

def matmul_hi(left, right):
    return jnp.dot(left, right, precision=lax.Precision.HIGHEST, preferred_element_type=jnp.float32)

def rms_scale(values):
    return lax.rsqrt(lax.optimization_barrier(jnp.mean(values * values, axis=-1, keepdims=True)) + epsilon)

def layout(lengths, seq_order, group_rows):
    flat_lengths = lengths.reshape(-1)
    total_seqs = flat_lengths.shape[0]
    slot_length = jnp.take(flat_lengths, seq_order).astype(jnp.int32)
    input_start = (jnp.cumsum(slot_length) - slot_length).astype(jnp.int32)
    slot_of = jnp.zeros((total_seqs,), jnp.int32).at[seq_order].set(jnp.arange(total_seqs, dtype=jnp.int32))
    seq_input = jnp.take(input_start, slot_of).reshape(lengths.shape).astype(jnp.int32)
    group_start = (jnp.cumsum(lengths, axis=1) - lengths).astype(jnp.int32)
    places = jnp.arange(group_rows, dtype=jnp.int32)
    member = (lax.optimization_barrier(jnp.sum((places[None, :, None] >= group_start[:, None, :]).astype(jnp.int32), axis=2)) - 1).astype(jnp.int32)
    begin_at = jnp.take_along_axis(group_start, member, axis=1).astype(jnp.int32)
    within = (places[None, :] - begin_at).astype(jnp.int32)
    source = (jnp.take_along_axis(seq_input, member, axis=1) + within).astype(jnp.int32)
    return (source, within)

def combine(earlier, later):
    return (earlier[0] * later[0], later[0] * earlier[1] + later[1])

def selective(inner_u, step_size, enter_b, leave_c, decay_rate, keep_mask):
    row_total, chan_width = inner_u.shape
    block_len = min(128, row_total)
    blocks = row_total // block_len

    def one_block(carry_state, pieces):
        u_block, step_block, b_block, c_block, keep_block = pieces
        decay_now = jnp.exp(step_block[:, :, None] * decay_rate[None]) * keep_block[:, None, None]
        drive_now = (step_block * u_block)[:, :, None] * b_block[:, None, :]
        acc_decay, acc_drive = lax.associative_scan(combine, (decay_now, drive_now), axis=0)
        states = acc_decay * carry_state[None] + acc_drive
        return (states[-1], lax.optimization_barrier(jnp.sum(states * c_block[:, None, :], axis=2)))
    pieces = (inner_u.reshape(blocks, block_len, chan_width), step_size.reshape(blocks, block_len, chan_width), enter_b.reshape(blocks, block_len, -1), leave_c.reshape(blocks, block_len, -1), keep_mask.reshape(blocks, block_len))
    start_state = jnp.zeros(decay_rate.shape, jnp.float32)
    _, outputs = lax.scan(jax.checkpoint(one_block), start_state, pieces)
    return outputs.reshape(row_total, chan_width)

def forward(values, weights, places):
    gain_one, in_x, in_z, kernel, kernel_bias, proj_w, step_w, step_bias, log_rate, skip_w, out_w, gain_two, gate_w, up_w, down_w = weights
    normed_one = low(values * rms_scale(values) * gain_one[None, :])
    inner_x = low_back(matmul_hi(normed_one, in_x))
    inner_z = low_back(matmul_hi(normed_one, in_z))
    tap_count = kernel.shape[1]
    conv_sum = kernel_bias[None, :] + inner_x * kernel[:, tap_count - 1][None, :]
    for shift_by in range(1, tap_count):
        shifted = jnp.concatenate([jnp.zeros((shift_by, inner_x.shape[1]), jnp.float32), inner_x[:-shift_by]], axis=0)
        conv_sum = conv_sum + shifted * (places >= shift_by).astype(jnp.float32)[:, None] * kernel[:, tap_count - 1 - shift_by][None, :]
    inner_u = low(jax.nn.silu(conv_sum))
    projected = low_back(matmul_hi(inner_u, proj_w))
    step_low = low(projected[:, :R])
    enter_b = projected[:, R:R + NSTATE]
    leave_c = projected[:, R + NSTATE:]
    step_size = jax.nn.softplus(low_back(matmul_hi(step_low, step_w)) + step_bias[None, :])
    keep_mask = (places > 0).astype(jnp.float32)
    mixer_y = selective(inner_u, step_size, enter_b, leave_c, -jnp.exp(log_rate), keep_mask) + skip_w[None, :] * inner_u
    gated_out = low(mixer_y * jax.nn.silu(inner_z))
    first_sum = values + low_back(matmul_hi(gated_out, out_w))
    normed_two = low(first_sum * rms_scale(first_sum) * gain_two[None, :])
    gate_val = low_back(matmul_hi(normed_two, gate_w))
    up_val = low_back(matmul_hi(normed_two, up_w))
    hidden = low(jax.nn.silu(gate_val) * up_val)
    return first_sum + low_back(matmul_hi(hidden, down_w))

def reference(x_in, lengths, seq_order, norm1_gain, w_in_x, w_in_z, conv_w, conv_b, w_xp, w_dt, dt_bias, a_log, skip_weight, w_out, norm2_gain, w_gate, w_up, w_down, cotangent):
    source, position = layout(lengths, seq_order, TOKENS_G)
    params = tuple((item.astype(jnp.float32) for item in (norm1_gain, w_in_x, w_in_z, conv_w, conv_b, w_xp, w_dt, dt_bias, a_log, skip_weight, w_out, norm2_gain, w_gate, w_up, w_down)))

    def one_group(totals, pieces):
        row_ids, places = pieces
        inputs = jnp.take(x_in, row_ids, axis=0).astype(jnp.float32)
        back_rows = jnp.take(cotangent, row_ids, axis=0).astype(jnp.float32)

        def run_layer(values, weights):
            return forward(values, weights, places)
        result, pullback = jax.vjp(run_layer, inputs, params)
        input_grad, weight_grads = pullback(back_rows)
        new_totals = tuple((total + grad for total, grad in zip(totals, weight_grads)))
        return (new_totals, (result, input_grad))
    zero_grads = tuple((jnp.zeros_like(item) for item in params))
    totals, (results, input_grads) = lax.scan(one_group, zero_grads, (source, position))
    flat_source = source.reshape(-1)
    y_out = jnp.zeros((TOKENS, D), jnp.float32).at[flat_source].set(results.reshape(-1, D)).astype(jnp.bfloat16)
    dx_out = jnp.zeros((TOKENS, D), jnp.float32).at[flat_source].set(input_grads.reshape(-1, D)).astype(jnp.bfloat16)
    return (y_out, dx_out, totals[0], totals[1], totals[2], totals[3], totals[4], totals[5], totals[6], totals[7], totals[8], totals[9], totals[10], totals[11], totals[12], totals[13], totals[14])
```

```python
import jax
import jax.numpy as jnp
from jax import lax
from jax.experimental import pallas as pl
from jax.experimental.pallas import tpu as pltpu
from jax.sharding import PartitionSpec as P

epsilon = 1e-05


def layout(lengths, seq_order, group_rows):
    flat_lengths = lengths.reshape(-1)
    total_seqs = flat_lengths.shape[0]
    slot_length = jnp.take(flat_lengths, seq_order)
    input_start = jnp.cumsum(slot_length) - slot_length
    slot_of = (
        jnp.zeros((total_seqs,), jnp.int32)
        .at[seq_order]
        .set(jnp.arange(total_seqs, dtype=jnp.int32))
    )
    seq_input = jnp.take(input_start, slot_of).reshape(lengths.shape)
    group_start = jnp.cumsum(lengths, axis=1) - lengths
    places = jnp.arange(group_rows, dtype=jnp.int32)
    member = (
        jnp.sum((places[None, :, None] >= group_start[:, None, :]).astype(jnp.int32), axis=2) - 1
    )
    begin_at = jnp.take_along_axis(group_start, member, axis=1)
    within = places[None, :] - begin_at
    source = jnp.take_along_axis(seq_input, member, axis=1) + within
    return (source, within)


def silu_slope(values):
    sigmoid_v = jax.nn.sigmoid(values)
    return sigmoid_v * (1.0 + values * (1.0 - sigmoid_v))


def contract(left, right, left_dim, right_dim):
    return lax.dot_general(
        left, right, (((left_dim,), (right_dim,)), ((), ())), preferred_element_type=jnp.float32
    )


def convolve(inner_x, kernel, kernel_bias, places):
    tap_count = kernel.shape[1]
    conv_sum = kernel_bias[:, None] + inner_x * kernel[:, tap_count - 1][:, None]
    for shift_by in range(1, tap_count):
        shifted = jnp.pad(inner_x, ((0, 0), (shift_by, 0)))[:, :-shift_by]
        conv_sum = (
            conv_sum
            + shifted
            * (places >= shift_by).astype(jnp.float32)[None, :]
            * kernel[:, tap_count - 1 - shift_by][:, None]
        )
    return jax.nn.silu(conv_sum)


def lanes_like(tile, ch):
    if tile.shape[-1]==ch: return tile
    return jnp.concatenate([tile]*(ch//tile.shape[-1]),axis=-1)

def spread(cols, wide):
    t,n=cols.shape
    eye=(lax.broadcasted_iota(jnp.int32,(n,n),0)==lax.broadcasted_iota(jnp.int32,(n,n),1)).astype(jnp.float32)
    rep=(jnp.broadcast_to(cols[:,None,:],(t,n,n))*eye[None]).reshape(t*n,n)
    return lax.dot_general(rep,jnp.ones((n,wide),jnp.float32),(((1,),(0,)),((),())),precision=lax.Precision.HIGHEST,preferred_element_type=jnp.float32)

def gather_cols(v, t, n):
    s=lax.dot_general(v,jnp.ones((v.shape[1],n),jnp.float32),(((1,),(0,)),((),())),precision=lax.Precision.HIGHEST,preferred_element_type=jnp.float32)
    eye=(lax.broadcasted_iota(jnp.int32,(n,n),0)==lax.broadcasted_iota(jnp.int32,(n,n),1)).astype(jnp.float32)
    return jnp.sum(s.reshape(t,n,n)*eye[None],axis=1)

def fwd_kernel(u_ref,dt_ref,dtk_ref,b_ref,c_ref,a_ref,y_ref,bb,cb,ub):
    t,ch=u_ref.shape; n=a_ref.shape[0]
    piece,_,wide=bb.shape
    ub[...]=u_ref[...]*dt_ref[...]
    a=a_ref[...]
    def part(j,h):
        start=pl.multiple_of(j*piece,piece)
        bb[...]=spread(b_ref[pl.ds(start,piece),:],wide).reshape(bb.shape)
        cb[...]=spread(c_ref[pl.ds(start,piece),:],wide).reshape(cb.shape)
        def step(k,h):
            inner=pl.multiple_of(k*8,8)
            base=pl.multiple_of(start+k*8,8)
            dk=dtk_ref[pl.ds(base,8),:]; uu=ub[pl.ds(base,8),:]
            rows=[]
            for i in range(8):
                dec=jnp.exp(dk[i:i+1,:]*a)
                h=dec*h+uu[i:i+1,:]*lanes_like(bb[inner+i],ch)
                rows.append(jnp.sum(h*lanes_like(cb[inner+i],ch),axis=0,keepdims=True))
            y_ref[pl.ds(base,8),:]=jnp.concatenate(rows,axis=0)
            return h
        return lax.fori_loop(0,piece//8,step,h)
    lax.fori_loop(0,t//piece,part,jnp.zeros((n,ch),jnp.float32))

def fwd(u,dt,dtk,b,c,a):
    t,ch=u.shape; n=a.shape[0]; wide=128 if ch%128==0 else ch; piece=min(128,t)
    return pl.pallas_call(fwd_kernel,out_shape=jax.ShapeDtypeStruct((t,ch),jnp.float32),
      scratch_shapes=[pltpu.VMEM((piece,n,wide),jnp.float32),pltpu.VMEM((piece,n,wide),jnp.float32),pltpu.VMEM((t,ch),jnp.float32)],
      compiler_params=pltpu.CompilerParams(vmem_limit_bytes=48<<20),name="scan_forward")(u,dt,dtk,b,c,a)

def bwd_kernel(u_ref,dt_ref,dtk_ref,b_ref,c_ref,a_ref,dy_ref,
               du_ref,ddt_ref,db_ref,dc_ref,da_ref,bb,cb,ub,hs,ds,pb,pc):
    t,ch=u_ref.shape; n=a_ref.shape[0]
    piece,_,wide=bb.shape
    ub[...]=u_ref[...]*dt_ref[...]
    a=a_ref[...]
    hs[0]=jnp.zeros((n,ch),jnp.float32)
    def part(j,h):
        start=pl.multiple_of(j*piece,piece)
        bb[...]=spread(b_ref[pl.ds(start,piece),:],wide).reshape(bb.shape)
        def step(k,h):
            inner=pl.multiple_of(k*8,8)
            base=pl.multiple_of(start+k*8,8)
            dk=dtk_ref[pl.ds(base,8),:]; uu=ub[pl.ds(base,8),:]
            for i in range(8):
                dec=jnp.exp(dk[i:i+1,:]*a)
                ds[base+i]=dec
                h=dec*h+uu[i:i+1,:]*lanes_like(bb[inner+i],ch)
                hs[base+i+1]=h
            return h
        return lax.fori_loop(0,piece//8,step,h)
    lax.fori_loop(0,t//piece,part,jnp.zeros((n,ch),jnp.float32))
    def fold(v):
        if v.shape[1]==wide: return v
        return sum(v[:,j*wide:(j+1)*wide] for j in range(v.shape[1]//wide))
    def back_part(j,carry):
        start=pl.multiple_of((t//piece-1-j)*piece,piece)
        bb[...]=spread(b_ref[pl.ds(start,piece),:],wide).reshape(bb.shape)
        cb[...]=spread(c_ref[pl.ds(start,piece),:],wide).reshape(cb.shape)
        def back(k,carry):
            g,acc=carry
            inner=pl.multiple_of((piece//8-1-k)*8,8)
            base=pl.multiple_of(start+inner,8)
            dtv=dt_ref[pl.ds(base,8),:]; uu=ub[pl.ds(base,8),:]; uv=u_ref[pl.ds(base,8),:]; dyv=dy_ref[pl.ds(base,8),:]
            s1=[None]*8; s2=[None]*8
            for i in reversed(range(8)):
                dyr=dyv[i:i+1,:]
                lam=lanes_like(cb[inner+i],ch)*dyr+g
                g=ds[base+i]*lam
                q=g*hs[base+i]
                acc=acc+q*dtv[i:i+1,:]
                s1[i]=jnp.sum(lam*lanes_like(bb[inner+i],ch),axis=0,keepdims=True)
                s2[i]=jnp.sum(q*a,axis=0,keepdims=True)
                pb[inner+i]=fold(lam*uu[i:i+1,:])
                pc[inner+i]=fold(hs[base+i+1]*dyr)
            s1=jnp.concatenate(s1,axis=0); s2=jnp.concatenate(s2,axis=0)
            du_ref[pl.ds(base,8),:]=s1*dtv
            ddt_ref[pl.ds(base,8),:]=s2+s1*uv
            return g,acc
        carry=lax.fori_loop(0,piece//8,back,carry)
        db_ref[pl.ds(start,piece),:]=gather_cols(pb[...].reshape(piece*n,wide),piece,n)
        dc_ref[pl.ds(start,piece),:]=gather_cols(pc[...].reshape(piece*n,wide),piece,n)
        return carry
    z=jnp.zeros((n,ch),jnp.float32)
    _,acc=lax.fori_loop(0,t//piece,back_part,(z,z))
    da_ref[...]=acc*a

def bwd(u,dt,dtk,b,c,a,dy):
    t,ch=u.shape; n=a.shape[0]; wide=128 if ch%128==0 else ch; piece=min(128,t)
    f=jnp.float32; S=jax.ShapeDtypeStruct
    return pl.pallas_call(bwd_kernel,out_shape=(S((t,ch),f),S((t,ch),f),S((t,n),f),S((t,n),f),S((n,ch),f)),
      scratch_shapes=[pltpu.VMEM((piece,n,wide),f),pltpu.VMEM((piece,n,wide),f),pltpu.VMEM((t,ch),f),
        pltpu.VMEM((t+1,n,ch),f),pltpu.VMEM((t,n,ch),f),pltpu.VMEM((piece,n,wide),f),pltpu.VMEM((piece,n,wide),f)],
      compiler_params=pltpu.CompilerParams(vmem_limit_bytes=56<<20),name="scan_backward")(u,dt,dtk,b,c,a,dy)


def on_device(
    x_in,
    lengths,
    seq_order,
    norm1_gain,
    w_in_x,
    w_in_z,
    conv_w,
    conv_b,
    w_xp,
    w_dt,
    dt_bias,
    a_log,
    skip_weight,
    w_out,
    norm2_gain,
    w_gate,
    w_up,
    w_down,
    cotangent,
):
    rows_in, width_row = x_in.shape
    row_devices = lax.axis_size("row")
    col_devices = lax.axis_size("col")
    group_rows = rows_in * col_devices
    model_width = width_row * row_devices
    rank_cols = w_dt.shape[0]
    state_count = a_log.shape[1]
    channels = conv_w.shape[0]
    ff_cols = w_gate.shape[1]
    my_group = lax.axis_index("dp")
    my_column = lax.axis_index("col")
    source, position_all = layout(lengths, seq_order, group_rows)
    my_source = lax.dynamic_index_in_dim(source, my_group, 0, keepdims=False)
    position = lax.dynamic_index_in_dim(position_all, my_group, 0, keepdims=False)
    slice_source = lax.dynamic_slice_in_dim(my_source, my_column * rows_in, rows_in, 0)

    def row_total(values):
        return lax.psum(values, "row")

    def token_rows(values):
        return lax.all_gather(values, "col", axis=0, tiled=True)

    def row_pieces(values):
        return lax.all_gather(values, "row", axis=0, tiled=True)

    def col_reduce(term_fn):
        return lax.psum_scatter(
            term_fn(jnp.int32(0), lax.axis_size("col") * rows_in),
            "col",
            scatter_dimension=0,
            tiled=True,
        )

    def row_reduce(term_fn, keep_rows):
        return lax.psum_scatter(
            term_fn(jnp.int32(0), lax.axis_size("row") * keep_rows),
            "row",
            scatter_dimension=0,
            tiled=True,
        )

    def projection_total(values):
        return lax.psum(values, ("row", "col"))

    blank_rows = jnp.zeros((rows_in, width_row), jnp.bfloat16)
    pieces = (
        lax.all_gather(x_in, ("dp", "col"), axis=0, tiled=True),
        lax.all_gather(cotangent, ("dp", "col"), axis=0, tiled=True),
    )
    row_count = pieces[0].shape[0]
    offset = slice_source
    inside = ((offset >= 0) & (offset < row_count))[:, None]
    index = jnp.clip(offset, 0, row_count - 1)
    x_rows = jnp.where(inside, jnp.take(pieces[0], index, axis=0), blank_rows)
    cot_rows = jnp.where(inside, jnp.take(pieces[1], index, axis=0), blank_rows)
    x_val = x_rows.astype(jnp.float32)
    scale_one = lax.rsqrt(row_total(jnp.sum(x_val * x_val, axis=1)) / model_width + epsilon)
    normed_one = (x_val * scale_one[:, None] * norm1_gain[None, :]).astype(jnp.bfloat16)
    normed_all = token_rows(normed_one)

    def inner_term(begin_row, row_count):
        return jnp.concatenate(
            [contract(w_in_x, normed_all, 0, 1), contract(w_in_z, normed_all, 0, 1)], axis=1
        )

    inner = row_reduce(inner_term, channels)
    inner_x = inner[:, :group_rows]
    inner_z = inner[:, group_rows:]

    def conv_part(values, kernel, kernel_bias):
        return convolve(values, kernel, kernel_bias, position)

    conv_out, conv_pull = jax.vjp(conv_part, inner_x, conv_w, conv_b)
    u_low = conv_out.astype(jnp.bfloat16)
    u_val = u_low.astype(jnp.float32)
    projected = projection_total(contract(w_xp, u_low, 0, 0))
    step_low = projected[:rank_cols].astype(jnp.bfloat16)
    enter_b = projected[rank_cols : rank_cols + state_count]
    leave_c = projected[rank_cols + state_count :]
    pre_step = contract(w_dt, step_low, 0, 0) + dt_bias[:, None]
    step_size = jax.nn.softplus(pre_step)

    decay_rate = -jnp.exp(a_log).T
    u_rows = u_val.T
    step_rows = step_size.T
    decay_rows = jnp.where(position[:, None] > 0, step_rows, 1e30)
    b_rows = enter_b.T
    c_rows = leave_c.T
    scanned = fwd(u_rows, step_rows, decay_rows, b_rows, c_rows, decay_rate)
    mixer_y = scanned.T + skip_weight[:, None] * u_val
    gated = mixer_y * jax.nn.silu(inner_z)
    gated_low = gated.astype(jnp.bfloat16)
    gated_all = row_pieces(gated_low)

    def mix_term(begin_row, row_count):
        return contract(gated_all, w_out, 0, 0)

    first_sum = x_val + col_reduce(mix_term)
    scale_two = lax.rsqrt(row_total(jnp.sum(first_sum * first_sum, axis=1)) / model_width + epsilon)
    normed_two = (first_sum * scale_two[:, None] * norm2_gain[None, :]).astype(jnp.bfloat16)
    normed_rows = token_rows(normed_two)

    def ffn_term(begin_row, row_count):
        return jnp.concatenate(
            [
                jnp.dot(normed_rows, w_gate, preferred_element_type=jnp.float32),
                jnp.dot(normed_rows, w_up, preferred_element_type=jnp.float32),
            ],
            axis=1,
        )

    gate_up = row_reduce(ffn_term, group_rows // row_devices)
    gate_val = gate_up[:, :ff_cols]
    up_val = gate_up[:, ff_cols:]
    hidden = (jax.nn.silu(gate_val) * up_val).astype(jnp.bfloat16)
    hidden_all = row_pieces(hidden)

    def down_term(begin_row, row_count):
        return jnp.dot(hidden_all, w_down, preferred_element_type=jnp.float32)

    second_sum = first_sum + col_reduce(down_term)
    out_low = second_sum.astype(jnp.bfloat16)
    back_down_all = token_rows(cot_rows)
    grad_down = contract(hidden_all, back_down_all, 0, 0)

    def hidden_term(begin_row, row_count):
        return contract(back_down_all, w_down, 1, 1)

    d_hidden = row_reduce(hidden_term, group_rows // row_devices)
    d_gate = (d_hidden * up_val * silu_slope(gate_val)).astype(jnp.bfloat16)
    d_up = (d_hidden * jax.nn.silu(gate_val)).astype(jnp.bfloat16)
    d_gate_up_all = row_pieces(jnp.concatenate([d_gate, d_up], axis=1))
    grad_gate = contract(normed_rows, d_gate_up_all[:, :ff_cols], 0, 0)
    grad_up = contract(normed_rows, d_gate_up_all[:, ff_cols:], 0, 0)

    def norm_two_term(begin_row, row_count):
        return contract(d_gate_up_all[:, :ff_cols], w_gate, 1, 1) + contract(
            d_gate_up_all[:, ff_cols:], w_up, 1, 1
        )

    d_normed_two = col_reduce(norm_two_term)
    cot_val = cot_rows.astype(jnp.float32)
    weighted_two = d_normed_two * norm2_gain[None, :]
    grad_norm_two = jnp.sum(d_normed_two * first_sum * scale_two[:, None], axis=0)
    dot_two = row_total(jnp.sum(weighted_two * first_sum, axis=1))
    d_first = (
        cot_val
        + scale_two[:, None] * weighted_two
        - first_sum * (scale_two**3 * dot_two / model_width)[:, None]
    )
    d_mix_all = token_rows(d_first.astype(jnp.bfloat16))
    grad_out = contract(gated_all, d_mix_all, 1, 0)

    def gated_term(begin_row, row_count):
        return contract(w_out, d_mix_all, 1, 1)

    d_gated = row_reduce(gated_term, channels)
    d_inner_z = d_gated * mixer_y * silu_slope(inner_z)
    d_mixer = d_gated * jax.nn.silu(inner_z)
    d_u_rows, d_step_rows, d_b_rows, d_c_rows, grad_rate_rows = bwd(
        u_rows, step_rows, decay_rows, b_rows, c_rows, decay_rate, d_mixer.T
    )
    d_u_mix = d_u_rows.T + skip_weight[:, None] * d_mixer
    d_step = d_step_rows.T
    d_enter = d_b_rows.T
    d_leave = d_c_rows.T
    grad_rate = grad_rate_rows.T
    grad_skip = jnp.sum(d_mixer * u_val, axis=1)
    d_pre = d_step * jax.nn.sigmoid(pre_step)
    grad_step_bias = jnp.sum(d_pre, axis=1)
    d_pre_low = d_pre.astype(jnp.bfloat16)
    grad_step_w = contract(step_low, d_pre_low, 1, 1)
    d_projected = projection_total(
        jnp.concatenate(
            [jnp.dot(w_dt, d_pre_low, preferred_element_type=jnp.float32), d_enter, d_leave], axis=0
        )
    )
    d_proj_low = d_projected.astype(jnp.bfloat16)
    grad_proj_w = contract(u_low, d_proj_low, 1, 1)
    d_u_all = d_u_mix + jnp.dot(w_xp, d_proj_low, preferred_element_type=jnp.float32)
    d_inner_x, grad_kernel, grad_kernel_bias = conv_pull(d_u_all)
    d_inner_all = row_pieces(
        jnp.concatenate([d_inner_x.astype(jnp.bfloat16), d_inner_z.astype(jnp.bfloat16)], axis=1)
    )
    grad_in_x = contract(normed_all, d_inner_all[:, :group_rows], 0, 1)
    grad_in_z = contract(normed_all, d_inner_all[:, group_rows:], 0, 1)

    def norm_one_term(begin_row, row_count):
        piece_x = lax.dynamic_slice_in_dim(d_inner_all, begin_row, row_count, 1)
        piece_z = lax.dynamic_slice_in_dim(d_inner_all, group_rows, row_count, 1)
        return contract(piece_x, w_in_x, 0, 1) + contract(piece_z, w_in_z, 0, 1)

    d_normed_one = col_reduce(norm_one_term)
    weighted_one = d_normed_one * norm1_gain[None, :]
    grad_norm_one = jnp.sum(d_normed_one * x_val * scale_one[:, None], axis=0)
    dot_one = row_total(jnp.sum(weighted_one * x_val, axis=1))
    d_input = (
        d_first
        + scale_one[:, None] * weighted_one
        - x_val * (scale_one**3 * dot_one / model_width)[:, None]
    )
    d_input_low = d_input.astype(jnp.bfloat16)
    grad_norm_one, grad_norm_two = lax.psum((grad_norm_one, grad_norm_two), ("dp", "col"))
    (
        grad_in_x,
        grad_in_z,
        grad_kernel,
        grad_kernel_bias,
        grad_proj_w,
        grad_step_w,
        grad_step_bias,
        grad_rate,
        grad_skip,
        grad_out,
        grad_gate,
        grad_up,
        grad_down,
    ) = (
        lax.psum(grad_in_x.astype(jnp.bfloat16), "dp").astype(jnp.float32),
        lax.psum(grad_in_z.astype(jnp.bfloat16), "dp").astype(jnp.float32),
        lax.psum(grad_kernel.astype(jnp.bfloat16), "dp").astype(jnp.float32),
        lax.psum(grad_kernel_bias.astype(jnp.bfloat16), "dp").astype(jnp.float32),
        lax.psum(grad_proj_w.astype(jnp.bfloat16), "dp").astype(jnp.float32),
        lax.psum(grad_step_w.astype(jnp.bfloat16), "dp").astype(jnp.float32),
        lax.psum(grad_step_bias.astype(jnp.bfloat16), "dp").astype(jnp.float32),
        lax.psum(grad_rate.astype(jnp.bfloat16), "dp").astype(jnp.float32),
        lax.psum(grad_skip.astype(jnp.bfloat16), "dp").astype(jnp.float32),
        lax.psum(grad_out.astype(jnp.bfloat16), "dp").astype(jnp.float32),
        lax.psum(grad_gate.astype(jnp.bfloat16), "dp").astype(jnp.float32),
        lax.psum(grad_up.astype(jnp.bfloat16), "dp").astype(jnp.float32),
        lax.psum(grad_down.astype(jnp.bfloat16), "dp").astype(jnp.float32),
    )
    payload = jnp.concatenate([out_low, d_input_low], axis=1)
    tokens_all = lengths.shape[0] * group_rows
    owner = (
        jnp.zeros((tokens_all,), jnp.int32)
        .at[source.reshape(-1)]
        .set(jnp.arange(tokens_all, dtype=jnp.int32))
    )
    my_rows = lax.dynamic_slice_in_dim(
        owner, (my_group * col_devices + my_column) * rows_in, rows_in, 0
    )
    pieces = lax.all_gather(payload, ("dp", "col"), axis=0, tiled=True)
    row_count = pieces.shape[0]
    offset = my_rows
    inside = ((offset >= 0) & (offset < row_count))[:, None]
    returned = jnp.where(
        inside,
        jnp.take(pieces, jnp.clip(offset, 0, row_count - 1), axis=0),
        jnp.zeros_like(payload),
    )
    y_out = returned[:, :width_row]
    dx_out = returned[:, width_row:]
    return (
        y_out,
        dx_out,
        grad_norm_one,
        grad_in_x,
        grad_in_z,
        grad_kernel,
        grad_kernel_bias,
        grad_proj_w,
        grad_step_w,
        grad_step_bias,
        grad_rate,
        grad_skip,
        grad_out,
        grad_norm_two,
        grad_gate,
        grad_up,
        grad_down,
    )


def solution(mesh):
    placed = (
        P(("dp", "col"), "row"),
        P(),
        P(),
        P("row"),
        P("row", "col"),
        P("row", "col"),
        P(("col", "row"), None),
        P(("col", "row")),
        P(("col", "row"), None),
        P(None, ("col", "row")),
        P(("col", "row")),
        P(("col", "row"), None),
        P(("col", "row")),
        P("col", "row"),
        P("row"),
        P("row", "col"),
        P("row", "col"),
        P("col", "row"),
        P(("dp", "col"), "row"),
    )
    return jax.shard_map(
        on_device,
        mesh=mesh,
        in_specs=placed,
        out_specs=(
            P(("dp", "col"), "row"),
            P(("dp", "col"), "row"),
            P("row"),
            P("row", "col"),
            P("row", "col"),
            P(("col", "row"), None),
            P(("col", "row")),
            P(("col", "row"), None),
            P(None, ("col", "row")),
            P(("col", "row")),
            P(("col", "row"), None),
            P(("col", "row")),
            P("col", "row"),
            P("row"),
            P("row", "col"),
            P("row", "col"),
            P("col", "row"),
        ),
        check_vma=False,
    )
```

```python
import functools

import jax
import jax.numpy as jnp
from jax import lax
from jax.experimental import pallas as pl
from jax.experimental.pallas import tpu as pltpu
from jax.sharding import PartitionSpec as P

epsilon = 1e-05


def layout(lengths, seq_order, group_rows):
    flat_lengths = lengths.reshape(-1)
    total_seqs = flat_lengths.shape[0]
    slot_length = jnp.take(flat_lengths, seq_order)
    input_start = jnp.cumsum(slot_length) - slot_length
    slot_of = (
        jnp.zeros((total_seqs,), jnp.int32)
        .at[seq_order]
        .set(jnp.arange(total_seqs, dtype=jnp.int32))
    )
    seq_input = jnp.take(input_start, slot_of).reshape(lengths.shape)
    group_start = jnp.cumsum(lengths, axis=1) - lengths
    places = jnp.arange(group_rows, dtype=jnp.int32)
    member = (
        jnp.sum((places[None, :, None] >= group_start[:, None, :]).astype(jnp.int32), axis=2) - 1
    )
    begin_at = jnp.take_along_axis(group_start, member, axis=1)
    within = places[None, :] - begin_at
    source = jnp.take_along_axis(seq_input, member, axis=1) + within
    return (source, within)


def silu_slope(values):
    sigmoid_v = jax.nn.sigmoid(values)
    return sigmoid_v * (1.0 + values * (1.0 - sigmoid_v))


def contract(left, right, left_dim, right_dim):
    return lax.dot_general(
        left, right, (((left_dim,), (right_dim,)), ((), ())), preferred_element_type=jnp.float32
    )


def convolve(inner_x, kernel, kernel_bias, places):
    tap_count = kernel.shape[1]
    conv_sum = kernel_bias[:, None] + inner_x * kernel[:, tap_count - 1][:, None]
    for shift_by in range(1, tap_count):
        shifted = jnp.pad(inner_x, ((0, 0), (shift_by, 0)))[:, :-shift_by]
        conv_sum = (
            conv_sum
            + shifted
            * (places >= shift_by).astype(jnp.float32)[None, :]
            * kernel[:, tap_count - 1 - shift_by][:, None]
        )
    return jax.nn.silu(conv_sum)


MESH = pl.DeviceIdType.MESH
f32 = jnp.float32
bf16 = jnp.bfloat16


def remote(src, dst, send, recv, where):
    return pltpu.make_async_remote_copy(
        src_ref=src, dst_ref=dst, send_sem=send, recv_sem=recv, device_id=where, device_id_type=MESH
    )


def away(axis, offset):
    return {axis: lax.rem(lax.axis_index(axis) + offset, lax.axis_size(axis))}


def greet(*axes):
    barrier = pltpu.get_barrier_semaphore()
    total = 0
    for axis in axes:
        for offset in range(1, lax.axis_size(axis)):
            pl.semaphore_signal(barrier, inc=1, device_id=away(axis, offset), device_id_type=MESH)
            total += 1
    pl.semaphore_wait(barrier, total)


def matmul(left, right):
    return jnp.dot(left, right, preferred_element_type=f32)


def silu(values):
    return values * jax.nn.sigmoid(values)


def rows_form(values):
    ones = jnp.ones((8, values.shape[1]), f32)
    return lax.dot_general(
        ones,
        values,
        (((1,), (1,)), ((), ())),
        precision=lax.Precision.HIGHEST,
        preferred_element_type=f32,
    )


def column_form(row_values):
    return jnp.transpose(row_values)[:, 0:1]


class Line:
    def __init__(self, axis, send, recv):
        self.axis, self.send, self.recv = axis, send, recv
        self.size = lax.axis_size(axis)
        self.me = lax.axis_index(axis)

    def right(self, src, dst, d):
        return remote(
            src, dst, self.send.at[0, d], self.recv.at[0, d], {self.axis: jnp.minimum(self.me + 1, self.size - 1)}
        )

    def left(self, src, dst, d):
        return remote(
            src, dst, self.send.at[1, d], self.recv.at[1, d], {self.axis: jnp.maximum(self.me - 1, 0)}
        )


def line_gather(axis, buf, send, recv, between=None):
    line = Line(axis, send, recv)
    size, me = line.size, line.me

    def go_right(s):
        return (me - s >= 0) & (me + 1 < size), line.right(
            buf.at[jnp.maximum(me - s, 0)], buf.at[jnp.maximum(me - s, 0)], jnp.maximum(me - s, 0)
        )

    def go_left(s):
        slot = jnp.minimum(me + s, size - 1)
        return (me + s < size) & (me > 0), line.left(buf.at[slot], buf.at[slot], slot)

    for s in range(size - 1):
        for valid, copy in (go_right(s), go_left(s)):
            pl.when(valid)(copy.start)
        if s == 0 and between is not None:
            between()
        slot = jnp.maximum(me - 1 - s, 0)
        pl.when(me - 1 - s >= 0)(line.right(buf.at[slot], buf.at[slot], slot).wait_recv)
        slot = jnp.minimum(me + 1 + s, size - 1)
        pl.when(me + 1 + s < size)(line.left(buf.at[slot], buf.at[slot], slot).wait_recv)

    def finish():
        for s in range(size - 1):
            for valid, copy in (go_right(s), go_left(s)):
                pl.when(valid)(copy.wait_send)

    return finish


def line_scatter(axis, block_of, out, held, from_left, from_right, send, recv):
    line = Line(axis, send, recv)
    size, me = line.size, line.me
    last = size - 1

    def right_at(t):
        d = jnp.clip(last - t + me, 0, last)
        return (t >= me) & (me < last), d, line.right(held.at[d], from_left.at[d], d)

    def left_at(t):
        d = jnp.clip(t - (last - me), 0, last)
        return (t >= last - me) & (me > 0), d, line.left(held.at[d], from_right.at[d], d)

    for t in range(size - 1):
        valid, d, copy = right_at(t)

        @pl.when(valid)
        def _():
            part = block_of(d)

            @pl.when(me > 0)
            def _():
                line.right(held.at[d], from_left.at[d], d).wait_recv()
                held[d] = (part + from_left[d].astype(f32)).astype(held.dtype)

            @pl.when(me == 0)
            def _():
                held[d] = part.astype(held.dtype)

            copy.start()

        valid, d, copy = left_at(t)

        @pl.when(valid)
        def _():
            part = block_of(d)

            @pl.when(me < last)
            def _():
                line.left(held.at[d], from_right.at[d], d).wait_recv()
                held[d] = (part + from_right[d].astype(f32)).astype(held.dtype)

            @pl.when(me == last)
            def _():
                held[d] = part.astype(held.dtype)

            copy.start()

    out[...] = block_of(me)

    def finish():
        @pl.when(me > 0)
        def _():
            line.right(held.at[me], from_left.at[me], me).wait_recv()
            out[...] += from_left[me].astype(f32)

        @pl.when(me < last)
        def _():
            line.left(held.at[me], from_right.at[me], me).wait_recv()
            out[...] += from_right[me].astype(f32)

        for t in range(size - 1):
            for valid, _, copy in (right_at(t), left_at(t)):
                pl.when(valid)(copy.wait_send)

    return finish


def spray(axis, src_of, dst, send, recv, base=0):
    copies = []
    for k in range(1, lax.axis_size(axis)):
        copy = remote(src_of(k), dst.at[k - 1], send.at[base + k - 1], recv.at[base + k - 1], away(axis, k))
        copy.start()
        copies.append(copy)
    return copies


def wait_all(copies):
    for copy in copies:
        copy.wait()


def swap(axis, src, dst, send, recv):
    copy = remote(src, dst, send, recv, away(axis, 1))
    copy.start()
    return copy


def sequence_rows(lens_row, order_row, per_group):
    count = lens_row.shape[1]
    ri = lax.broadcasted_iota(jnp.int32, (count, count), 0)
    ci = lax.broadcasted_iota(jnp.int32, (count, count), 1)
    lens_f = lens_row.astype(f32)

    def to_column(row):
        return jnp.sum(jnp.where(ri == ci, row, 0.0), axis=1, keepdims=True)

    order_col = to_column(order_row.astype(f32)).astype(jnp.int32)
    lens_col = to_column(lens_f)
    pick = order_row == ri
    pick_t = order_col == ci
    slot_col = jnp.sum(jnp.where(pick_t, lens_f, 0.0), axis=1, keepdims=True)
    slot_row = jnp.sum(jnp.where(pick, lens_col, 0.0), axis=0, keepdims=True)
    start_col = jnp.sum(jnp.where(ci < ri, slot_row, 0.0), axis=1, keepdims=True)
    input_row = jnp.sum(jnp.where(pick_t, start_col, 0.0), axis=0, keepdims=True)
    same = (ri // per_group) == (ci // per_group)
    group_row = jnp.sum(jnp.where((ri < ci) & same, lens_col, 0.0), axis=0, keepdims=True)
    return lens_f, input_row, group_row


def place_rows(lens_row, order_row, per_group, group_rows, group):
    lens_f, input_row, group_row = sequence_rows(lens_row, order_row, per_group)
    count = lens_row.shape[1]
    rows = lax.broadcasted_iota(jnp.int32, (group_rows, count), 0).astype(f32)
    mine = (lax.broadcasted_iota(jnp.int32, (group_rows, count), 1) // per_group) == group
    inside = (rows >= group_row) & (rows < group_row + lens_f) & mine
    within = jnp.sum(jnp.where(inside, rows - group_row, 0.0), axis=1, keepdims=True)
    begin = jnp.sum(jnp.where(inside, input_row, 0.0), axis=1, keepdims=True)
    return begin + within, within


def owner_rows(lens_row, order_row, per_group, group_rows, block_rows, first):
    lens_f, input_row, group_row = sequence_rows(lens_row, order_row, per_group)
    count = lens_row.shape[1]
    rows = (lax.broadcasted_iota(jnp.int32, (block_rows, count), 0) + first).astype(f32)
    base = (lax.broadcasted_iota(jnp.int32, (block_rows, count), 1) // per_group) * group_rows
    inside = (rows >= input_row) & (rows < input_row + lens_f)
    found = jnp.where(inside, base.astype(f32) + group_row + rows - input_row, 0.0)
    return jnp.sum(found, axis=1, keepdims=True)


def plane_origin(rows, dp_size, col_size, block_rows):
    at = lax.broadcasted_iota(jnp.int32, (rows, dp_size * col_size * block_rows), 1)
    block = at // block_rows
    group = lax.rem(block, dp_size)
    column = block // dp_size
    return ((group * col_size + column) * block_rows + lax.rem(at, block_rows)).astype(f32)


def pick_rows(wanted, held):
    col_size, dp_size, block_rows, width = held.shape
    total = col_size * dp_size * block_rows
    chosen = wanted == plane_origin(wanted.shape[0], dp_size, col_size, block_rows)
    chosen = jnp.where(chosen, 1.0, 0.0).astype(bf16)
    return matmul(chosen, held.reshape(total, width)).astype(bf16)


def plane_start(src, held, send, recv):
    me, column = lax.axis_index("dp"), lax.axis_index("col")
    held[column, me] = src[...]
    copies = []
    for k in range(1, lax.axis_size("dp")):
        copy = remote(src, held.at[column, me], send.at[k], recv.at[k], away("dp", k))
        copy.start()
        copies.append(copy)
    return copies


def plane_finish(copies, held, send, recv):
    column = lax.axis_index("col")
    for copy in copies:
        copy.wait_recv()
    copy = swap("col", held.at[column], held.at[column], send.at[0], recv.at[0])
    copy.wait_recv()
    for one in copies + [copy]:
        one.wait_send()


def total_of_sums(part, half_own, half_in, low_own, low_in, full, sems):
    send, recv = sems
    rows = part.shape[0] // 2
    column = lax.axis_index("col")
    mine = pl.ds(pl.multiple_of(column * rows, rows), rows)
    other = pl.ds(pl.multiple_of((1 - column) * rows, rows), rows)
    half_own[...] = part[other, :]
    copy = swap("col", half_own, half_in, send.at[0], recv.at[0])
    copy.wait()
    low_own[...] = (part[mine, :] + half_in[...]).astype(bf16)
    copies = spray("row", lambda k: low_own, low_in, send, recv, 1)
    wait_all(copies)
    total = low_own[...].astype(f32)
    for k in range(low_in.shape[0]):
        total = total + low_in[k].astype(f32)
    full[mine, :] = total
    copy = swap("col", full.at[mine], full.at[mine], send.at[4], recv.at[4])
    copy.wait()


def lanes_like(tile, width):
    if tile.shape[-1] == width:
        return tile
    return jnp.concatenate([tile] * (width // tile.shape[-1]), axis=-1)


def lane_mask(count, lanes, first):
    lane = lax.broadcasted_iota(jnp.int32, (count, lanes), 1)
    return lane == lax.broadcasted_iota(jnp.int32, (count, lanes), 0) + first


def spread(values, first, count, wide):
    rows, lanes = values.shape
    chosen = jnp.where(lane_mask(count, lanes, first)[None], values[:, None, :], 0.0)
    chosen = chosen.reshape(rows * count, lanes)
    high = chosen.astype(bf16)
    rest = (chosen - high.astype(f32)).astype(bf16)
    ones = jnp.ones((lanes, wide), bf16)
    return matmul(high, ones) + matmul(rest, ones)


def lane_sums(values, first, lanes):
    rows, count, wide = values.shape
    flat = values.reshape(rows * count, wide)
    high = flat.astype(bf16)
    rest = (flat - high.astype(f32)).astype(bf16)
    ones = jnp.ones((wide, lanes), bf16)
    sums = (matmul(high, ones) + matmul(rest, ones)).reshape(rows, count, lanes)
    return jnp.sum(jnp.where(lane_mask(count, lanes, first)[None], sums, 0.0), axis=1)


def scan_forward(proj, b_at, c_at, step, gone_step, drive, rate, bb, cb, y=None, hs=None, ds=None):
    rows, width = drive.shape
    count = rate.shape[0]
    piece, _, wide = bb.shape

    def part(j, state):
        start = pl.multiple_of(j * piece, piece)
        values = proj[pl.ds(start, piece), :]
        bb[...] = spread(values, b_at, count, wide).reshape(bb.shape)
        if y is not None:
            cb[...] = spread(values, c_at, count, wide).reshape(cb.shape)

        def eight(k, state):
            inner = pl.multiple_of(k * 8, 8)
            base = pl.multiple_of(start + k * 8, 8)
            gone = gone_step[pl.ds(base, 8), :]
            driven = drive[pl.ds(base, 8), :]
            found = []
            for i in range(8):
                decay = jnp.exp(gone[i : i + 1, :] * rate)
                state = decay * state + driven[i : i + 1, :] * lanes_like(bb[inner + i], width)
                if y is not None:
                    found.append(
                        jnp.sum(state * lanes_like(cb[inner + i], width), axis=0, keepdims=True)
                    )
                else:
                    ds[base + i] = decay
                    hs[base + i + 1] = state
            if y is not None:
                y[pl.ds(base, 8), :] = jnp.concatenate(found, axis=0)
            return state

        return lax.fori_loop(0, piece // 8, eight, state)

    if hs is not None:
        hs[0] = jnp.zeros((count, width), f32)
    lax.fori_loop(0, rows // piece, part, jnp.zeros((count, width), f32))


def scan_backward(
    proj, b_at, c_at, step, drive, inner_u, dy, rate, hs, ds, bb, cb, pb, pc, du, dstep, dproj
):
    rows, width = drive.shape
    count = rate.shape[0]
    piece, _, wide = bb.shape

    def fold(values):
        total = values[:, 0:wide]
        for j in range(1, width // wide):
            total = total + values[:, j * wide : (j + 1) * wide]
        return total

    def part(j, carry):
        start = pl.multiple_of((rows // piece - 1 - j) * piece, piece)
        values = proj[pl.ds(start, piece), :]
        bb[...] = spread(values, b_at, count, wide).reshape(bb.shape)
        cb[...] = spread(values, c_at, count, wide).reshape(cb.shape)

        def eight(k, carry):
            later, total = carry
            inner = pl.multiple_of((piece // 8 - 1 - k) * 8, 8)
            base = pl.multiple_of(start + inner, 8)
            step8 = step[pl.ds(base, 8), :]
            drive8 = drive[pl.ds(base, 8), :]
            u8 = inner_u[pl.ds(base, 8), :]
            dy8 = dy[pl.ds(base, 8), :]
            by_b = [None] * 8
            by_rate = [None] * 8
            for i in reversed(range(8)):
                dy_row = dy8[i : i + 1, :]
                lam = lanes_like(cb[inner + i], width) * dy_row + later
                later = ds[base + i] * lam
                kept = later * hs[base + i]
                total = total + kept * step8[i : i + 1, :]
                by_b[i] = jnp.sum(lam * lanes_like(bb[inner + i], width), axis=0, keepdims=True)
                by_rate[i] = jnp.sum(kept * rate, axis=0, keepdims=True)
                pb[inner + i] = fold(lam * drive8[i : i + 1, :])
                pc[inner + i] = fold(hs[base + i + 1] * dy_row)
            by_b = jnp.concatenate(by_b, axis=0)
            by_rate = jnp.concatenate(by_rate, axis=0)
            du[pl.ds(base, 8), :] = by_b * step8
            dstep[pl.ds(base, 8), :] = by_rate + by_b * u8
            return later, total

        carry = lax.fori_loop(0, piece // 8, eight, carry)
        dproj[pl.ds(start, piece), :] += lane_sums(pb[...], b_at, dproj.shape[1]) + lane_sums(
            pc[...], c_at, dproj.shape[1]
        )
        return carry

    blank = jnp.zeros((count, width), f32)
    _, total = lax.fori_loop(0, rows // piece, part, (blank, blank))
    return total * rate


RANK_LANES = 128


def scan_kernel(proj, step, gone, drive, rate, y, bb, cb, *, b_at, c_at):
    scan_forward(proj, b_at, c_at, step, gone, drive, rate[...], bb, cb, y=y)


def adjoint_kernel(
    proj, step, gone, drive, inner_u, dy, rate, du, dstep, dproj, drate, bb, cb, hs, ds, pb, pc, *, b_at, c_at
):
    scan_forward(proj, b_at, c_at, step, gone, drive, rate[...], bb, cb, hs=hs, ds=ds)
    dproj[...] = jnp.zeros_like(dproj)
    drate[...] = scan_backward(
        proj, b_at, c_at, step, drive, inner_u, dy, rate[...], hs, ds, bb, cb, pb, pc, du, dstep, dproj
    )


def scan_sizes(rows, width, count):
    wide = 128 if width % 128 == 0 else width
    piece = min(128, rows)
    return pltpu.VMEM((piece, count, wide), f32)


def scan_alone(proj, step, gone, drive, rate, b_at, c_at):
    rows, width = step.shape
    block = scan_sizes(rows, width, rate.shape[0])
    return pl.pallas_call(
        functools.partial(scan_kernel, b_at=b_at, c_at=c_at),
        out_shape=jax.ShapeDtypeStruct((rows, width), f32),
        scratch_shapes=[block, block],
        compiler_params=pltpu.CompilerParams(vmem_limit_bytes=VMEM_BYTES),
        name="scan_states",
    )(proj, step, gone, drive, rate)


def adjoint_alone(proj, step, gone, drive, inner_u, dy, rate, b_at, c_at):
    rows, width = step.shape
    count = rate.shape[0]
    block = scan_sizes(rows, width, count)
    shape = jax.ShapeDtypeStruct
    return pl.pallas_call(
        functools.partial(adjoint_kernel, b_at=b_at, c_at=c_at),
        out_shape=(
            shape((rows, width), f32),
            shape((rows, width), f32),
            shape(proj.shape, f32),
            shape((count, width), f32),
        ),
        scratch_shapes=[
            block,
            block,
            pltpu.VMEM((rows + 1, count, width), f32),
            pltpu.VMEM((rows, count, width), f32),
            block,
            block,
        ],
        compiler_params=pltpu.CompilerParams(vmem_limit_bytes=VMEM_BYTES),
        name="scan_adjoint",
    )(proj, step, gone, drive, inner_u, dy, rate)


def conv_sum(inner_x, place, taps, bias):
    count = taps.shape[0]
    total = bias + inner_x * taps[count - 1 : count, :]
    for shift in range(1, count):
        moved = jnp.where(place >= shift, pltpu.roll(inner_x, shift, 0), 0.0)
        total = total + moved * taps[count - 1 - shift : count - shift, :]
    return total


def mixer_forward(
    x, cot, lens, order, gain, w_x, w_z, taps, bias, w_xp, w_dt, dt_bias, rate, skip, w_down,
    xg_o, cg_o, n1_o, s1_o, place_o, xi_o, z_o, proj_o, yv_o, go_o, dhid_o,
    x_all, c_all, sum_own, sum_in, xw, held, from_left, from_right, z_held, z_in, h_held, h_in,
    part_s, half_own, half_in, low_own, low_in, bb, cb, step, gone, drive,
    x_send, x_recv, c_send, c_recv, sum_send, sum_recv, line_send, line_recv,
    z_send, z_recv, h_send, h_recv, t_send, t_recv,
    *, per_group, model_width, rank, count
):
    rows, width = xi_o.shape
    hidden = dhid_o.shape[1]
    group, row = lax.axis_index("dp"), lax.axis_index("row")
    row_size = lax.axis_size("row")
    greet("dp", "row", "col")
    x_copies = plane_start(x, x_all, x_send, x_recv)
    c_copies = plane_start(cot, c_all, c_send, c_recv)
    source, place = place_rows(lens[...], order[...], per_group, rows, group)
    place_o[...] = place
    plane_finish(x_copies, x_all, x_send, x_recv)
    xg_low = pick_rows(source, x_all[...])
    xg_o[...] = xg_low
    xg = xg_low.astype(f32)
    sum_own[...] = rows_form(xg * xg)
    sum_copies = spray("row", lambda k: sum_own, sum_in, sum_send, sum_recv)
    xw[...] = (xg * gain[...]).astype(bf16)

    def columns(d, size):
        return pl.ds(pl.multiple_of(d * size, size), size)

    finish = line_scatter(
        "row",
        lambda d: matmul(xw[...], w_x[:, columns(d, width)]),
        xi_o,
        held,
        from_left,
        from_right,
        line_send,
        line_recv,
    )
    plane_finish(c_copies, c_all, c_send, c_recv)
    cg = pick_rows(source, c_all[...])
    cg_o[...] = cg
    finish()
    for k in range(1, row_size):
        d = lax.rem(row + k, row_size)
        z_held[k - 1] = matmul(xw[...], w_z[:, columns(d, width)]).astype(bf16)
    z_copies = spray("row", lambda k: z_held.at[k - 1], z_in, z_send, z_recv)
    z_o[...] = matmul(xw[...], w_z[:, columns(row, width)])
    wait_all(sum_copies)
    square = sum_own[...]
    for k in range(row_size - 1):
        square = square + sum_in[k]
    s1 = column_form(lax.rsqrt(square / model_width + epsilon))
    s1_o[...] = s1
    n1_o[...] = (xg * s1 * gain[...]).astype(bf16)
    inner_x = xi_o[...] * s1
    xi_o[...] = inner_x
    u_low = silu(conv_sum(inner_x, place, taps[...], bias[...])).astype(bf16)
    u = u_low.astype(f32)
    part_s[...] = matmul(u_low, w_xp[...])
    total_of_sums(part_s, half_own, half_in, low_own, low_in, proj_o, (t_send, t_recv))
    for k in range(1, row_size):
        d = lax.rem(row + k, row_size)
        h_held[k - 1] = hidden_block(cg, w_down, d, hidden).astype(bf16)
    h_copies = spray("row", lambda k: h_held.at[k - 1], h_in, h_send, h_recv)
    dhid_o[...] = hidden_block(cg, w_down, row, hidden)
    pre = matmul(proj_o[...].astype(bf16), w_dt[...]) + dt_bias[...]
    step_now = jax.nn.softplus(pre)
    step[...] = step_now
    gone[...] = jnp.where(place > 0.0, step_now, 1e30)
    drive[...] = step_now * u
    scan_forward(proj_o, rank, rank + count, step, gone, drive, rate[...], bb, cb, y=yv_o)
    yv = yv_o[...] + skip[...] * u
    yv_o[...] = yv
    wait_all(z_copies)
    z = z_o[...]
    for k in range(row_size - 1):
        z = z + z_in[k].astype(f32)
    z = z * s1
    z_o[...] = z
    go_o[...] = (yv * silu(z)).astype(bf16)
    wait_all(h_copies)
    total = dhid_o[...]
    for k in range(row_size - 1):
        total = total + h_in[k].astype(f32)
    dhid_o[...] = total


def hidden_block(cg, w_down, d, hidden):
    rows = pl.ds(pl.multiple_of(d * hidden, hidden), hidden)
    return lax.dot_general(cg, w_down[rows, :], (((1,), (1,)), ((), ())), preferred_element_type=f32)


def ffn_forward(
    go, xg, w_out, gain, w_gate, w_up, dhid,
    go_all, h1_o, n2_o, s2_o, hid_all, dgu_o, dot_o,
    own, other, sum_own, sum_in, hw, gu, held, from_left, from_right,
    g_send, g_recv, o_send, o_recv, sum_send, sum_recv, line_send, line_recv, a_send, a_recv,
    *, model_width
):
    rows, width = go.shape
    hidden = dhid.shape[1]
    row = lax.axis_index("row")
    row_size = lax.axis_size("row")
    greet("row", "col")
    go_all[row] = go[...]
    finish = line_gather("row", go_all, g_send, g_recv)
    total = matmul(go_all[0], w_out[0:width, :])
    for d in range(1, row_size):
        total = total + matmul(go_all[d], w_out[d * width : (d + 1) * width, :])
    own[...] = total
    copy = swap("col", own, other, o_send.at[0], o_recv.at[0])
    finish()
    copy.wait()
    h1 = xg[...].astype(f32) + (own[...] + other[...])
    h1_o[...] = h1
    sum_own[...] = rows_form(h1 * h1)
    sum_copies = spray("row", lambda k: sum_own, sum_in, sum_send, sum_recv)
    hw[...] = (h1 * gain[...]).astype(bf16)

    def block_of(d):
        at = pl.ds(pl.multiple_of(d * hidden, hidden), hidden)
        return jnp.concatenate([matmul(hw[...], w_gate[:, at]), matmul(hw[...], w_up[:, at])], axis=1)

    finish = line_scatter("row", block_of, gu, held, from_left, from_right, line_send, line_recv)
    wait_all(sum_copies)
    square = sum_own[...]
    for k in range(row_size - 1):
        square = square + sum_in[k]
    s2 = column_form(lax.rsqrt(square / model_width + epsilon))
    s2_o[...] = s2
    n2_o[...] = (h1 * s2 * gain[...]).astype(bf16)
    finish()
    gate = gu[:, 0:hidden] * s2
    up = gu[:, hidden:] * s2
    sig = jax.nn.sigmoid(gate)
    act = gate * sig
    hid_all[row] = (act * up).astype(bf16)
    d_hid = dhid[...]
    d_gate = (d_hid * up * (sig * (1.0 + gate * (1.0 - sig)))).astype(bf16)
    d_up = (d_hid * act).astype(bf16)
    dgu_o[:, 0:hidden] = d_gate
    dgu_o[:, hidden:] = d_up

    def between():
        dot_o[...] = rows_form(d_gate.astype(f32) * gate + d_up.astype(f32) * up)

    line_gather("row", hid_all, a_send, a_recv, between)()


def ffn_backward(
    dgu, dot, w_gate, w_up, gain, cg, h1, s2, w_out, hid_all, w_down, xg,
    dgu_all, dh1_o, dmix_o, dgo_o, gnorm_o, y_o,
    own, other, y_own, y_other, dot_in, dot_own, dot_other, held, from_left, from_right,
    g_send, g_recv, o_send, o_recv, dot_send, dot_recv, line_send, line_recv,
    *, model_width
):
    rows, hidden = dgu.shape[0], dgu.shape[1] // 2
    width = dgo_o.shape[1]
    row = lax.axis_index("row")
    row_size = lax.axis_size("row")
    greet("row", "col")
    dot_copies = spray("row", lambda k: dot, dot_in, dot_send, dot_recv)
    dgu_all[row] = dgu[...]

    def between():
        total = matmul(hid_all[0], w_down[0:hidden, :])
        for d in range(1, row_size):
            total = total + matmul(hid_all[d], w_down[d * hidden : (d + 1) * hidden, :])
        y_own[...] = total

    finish = line_gather("row", dgu_all, g_send, g_recv, between)
    y_copy = swap("col", y_own, y_other, o_send.at[0], o_recv.at[0])

    def transposed(left, right):
        return lax.dot_general(left, right, (((1,), (1,)), ((), ())), preferred_element_type=f32)

    total = jnp.zeros((rows, own.shape[1]), f32)
    for d in range(row_size):
        at = slice(d * hidden, (d + 1) * hidden)
        total = total + transposed(dgu_all[d, :, 0:hidden], w_gate[:, at])
        total = total + transposed(dgu_all[d, :, hidden:], w_up[:, at])
    own[...] = total
    copy = swap("col", own, other, o_send.at[1], o_recv.at[1])
    wait_all(dot_copies)
    dot_sum = dot[...]
    for k in range(row_size - 1):
        dot_sum = dot_sum + dot_in[k]
    dot_own[...] = dot_sum
    dot_copy = swap("col", dot_own, dot_other, o_send.at[2], o_recv.at[2])
    finish()
    dot_copy.wait()
    copy.wait()
    h1_now, s2_now = h1[...], s2[...]
    dn2 = own[...] + other[...]
    dots = column_form(dot_own[...] + dot_other[...])
    dh1 = (
        cg[...].astype(f32)
        + s2_now * (gain[...] * dn2)
        - h1_now * (s2_now * s2_now * dots / model_width)
    )
    dh1_o[...] = dh1
    dmix_o[...] = dh1.astype(bf16)
    gnorm_o[...] = jnp.sum(dn2 * h1_now * s2_now, axis=0, keepdims=True)

    def block_of(d):
        at = pl.ds(pl.multiple_of(d * width, width), width)
        return transposed(dmix_o[...], w_out[at, :])

    finish = line_scatter("row", block_of, dgo_o, held, from_left, from_right, line_send, line_recv)
    y_copy.wait()
    y_o[...] = (h1_now + (y_own[...] + y_other[...])).astype(bf16)
    finish()


def mixer_backward(
    dgo, z, yv, xi, proj, place, taps, bias, w_xp, w_dt, dt_bias, rate, skip, xg, s1, gain, w_x, w_z, dh1, gnorm2,
    dz_all, dxi_all, dx_o, small_o,
    hs, ds, bb, cb, pb, pc, step, gone, drive, u_s, dy_s, du_s, dstep, dproj,
    half_own, half_in, low_own, low_in, full, own, other, dot_own, dot_in, dot_sum, dot_other,
    z_send, z_recv, t_send, t_recv, x_send, x_recv, o_send, o_recv, dot_send, dot_recv,
    *, rank, model_width
):
    rows, width = dgo.shape
    count = rate.shape[0]
    tap_count = taps.shape[0]
    row = lax.axis_index("row")
    row_size = lax.axis_size("row")
    greet("row", "col")
    z_now = z[...]
    sig_z = jax.nn.sigmoid(z_now)
    d_z = dgo[...] * yv[...] * (sig_z * (1.0 + z_now * (1.0 - sig_z)))
    d_z = d_z.astype(bf16)
    dz_all[row] = d_z
    z_copies = []
    for k in range(1, row_size):
        copy = remote(dz_all.at[row], dz_all.at[row], z_send.at[k - 1], z_recv.at[k - 1], away("row", k))
        copy.start()
        z_copies.append(copy)
    dy = dgo[...] * (z_now * sig_z)
    dy_s[...] = dy
    inner_x = xi[...]
    place_now = place[...]
    xc = conv_sum(inner_x, place_now, taps[...], bias[...])
    sig_c = jax.nn.sigmoid(xc)
    u_low = (xc * sig_c).astype(bf16)
    u = u_low.astype(f32)
    u_s[...] = u
    step_low = proj[...].astype(bf16)
    pre = matmul(step_low, w_dt[...]) + dt_bias[...]
    step_now = jax.nn.softplus(pre)
    step[...] = step_now
    gone[...] = jnp.where(place_now > 0.0, step_now, 1e30)
    drive[...] = step_now * u
    scan_forward(proj, rank, rank + count, step, gone, drive, rate[...], bb, cb, hs=hs, ds=ds)
    dproj[...] = jnp.zeros_like(dproj)
    g_rate = scan_backward(
        proj, rank, rank + count, step, drive, u_s, dy_s, rate[...], hs, ds, bb, cb, pb, pc, du_s, dstep, dproj
    )
    d_pre = dstep[...] * jax.nn.sigmoid(pre)
    d_pre_low = d_pre.astype(bf16)
    w_dt_now = w_dt[...]

    def transposed(left, right):
        return lax.dot_general(left, right, (((1,), (1,)), ((), ())), preferred_element_type=f32)

    def over_rows(left, right):
        return lax.dot_general(left, right, (((0,), (0,)), ((), ())), preferred_element_type=f32)

    dproj[...] += transposed(d_pre_low, w_dt_now)
    total_of_sums(dproj, half_own, half_in, low_own, low_in, full, (t_send, t_recv))
    dproj_low = full[...].astype(bf16)
    du = du_s[...] + skip[...] * dy + transposed(dproj_low, w_xp[...])
    dxc = du * (sig_c * (1.0 + xc * (1.0 - sig_c)))
    taps_now = taps[...]
    d_inner = dxc * taps_now[tap_count - 1 : tap_count, :]
    g_taps = [None] * tap_count
    g_taps[tap_count - 1] = jnp.sum(dxc * inner_x, axis=0, keepdims=True)
    for shift in range(1, tap_count):
        masked = jnp.where(place_now >= shift, dxc, 0.0)
        k = tap_count - 1 - shift
        g_taps[k] = jnp.sum(masked * pltpu.roll(inner_x, shift, 0), axis=0, keepdims=True)
        d_inner = d_inner + pltpu.roll(masked, rows - shift, 0) * taps_now[k : k + 1, :]
    d_inner = d_inner.astype(bf16)
    dxi_all[row] = d_inner
    dot_own[...] = rows_form(d_inner.astype(f32) * inner_x + d_z.astype(f32) * z_now)
    dot_copies = spray("row", lambda k: dot_own, dot_in, dot_send, dot_recv)

    def between():
        small_o[0:RANK_LANES, :] = over_rows(dproj_low, u_low).astype(bf16)
        small_o[RANK_LANES : RANK_LANES + rank, :] = over_rows(step_low, d_pre_low)[0:rank, :].astype(bf16)
        pieces = [
            g_rate,
            *g_taps,
            jnp.sum(dxc, axis=0, keepdims=True),
            jnp.sum(d_pre, axis=0, keepdims=True),
            jnp.sum(dy * u, axis=0, keepdims=True),
            jnp.zeros((1, width), f32),
            gnorm2[...],
        ]
        found = sum(piece.shape[0] for piece in pieces)
        room = small_o.shape[0] - RANK_LANES - rank - found
        pieces.append(jnp.zeros((room, width), f32))
        small_o[RANK_LANES + rank :, :] = jnp.concatenate(pieces, axis=0).astype(bf16)

    finish = line_gather("row", dxi_all, x_send, x_recv, between)
    wait_all(dot_copies)
    total = dot_own[...]
    for k in range(row_size - 1):
        total = total + dot_in[k]
    dot_sum[...] = total
    dot_copy = swap("col", dot_sum, dot_other, o_send.at[0], o_recv.at[0])
    wait_all(z_copies)
    total = jnp.zeros((rows, own.shape[1]), f32)
    for d in range(row_size):
        at = slice(d * width, (d + 1) * width)
        total = total + transposed(dxi_all[d], w_x[:, at]) + transposed(dz_all[d], w_z[:, at])
    own[...] = total
    copy = swap("col", own, other, o_send.at[1], o_recv.at[1])
    finish()
    dot_copy.wait()
    copy.wait()
    dn1 = own[...] + other[...]
    s1_now = s1[...]
    xg_now = xg[...].astype(f32)
    dots = column_form(dot_sum[...] + dot_other[...])
    dx = dh1[...] + s1_now * (gain[...] * dn1) - xg_now * (s1_now * s1_now * dots / model_width)
    dx_o[...] = dx.astype(bf16)
    at = RANK_LANES + rank + count + tap_count + 3
    gnorm = jnp.sum(dn1 * xg_now * s1_now, axis=0, keepdims=True).astype(bf16)
    base = at // 16 * 16
    tile = small_o[base : base + 16, :]
    here = lax.broadcasted_iota(jnp.int32, tile.shape, 0) == at - base
    small_o[base : base + 16, :] = jnp.where(here, gnorm, tile)


def rows_return(y, dx, lens, order, y_o, dx_o, mine, held, send, recv, *, per_group):
    group_rows, width = y.shape
    block_rows = y_o.shape[0]
    group, column = lax.axis_index("dp"), lax.axis_index("col")
    greet("dp", "col")
    at = pl.ds(pl.multiple_of(column * block_rows, block_rows), block_rows)
    mine[:, 0:width] = y[at, :]
    mine[:, width:] = dx[at, :]
    copies = plane_start(mine, held, send, recv)
    first = (group * lax.axis_size("col") + column) * block_rows
    wanted = owner_rows(lens[...], order[...], per_group, group_rows, block_rows, first)
    plane_finish(copies, held, send, recv)
    found = pick_rows(wanted, held[...])
    y_o[...] = found[:, 0:width]
    dx_o[...] = found[:, width:]


VMEM_BYTES = 56 << 20
DMA = pltpu.SemaphoreType.DMA


def in_vmem(kernel, name, ident, outs, scratch, args):
    space = pl.BlockSpec(memory_space=pltpu.VMEM)
    return pl.pallas_call(
        kernel,
        out_shape=tuple(jax.ShapeDtypeStruct(shape, kind) for shape, kind in outs),
        in_specs=[space] * len(args),
        out_specs=tuple([space] * len(outs)),
        scratch_shapes=scratch,
        compiler_params=pltpu.CompilerParams(
            collective_id=ident, has_side_effects=True, vmem_limit_bytes=VMEM_BYTES
        ),
        name=name,
    )(*args)


def both(*shape):
    return [DMA(shape), DMA(shape)]


def on_pairs(
    x_in, lengths, seq_order, norm1_gain, w_in_x, w_in_z, conv_w, conv_b, w_xp, w_dt, dt_bias, a_log,
    skip_weight, w_out, norm2_gain, w_gate, w_up, w_down, cotangent,
):
    dp, rs = lax.axis_size("dp"), lax.axis_size("row")
    block, wide_d = x_in.shape
    rows = block * 2
    model_width = wide_d * rs
    width = conv_w.shape[0]
    hidden = w_gate.shape[1] // rs
    rank, count, taps = w_dt.shape[0], a_log.shape[1], conv_w.shape[1]
    per_group = lengths.shape[1]
    lens = lengths.reshape(1, -1)
    order = seq_order.reshape(1, -1)
    gain1, gain2 = norm1_gain[None, :], norm2_gain[None, :]
    conv_taps, conv_bias = conv_w.T, conv_b[None, :]
    step_w = jnp.pad(w_dt, ((0, RANK_LANES - rank), (0, 0)))
    step_bias, skip = dt_bias[None, :], skip_weight[None, :]
    rate = -jnp.exp(a_log).T
    vm = pltpu.VMEM
    tile = vm((128, count, 128), f32)
    big = vm((rows, width), f32)
    sums_scratch = [
        vm((rows // 2, RANK_LANES), f32),
        vm((rows // 2, RANK_LANES), f32),
        vm((rows // 2, RANK_LANES), bf16),
        vm((rs - 1, rows // 2, RANK_LANES), bf16),
    ]
    xg, cg, n1, s1, place, xi, z, proj, yv, go, d_hid = in_vmem(
        functools.partial(
            mixer_forward, per_group=per_group, model_width=model_width, rank=rank, count=count
        ),
        "mixer_forward",
        0,
        [
            ((rows, wide_d), bf16), ((rows, wide_d), bf16), ((rows, wide_d), bf16), ((rows, 1), f32), ((rows, 1), f32),
            ((rows, width), f32), ((rows, width), f32), ((rows, RANK_LANES), f32), ((rows, width), f32),
            ((rows, width), bf16), ((rows, hidden), f32),
        ],
        [
            vm((2, dp, block, wide_d), bf16), vm((2, dp, block, wide_d), bf16),
            vm((8, rows), f32), vm((rs - 1, 8, rows), f32), vm((rows, wide_d), bf16),
            vm((rs, rows, width), bf16), vm((rs, rows, width), bf16), vm((rs, rows, width), bf16),
            vm((rs - 1, rows, width), bf16), vm((rs - 1, rows, width), bf16),
            vm((rs - 1, rows, hidden), bf16), vm((rs - 1, rows, hidden), bf16),
            vm((rows, RANK_LANES), f32), *sums_scratch, tile, tile, big, big, big,
            *both(dp), *both(dp), *both(rs - 1), *both(2, rs), *both(rs - 1), *both(rs - 1), *both(rs + 1),
        ],
        (
            x_in, cotangent, lens, order, gain1, w_in_x, w_in_z, conv_taps, conv_bias, w_xp, step_w, step_bias,
            rate, skip, w_down,
        ),
    )
    go_all, h1, n2, s2, hid_all, dgu, dot = in_vmem(
        functools.partial(ffn_forward, model_width=model_width),
        "ffn_forward",
        1,
        [
            ((rs, rows, width), bf16), ((rows, wide_d), f32), ((rows, wide_d), bf16), ((rows, 1), f32),
            ((rs, rows, hidden), bf16), ((rows, 2 * hidden), bf16), ((8, rows), f32),
        ],
        [
            vm((rows, wide_d), f32), vm((rows, wide_d), f32), vm((8, rows), f32), vm((rs - 1, 8, rows), f32),
            vm((rows, wide_d), bf16), vm((rows, 2 * hidden), f32),
            vm((rs, rows, 2 * hidden), bf16), vm((rs, rows, 2 * hidden), bf16), vm((rs, rows, 2 * hidden), bf16),
            *both(2, rs), *both(1), *both(rs - 1), *both(2, rs), *both(2, rs),
        ],
        (go, xg, w_out, gain2, w_gate, w_up, d_hid),
    )

    def summed(value):
        return lax.psum(value.astype(bf16), "dp")

    g_down = summed(jnp.einsum("dtf,tc->dfc", hid_all, cg, preferred_element_type=f32))
    dgu_all, dh1, dmix, dgo, gnorm2, y = in_vmem(
        functools.partial(ffn_backward, model_width=model_width),
        "ffn_backward",
        2,
        [
            ((rs, rows, 2 * hidden), bf16), ((rows, wide_d), f32), ((rows, wide_d), bf16), ((rows, width), f32),
            ((1, wide_d), f32), ((rows, wide_d), bf16),
        ],
        [
            vm((rows, wide_d), f32), vm((rows, wide_d), f32), vm((rows, wide_d), f32), vm((rows, wide_d), f32),
            vm((rs - 1, 8, rows), f32), vm((8, rows), f32), vm((8, rows), f32),
            vm((rs, rows, width), bf16), vm((rs, rows, width), bf16), vm((rs, rows, width), bf16),
            *both(2, rs), *both(3), *both(rs - 1), *both(2, rs),
        ],
        (dgu, dot, w_gate, w_up, gain2, cg, h1, s2, w_out, hid_all, w_down, xg),
    )
    g_gate = summed(jnp.einsum("tc,dtf->cdf", n2, dgu_all[:, :, :hidden], preferred_element_type=f32))
    g_up = summed(jnp.einsum("tc,dtf->cdf", n2, dgu_all[:, :, hidden:], preferred_element_type=f32))
    g_out = summed(jnp.einsum("dte,tc->dec", go_all, dmix, preferred_element_type=f32))
    dz_all, dxi_all, dx, small = in_vmem(
        functools.partial(mixer_backward, rank=rank, model_width=model_width),
        "mixer_backward",
        3,
        [
            ((rs, rows, width), bf16), ((rs, rows, width), bf16), ((rows, wide_d), bf16),
            ((2 * RANK_LANES, width), bf16),
        ],
        [
            vm((rows + 1, count, width), f32), vm((rows, count, width), f32), tile, tile, tile, tile,
            big, big, big, big, big, big, big, vm((rows, RANK_LANES), f32), *sums_scratch,
            vm((rows, RANK_LANES), f32), vm((rows, wide_d), f32), vm((rows, wide_d), f32),
            vm((8, rows), f32), vm((rs - 1, 8, rows), f32), vm((8, rows), f32), vm((8, rows), f32),
            *both(rs - 1), *both(rs + 1), *both(2, rs), *both(2), *both(rs - 1),
        ],
        (
            dgo, z, yv, xi, proj, place, conv_taps, conv_bias, w_xp, step_w, step_bias, rate, skip, xg, s1, gain1,
            w_in_x, w_in_z, dh1, gnorm2,
        ),
    )
    y_out, dx_out = in_vmem(
        functools.partial(rows_return, per_group=per_group),
        "rows_return",
        4,
        [((block, wide_d), bf16), ((block, wide_d), bf16)],
        [vm((block, 2 * wide_d), bf16), vm((2, dp, block, 2 * wide_d), bf16), *both(dp)],
        (y, dx, lens, order),
    )
    g_x = summed(jnp.einsum("tc,dte->cde", n1, dxi_all, preferred_element_type=f32))
    g_z = summed(jnp.einsum("tc,dte->cde", n1, dz_all, preferred_element_type=f32))
    small = lax.psum(small, "dp").astype(f32)
    at = RANK_LANES + rank

    def wide(value, *shape):
        return value.reshape(*shape).astype(f32)

    return (
        y_out,
        dx_out,
        small[at + count + taps + 3],
        wide(g_x, wide_d, -1),
        wide(g_z, wide_d, -1),
        small[at + count : at + count + taps].T,
        small[at + count + taps],
        small[:RANK_LANES].T,
        small[RANK_LANES:at],
        small[at + count + taps + 1],
        small[at : at + count].T,
        small[at + count + taps + 2],
        wide(g_out, -1, wide_d),
        small[at + count + taps + 4],
        wide(g_gate, wide_d, -1),
        wide(g_up, wide_d, -1),
        wide(g_down, -1, wide_d),
    )


def on_device(
    x_in,
    lengths,
    seq_order,
    norm1_gain,
    w_in_x,
    w_in_z,
    conv_w,
    conv_b,
    w_xp,
    w_dt,
    dt_bias,
    a_log,
    skip_weight,
    w_out,
    norm2_gain,
    w_gate,
    w_up,
    w_down,
    cotangent,
):
    rows_in, width_row = x_in.shape
    row_devices = lax.axis_size("row")
    col_devices = lax.axis_size("col")
    group_rows = rows_in * col_devices
    model_width = width_row * row_devices
    rank_cols = w_dt.shape[0]
    state_count = a_log.shape[1]
    channels = conv_w.shape[0]
    ff_cols = w_gate.shape[1]
    my_group = lax.axis_index("dp")
    my_column = lax.axis_index("col")
    source, position_all = layout(lengths, seq_order, group_rows)
    my_source = lax.dynamic_index_in_dim(source, my_group, 0, keepdims=False)
    position = lax.dynamic_index_in_dim(position_all, my_group, 0, keepdims=False)
    slice_source = lax.dynamic_slice_in_dim(my_source, my_column * rows_in, rows_in, 0)

    def row_total(values):
        return lax.psum(values, "row")

    def token_rows(values):
        return lax.all_gather(values, "col", axis=0, tiled=True)

    def row_pieces(values):
        return lax.all_gather(values, "row", axis=0, tiled=True)

    def col_reduce(term_fn):
        return lax.psum_scatter(
            term_fn(jnp.int32(0), lax.axis_size("col") * rows_in),
            "col",
            scatter_dimension=0,
            tiled=True,
        )

    def row_reduce(term_fn, keep_rows):
        return lax.psum_scatter(
            term_fn(jnp.int32(0), lax.axis_size("row") * keep_rows),
            "row",
            scatter_dimension=0,
            tiled=True,
        )

    def projection_total(values):
        return lax.psum(values, ("row", "col"))

    blank_rows = jnp.zeros((rows_in, width_row), jnp.bfloat16)
    pieces = (
        lax.all_gather(x_in, ("dp", "col"), axis=0, tiled=True),
        lax.all_gather(cotangent, ("dp", "col"), axis=0, tiled=True),
    )
    row_count = pieces[0].shape[0]
    offset = slice_source
    inside = ((offset >= 0) & (offset < row_count))[:, None]
    index = jnp.clip(offset, 0, row_count - 1)
    x_rows = jnp.where(inside, jnp.take(pieces[0], index, axis=0), blank_rows)
    cot_rows = jnp.where(inside, jnp.take(pieces[1], index, axis=0), blank_rows)
    x_val = x_rows.astype(jnp.float32)
    scale_one = lax.rsqrt(row_total(jnp.sum(x_val * x_val, axis=1)) / model_width + epsilon)
    normed_one = (x_val * scale_one[:, None] * norm1_gain[None, :]).astype(jnp.bfloat16)
    normed_all = token_rows(normed_one)

    def inner_term(begin_row, row_count):
        return jnp.concatenate(
            [contract(w_in_x, normed_all, 0, 1), contract(w_in_z, normed_all, 0, 1)], axis=1
        )

    inner = row_reduce(inner_term, channels)
    inner_x = inner[:, :group_rows]
    inner_z = inner[:, group_rows:]

    def conv_part(values, kernel, kernel_bias):
        return convolve(values, kernel, kernel_bias, position)

    conv_out, conv_pull = jax.vjp(conv_part, inner_x, conv_w, conv_b)
    u_low = conv_out.astype(jnp.bfloat16)
    u_val = u_low.astype(jnp.float32)
    projected = projection_total(contract(w_xp, u_low, 0, 0))
    step_low = projected[:rank_cols].astype(jnp.bfloat16)
    pre_step = contract(w_dt, step_low, 0, 0) + dt_bias[:, None]
    step_size = jax.nn.softplus(pre_step)

    decay_rate = -jnp.exp(a_log).T
    proj_rows = projected.T
    u_rows = u_val.T
    step_rows = step_size.T
    gone_rows = jnp.where(position[:, None] > 0, step_rows, 1e30)
    drive_rows = step_rows * u_rows
    at_b, at_c = rank_cols, rank_cols + state_count
    scanned = scan_alone(proj_rows, step_rows, gone_rows, drive_rows, decay_rate, at_b, at_c)
    mixer_y = scanned.T + skip_weight[:, None] * u_val
    gated = mixer_y * jax.nn.silu(inner_z)
    gated_low = gated.astype(jnp.bfloat16)
    gated_all = row_pieces(gated_low)

    def mix_term(begin_row, row_count):
        return contract(gated_all, w_out, 0, 0)

    first_sum = x_val + col_reduce(mix_term)
    scale_two = lax.rsqrt(row_total(jnp.sum(first_sum * first_sum, axis=1)) / model_width + epsilon)
    normed_two = (first_sum * scale_two[:, None] * norm2_gain[None, :]).astype(jnp.bfloat16)
    normed_rows = token_rows(normed_two)

    def ffn_term(begin_row, row_count):
        return jnp.concatenate(
            [
                jnp.dot(normed_rows, w_gate, preferred_element_type=jnp.float32),
                jnp.dot(normed_rows, w_up, preferred_element_type=jnp.float32),
            ],
            axis=1,
        )

    gate_up = row_reduce(ffn_term, group_rows // row_devices)
    gate_val = gate_up[:, :ff_cols]
    up_val = gate_up[:, ff_cols:]
    hidden = (jax.nn.silu(gate_val) * up_val).astype(jnp.bfloat16)
    hidden_all = row_pieces(hidden)

    def down_term(begin_row, row_count):
        return jnp.dot(hidden_all, w_down, preferred_element_type=jnp.float32)

    second_sum = first_sum + col_reduce(down_term)
    out_low = second_sum.astype(jnp.bfloat16)
    back_down_all = token_rows(cot_rows)
    grad_down = contract(hidden_all, back_down_all, 0, 0)

    def hidden_term(begin_row, row_count):
        return contract(back_down_all, w_down, 1, 1)

    d_hidden = row_reduce(hidden_term, group_rows // row_devices)
    d_gate = (d_hidden * up_val * silu_slope(gate_val)).astype(jnp.bfloat16)
    d_up = (d_hidden * jax.nn.silu(gate_val)).astype(jnp.bfloat16)
    d_gate_up_all = row_pieces(jnp.concatenate([d_gate, d_up], axis=1))
    grad_gate = contract(normed_rows, d_gate_up_all[:, :ff_cols], 0, 0)
    grad_up = contract(normed_rows, d_gate_up_all[:, ff_cols:], 0, 0)

    def norm_two_term(begin_row, row_count):
        return contract(d_gate_up_all[:, :ff_cols], w_gate, 1, 1) + contract(
            d_gate_up_all[:, ff_cols:], w_up, 1, 1
        )

    d_normed_two = col_reduce(norm_two_term)
    cot_val = cot_rows.astype(jnp.float32)
    weighted_two = d_normed_two * norm2_gain[None, :]
    grad_norm_two = jnp.sum(d_normed_two * first_sum * scale_two[:, None], axis=0)
    dot_two = row_total(jnp.sum(weighted_two * first_sum, axis=1))
    d_first = (
        cot_val
        + scale_two[:, None] * weighted_two
        - first_sum * (scale_two**3 * dot_two / model_width)[:, None]
    )
    d_mix_all = token_rows(d_first.astype(jnp.bfloat16))
    grad_out = contract(gated_all, d_mix_all, 1, 0)

    def gated_term(begin_row, row_count):
        return contract(w_out, d_mix_all, 1, 1)

    d_gated = row_reduce(gated_term, channels)
    d_inner_z = d_gated * mixer_y * silu_slope(inner_z)
    d_mixer = d_gated * jax.nn.silu(inner_z)
    d_u_rows, d_step_rows, d_proj_rows, grad_rate_rows = adjoint_alone(
        proj_rows, step_rows, gone_rows, drive_rows, u_rows, d_mixer.T, decay_rate, at_b, at_c
    )
    d_u_mix = d_u_rows.T + skip_weight[:, None] * d_mixer
    d_step = d_step_rows.T
    d_enter = d_proj_rows.T[at_b:at_c]
    d_leave = d_proj_rows.T[at_c:]
    grad_rate = grad_rate_rows.T
    grad_skip = jnp.sum(d_mixer * u_val, axis=1)
    d_pre = d_step * jax.nn.sigmoid(pre_step)
    grad_step_bias = jnp.sum(d_pre, axis=1)
    d_pre_low = d_pre.astype(jnp.bfloat16)
    grad_step_w = contract(step_low, d_pre_low, 1, 1)
    d_projected = projection_total(
        jnp.concatenate(
            [jnp.dot(w_dt, d_pre_low, preferred_element_type=jnp.float32), d_enter, d_leave], axis=0
        )
    )
    d_proj_low = d_projected.astype(jnp.bfloat16)
    grad_proj_w = contract(u_low, d_proj_low, 1, 1)
    d_u_all = d_u_mix + jnp.dot(w_xp, d_proj_low, preferred_element_type=jnp.float32)
    d_inner_x, grad_kernel, grad_kernel_bias = conv_pull(d_u_all)
    d_inner_all = row_pieces(
        jnp.concatenate([d_inner_x.astype(jnp.bfloat16), d_inner_z.astype(jnp.bfloat16)], axis=1)
    )
    grad_in_x = contract(normed_all, d_inner_all[:, :group_rows], 0, 1)
    grad_in_z = contract(normed_all, d_inner_all[:, group_rows:], 0, 1)

    def norm_one_term(begin_row, row_count):
        piece_x = lax.dynamic_slice_in_dim(d_inner_all, begin_row, row_count, 1)
        piece_z = lax.dynamic_slice_in_dim(d_inner_all, group_rows, row_count, 1)
        return contract(piece_x, w_in_x, 0, 1) + contract(piece_z, w_in_z, 0, 1)

    d_normed_one = col_reduce(norm_one_term)
    weighted_one = d_normed_one * norm1_gain[None, :]
    grad_norm_one = jnp.sum(d_normed_one * x_val * scale_one[:, None], axis=0)
    dot_one = row_total(jnp.sum(weighted_one * x_val, axis=1))
    d_input = (
        d_first
        + scale_one[:, None] * weighted_one
        - x_val * (scale_one**3 * dot_one / model_width)[:, None]
    )
    d_input_low = d_input.astype(jnp.bfloat16)
    grad_norm_one, grad_norm_two = lax.psum((grad_norm_one, grad_norm_two), ("dp", "col"))
    (
        grad_in_x,
        grad_in_z,
        grad_kernel,
        grad_kernel_bias,
        grad_proj_w,
        grad_step_w,
        grad_step_bias,
        grad_rate,
        grad_skip,
        grad_out,
        grad_gate,
        grad_up,
        grad_down,
    ) = (
        lax.psum(grad_in_x.astype(jnp.bfloat16), "dp").astype(jnp.float32),
        lax.psum(grad_in_z.astype(jnp.bfloat16), "dp").astype(jnp.float32),
        lax.psum(grad_kernel.astype(jnp.bfloat16), "dp").astype(jnp.float32),
        lax.psum(grad_kernel_bias.astype(jnp.bfloat16), "dp").astype(jnp.float32),
        lax.psum(grad_proj_w.astype(jnp.bfloat16), "dp").astype(jnp.float32),
        lax.psum(grad_step_w.astype(jnp.bfloat16), "dp").astype(jnp.float32),
        lax.psum(grad_step_bias.astype(jnp.bfloat16), "dp").astype(jnp.float32),
        lax.psum(grad_rate.astype(jnp.bfloat16), "dp").astype(jnp.float32),
        lax.psum(grad_skip.astype(jnp.bfloat16), "dp").astype(jnp.float32),
        lax.psum(grad_out.astype(jnp.bfloat16), "dp").astype(jnp.float32),
        lax.psum(grad_gate.astype(jnp.bfloat16), "dp").astype(jnp.float32),
        lax.psum(grad_up.astype(jnp.bfloat16), "dp").astype(jnp.float32),
        lax.psum(grad_down.astype(jnp.bfloat16), "dp").astype(jnp.float32),
    )
    payload = jnp.concatenate([out_low, d_input_low], axis=1)
    tokens_all = lengths.shape[0] * group_rows
    owner = (
        jnp.zeros((tokens_all,), jnp.int32)
        .at[source.reshape(-1)]
        .set(jnp.arange(tokens_all, dtype=jnp.int32))
    )
    my_rows = lax.dynamic_slice_in_dim(
        owner, (my_group * col_devices + my_column) * rows_in, rows_in, 0
    )
    pieces = lax.all_gather(payload, ("dp", "col"), axis=0, tiled=True)
    row_count = pieces.shape[0]
    offset = my_rows
    inside = ((offset >= 0) & (offset < row_count))[:, None]
    returned = jnp.where(
        inside,
        jnp.take(pieces, jnp.clip(offset, 0, row_count - 1), axis=0),
        jnp.zeros_like(payload),
    )
    y_out = returned[:, :width_row]
    dx_out = returned[:, width_row:]
    return (
        y_out,
        dx_out,
        grad_norm_one,
        grad_in_x,
        grad_in_z,
        grad_kernel,
        grad_kernel_bias,
        grad_proj_w,
        grad_step_w,
        grad_step_bias,
        grad_rate,
        grad_skip,
        grad_out,
        grad_norm_two,
        grad_gate,
        grad_up,
        grad_down,
    )


def solution(mesh):
    placed = (
        P(("dp", "col"), "row"),
        P(),
        P(),
        P("row"),
        P("row", "col"),
        P("row", "col"),
        P(("col", "row"), None),
        P(("col", "row")),
        P(("col", "row"), None),
        P(None, ("col", "row")),
        P(("col", "row")),
        P(("col", "row"), None),
        P(("col", "row")),
        P("col", "row"),
        P("row"),
        P("row", "col"),
        P("row", "col"),
        P("col", "row"),
        P(("dp", "col"), "row"),
    )
    paired = mesh.shape["col"] == 2
    return jax.shard_map(
        on_pairs if paired else on_device,
        mesh=mesh,
        in_specs=placed,
        out_specs=(
            P(("dp", "col"), "row"),
            P(("dp", "col"), "row"),
            P("row"),
            P("row", "col"),
            P("row", "col"),
            P(("col", "row"), None),
            P(("col", "row")),
            P(("col", "row"), None),
            P(None, ("col", "row")),
            P(("col", "row")),
            P(("col", "row"), None),
            P(("col", "row")),
            P("col", "row"),
            P("row"),
            P("row", "col"),
            P("row", "col"),
            P("col", "row"),
        ),
        check_vma=False,
    )
```

```python
import functools

import jax
import jax.numpy as jnp
from jax import lax
from jax.experimental import pallas as pl
from jax.experimental.pallas import tpu as pltpu
from jax.sharding import PartitionSpec as P

epsilon = 1e-05


def layout(lengths, seq_order, group_rows):
    flat_lengths = lengths.reshape(-1)
    total_seqs = flat_lengths.shape[0]
    slot_length = jnp.take(flat_lengths, seq_order)
    input_start = jnp.cumsum(slot_length) - slot_length
    slot_of = (
        jnp.zeros((total_seqs,), jnp.int32)
        .at[seq_order]
        .set(jnp.arange(total_seqs, dtype=jnp.int32))
    )
    seq_input = jnp.take(input_start, slot_of).reshape(lengths.shape)
    group_start = jnp.cumsum(lengths, axis=1) - lengths
    places = jnp.arange(group_rows, dtype=jnp.int32)
    member = (
        jnp.sum((places[None, :, None] >= group_start[:, None, :]).astype(jnp.int32), axis=2) - 1
    )
    begin_at = jnp.take_along_axis(group_start, member, axis=1)
    within = places[None, :] - begin_at
    source = jnp.take_along_axis(seq_input, member, axis=1) + within
    return (source, within)


def silu_slope(values):
    sigmoid_v = jax.nn.sigmoid(values)
    return sigmoid_v * (1.0 + values * (1.0 - sigmoid_v))


def contract(left, right, left_dim, right_dim):
    return lax.dot_general(
        left, right, (((left_dim,), (right_dim,)), ((), ())), preferred_element_type=jnp.float32
    )


def convolve(inner_x, kernel, kernel_bias, places):
    tap_count = kernel.shape[1]
    conv_sum = kernel_bias[:, None] + inner_x * kernel[:, tap_count - 1][:, None]
    for shift_by in range(1, tap_count):
        shifted = jnp.pad(inner_x, ((0, 0), (shift_by, 0)))[:, :-shift_by]
        conv_sum = (
            conv_sum
            + shifted
            * (places >= shift_by).astype(jnp.float32)[None, :]
            * kernel[:, tap_count - 1 - shift_by][:, None]
        )
    return jax.nn.silu(conv_sum)


MESH = pl.DeviceIdType.MESH
f32 = jnp.float32
bf16 = jnp.bfloat16


def remote(src, dst, send, recv, where):
    return pltpu.make_async_remote_copy(
        src_ref=src, dst_ref=dst, send_sem=send, recv_sem=recv, device_id=where, device_id_type=MESH
    )


def away(axis, offset):
    return {axis: lax.rem(lax.axis_index(axis) + offset, lax.axis_size(axis))}


def greet(*axes):
    barrier = pltpu.get_barrier_semaphore()
    total = 0
    for axis in axes:
        for offset in range(1, lax.axis_size(axis)):
            pl.semaphore_signal(barrier, inc=1, device_id=away(axis, offset), device_id_type=MESH)
            total += 1
    pl.semaphore_wait(barrier, total)


def matmul(left, right):
    return jnp.dot(left, right, preferred_element_type=f32)


def silu(values):
    return values * jax.nn.sigmoid(values)


def rows_form(values):
    ones = jnp.ones((8, values.shape[1]), f32)
    return lax.dot_general(
        ones,
        values,
        (((1,), (1,)), ((), ())),
        precision=lax.Precision.HIGHEST,
        preferred_element_type=f32,
    )


def column_form(row_values):
    return jnp.transpose(row_values)[:, 0:1]


class Line:
    def __init__(self, axis, send, recv):
        self.axis, self.send, self.recv = axis, send, recv
        self.size = lax.axis_size(axis)
        self.me = lax.axis_index(axis)

    def right(self, src, dst, d):
        return remote(
            src, dst, self.send.at[0, d], self.recv.at[0, d], {self.axis: jnp.minimum(self.me + 1, self.size - 1)}
        )

    def left(self, src, dst, d):
        return remote(
            src, dst, self.send.at[1, d], self.recv.at[1, d], {self.axis: jnp.maximum(self.me - 1, 0)}
        )


def line_gather(axis, slot_of, send, recv):
    line = Line(axis, send, recv)
    size, me = line.size, line.me
    last = size - 1

    def go_right(s):
        slot = jnp.maximum(me - s, 0)
        return (me - s >= 0) & (me < last), line.right(slot_of(slot), slot_of(slot), slot)

    def go_left(s):
        slot = jnp.minimum(me + s, last)
        return (me + s <= last) & (me > 0), line.left(slot_of(slot), slot_of(slot), slot)

    for s in range(last):
        for valid, copy in (go_right(s), go_left(s)):
            pl.when(valid)(copy.start)
        yield
        slot = jnp.maximum(me - 1 - s, 0)
        pl.when(me - 1 - s >= 0)(line.right(slot_of(slot), slot_of(slot), slot).wait_recv)
        slot = jnp.minimum(me + 1 + s, last)
        pl.when(me + 1 + s <= last)(line.left(slot_of(slot), slot_of(slot), slot).wait_recv)
    yield
    for s in range(last):
        for valid, copy in (go_right(s), go_left(s)):
            pl.when(valid)(copy.wait_send)


def line_scatter(axis, block_of, out, held, from_left, from_right, send, recv):
    line = Line(axis, send, recv)
    size, me = line.size, line.me
    last = size - 1

    def right_at(t):
        d = jnp.clip(last - t + me, 0, last)
        return (t >= me) & (me < last), d, line.right(held.at[d], from_left.at[d], d)

    def left_at(t):
        d = jnp.clip(t - (last - me), 0, last)
        return (t >= last - me) & (me > 0), d, line.left(held.at[d], from_right.at[d], d)

    def pass_on(valid, first, d, copy, arrived):
        @pl.when(valid)
        def _():
            part = block_of(d)

            @pl.when(jnp.logical_not(first))
            def _():
                copy.wait_recv()
                held[d] = (part + arrived[d].astype(f32)).astype(held.dtype)

            @pl.when(first)
            def _():
                held[d] = part.astype(held.dtype)

            copy.start()

    for t in range(last):
        valid, d, copy = right_at(t)
        pass_on(valid, me == 0, d, copy, from_left)
        valid, d, copy = left_at(t)
        pass_on(valid, me == last, d, copy, from_right)
        if t == 0:
            out[...] = block_of(me)
        yield
    yield

    @pl.when(me > 0)
    def _():
        line.right(held.at[me], from_left.at[me], me).wait_recv()
        out[...] += from_left[me].astype(f32)

    @pl.when(me < last)
    def _():
        line.left(held.at[me], from_right.at[me], me).wait_recv()
        out[...] += from_right[me].astype(f32)

    for t in range(last):
        for valid, _, copy in (right_at(t), left_at(t)):
            pl.when(valid)(copy.wait_send)


def run(*flows):
    flows = list(flows)
    while flows:
        flows = [flow for flow in flows if next(flow, flows) is not flows]


def lanes(ref, size):
    return lambda d: ref.at[:, pl.ds(pl.multiple_of(d * size, size), size)]


def fetch(sources, targets, sems):
    copies = [pltpu.make_async_copy(s, t, sems.at[i]) for i, (s, t) in enumerate(zip(sources, targets))]
    for copy in copies:
        copy.start()
    return copies


def as_row(ref):
    return ref[...].reshape(1, ref.shape[0])


def lengths_row(lens):
    groups, per_group = lens.shape
    values = lens[...].astype(f32)
    at = lax.broadcasted_iota(jnp.int32, (per_group, groups * per_group), 1)
    inner = lax.broadcasted_iota(jnp.int32, (per_group, groups * per_group), 0)
    total = jnp.zeros((1, groups * per_group), f32)
    for g in range(groups):
        place = jnp.where(at == inner + g * per_group, 1.0, 0.0)
        total = total + jnp.dot(
            values[g : g + 1, :], place, precision=lax.Precision.HIGHEST, preferred_element_type=f32
        )
    return total


def spray(axis, src_of, dst, send, recv, base=0):
    copies = []
    for k in range(1, lax.axis_size(axis)):
        copy = remote(src_of(k), dst.at[k - 1], send.at[base + k - 1], recv.at[base + k - 1], away(axis, k))
        copy.start()
        copies.append(copy)
    return copies


def wait_all(copies):
    for copy in copies:
        copy.wait()


def swap(axis, src, dst, send, recv):
    copy = remote(src, dst, send, recv, away(axis, 1))
    copy.start()
    return copy


def sequence_rows(lens_row, order_row, per_group):
    count = lens_row.shape[1]
    ri = lax.broadcasted_iota(jnp.int32, (count, count), 0)
    ci = lax.broadcasted_iota(jnp.int32, (count, count), 1)
    lens_f = lens_row

    def to_column(row):
        return jnp.sum(jnp.where(ri == ci, row, 0.0), axis=1, keepdims=True)

    order_col = to_column(order_row.astype(f32)).astype(jnp.int32)
    lens_col = to_column(lens_f)
    pick = order_row == ri
    pick_t = order_col == ci
    slot_col = jnp.sum(jnp.where(pick_t, lens_f, 0.0), axis=1, keepdims=True)
    slot_row = jnp.sum(jnp.where(pick, lens_col, 0.0), axis=0, keepdims=True)
    start_col = jnp.sum(jnp.where(ci < ri, slot_row, 0.0), axis=1, keepdims=True)
    input_row = jnp.sum(jnp.where(pick_t, start_col, 0.0), axis=0, keepdims=True)
    same = (ri // per_group) == (ci // per_group)
    group_row = jnp.sum(jnp.where((ri < ci) & same, lens_col, 0.0), axis=0, keepdims=True)
    return lens_f, input_row, group_row


def place_rows(lens_row, order_row, per_group, group_rows, group):
    lens_f, input_row, group_row = sequence_rows(lens_row, order_row, per_group)
    count = lens_row.shape[1]
    rows = lax.broadcasted_iota(jnp.int32, (group_rows, count), 0).astype(f32)
    mine = (lax.broadcasted_iota(jnp.int32, (group_rows, count), 1) // per_group) == group
    inside = (rows >= group_row) & (rows < group_row + lens_f) & mine
    within = jnp.sum(jnp.where(inside, rows - group_row, 0.0), axis=1, keepdims=True)
    begin = jnp.sum(jnp.where(inside, input_row, 0.0), axis=1, keepdims=True)
    return begin + within, within


def owner_rows(lens_row, order_row, per_group, group_rows, block_rows, first):
    lens_f, input_row, group_row = sequence_rows(lens_row, order_row, per_group)
    count = lens_row.shape[1]
    rows = (lax.broadcasted_iota(jnp.int32, (block_rows, count), 0) + first).astype(f32)
    base = (lax.broadcasted_iota(jnp.int32, (block_rows, count), 1) // per_group) * group_rows
    inside = (rows >= input_row) & (rows < input_row + lens_f)
    found = jnp.where(inside, base.astype(f32) + group_row + rows - input_row, 0.0)
    return jnp.sum(found, axis=1, keepdims=True)


def plane_origin(rows, dp_size, col_size, block_rows):
    at = lax.broadcasted_iota(jnp.int32, (rows, dp_size * col_size * block_rows), 1)
    block = at // block_rows
    group = lax.rem(block, dp_size)
    column = block // dp_size
    return ((group * col_size + column) * block_rows + lax.rem(at, block_rows)).astype(f32)


def pick_rows(wanted, held):
    col_size, dp_size, block_rows, width = held.shape
    total = col_size * dp_size * block_rows
    chosen = wanted == plane_origin(wanted.shape[0], dp_size, col_size, block_rows)
    chosen = jnp.where(chosen, 1.0, 0.0).astype(bf16)
    return matmul(chosen, held.reshape(total, width)).astype(bf16)


def plane_start(src, held, send, recv):
    me, column = lax.axis_index("dp"), lax.axis_index("col")
    held[column, me] = src[...]
    copies = []
    for k in range(1, lax.axis_size("dp")):
        copy = remote(src, held.at[column, me], send.at[k], recv.at[k], away("dp", k))
        copy.start()
        copies.append(copy)
    return copies


def plane_finish(copies, held, send, recv):
    column = lax.axis_index("col")
    for copy in copies:
        copy.wait_recv()
    copy = swap("col", held.at[column], held.at[column], send.at[0], recv.at[0])
    copy.wait_recv()
    for one in copies + [copy]:
        one.wait_send()


def total_of_sums(part, half_own, half_in, low_own, low_in, full, sems):
    send, recv = sems
    rows = part.shape[0] // 2
    column = lax.axis_index("col")
    mine = pl.ds(pl.multiple_of(column * rows, rows), rows)
    other = pl.ds(pl.multiple_of((1 - column) * rows, rows), rows)
    half_own[...] = part[other, :]
    copy = swap("col", half_own, half_in, send.at[0], recv.at[0])
    copy.wait()
    low_own[...] = (part[mine, :] + half_in[...]).astype(bf16)
    copies = spray("row", lambda k: low_own, low_in, send, recv, 1)
    wait_all(copies)
    total = low_own[...].astype(f32)
    for k in range(low_in.shape[0]):
        total = total + low_in[k].astype(f32)
    full[mine, :] = total
    copy = swap("col", full.at[mine], full.at[mine], send.at[4], recv.at[4])
    copy.wait()


def lanes_like(tile, width):
    if tile.shape[-1] == width:
        return tile
    return jnp.concatenate([tile] * (width // tile.shape[-1]), axis=-1)


def lane_mask(count, lanes, first):
    lane = lax.broadcasted_iota(jnp.int32, (count, lanes), 1)
    return lane == lax.broadcasted_iota(jnp.int32, (count, lanes), 0) + first


def spread(values, first, count, wide):
    rows, lanes = values.shape
    chosen = jnp.where(lane_mask(count, lanes, first)[None], values[:, None, :], 0.0)
    chosen = chosen.reshape(rows * count, lanes)
    high = chosen.astype(bf16)
    rest = (chosen - high.astype(f32)).astype(bf16)
    ones = jnp.ones((lanes, wide), bf16)
    return matmul(high, ones) + matmul(rest, ones)


def lane_sums(values, first, lanes):
    rows, count, wide = values.shape
    flat = values.reshape(rows * count, wide)
    high = flat.astype(bf16)
    rest = (flat - high.astype(f32)).astype(bf16)
    ones = jnp.ones((wide, lanes), bf16)
    sums = (matmul(high, ones) + matmul(rest, ones)).reshape(rows, count, lanes)
    return jnp.sum(jnp.where(lane_mask(count, lanes, first)[None], sums, 0.0), axis=1)


def scan_forward(proj, b_at, c_at, step, gone_step, drive, rate, bb, cb, y):
    rows, width = drive.shape
    count = rate.shape[0]
    piece, _, wide = bb.shape

    def part(j, state):
        start = pl.multiple_of(j * piece, piece)
        values = proj[pl.ds(start, piece), :]
        bb[...] = spread(values, b_at, count, wide).reshape(bb.shape)
        cb[...] = spread(values, c_at, count, wide).reshape(cb.shape)

        def eight(k, state):
            inner = pl.multiple_of(k * 8, 8)
            base = pl.multiple_of(start + k * 8, 8)
            gone = gone_step[pl.ds(base, 8), :]
            driven = drive[pl.ds(base, 8), :]
            found = []
            for i in range(8):
                decay = jnp.exp(gone[i : i + 1, :] * rate)
                state = decay * state + driven[i : i + 1, :] * lanes_like(bb[inner + i], width)
                found.append(jnp.sum(state * lanes_like(cb[inner + i], width), axis=0, keepdims=True))
            y[pl.ds(base, 8), :] = jnp.concatenate(found, axis=0)
            return state

        return lax.fori_loop(0, piece // 8, eight, state)

    lax.fori_loop(0, rows // piece, part, jnp.zeros((count, width), f32))


def scan_states(proj, b_at, gone_step, drive, rate, bb, hs, ds):
    rows, width = drive.shape
    count = rate.shape[0]
    piece, _, wide = bb.shape
    hs[0] = jnp.zeros((count, width), f32)
    for start in range(0, rows, piece):
        bb[...] = spread(proj[start : start + piece, :], b_at, count, wide).reshape(bb.shape)

        def eight(k, state):
            inner = pl.multiple_of(k * 8, 8)
            base = pl.multiple_of(start + k * 8, 8)
            gone = gone_step[pl.ds(base, 8), :]
            driven = drive[pl.ds(base, 8), :]
            for i in range(8):
                decay = jnp.exp(gone[i : i + 1, :] * rate)
                state = decay * state + driven[i : i + 1, :] * lanes_like(bb[inner + i], width)
                ds[base + i] = decay
                hs[base + i + 1] = state
            return state

        lax.fori_loop(0, piece // 8, eight, hs[start])
        yield


def scan_backward(
    proj, b_at, c_at, step, drive, inner_u, dy, rate, hs, ds, bb, cb, pb, pc, du, dstep, dproj
):
    rows, width = drive.shape
    count = rate.shape[0]
    piece, _, wide = bb.shape

    def fold(values):
        total = values[:, 0:wide]
        for j in range(1, width // wide):
            total = total + values[:, j * wide : (j + 1) * wide]
        return total

    def part(j, carry):
        start = pl.multiple_of((rows // piece - 1 - j) * piece, piece)
        values = proj[pl.ds(start, piece), :]
        bb[...] = spread(values, b_at, count, wide).reshape(bb.shape)
        cb[...] = spread(values, c_at, count, wide).reshape(cb.shape)

        def eight(k, carry):
            later, total = carry
            inner = pl.multiple_of((piece // 8 - 1 - k) * 8, 8)
            base = pl.multiple_of(start + inner, 8)
            step8 = step[pl.ds(base, 8), :]
            drive8 = drive[pl.ds(base, 8), :]
            u8 = inner_u[pl.ds(base, 8), :]
            dy8 = dy[pl.ds(base, 8), :]
            by_b = [None] * 8
            by_rate = [None] * 8
            for i in reversed(range(8)):
                dy_row = dy8[i : i + 1, :]
                lam = lanes_like(cb[inner + i], width) * dy_row + later
                later = ds[base + i] * lam
                kept = later * hs[base + i]
                total = total + kept * step8[i : i + 1, :]
                by_b[i] = jnp.sum(lam * lanes_like(bb[inner + i], width), axis=0, keepdims=True)
                by_rate[i] = jnp.sum(kept * rate, axis=0, keepdims=True)
                pb[inner + i] = fold(lam * drive8[i : i + 1, :])
                pc[inner + i] = fold(hs[base + i + 1] * dy_row)
            by_b = jnp.concatenate(by_b, axis=0)
            by_rate = jnp.concatenate(by_rate, axis=0)
            du[pl.ds(base, 8), :] = by_b * step8
            dstep[pl.ds(base, 8), :] = by_rate + by_b * u8
            return later, total

        carry = lax.fori_loop(0, piece // 8, eight, carry)
        dproj[pl.ds(start, piece), :] += lane_sums(pb[...], b_at, dproj.shape[1]) + lane_sums(
            pc[...], c_at, dproj.shape[1]
        )
        return carry

    blank = jnp.zeros((count, width), f32)
    _, total = lax.fori_loop(0, rows // piece, part, (blank, blank))
    return total * rate


RANK_LANES = 128


def scan_kernel(proj, step, gone, drive, rate, y, bb, cb, *, b_at, c_at):
    scan_forward(proj, b_at, c_at, step, gone, drive, rate[...], bb, cb, y=y)


def adjoint_kernel(
    proj, step, gone, drive, inner_u, dy, rate, du, dstep, dproj, drate, bb, cb, hs, ds, pb, pc, *, b_at, c_at
):
    run(scan_states(proj, b_at, gone, drive, rate[...], bb, hs, ds))
    dproj[...] = jnp.zeros_like(dproj)
    drate[...] = scan_backward(
        proj, b_at, c_at, step, drive, inner_u, dy, rate[...], hs, ds, bb, cb, pb, pc, du, dstep, dproj
    )


def scan_sizes(rows, width, count):
    wide = 128 if width % 128 == 0 else width
    piece = min(128, rows)
    return pltpu.VMEM((piece, count, wide), f32)


def scan_alone(proj, step, gone, drive, rate, b_at, c_at):
    rows, width = step.shape
    block = scan_sizes(rows, width, rate.shape[0])
    return pl.pallas_call(
        functools.partial(scan_kernel, b_at=b_at, c_at=c_at),
        out_shape=jax.ShapeDtypeStruct((rows, width), f32),
        scratch_shapes=[block, block],
        compiler_params=pltpu.CompilerParams(vmem_limit_bytes=VMEM_BYTES),
        name="scan_states",
    )(proj, step, gone, drive, rate)


def adjoint_alone(proj, step, gone, drive, inner_u, dy, rate, b_at, c_at):
    rows, width = step.shape
    count = rate.shape[0]
    block = scan_sizes(rows, width, count)
    shape = jax.ShapeDtypeStruct
    return pl.pallas_call(
        functools.partial(adjoint_kernel, b_at=b_at, c_at=c_at),
        out_shape=(
            shape((rows, width), f32),
            shape((rows, width), f32),
            shape(proj.shape, f32),
            shape((count, width), f32),
        ),
        scratch_shapes=[
            block,
            block,
            pltpu.VMEM((rows + 1, count, width), f32),
            pltpu.VMEM((rows, count, width), f32),
            block,
            block,
        ],
        compiler_params=pltpu.CompilerParams(vmem_limit_bytes=VMEM_BYTES),
        name="scan_adjoint",
    )(proj, step, gone, drive, inner_u, dy, rate)


def conv_sum(inner_x, place, taps, bias):
    count = taps.shape[0]
    total = bias + inner_x * taps[count - 1 : count, :]
    for shift in range(1, count):
        moved = jnp.where(place >= shift, pltpu.roll(inner_x, shift, 0), 0.0)
        total = total + moved * taps[count - 1 - shift : count - shift, :]
    return total


def transposed(left, right):
    return lax.dot_general(left, right, (((1,), (1,)), ((), ())), preferred_element_type=f32)


def over_rows(left, right):
    return lax.dot_general(left, right, (((0,), (0,)), ((), ())), preferred_element_type=f32)


def columns(d, size):
    return pl.ds(pl.multiple_of(d * size, size), size)


def line_total(own, arrived):
    total = own
    for k in range(arrived.shape[0]):
        total = total + arrived[k]
    return total


def forward_kernel(
    x, cot, lens, order, gain1, taps, bias, w_xp, w_dt, dt_bias, rate, skip, gain2,
    w_x_h, w_z_h, w_out_h, w_gate_h, w_up_h, w_down_h,
    xg_o, cg_o, n1_o, s1_o, place_o, xi_o, z_o, proj_o, yv_o, go_all, h1_o, s2_o, n2_o, hid_all, dgu_o, dot_o,
    w_x, w_z, w_out, w_gate, w_up, w_down, w_step,
    x_all, c_all, sum_own, sum_in, low, xi_held, xi_left, xi_right, z_held, z_in,
    part_s, half_own, half_in, low_own, low_in, bb, cb, step, gone, drive,
    own, other, gu, gu_held, gu_left, gu_right, dhid, h_held, h_left, h_right,
    w_sems, x_send, x_recv, c_send, c_recv, sum_send, sum_recv, xi_send, xi_recv, z_send, z_recv, t_send, t_recv,
    go_send, go_recv, o_send, o_recv, sum2_send, sum2_recv, gu_send, gu_recv, h_send, h_recv, hid_send, hid_recv,
    *, model_width, rank, count
):
    rows, width = xi_o.shape
    hidden = dgu_o.shape[1] // 2
    group, row = lax.axis_index("dp"), lax.axis_index("row")
    row_size = lax.axis_size("row")
    weights = fetch(
        (w_x_h, w_z_h, w_out_h, w_gate_h, w_up_h, w_down_h), (w_x, w_z, w_out, w_gate, w_up, w_down), w_sems
    )
    greet("dp", "row", "col")
    x_copies = plane_start(x, x_all, x_send, x_recv)
    lens_row = lengths_row(lens)
    source, place = place_rows(lens_row, as_row(order), lens.shape[1], rows, group)
    place_o[...] = place
    w_step[...] = jnp.zeros_like(w_step)
    w_step[0:rank, :] = w_dt[...]
    plane_finish(x_copies, x_all, x_send, x_recv)
    c_copies = plane_start(cot, c_all, c_send, c_recv)
    xg_low = pick_rows(source, x_all[...])
    xg_o[...] = xg_low
    xg = xg_low.astype(f32)
    sum_own[...] = rows_form(xg * xg)
    sum_copies = spray("row", lambda k: sum_own, sum_in, sum_send, sum_recv)
    gain1_now = as_row(gain1)
    low[...] = (xg * gain1_now).astype(bf16)
    weights[0].wait()
    run(
        line_scatter(
            "row", lambda d: matmul(low[...], w_x[:, columns(d, width)]), xi_o, xi_held, xi_left, xi_right,
            xi_send, xi_recv,
        )
    )
    weights[1].wait()
    for k in range(1, row_size):
        d = lax.rem(row + k, row_size)
        z_held[k - 1] = matmul(low[...], w_z[:, columns(d, width)]).astype(bf16)
    z_copies = spray("row", lambda k: z_held.at[k - 1], z_in, z_send, z_recv)
    z_o[...] = matmul(low[...], w_z[:, columns(row, width)])
    wait_all(sum_copies)
    s1 = column_form(lax.rsqrt(line_total(sum_own[...], sum_in) / model_width + epsilon))
    s1_o[...] = s1
    inner_x = xi_o[...] * s1
    xi_o[...] = inner_x
    u_low = silu(conv_sum(inner_x, place, taps[...], as_row(bias))).astype(bf16)
    u = u_low.astype(f32)
    part_s[...] = matmul(u_low, w_xp[...])
    total_of_sums(part_s, half_own, half_in, low_own, low_in, proj_o, (t_send, t_recv))
    pre = matmul(proj_o[...].astype(bf16), w_step[...]) + as_row(dt_bias)
    step_now = jax.nn.softplus(pre)
    step[...] = step_now
    gone[...] = jnp.where(place > 0.0, step_now, 1e30)
    drive[...] = step_now * u
    scan_forward(proj_o, rank, rank + count, step, gone, drive, rate[...], bb, cb, y=yv_o)
    yv = yv_o[...] + as_row(skip) * u
    yv_o[...] = yv
    wait_all(z_copies)
    z = z_o[...]
    for k in range(row_size - 1):
        z = z + z_in[k].astype(f32)
    z = z * s1
    z_o[...] = z
    go_all[:, columns(row, width)] = (yv * silu(z)).astype(bf16)

    def during_gather():
        n1_o[...] = (xg * s1 * gain1_now).astype(bf16)
        plane_finish(c_copies, c_all, c_send, c_recv)
        cg_o[...] = pick_rows(source, c_all[...])
        yield

    run(line_gather("row", lanes(go_all, width), go_send, go_recv), during_gather())
    weights[2].wait()
    own[...] = matmul(go_all[...], w_out[...])
    copy = swap("col", own, other, o_send.at[0], o_recv.at[0])
    weights[3].wait()
    weights[4].wait()
    copy.wait()
    h1 = xg + (own[...] + other[...])
    h1_o[...] = h1
    sum_own[...] = rows_form(h1 * h1)
    sum_copies = spray("row", lambda k: sum_own, sum_in, sum2_send, sum2_recv)
    gain2_now = as_row(gain2)
    low[...] = (h1 * gain2_now).astype(bf16)

    def gate_up(d):
        at = columns(d, hidden)
        return jnp.concatenate([matmul(low[...], w_gate[:, at]), matmul(low[...], w_up[:, at])], axis=1)

    def during_scatter():
        wait_all(sum_copies)
        s2 = column_form(lax.rsqrt(line_total(sum_own[...], sum_in) / model_width + epsilon))
        s2_o[...] = s2
        n2_o[...] = (h1 * s2 * gain2_now).astype(bf16)
        yield

    run(
        line_scatter("row", gate_up, gu, gu_held, gu_left, gu_right, gu_send, gu_recv),
        during_scatter(),
    )
    s2 = s2_o[...]
    gate = gu[:, 0:hidden] * s2
    up = gu[:, hidden:] * s2
    sig = jax.nn.sigmoid(gate)
    act = gate * sig
    hid_all[:, columns(row, hidden)] = (act * up).astype(bf16)
    weights[5].wait()
    run(
        line_gather("row", lanes(hid_all, hidden), hid_send, hid_recv),
        line_scatter(
            "row", lambda d: transposed(cg_o[...], w_down[columns(d, hidden), :]), dhid, h_held, h_left, h_right,
            h_send, h_recv,
        ),
    )
    d_hid = dhid[...]
    d_gate = (d_hid * up * (sig * (1.0 + gate * (1.0 - sig)))).astype(bf16)
    d_up = (d_hid * act).astype(bf16)
    dgu_o[:, 0:hidden] = d_gate
    dgu_o[:, hidden:] = d_up
    dot_o[...] = rows_form(d_gate.astype(f32) * gate + d_up.astype(f32) * up)


def middle_kernel(
    dgu, dot, gain2, cg, h1, s2, hid_all, w_gate_h, w_up_h, w_down_h,
    dg_all, du_all, dh1_o, dmix_o, gnorm_o, y_o,
    w_gate, w_up, w_down, own, other, y_own, y_other, dot_in, dot_own, dot_other,
    w_sems, g_send, g_recv, u_send, u_recv, o_send, o_recv, dot_send, dot_recv,
    *, model_width
):
    hidden = dgu.shape[1] // 2
    row = lax.axis_index("row")
    weights = fetch((w_down_h, w_gate_h, w_up_h), (w_down, w_gate, w_up), w_sems)
    dg_all[:, columns(row, hidden)] = dgu[:, 0:hidden]
    du_all[:, columns(row, hidden)] = dgu[:, hidden:]
    greet("row", "col")
    dot_copies = spray("row", lambda k: dot, dot_in, dot_send, dot_recv)

    def during():
        weights[0].wait()
        y_own[...] = matmul(hid_all[...], w_down[...])
        y_copy = swap("col", y_own, y_other, o_send.at[0], o_recv.at[0])
        yield
        wait_all(dot_copies)
        dot_own[...] = line_total(dot[...], dot_in)
        dot_copy = swap("col", dot_own, dot_other, o_send.at[2], o_recv.at[2])
        weights[1].wait()
        weights[2].wait()
        yield
        y_copy.wait()
        dot_copy.wait()
        y_o[...] = (h1[...] + (y_own[...] + y_other[...])).astype(bf16)

    run(
        line_gather("row", lanes(dg_all, hidden), g_send, g_recv),
        line_gather("row", lanes(du_all, hidden), u_send, u_recv),
        during(),
    )
    own[...] = transposed(dg_all[...], w_gate[...]) + transposed(du_all[...], w_up[...])
    copy = swap("col", own, other, o_send.at[1], o_recv.at[1])
    copy.wait()
    h1_now, s2_now = h1[...], s2[...]
    dn2 = own[...] + other[...]
    dots = column_form(dot_own[...] + dot_other[...])
    dh1 = (
        cg[...].astype(f32)
        + s2_now * (as_row(gain2) * dn2)
        - h1_now * (s2_now * s2_now * dots / model_width)
    )
    dh1_o[...] = dh1
    dmix_o[...] = dh1.astype(bf16)
    gnorm_o[...] = jnp.sum(dn2 * h1_now * s2_now, axis=0, keepdims=True)


def backward_kernel(
    lens, order, y, dmix, z, yv, xi, proj, place, taps, bias, w_xp, w_dt, dt_bias, rate, skip, xg, s1, gain1, dh1,
    gnorm2, w_out_h, w_x_h, w_z_h,
    dz_all, dxi_all, small_o, y_o, dx_o,
    w_out, w_x, w_z, w_step, dgo, d_held, d_left, d_right,
    hs, ds, bb, cb, pb, pc, step, gone, drive, u_s, dy_s, du_s, dstep, dproj,
    half_own, half_in, low_own, low_in, full, own, other, dot_own, dot_in, dot_sum, dot_other,
    y_all, dx_own, dx_all,
    w_sems, y_send, y_recv, dx_send, dx_recv, d_send, d_recv, z_send, z_recv, t_send, t_recv, x_send, x_recv,
    o_send, o_recv, dot_send, dot_recv,
    *, rank, model_width
):
    rows, width = z.shape
    count = rate.shape[0]
    block = y_o.shape[0]
    tap_count = taps.shape[0]
    group, row, column = lax.axis_index("dp"), lax.axis_index("row"), lax.axis_index("col")
    row_size, col_size = lax.axis_size("row"), lax.axis_size("col")
    weights = fetch((w_out_h, w_x_h, w_z_h), (w_out, w_x, w_z), w_sems)
    half = columns(column, block)
    greet("dp", "row", "col")
    y_copies = plane_start(y.at[half], y_all, y_send, y_recv)
    inner_x = xi[...]
    place_now = place[...]
    kept = {}

    def states():
        w_step[...] = jnp.zeros_like(w_step)
        w_step[0:rank, :] = w_dt[...]
        xc = conv_sum(inner_x, place_now, taps[...], as_row(bias))
        sig_c = jax.nn.sigmoid(xc)
        u_low = (xc * sig_c).astype(bf16)
        u = u_low.astype(f32)
        u_s[...] = u
        step_low = proj[...].astype(bf16)
        pre = matmul(step_low, w_step[...]) + as_row(dt_bias)
        step_now = jax.nn.softplus(pre)
        step[...] = step_now
        gone[...] = jnp.where(place_now > 0.0, step_now, 1e30)
        drive[...] = step_now * u
        kept.update(xc=xc, sig_c=sig_c, u_low=u_low, u=u, step_low=step_low, pre=pre)
        yield from scan_states(proj, rank, gone, drive, rate[...], bb, hs, ds)

    weights[0].wait()
    run(
        line_scatter(
            "row", lambda d: transposed(dmix[...], w_out[columns(d, width), :]), dgo, d_held, d_left, d_right,
            d_send, d_recv,
        ),
        states(),
    )
    xc, sig_c, u_low, u = kept["xc"], kept["sig_c"], kept["u_low"], kept["u"]
    step_low, pre = kept["step_low"], kept["pre"]
    z_now = z[...]
    sig_z = jax.nn.sigmoid(z_now)
    d_z = (dgo[...] * yv[...] * (sig_z * (1.0 + z_now * (1.0 - sig_z)))).astype(bf16)
    mine = dz_all.at[:, columns(row, width)]
    mine[...] = d_z
    z_copies = []
    for k in range(1, row_size):
        copy = remote(mine, mine, z_send.at[k - 1], z_recv.at[k - 1], away("row", k))
        copy.start()
        z_copies.append(copy)
    dy = dgo[...] * (z_now * sig_z)
    dy_s[...] = dy
    dproj[...] = jnp.zeros_like(dproj)
    g_rate = scan_backward(
        proj, rank, rank + count, step, drive, u_s, dy_s, rate[...], hs, ds, bb, cb, pb, pc, du_s, dstep, dproj
    )
    d_pre = dstep[...] * jax.nn.sigmoid(pre)
    d_pre_low = d_pre.astype(bf16)
    dproj[...] += transposed(d_pre_low, w_step[...])
    total_of_sums(dproj, half_own, half_in, low_own, low_in, full, (t_send, t_recv))
    dproj_low = full[...].astype(bf16)
    du = du_s[...] + as_row(skip) * dy + transposed(dproj_low, w_xp[...])
    dxc = du * (sig_c * (1.0 + xc * (1.0 - sig_c)))
    taps_now = taps[...]
    d_inner = dxc * taps_now[tap_count - 1 : tap_count, :]
    masked = [dxc]
    for shift in range(1, tap_count):
        masked.append(jnp.where(place_now >= shift, dxc, 0.0))
        k = tap_count - 1 - shift
        d_inner = d_inner + pltpu.roll(masked[shift], rows - shift, 0) * taps_now[k : k + 1, :]
    d_inner = d_inner.astype(bf16)
    dxi_all[:, columns(row, width)] = d_inner

    def during():
        dot_own[...] = rows_form(d_inner.astype(f32) * inner_x + d_z.astype(f32) * z_now)
        dot_copies = spray("row", lambda k: dot_own, dot_in, dot_send, dot_recv)
        small_o[0:RANK_LANES, :] = over_rows(dproj_low, u_low).astype(bf16)
        small_o[RANK_LANES : RANK_LANES + rank, :] = over_rows(step_low, d_pre_low)[0:rank, :].astype(bf16)
        g_taps = [None] * tap_count
        for shift in range(tap_count):
            moved = pltpu.roll(inner_x, shift, 0) if shift else inner_x
            g_taps[tap_count - 1 - shift] = jnp.sum(masked[shift] * moved, axis=0, keepdims=True)
        pieces = [
            g_rate,
            *g_taps,
            jnp.sum(dxc, axis=0, keepdims=True),
            jnp.sum(d_pre, axis=0, keepdims=True),
            jnp.sum(dy * u, axis=0, keepdims=True),
            jnp.zeros((1, width), f32),
            gnorm2[...],
        ]
        found = sum(piece.shape[0] for piece in pieces)
        pieces.append(jnp.zeros((small_o.shape[0] - RANK_LANES - rank - found, width), f32))
        small_o[RANK_LANES + rank :, :] = jnp.concatenate(pieces, axis=0).astype(bf16)
        yield
        wait_all(dot_copies)
        dot_sum[...] = line_total(dot_own[...], dot_in)
        dot_copy = swap("col", dot_sum, dot_other, o_send.at[0], o_recv.at[0])
        wait_all(z_copies)
        weights[1].wait()
        weights[2].wait()
        own[...] = transposed(dz_all[...], w_z[...])
        yield
        dot_copy.wait()
        plane_finish(y_copies, y_all, y_send, y_recv)

    run(line_gather("row", lanes(dxi_all, width), x_send, x_recv), during())
    own[...] += transposed(dxi_all[...], w_x[...])
    copy = swap("col", own, other, o_send.at[1], o_recv.at[1])
    first = (group * col_size + column) * block
    wanted = owner_rows(lengths_row(lens), as_row(order), lens.shape[1], rows, block, first)
    y_o[...] = pick_rows(wanted, y_all[...])
    copy.wait()
    dn1 = own[...] + other[...]
    s1_now = s1[...]
    xg_now = xg[...].astype(f32)
    dots = column_form(dot_sum[...] + dot_other[...])
    dx = dh1[...] + s1_now * (as_row(gain1) * dn1) - xg_now * (s1_now * s1_now * dots / model_width)
    dx_own[...] = dx.astype(bf16)
    dx_copies = plane_start(dx_own.at[half], dx_all, dx_send, dx_recv)
    at = RANK_LANES + rank + count + tap_count + 3
    gnorm = jnp.sum(dn1 * xg_now * s1_now, axis=0, keepdims=True).astype(bf16)
    base = at // 16 * 16
    tile = small_o[base : base + 16, :]
    here = lax.broadcasted_iota(jnp.int32, tile.shape, 0) == at - base
    small_o[base : base + 16, :] = jnp.where(here, gnorm, tile)
    plane_finish(dx_copies, dx_all, dx_send, dx_recv)
    dx_o[...] = pick_rows(wanted, dx_all[...])


VMEM_BYTES = 56 << 20
DMA = pltpu.SemaphoreType.DMA


def in_vmem(kernel, name, ident, outs, scratch, args, far=(), micros=50):
    space = pl.BlockSpec(memory_space=pltpu.VMEM)
    anywhere = pl.BlockSpec(memory_space=pl.ANY)
    return pl.pallas_call(
        kernel,
        out_shape=tuple(jax.ShapeDtypeStruct(shape, kind) for shape, kind in outs),
        in_specs=[space] * len(args) + [anywhere] * len(far),
        out_specs=tuple([space] * len(outs)),
        scratch_shapes=scratch,
        compiler_params=pltpu.CompilerParams(
            collective_id=ident, has_side_effects=True, vmem_limit_bytes=VMEM_BYTES
        ),
        cost_estimate=pl.CostEstimate(flops=micros * 10**9, bytes_accessed=1 << 20, transcendentals=0),
        name=name,
    )(*args, *far)


def both(*shape):
    return [DMA(shape), DMA(shape)]


def on_pairs(
    x_in, lengths, seq_order, norm1_gain, w_in_x, w_in_z, conv_w, conv_b, w_xp, w_dt, dt_bias, a_log,
    skip_weight, w_out, norm2_gain, w_gate, w_up, w_down, cotangent,
):
    dp, rs = lax.axis_size("dp"), lax.axis_size("row")
    block, wide_d = x_in.shape
    rows = block * 2
    model_width = wide_d * rs
    width = conv_w.shape[0]
    hidden = w_gate.shape[1] // rs
    rank, count, taps = w_dt.shape[0], a_log.shape[1], conv_w.shape[1]
    conv_taps = conv_w.T
    rate = -jnp.exp(a_log).T
    vm = pltpu.VMEM
    tile = vm((128, count, 128), f32)
    big = vm((rows, width), f32)
    model = vm((rows, wide_d), f32)
    sums = [vm((8, rows), f32), vm((rs - 1, 8, rows), f32)]
    sums_scratch = [
        vm((rows // 2, RANK_LANES), f32),
        vm((rows // 2, RANK_LANES), f32),
        vm((rows // 2, RANK_LANES), bf16),
        vm((rs - 1, rows // 2, RANK_LANES), bf16),
    ]

    def weight(value):
        return vm(value.shape, value.dtype)

    def line(size, width):
        return [vm((size, rows, width), bf16)] * 3

    (xg, cg, n1, s1, place, xi, z, proj, yv, go_all, h1, s2, n2, hid_all, dgu, dot) = in_vmem(
        functools.partial(forward_kernel, model_width=model_width, rank=rank, count=count),
        "forward",
        0,
        [
            ((rows, wide_d), bf16), ((rows, wide_d), bf16), ((rows, wide_d), bf16), ((rows, 1), f32), ((rows, 1), f32),
            ((rows, width), f32), ((rows, width), f32), ((rows, RANK_LANES), f32), ((rows, width), f32),
            ((rows, rs * width), bf16), ((rows, wide_d), f32), ((rows, 1), f32), ((rows, wide_d), bf16),
            ((rows, rs * hidden), bf16), ((rows, 2 * hidden), bf16), ((8, rows), f32),
        ],
        [
            weight(w_in_x), weight(w_in_z), weight(w_out), weight(w_gate), weight(w_up), weight(w_down),
            vm((RANK_LANES, width), bf16),
            vm((2, dp, block, wide_d), bf16), vm((2, dp, block, wide_d), bf16), *sums, vm((rows, wide_d), bf16),
            *line(rs, width), vm((rs - 1, rows, width), bf16), vm((rs - 1, rows, width), bf16),
            vm((rows, RANK_LANES), f32), *sums_scratch, tile, tile, big, big, big,
            model, model, vm((rows, 2 * hidden), f32), *line(rs, 2 * hidden), vm((rows, hidden), f32), *line(rs, hidden),
            DMA((6,)), *both(dp), *both(dp), *both(rs - 1), *both(2, rs), *both(rs - 1), *both(rs + 1),
            *both(2, rs), *both(1), *both(rs - 1), *both(2, rs), *both(2, rs), *both(2, rs),
        ],
        (
            x_in, cotangent, lengths, seq_order, norm1_gain, conv_taps, conv_b, w_xp, w_dt, dt_bias, rate, skip_weight,
            norm2_gain,
        ),
        (w_in_x, w_in_z, w_out, w_gate, w_up, w_down),
        130,
    )

    def product(left, right):
        return over_rows(left, right).astype(bf16)

    g_down = product(hid_all, cg)
    g_down = lax.psum(g_down, "dp")
    dg_all, du_all, dh1, dmix, gnorm2, y = in_vmem(
        functools.partial(middle_kernel, model_width=model_width),
        "middle",
        1,
        [
            ((rows, rs * hidden), bf16), ((rows, rs * hidden), bf16), ((rows, wide_d), f32), ((rows, wide_d), bf16),
            ((1, wide_d), f32), ((rows, wide_d), bf16),
        ],
        [
            weight(w_gate), weight(w_up), weight(w_down), model, model, model, model,
            vm((rs - 1, 8, rows), f32), vm((8, rows), f32), vm((8, rows), f32),
            DMA((3,)), *both(2, rs), *both(2, rs), *both(3), *both(rs - 1),
        ],
        (dgu, dot, norm2_gain, cg, h1, s2, hid_all),
        (w_gate, w_up, w_down),
        45,
    )
    g_middle = (product(n2, dg_all), product(n2, du_all), product(go_all, dmix))
    g_middle, g_down = lax.optimization_barrier((g_middle, g_down))
    g_gate, g_up, g_out = lax.psum(g_middle, "dp")
    dz_all, dxi_all, small, y_out, dx_out = in_vmem(
        functools.partial(backward_kernel, rank=rank, model_width=model_width),
        "backward",
        2,
        [
            ((rows, rs * width), bf16), ((rows, rs * width), bf16), ((2 * RANK_LANES, width), bf16),
            ((block, wide_d), bf16), ((block, wide_d), bf16),
        ],
        [
            weight(w_out), weight(w_in_x), weight(w_in_z), vm((RANK_LANES, width), bf16), big, *line(rs, width),
            vm((rows + 1, count, width), f32), vm((rows, count, width), f32), tile, tile, tile, tile,
            big, big, big, big, big, big, big, vm((rows, RANK_LANES), f32), *sums_scratch,
            vm((rows, RANK_LANES), f32), model, model, *sums, vm((8, rows), f32), vm((8, rows), f32),
            vm((2, dp, block, wide_d), bf16), vm((rows, wide_d), bf16), vm((2, dp, block, wide_d), bf16),
            DMA((3,)), *both(dp), *both(dp), *both(2, rs), *both(rs - 1), *both(rs + 1), *both(2, rs), *both(2),
            *both(rs - 1),
        ],
        (
            lengths, seq_order, y, dmix, z, yv, xi, proj, place, conv_taps, conv_b, w_xp, w_dt, dt_bias, rate,
            skip_weight, xg, s1, norm1_gain, dh1, gnorm2,
        ),
        (w_out, w_in_x, w_in_z),
        85,
    )
    g_late = (product(n1, dxi_all), product(n1, dz_all), small)
    g_late, (g_gate, g_up, g_out) = lax.optimization_barrier((g_late, (g_gate, g_up, g_out)))
    g_x, g_z, small = lax.psum(g_late, "dp")
    small = small.astype(f32)
    at = RANK_LANES + rank
    return (
        y_out,
        dx_out,
        small[at + count + taps + 3],
        g_x.astype(f32),
        g_z.astype(f32),
        small[at + count : at + count + taps].T,
        small[at + count + taps],
        small[:RANK_LANES].T,
        small[RANK_LANES:at],
        small[at + count + taps + 1],
        small[at : at + count].T,
        small[at + count + taps + 2],
        g_out.astype(f32),
        small[at + count + taps + 4],
        g_gate.astype(f32),
        g_up.astype(f32),
        g_down.astype(f32),
    )


def on_device(
    x_in,
    lengths,
    seq_order,
    norm1_gain,
    w_in_x,
    w_in_z,
    conv_w,
    conv_b,
    w_xp,
    w_dt,
    dt_bias,
    a_log,
    skip_weight,
    w_out,
    norm2_gain,
    w_gate,
    w_up,
    w_down,
    cotangent,
):
    rows_in, width_row = x_in.shape
    row_devices = lax.axis_size("row")
    col_devices = lax.axis_size("col")
    group_rows = rows_in * col_devices
    model_width = width_row * row_devices
    rank_cols = w_dt.shape[0]
    state_count = a_log.shape[1]
    channels = conv_w.shape[0]
    ff_cols = w_gate.shape[1]
    my_group = lax.axis_index("dp")
    my_column = lax.axis_index("col")
    source, position_all = layout(lengths, seq_order, group_rows)
    my_source = lax.dynamic_index_in_dim(source, my_group, 0, keepdims=False)
    position = lax.dynamic_index_in_dim(position_all, my_group, 0, keepdims=False)
    slice_source = lax.dynamic_slice_in_dim(my_source, my_column * rows_in, rows_in, 0)

    def row_total(values):
        return lax.psum(values, "row")

    def token_rows(values):
        return lax.all_gather(values, "col", axis=0, tiled=True)

    def row_pieces(values):
        return lax.all_gather(values, "row", axis=0, tiled=True)

    def col_reduce(term_fn):
        return lax.psum_scatter(
            term_fn(jnp.int32(0), lax.axis_size("col") * rows_in),
            "col",
            scatter_dimension=0,
            tiled=True,
        )

    def row_reduce(term_fn, keep_rows):
        return lax.psum_scatter(
            term_fn(jnp.int32(0), lax.axis_size("row") * keep_rows),
            "row",
            scatter_dimension=0,
            tiled=True,
        )

    def projection_total(values):
        return lax.psum(values, ("row", "col"))

    blank_rows = jnp.zeros((rows_in, width_row), jnp.bfloat16)
    pieces = (
        lax.all_gather(x_in, ("dp", "col"), axis=0, tiled=True),
        lax.all_gather(cotangent, ("dp", "col"), axis=0, tiled=True),
    )
    row_count = pieces[0].shape[0]
    offset = slice_source
    inside = ((offset >= 0) & (offset < row_count))[:, None]
    index = jnp.clip(offset, 0, row_count - 1)
    x_rows = jnp.where(inside, jnp.take(pieces[0], index, axis=0), blank_rows)
    cot_rows = jnp.where(inside, jnp.take(pieces[1], index, axis=0), blank_rows)
    x_val = x_rows.astype(jnp.float32)
    scale_one = lax.rsqrt(row_total(jnp.sum(x_val * x_val, axis=1)) / model_width + epsilon)
    normed_one = (x_val * scale_one[:, None] * norm1_gain[None, :]).astype(jnp.bfloat16)
    normed_all = token_rows(normed_one)

    def inner_term(begin_row, row_count):
        return jnp.concatenate(
            [contract(w_in_x, normed_all, 0, 1), contract(w_in_z, normed_all, 0, 1)], axis=1
        )

    inner = row_reduce(inner_term, channels)
    inner_x = inner[:, :group_rows]
    inner_z = inner[:, group_rows:]

    def conv_part(values, kernel, kernel_bias):
        return convolve(values, kernel, kernel_bias, position)

    conv_out, conv_pull = jax.vjp(conv_part, inner_x, conv_w, conv_b)
    u_low = conv_out.astype(jnp.bfloat16)
    u_val = u_low.astype(jnp.float32)
    projected = projection_total(contract(w_xp, u_low, 0, 0))
    step_low = projected[:rank_cols].astype(jnp.bfloat16)
    pre_step = contract(w_dt, step_low, 0, 0) + dt_bias[:, None]
    step_size = jax.nn.softplus(pre_step)

    decay_rate = -jnp.exp(a_log).T
    proj_rows = projected.T
    u_rows = u_val.T
    step_rows = step_size.T
    gone_rows = jnp.where(position[:, None] > 0, step_rows, 1e30)
    drive_rows = step_rows * u_rows
    at_b, at_c = rank_cols, rank_cols + state_count
    scanned = scan_alone(proj_rows, step_rows, gone_rows, drive_rows, decay_rate, at_b, at_c)
    mixer_y = scanned.T + skip_weight[:, None] * u_val
    gated = mixer_y * jax.nn.silu(inner_z)
    gated_low = gated.astype(jnp.bfloat16)
    gated_all = row_pieces(gated_low)

    def mix_term(begin_row, row_count):
        return contract(gated_all, w_out, 0, 0)

    first_sum = x_val + col_reduce(mix_term)
    scale_two = lax.rsqrt(row_total(jnp.sum(first_sum * first_sum, axis=1)) / model_width + epsilon)
    normed_two = (first_sum * scale_two[:, None] * norm2_gain[None, :]).astype(jnp.bfloat16)
    normed_rows = token_rows(normed_two)

    def ffn_term(begin_row, row_count):
        return jnp.concatenate(
            [
                jnp.dot(normed_rows, w_gate, preferred_element_type=jnp.float32),
                jnp.dot(normed_rows, w_up, preferred_element_type=jnp.float32),
            ],
            axis=1,
        )

    gate_up = row_reduce(ffn_term, group_rows // row_devices)
    gate_val = gate_up[:, :ff_cols]
    up_val = gate_up[:, ff_cols:]
    hidden = (jax.nn.silu(gate_val) * up_val).astype(jnp.bfloat16)
    hidden_all = row_pieces(hidden)

    def down_term(begin_row, row_count):
        return jnp.dot(hidden_all, w_down, preferred_element_type=jnp.float32)

    second_sum = first_sum + col_reduce(down_term)
    out_low = second_sum.astype(jnp.bfloat16)
    back_down_all = token_rows(cot_rows)
    grad_down = contract(hidden_all, back_down_all, 0, 0)

    def hidden_term(begin_row, row_count):
        return contract(back_down_all, w_down, 1, 1)

    d_hidden = row_reduce(hidden_term, group_rows // row_devices)
    d_gate = (d_hidden * up_val * silu_slope(gate_val)).astype(jnp.bfloat16)
    d_up = (d_hidden * jax.nn.silu(gate_val)).astype(jnp.bfloat16)
    d_gate_up_all = row_pieces(jnp.concatenate([d_gate, d_up], axis=1))
    grad_gate = contract(normed_rows, d_gate_up_all[:, :ff_cols], 0, 0)
    grad_up = contract(normed_rows, d_gate_up_all[:, ff_cols:], 0, 0)

    def norm_two_term(begin_row, row_count):
        return contract(d_gate_up_all[:, :ff_cols], w_gate, 1, 1) + contract(
            d_gate_up_all[:, ff_cols:], w_up, 1, 1
        )

    d_normed_two = col_reduce(norm_two_term)
    cot_val = cot_rows.astype(jnp.float32)
    weighted_two = d_normed_two * norm2_gain[None, :]
    grad_norm_two = jnp.sum(d_normed_two * first_sum * scale_two[:, None], axis=0)
    dot_two = row_total(jnp.sum(weighted_two * first_sum, axis=1))
    d_first = (
        cot_val
        + scale_two[:, None] * weighted_two
        - first_sum * (scale_two**3 * dot_two / model_width)[:, None]
    )
    d_mix_all = token_rows(d_first.astype(jnp.bfloat16))
    grad_out = contract(gated_all, d_mix_all, 1, 0)

    def gated_term(begin_row, row_count):
        return contract(w_out, d_mix_all, 1, 1)

    d_gated = row_reduce(gated_term, channels)
    d_inner_z = d_gated * mixer_y * silu_slope(inner_z)
    d_mixer = d_gated * jax.nn.silu(inner_z)
    d_u_rows, d_step_rows, d_proj_rows, grad_rate_rows = adjoint_alone(
        proj_rows, step_rows, gone_rows, drive_rows, u_rows, d_mixer.T, decay_rate, at_b, at_c
    )
    d_u_mix = d_u_rows.T + skip_weight[:, None] * d_mixer
    d_step = d_step_rows.T
    d_enter = d_proj_rows.T[at_b:at_c]
    d_leave = d_proj_rows.T[at_c:]
    grad_rate = grad_rate_rows.T
    grad_skip = jnp.sum(d_mixer * u_val, axis=1)
    d_pre = d_step * jax.nn.sigmoid(pre_step)
    grad_step_bias = jnp.sum(d_pre, axis=1)
    d_pre_low = d_pre.astype(jnp.bfloat16)
    grad_step_w = contract(step_low, d_pre_low, 1, 1)
    d_projected = projection_total(
        jnp.concatenate(
            [jnp.dot(w_dt, d_pre_low, preferred_element_type=jnp.float32), d_enter, d_leave], axis=0
        )
    )
    d_proj_low = d_projected.astype(jnp.bfloat16)
    grad_proj_w = contract(u_low, d_proj_low, 1, 1)
    d_u_all = d_u_mix + jnp.dot(w_xp, d_proj_low, preferred_element_type=jnp.float32)
    d_inner_x, grad_kernel, grad_kernel_bias = conv_pull(d_u_all)
    d_inner_all = row_pieces(
        jnp.concatenate([d_inner_x.astype(jnp.bfloat16), d_inner_z.astype(jnp.bfloat16)], axis=1)
    )
    grad_in_x = contract(normed_all, d_inner_all[:, :group_rows], 0, 1)
    grad_in_z = contract(normed_all, d_inner_all[:, group_rows:], 0, 1)

    def norm_one_term(begin_row, row_count):
        piece_x = lax.dynamic_slice_in_dim(d_inner_all, begin_row, row_count, 1)
        piece_z = lax.dynamic_slice_in_dim(d_inner_all, group_rows, row_count, 1)
        return contract(piece_x, w_in_x, 0, 1) + contract(piece_z, w_in_z, 0, 1)

    d_normed_one = col_reduce(norm_one_term)
    weighted_one = d_normed_one * norm1_gain[None, :]
    grad_norm_one = jnp.sum(d_normed_one * x_val * scale_one[:, None], axis=0)
    dot_one = row_total(jnp.sum(weighted_one * x_val, axis=1))
    d_input = (
        d_first
        + scale_one[:, None] * weighted_one
        - x_val * (scale_one**3 * dot_one / model_width)[:, None]
    )
    d_input_low = d_input.astype(jnp.bfloat16)
    grad_norm_one, grad_norm_two = lax.psum((grad_norm_one, grad_norm_two), ("dp", "col"))
    (
        grad_in_x,
        grad_in_z,
        grad_kernel,
        grad_kernel_bias,
        grad_proj_w,
        grad_step_w,
        grad_step_bias,
        grad_rate,
        grad_skip,
        grad_out,
        grad_gate,
        grad_up,
        grad_down,
    ) = (
        lax.psum(grad_in_x.astype(jnp.bfloat16), "dp").astype(jnp.float32),
        lax.psum(grad_in_z.astype(jnp.bfloat16), "dp").astype(jnp.float32),
        lax.psum(grad_kernel.astype(jnp.bfloat16), "dp").astype(jnp.float32),
        lax.psum(grad_kernel_bias.astype(jnp.bfloat16), "dp").astype(jnp.float32),
        lax.psum(grad_proj_w.astype(jnp.bfloat16), "dp").astype(jnp.float32),
        lax.psum(grad_step_w.astype(jnp.bfloat16), "dp").astype(jnp.float32),
        lax.psum(grad_step_bias.astype(jnp.bfloat16), "dp").astype(jnp.float32),
        lax.psum(grad_rate.astype(jnp.bfloat16), "dp").astype(jnp.float32),
        lax.psum(grad_skip.astype(jnp.bfloat16), "dp").astype(jnp.float32),
        lax.psum(grad_out.astype(jnp.bfloat16), "dp").astype(jnp.float32),
        lax.psum(grad_gate.astype(jnp.bfloat16), "dp").astype(jnp.float32),
        lax.psum(grad_up.astype(jnp.bfloat16), "dp").astype(jnp.float32),
        lax.psum(grad_down.astype(jnp.bfloat16), "dp").astype(jnp.float32),
    )
    payload = jnp.concatenate([out_low, d_input_low], axis=1)
    tokens_all = lengths.shape[0] * group_rows
    owner = (
        jnp.zeros((tokens_all,), jnp.int32)
        .at[source.reshape(-1)]
        .set(jnp.arange(tokens_all, dtype=jnp.int32))
    )
    my_rows = lax.dynamic_slice_in_dim(
        owner, (my_group * col_devices + my_column) * rows_in, rows_in, 0
    )
    pieces = lax.all_gather(payload, ("dp", "col"), axis=0, tiled=True)
    row_count = pieces.shape[0]
    offset = my_rows
    inside = ((offset >= 0) & (offset < row_count))[:, None]
    returned = jnp.where(
        inside,
        jnp.take(pieces, jnp.clip(offset, 0, row_count - 1), axis=0),
        jnp.zeros_like(payload),
    )
    y_out = returned[:, :width_row]
    dx_out = returned[:, width_row:]
    return (
        y_out,
        dx_out,
        grad_norm_one,
        grad_in_x,
        grad_in_z,
        grad_kernel,
        grad_kernel_bias,
        grad_proj_w,
        grad_step_w,
        grad_step_bias,
        grad_rate,
        grad_skip,
        grad_out,
        grad_norm_two,
        grad_gate,
        grad_up,
        grad_down,
    )


def solution(mesh):
    placed = (
        P(("dp", "col"), "row"),
        P(),
        P(),
        P("row"),
        P("row", "col"),
        P("row", "col"),
        P(("col", "row"), None),
        P(("col", "row")),
        P(("col", "row"), None),
        P(None, ("col", "row")),
        P(("col", "row")),
        P(("col", "row"), None),
        P(("col", "row")),
        P("col", "row"),
        P("row"),
        P("row", "col"),
        P("row", "col"),
        P("col", "row"),
        P(("dp", "col"), "row"),
    )
    paired = mesh.shape["col"] == 2
    return jax.shard_map(
        on_pairs if paired else on_device,
        mesh=mesh,
        in_specs=placed,
        out_specs=(
            P(("dp", "col"), "row"),
            P(("dp", "col"), "row"),
            P("row"),
            P("row", "col"),
            P("row", "col"),
            P(("col", "row"), None),
            P(("col", "row")),
            P(("col", "row"), None),
            P(None, ("col", "row")),
            P(("col", "row")),
            P(("col", "row"), None),
            P(("col", "row")),
            P("col", "row"),
            P("row"),
            P("row", "col"),
            P("row", "col"),
            P("col", "row"),
        ),
        check_vma=False,
    )
```

```python
import functools

import jax
import jax.numpy as jnp
from jax import lax
from jax.experimental import pallas as pl
from jax.experimental.pallas import tpu as pltpu
from jax.sharding import PartitionSpec as P

epsilon = 1e-05


def layout(lengths, seq_order, group_rows):
    flat_lengths = lengths.reshape(-1)
    total_seqs = flat_lengths.shape[0]
    slot_length = jnp.take(flat_lengths, seq_order)
    input_start = jnp.cumsum(slot_length) - slot_length
    slot_of = (
        jnp.zeros((total_seqs,), jnp.int32)
        .at[seq_order]
        .set(jnp.arange(total_seqs, dtype=jnp.int32))
    )
    seq_input = jnp.take(input_start, slot_of).reshape(lengths.shape)
    group_start = jnp.cumsum(lengths, axis=1) - lengths
    places = jnp.arange(group_rows, dtype=jnp.int32)
    member = (
        jnp.sum((places[None, :, None] >= group_start[:, None, :]).astype(jnp.int32), axis=2) - 1
    )
    begin_at = jnp.take_along_axis(group_start, member, axis=1)
    within = places[None, :] - begin_at
    source = jnp.take_along_axis(seq_input, member, axis=1) + within
    return (source, within)


def silu_slope(values):
    sigmoid_v = jax.nn.sigmoid(values)
    return sigmoid_v * (1.0 + values * (1.0 - sigmoid_v))


def contract(left, right, left_dim, right_dim):
    return lax.dot_general(
        left, right, (((left_dim,), (right_dim,)), ((), ())), preferred_element_type=jnp.float32
    )


def convolve(inner_x, kernel, kernel_bias, places):
    tap_count = kernel.shape[1]
    conv_sum = kernel_bias[:, None] + inner_x * kernel[:, tap_count - 1][:, None]
    for shift_by in range(1, tap_count):
        shifted = jnp.pad(inner_x, ((0, 0), (shift_by, 0)))[:, :-shift_by]
        conv_sum = (
            conv_sum
            + shifted
            * (places >= shift_by).astype(jnp.float32)[None, :]
            * kernel[:, tap_count - 1 - shift_by][:, None]
        )
    return jax.nn.silu(conv_sum)


MESH = pl.DeviceIdType.MESH
f32 = jnp.float32
bf16 = jnp.bfloat16


def remote(src, dst, send, recv, where):
    return pltpu.make_async_remote_copy(
        src_ref=src, dst_ref=dst, send_sem=send, recv_sem=recv, device_id=where, device_id_type=MESH
    )


def away(axis, offset):
    return {axis: lax.rem(lax.axis_index(axis) + offset, lax.axis_size(axis))}


def greet(*axes):
    barrier = pltpu.get_barrier_semaphore()
    total = 0
    for axis in axes:
        for offset in range(1, lax.axis_size(axis)):
            pl.semaphore_signal(barrier, inc=1, device_id=away(axis, offset), device_id_type=MESH)
            total += 1
    pl.semaphore_wait(barrier, total)


def matmul(left, right):
    return jnp.dot(left, right, preferred_element_type=f32)


def silu(values):
    return values * jax.nn.sigmoid(values)


def rows_form(values):
    ones = jnp.ones((8, values.shape[1]), f32)
    return lax.dot_general(
        ones,
        values,
        (((1,), (1,)), ((), ())),
        precision=lax.Precision.HIGHEST,
        preferred_element_type=f32,
    )


def column_form(row_values):
    return jnp.transpose(row_values)[:, 0:1]


class Line:
    def __init__(self, axis, send, recv):
        self.axis, self.send, self.recv = axis, send, recv
        self.size = lax.axis_size(axis)
        self.me = lax.axis_index(axis)

    def right(self, src, dst, d):
        return remote(
            src, dst, self.send.at[0, d], self.recv.at[0, d], {self.axis: jnp.minimum(self.me + 1, self.size - 1)}
        )

    def left(self, src, dst, d):
        return remote(
            src, dst, self.send.at[1, d], self.recv.at[1, d], {self.axis: jnp.maximum(self.me - 1, 0)}
        )


def line_gather(axis, slot_of, send, recv):
    line = Line(axis, send, recv)
    size, me = line.size, line.me
    last = size - 1

    def go_right(s):
        slot = jnp.maximum(me - s, 0)
        return (me - s >= 0) & (me < last), line.right(slot_of(slot), slot_of(slot), slot)

    def go_left(s):
        slot = jnp.minimum(me + s, last)
        return (me + s <= last) & (me > 0), line.left(slot_of(slot), slot_of(slot), slot)

    for s in range(last):
        for valid, copy in (go_right(s), go_left(s)):
            pl.when(valid)(copy.start)
        yield
        slot = jnp.maximum(me - 1 - s, 0)
        pl.when(me - 1 - s >= 0)(line.right(slot_of(slot), slot_of(slot), slot).wait_recv)
        slot = jnp.minimum(me + 1 + s, last)
        pl.when(me + 1 + s <= last)(line.left(slot_of(slot), slot_of(slot), slot).wait_recv)
    yield
    for s in range(last):
        for valid, copy in (go_right(s), go_left(s)):
            pl.when(valid)(copy.wait_send)


def line_scatter(axis, block_of, out, held, from_left, from_right, send, recv):
    line = Line(axis, send, recv)
    size, me = line.size, line.me
    last = size - 1

    def right_at(t):
        d = jnp.clip(last - t + me, 0, last)
        return (t >= me) & (me < last), d, line.right(held.at[d], from_left.at[d], d)

    def left_at(t):
        d = jnp.clip(t - (last - me), 0, last)
        return (t >= last - me) & (me > 0), d, line.left(held.at[d], from_right.at[d], d)

    def pass_on(valid, first, d, copy, arrived):
        @pl.when(valid)
        def _():
            part = block_of(d)

            @pl.when(jnp.logical_not(first))
            def _():
                copy.wait_recv()
                held[d] = (part + arrived[d].astype(f32)).astype(held.dtype)

            @pl.when(first)
            def _():
                held[d] = part.astype(held.dtype)

            copy.start()

    for t in range(last):
        valid, d, copy = right_at(t)
        pass_on(valid, me == 0, d, copy, from_left)
        valid, d, copy = left_at(t)
        pass_on(valid, me == last, d, copy, from_right)
        if t == 0:
            out[...] = block_of(me)
        yield
    yield

    @pl.when(me > 0)
    def _():
        line.right(held.at[me], from_left.at[me], me).wait_recv()
        out[...] += from_left[me].astype(f32)

    @pl.when(me < last)
    def _():
        line.left(held.at[me], from_right.at[me], me).wait_recv()
        out[...] += from_right[me].astype(f32)

    for t in range(last):
        for valid, _, copy in (right_at(t), left_at(t)):
            pl.when(valid)(copy.wait_send)


def run(*flows, pump=None):
    flows = list(flows)
    turn = 0
    while flows:
        flows = [flow for flow in flows if next(flow, flows) is not flows]
        if pump is not None and turn < len(pump[1]):
            pump[0].pump(pump[1][turn])
        turn += 1


def lanes(ref, size):
    return lambda d: ref.at[:, pl.ds(pl.multiple_of(d * size, size), size)]


def fetch(sources, targets, sems):
    copies = [pltpu.make_async_copy(s, t, sems.at[i]) for i, (s, t) in enumerate(zip(sources, targets))]
    for copy in copies:
        copy.start()
    return copies


def as_row(ref):
    return ref[...].reshape(1, ref.shape[0])


def lengths_row(lens):
    groups, per_group = lens.shape
    values = lens[...].astype(f32)
    at = lax.broadcasted_iota(jnp.int32, (per_group, groups * per_group), 1)
    inner = lax.broadcasted_iota(jnp.int32, (per_group, groups * per_group), 0)
    total = jnp.zeros((1, groups * per_group), f32)
    for g in range(groups):
        place = jnp.where(at == inner + g * per_group, 1.0, 0.0)
        total = total + jnp.dot(
            values[g : g + 1, :], place, precision=lax.Precision.HIGHEST, preferred_element_type=f32
        )
    return total


def spray(axis, src_of, dst, send, recv, base=0):
    copies = []
    for k in range(1, lax.axis_size(axis)):
        copy = remote(src_of(k), dst.at[k - 1], send.at[base + k - 1], recv.at[base + k - 1], away(axis, k))
        copy.start()
        copies.append(copy)
    return copies


def wait_all(copies):
    for copy in copies:
        copy.wait()


def swap(axis, src, dst, send, recv):
    copy = remote(src, dst, send, recv, away(axis, 1))
    copy.start()
    return copy


def sequence_rows(lens_row, order_row, per_group):
    count = lens_row.shape[1]
    ri = lax.broadcasted_iota(jnp.int32, (count, count), 0)
    ci = lax.broadcasted_iota(jnp.int32, (count, count), 1)
    lens_f = lens_row

    def to_column(row):
        return jnp.sum(jnp.where(ri == ci, row, 0.0), axis=1, keepdims=True)

    order_col = to_column(order_row.astype(f32)).astype(jnp.int32)
    lens_col = to_column(lens_f)
    pick = order_row == ri
    pick_t = order_col == ci
    slot_col = jnp.sum(jnp.where(pick_t, lens_f, 0.0), axis=1, keepdims=True)
    slot_row = jnp.sum(jnp.where(pick, lens_col, 0.0), axis=0, keepdims=True)
    start_col = jnp.sum(jnp.where(ci < ri, slot_row, 0.0), axis=1, keepdims=True)
    input_row = jnp.sum(jnp.where(pick_t, start_col, 0.0), axis=0, keepdims=True)
    same = (ri // per_group) == (ci // per_group)
    group_row = jnp.sum(jnp.where((ri < ci) & same, lens_col, 0.0), axis=0, keepdims=True)
    return lens_f, input_row, group_row


def place_rows(lens_row, order_row, per_group, group_rows, group):
    lens_f, input_row, group_row = sequence_rows(lens_row, order_row, per_group)
    count = lens_row.shape[1]
    rows = lax.broadcasted_iota(jnp.int32, (group_rows, count), 0).astype(f32)
    mine = (lax.broadcasted_iota(jnp.int32, (group_rows, count), 1) // per_group) == group
    inside = (rows >= group_row) & (rows < group_row + lens_f) & mine
    within = jnp.sum(jnp.where(inside, rows - group_row, 0.0), axis=1, keepdims=True)
    begin = jnp.sum(jnp.where(inside, input_row, 0.0), axis=1, keepdims=True)
    return begin + within, within


def owner_rows(lens_row, order_row, per_group, group_rows, block_rows, first):
    lens_f, input_row, group_row = sequence_rows(lens_row, order_row, per_group)
    count = lens_row.shape[1]
    rows = (lax.broadcasted_iota(jnp.int32, (block_rows, count), 0) + first).astype(f32)
    base = (lax.broadcasted_iota(jnp.int32, (block_rows, count), 1) // per_group) * group_rows
    inside = (rows >= input_row) & (rows < input_row + lens_f)
    found = jnp.where(inside, base.astype(f32) + group_row + rows - input_row, 0.0)
    return jnp.sum(found, axis=1, keepdims=True)


def plane_origin(rows, dp_size, col_size, block_rows):
    at = lax.broadcasted_iota(jnp.int32, (rows, dp_size * col_size * block_rows), 1)
    block = at // block_rows
    group = lax.rem(block, dp_size)
    column = block // dp_size
    return ((group * col_size + column) * block_rows + lax.rem(at, block_rows)).astype(f32)


def pick_rows(wanted, held):
    col_size, dp_size, block_rows, width = held.shape
    total = col_size * dp_size * block_rows
    chosen = wanted == plane_origin(wanted.shape[0], dp_size, col_size, block_rows)
    chosen = jnp.where(chosen, 1.0, 0.0).astype(bf16)
    return matmul(chosen, held.reshape(total, width)).astype(bf16)


def plane_start(src, held, send, recv):
    me, column = lax.axis_index("dp"), lax.axis_index("col")
    held[column, me] = src[...]
    copies = []
    for k in range(1, lax.axis_size("dp")):
        copy = remote(src, held.at[column, me], send.at[k], recv.at[k], away("dp", k))
        copy.start()
        copies.append(copy)
    return copies


def plane_finish(copies, held, send, recv):
    column = lax.axis_index("col")
    for copy in copies:
        copy.wait_recv()
    copy = swap("col", held.at[column], held.at[column], send.at[0], recv.at[0])
    copy.wait_recv()
    for one in copies + [copy]:
        one.wait_send()


def total_of_sums(part, half_own, half_in, low_own, low_in, full, sems):
    send, recv = sems
    rows = part.shape[0] // 2
    column = lax.axis_index("col")
    mine = pl.ds(pl.multiple_of(column * rows, rows), rows)
    other = pl.ds(pl.multiple_of((1 - column) * rows, rows), rows)
    half_own[...] = part[other, :]
    copy = swap("col", half_own, half_in, send.at[0], recv.at[0])
    copy.wait()
    low_own[...] = (part[mine, :] + half_in[...]).astype(bf16)
    copies = spray("row", lambda k: low_own, low_in, send, recv, 1)
    wait_all(copies)
    total = low_own[...].astype(f32)
    for k in range(low_in.shape[0]):
        total = total + low_in[k].astype(f32)
    full[mine, :] = total
    copy = swap("col", full.at[mine], full.at[mine], send.at[4], recv.at[4])
    copy.wait()


def lanes_like(tile, width):
    if tile.shape[-1] == width:
        return tile
    return jnp.concatenate([tile] * (width // tile.shape[-1]), axis=-1)


def lane_mask(count, lanes, first):
    lane = lax.broadcasted_iota(jnp.int32, (count, lanes), 1)
    return lane == lax.broadcasted_iota(jnp.int32, (count, lanes), 0) + first


def spread(values, first, count, wide):
    rows, lanes = values.shape
    chosen = jnp.where(lane_mask(count, lanes, first)[None], values[:, None, :], 0.0)
    chosen = chosen.reshape(rows * count, lanes)
    high = chosen.astype(bf16)
    rest = (chosen - high.astype(f32)).astype(bf16)
    ones = jnp.ones((lanes, wide), bf16)
    return matmul(high, ones) + matmul(rest, ones)


def lane_sums(values, first, lanes):
    rows, count, wide = values.shape
    flat = values.reshape(rows * count, wide)
    high = flat.astype(bf16)
    rest = (flat - high.astype(f32)).astype(bf16)
    ones = jnp.ones((wide, lanes), bf16)
    sums = (matmul(high, ones) + matmul(rest, ones)).reshape(rows, count, lanes)
    return jnp.sum(jnp.where(lane_mask(count, lanes, first)[None], sums, 0.0), axis=1)


def scan_forward(proj, b_at, c_at, step, gone_step, drive, rate, bb, cb, y):
    rows, width = drive.shape
    count = rate.shape[0]
    piece, _, wide = bb.shape

    def part(j, state):
        start = pl.multiple_of(j * piece, piece)
        values = proj[pl.ds(start, piece), :]
        bb[...] = spread(values, b_at, count, wide).reshape(bb.shape)
        cb[...] = spread(values, c_at, count, wide).reshape(cb.shape)

        def eight(k, state):
            inner = pl.multiple_of(k * 8, 8)
            base = pl.multiple_of(start + k * 8, 8)
            gone = gone_step[pl.ds(base, 8), :]
            driven = drive[pl.ds(base, 8), :]
            found = []
            for i in range(8):
                decay = jnp.exp(gone[i : i + 1, :] * rate)
                state = decay * state + driven[i : i + 1, :] * lanes_like(bb[inner + i], width)
                found.append(jnp.sum(state * lanes_like(cb[inner + i], width), axis=0, keepdims=True))
            y[pl.ds(base, 8), :] = jnp.concatenate(found, axis=0)
            return state

        return lax.fori_loop(0, piece // 8, eight, state)

    lax.fori_loop(0, rows // piece, part, jnp.zeros((count, width), f32))


def scan_states(proj, b_at, gone_step, drive, rate, bb, hs):
    rows, width = drive.shape
    count = rate.shape[0]
    piece, _, wide = bb.shape
    hs[0] = jnp.zeros((count, width), f32)
    for start in range(0, rows, piece):
        bb[...] = spread(proj[start : start + piece, :], b_at, count, wide).reshape(bb.shape)

        def eight(k, state):
            inner = pl.multiple_of(k * 8, 8)
            base = pl.multiple_of(start + k * 8, 8)
            gone = gone_step[pl.ds(base, 8), :]
            driven = drive[pl.ds(base, 8), :]
            for i in range(8):
                decay = jnp.exp(gone[i : i + 1, :] * rate)
                state = decay * state + driven[i : i + 1, :] * lanes_like(bb[inner + i], width)
                hs[base + i + 1] = state
            return state

        lax.fori_loop(0, piece // 8, eight, hs[start])
        yield


def scan_backward(
    proj, b_at, c_at, step, gone_step, drive, inner_u, dy, rate, hs, bb, cb, pb, pc, du, dstep, dproj
):
    rows, width = drive.shape
    count = rate.shape[0]
    piece, _, wide = bb.shape

    def fold(values):
        total = values[:, 0:wide]
        for j in range(1, width // wide):
            total = total + values[:, j * wide : (j + 1) * wide]
        return total

    def part(j, carry):
        start = pl.multiple_of((rows // piece - 1 - j) * piece, piece)
        values = proj[pl.ds(start, piece), :]
        bb[...] = spread(values, b_at, count, wide).reshape(bb.shape)
        cb[...] = spread(values, c_at, count, wide).reshape(cb.shape)

        def eight(k, carry):
            later, total = carry
            inner = pl.multiple_of((piece // 8 - 1 - k) * 8, 8)
            base = pl.multiple_of(start + inner, 8)
            step8 = step[pl.ds(base, 8), :]
            gone8 = gone_step[pl.ds(base, 8), :]
            drive8 = drive[pl.ds(base, 8), :]
            u8 = inner_u[pl.ds(base, 8), :]
            dy8 = dy[pl.ds(base, 8), :]
            by_b = [None] * 8
            by_rate = [None] * 8
            for i in reversed(range(8)):
                dy_row = dy8[i : i + 1, :]
                lam = lanes_like(cb[inner + i], width) * dy_row + later
                later = jnp.exp(gone8[i : i + 1, :] * rate) * lam
                kept = later * hs[base + i]
                total = total + kept * step8[i : i + 1, :]
                by_b[i] = jnp.sum(lam * lanes_like(bb[inner + i], width), axis=0, keepdims=True)
                by_rate[i] = jnp.sum(kept * rate, axis=0, keepdims=True)
                pb[inner + i] = fold(lam * drive8[i : i + 1, :])
                pc[inner + i] = fold(hs[base + i + 1] * dy_row)
            by_b = jnp.concatenate(by_b, axis=0)
            by_rate = jnp.concatenate(by_rate, axis=0)
            du[pl.ds(base, 8), :] = by_b * step8
            dstep[pl.ds(base, 8), :] = by_rate + by_b * u8
            return later, total

        carry = lax.fori_loop(0, piece // 8, eight, carry)
        dproj[pl.ds(start, piece), :] += lane_sums(pb[...], b_at, dproj.shape[1]) + lane_sums(
            pc[...], c_at, dproj.shape[1]
        )
        return carry

    blank = jnp.zeros((count, width), f32)
    _, total = lax.fori_loop(0, rows // piece, part, (blank, blank))
    return total * rate


RANK_LANES = 128


def scan_kernel(proj, step, gone, drive, rate, y, bb, cb, *, b_at, c_at):
    scan_forward(proj, b_at, c_at, step, gone, drive, rate[...], bb, cb, y=y)


def adjoint_kernel(
    proj, step, gone, drive, inner_u, dy, rate, du, dstep, dproj, drate, bb, cb, hs, pb, pc, *, b_at, c_at
):
    run(scan_states(proj, b_at, gone, drive, rate[...], bb, hs))
    dproj[...] = jnp.zeros_like(dproj)
    drate[...] = scan_backward(
        proj, b_at, c_at, step, gone, drive, inner_u, dy, rate[...], hs, bb, cb, pb, pc, du, dstep, dproj
    )


def scan_sizes(rows, width, count):
    wide = 128 if width % 128 == 0 else width
    piece = min(128, rows)
    return pltpu.VMEM((piece, count, wide), f32)


def scan_alone(proj, step, gone, drive, rate, b_at, c_at):
    rows, width = step.shape
    block = scan_sizes(rows, width, rate.shape[0])
    return pl.pallas_call(
        functools.partial(scan_kernel, b_at=b_at, c_at=c_at),
        out_shape=jax.ShapeDtypeStruct((rows, width), f32),
        scratch_shapes=[block, block],
        compiler_params=pltpu.CompilerParams(vmem_limit_bytes=VMEM_BYTES),
        name="scan_states",
    )(proj, step, gone, drive, rate)


def adjoint_alone(proj, step, gone, drive, inner_u, dy, rate, b_at, c_at):
    rows, width = step.shape
    count = rate.shape[0]
    block = scan_sizes(rows, width, count)
    shape = jax.ShapeDtypeStruct
    return pl.pallas_call(
        functools.partial(adjoint_kernel, b_at=b_at, c_at=c_at),
        out_shape=(
            shape((rows, width), f32),
            shape((rows, width), f32),
            shape(proj.shape, f32),
            shape((count, width), f32),
        ),
        scratch_shapes=[
            block,
            block,
            pltpu.VMEM((rows + 1, count, width), f32),
            block,
            block,
        ],
        compiler_params=pltpu.CompilerParams(vmem_limit_bytes=VMEM_BYTES),
        name="scan_adjoint",
    )(proj, step, gone, drive, inner_u, dy, rate)


def conv_sum(inner_x, place, taps, bias):
    count = taps.shape[0]
    total = bias + inner_x * taps[count - 1 : count, :]
    for shift in range(1, count):
        moved = jnp.where(place >= shift, pltpu.roll(inner_x, shift, 0), 0.0)
        total = total + moved * taps[count - 1 - shift : count - shift, :]
    return total


def transposed(left, right):
    return lax.dot_general(left, right, (((1,), (1,)), ((), ())), preferred_element_type=f32)


def over_rows(left, right):
    return lax.dot_general(left, right, (((0,), (0,)), ((), ())), preferred_element_type=f32)


def columns(d, size):
    return pl.ds(pl.multiple_of(d * size, size), size)


def line_total(own, arrived):
    total = own
    for k in range(arrived.shape[0]):
        total = total + arrived[k]
    return total


def forward_kernel(
    x, cot, lens, order, gain1, taps, bias, w_xp, w_dt, dt_bias, rate, skip, gain2,
    w_x_h, w_z_h, w_out_h, w_gate_h, w_up_h, w_down_h,
    xg_o, cg_o, n1_o, s1_o, place_o, xi_o, z_o, proj_o, yv_o, go_all, h1_o, s2_o, n2_o, hid_all, dgu_o, dot_o,
    w_x, w_z, w_out, w_gate, w_up, w_down, w_step,
    x_all, c_all, sum_own, sum_in, low, xi_held, xi_left, xi_right, z_held, z_in,
    part_s, half_own, half_in, low_own, low_in, bb, cb, step, gone, drive,
    own, other, gu, gu_held, gu_left, gu_right, dhid, h_held, h_left, h_right,
    w_sems, x_send, x_recv, c_send, c_recv, sum_send, sum_recv, xi_send, xi_recv, z_send, z_recv, t_send, t_recv,
    go_send, go_recv, o_send, o_recv, sum2_send, sum2_recv, gu_send, gu_recv, h_send, h_recv, hid_send, hid_recv,
    *, model_width, rank, count
):
    rows, width = xi_o.shape
    hidden = dgu_o.shape[1] // 2
    group, row = lax.axis_index("dp"), lax.axis_index("row")
    row_size = lax.axis_size("row")
    weights = fetch(
        (w_x_h, w_z_h, w_out_h, w_gate_h, w_up_h, w_down_h), (w_x, w_z, w_out, w_gate, w_up, w_down), w_sems
    )
    greet("dp", "row", "col")
    x_copies = plane_start(x, x_all, x_send, x_recv)
    lens_row = lengths_row(lens)
    source, place = place_rows(lens_row, as_row(order), lens.shape[1], rows, group)
    place_o[...] = place
    w_step[...] = jnp.zeros_like(w_step)
    w_step[0:rank, :] = w_dt[...]
    plane_finish(x_copies, x_all, x_send, x_recv)
    c_copies = plane_start(cot, c_all, c_send, c_recv)
    xg_low = pick_rows(source, x_all[...])
    xg_o[...] = xg_low
    xg = xg_low.astype(f32)
    sum_own[...] = rows_form(xg * xg)
    sum_copies = spray("row", lambda k: sum_own, sum_in, sum_send, sum_recv)
    gain1_now = as_row(gain1)
    low[...] = (xg * gain1_now).astype(bf16)
    weights[0].wait()
    run(
        line_scatter(
            "row", lambda d: matmul(low[...], w_x[:, columns(d, width)]), xi_o, xi_held, xi_left, xi_right,
            xi_send, xi_recv,
        )
    )
    weights[1].wait()
    for k in range(1, row_size):
        d = lax.rem(row + k, row_size)
        z_held[k - 1] = matmul(low[...], w_z[:, columns(d, width)]).astype(bf16)
    z_copies = spray("row", lambda k: z_held.at[k - 1], z_in, z_send, z_recv)
    z_o[...] = matmul(low[...], w_z[:, columns(row, width)])
    wait_all(sum_copies)
    s1 = column_form(lax.rsqrt(line_total(sum_own[...], sum_in) / model_width + epsilon))
    s1_o[...] = s1
    inner_x = xi_o[...] * s1
    xi_o[...] = inner_x
    u_low = silu(conv_sum(inner_x, place, taps[...], as_row(bias))).astype(bf16)
    u = u_low.astype(f32)
    part_s[...] = matmul(u_low, w_xp[...])
    total_of_sums(part_s, half_own, half_in, low_own, low_in, proj_o, (t_send, t_recv))
    pre = matmul(proj_o[...].astype(bf16), w_step[...]) + as_row(dt_bias)
    step_now = jax.nn.softplus(pre)
    step[...] = step_now
    gone[...] = jnp.where(place > 0.0, step_now, 1e30)
    drive[...] = step_now * u
    scan_forward(proj_o, rank, rank + count, step, gone, drive, rate[...], bb, cb, y=yv_o)
    yv = yv_o[...] + as_row(skip) * u
    yv_o[...] = yv
    wait_all(z_copies)
    z = z_o[...]
    for k in range(row_size - 1):
        z = z + z_in[k].astype(f32)
    z = z * s1
    z_o[...] = z
    go_all[:, columns(row, width)] = (yv * silu(z)).astype(bf16)

    def during_gather():
        n1_o[...] = (xg * s1 * gain1_now).astype(bf16)
        plane_finish(c_copies, c_all, c_send, c_recv)
        cg_o[...] = pick_rows(source, c_all[...])
        yield

    run(line_gather("row", lanes(go_all, width), go_send, go_recv), during_gather())
    weights[2].wait()
    own[...] = matmul(go_all[...], w_out[...])
    copy = swap("col", own, other, o_send.at[0], o_recv.at[0])
    weights[3].wait()
    weights[4].wait()
    copy.wait()
    h1 = xg + (own[...] + other[...])
    h1_o[...] = h1
    sum_own[...] = rows_form(h1 * h1)
    sum_copies = spray("row", lambda k: sum_own, sum_in, sum2_send, sum2_recv)
    gain2_now = as_row(gain2)
    low[...] = (h1 * gain2_now).astype(bf16)

    def gate_up(d):
        at = columns(d, hidden)
        return jnp.concatenate([matmul(low[...], w_gate[:, at]), matmul(low[...], w_up[:, at])], axis=1)

    def during_scatter():
        wait_all(sum_copies)
        s2 = column_form(lax.rsqrt(line_total(sum_own[...], sum_in) / model_width + epsilon))
        s2_o[...] = s2
        n2_o[...] = (h1 * s2 * gain2_now).astype(bf16)
        yield

    run(
        line_scatter("row", gate_up, gu, gu_held, gu_left, gu_right, gu_send, gu_recv),
        during_scatter(),
    )
    s2 = s2_o[...]
    gate = gu[:, 0:hidden] * s2
    up = gu[:, hidden:] * s2
    sig = jax.nn.sigmoid(gate)
    act = gate * sig
    hid_all[:, columns(row, hidden)] = (act * up).astype(bf16)
    weights[5].wait()
    run(
        line_gather("row", lanes(hid_all, hidden), hid_send, hid_recv),
        line_scatter(
            "row", lambda d: transposed(cg_o[...], w_down[columns(d, hidden), :]), dhid, h_held, h_left, h_right,
            h_send, h_recv,
        ),
    )
    d_hid = dhid[...]
    d_gate = (d_hid * up * (sig * (1.0 + gate * (1.0 - sig)))).astype(bf16)
    d_up = (d_hid * act).astype(bf16)
    dgu_o[:, 0:hidden] = d_gate
    dgu_o[:, hidden:] = d_up
    dot_o[...] = rows_form(d_gate.astype(f32) * gate + d_up.astype(f32) * up)


def add_rows(target, base, source, rows):
    def piece(j, _):
        at = pl.ds(pl.multiple_of(base + j * 16, 16), 16)
        found = target[at, :].astype(f32) + source[pl.ds(pl.multiple_of(j * 16, 16), 16), :].astype(f32)
        target[at, :] = found.astype(target.dtype)
        return 0

    lax.fori_loop(0, rows // 16, piece, 0)


def plane_sum(grad, first_in, second_in, send, recv, free):
    quarter = grad.shape[0] // 4
    eighth = quarter // 2
    me = lax.axis_index("dp")
    bits = (lax.rem(me, 2), me // 2)
    partners = ({"dp": me + 1 - 2 * bits[0]}, {"dp": me + 2 - 4 * bits[1]})

    def rows(ref, start, count):
        return ref.at[pl.ds(pl.multiple_of(start, 16), count), :]

    class Half:
        def __init__(self, h):
            near, far = bits[h], bits[1 - h]
            self.free, self.mate, self.first = free.at[h], partners[h], first_in.at[h]
            base = h * 2 * quarter
            self.kept = base + near * quarter
            self.own = self.kept + far * eighth
            self.rest = self.kept + (1 - far) * eighth
            self.rest_in = (1 - far) * eighth
            across = base + (1 - near) * quarter
            self.second = second_in.at[h]

            def copy(stage, src, dst, to):
                return remote(src, dst, send.at[stage, h], recv.at[stage, h], to)

            mate, other = partners[h], partners[1 - h]
            own, rest = rows(grad, self.own, eighth), rows(grad, self.rest, eighth)
            there = (rows(grad, across + far * eighth, eighth), rows(grad, across + (1 - far) * eighth, eighth))
            back = rows(self.first, self.rest_in, eighth)
            self.out = (
                copy(0, rows(grad, across, quarter), self.first, mate),
                copy(1, rest, self.second, other),
                copy(2, own, rows(self.first, far * eighth, eighth), other),
                copy(3, own, own, mate),
                copy(4, rest, rest, mate),
            )
            self.back = (
                None,
                None,
                copy(2, back, back, other),
                copy(3, there[0], there[0], mate),
                copy(4, there[1], there[1], mate),
            )

    halves = (Half(0), Half(1))
    for half in halves:
        half.out[0].start()
    yield
    for half in halves:
        half.out[0].wait_recv()
        add_rows(grad, half.kept, half.first, quarter)
        half.out[1].start()
        half.out[0].wait_send()
        pl.semaphore_signal(half.free, inc=1, device_id=half.mate, device_id_type=MESH)
    yield
    for half in halves:
        half.out[1].wait_recv()
        add_rows(grad, half.own, half.second, eighth)
        half.out[2].start()
        pl.semaphore_wait(half.free, 1)
        half.out[3].start()
    yield
    for half in halves:
        half.back[2].wait_recv()
        half.out[1].wait_send()
        grad[pl.ds(pl.multiple_of(half.rest, 16), eighth), :] = half.first[
            pl.ds(pl.multiple_of(half.rest_in, 16), eighth), :
        ]
        half.out[4].start()
    yield
    for half in halves:
        half.back[3].wait_recv()
        half.back[4].wait_recv()
        for copy in half.out[2:]:
            copy.wait_send()


class Sums:
    def __init__(self):
        self.active = []

    def add(self, flow):
        next(flow)
        self.active.append(flow)

    def pump(self, count=1):
        for _ in range(count):
            if self.active:
                flow = self.active.pop(0)
                if next(flow, self) is not self:
                    self.active.append(flow)

    def drain(self):
        while self.active:
            self.pump()


class Writer:
    def __init__(self, stage, sems):
        self.stage, self.sems, self.pending, self.turn = stage, sems, [None, None], 0

    def write(self, grad, result):
        size = self.stage.shape[1]
        for start in range(0, grad.shape[0], size):
            slot = self.turn
            self.turn = 1 - slot
            if self.pending[slot] is not None:
                self.pending[slot].wait()
            self.stage[slot] = grad[start : start + size, :].astype(f32)
            copy = pltpu.make_async_copy(self.stage.at[slot], result.at[start : start + size, :], self.sems.at[slot])
            copy.start()
            self.pending[slot] = copy

    def finish(self):
        for copy in self.pending:
            if copy is not None:
                copy.wait()


def backward_kernel(
    lens, order, dgu, dot, gain2, cg, h1, s2, hid_all, go_all, n1, n2,
    z, yv, xi, proj, place, taps, bias, w_xp, w_dt, dt_bias, rate, skip, xg, s1, gain1,
    w_gate_h, w_up_h, w_down_h, w_out_h, w_x_h, w_z_h,
    small_o, y_o, dx_o, g_down_o, g_gate_o, g_up_o, g_out_o, g_z_o, g_x_o,
    w_gate, w_up, w_down, w_out, w_x, w_z, w_step,
    dg_all, du_all, dz_all, dxi_all, dh1, dmix, y_own, dx_own, y_all, dx_all,
    own, other, y_part, y_other, dot_in, dot_own, dot_sum, dot_other,
    dgo, d_held, d_left, d_right,
    hs, bb, cb, pb, pc, step, gone, drive, u_s, dy_s, du_s, dstep, dproj,
    half_own, half_in, low_own, low_in, full,
    g_down, g_gate, g_up, g_out, g_z, g_x, small,
    g_down_1, g_gate_1, g_up_1, g_out_1, g_z_1, g_x_1, small_1,
    g_down_2, g_gate_2, g_up_2, g_out_2, g_z_2, g_x_2, small_2,
    stage_d, stage_f, stage_e,
    w_sems, g_send, g_recv, u_send, u_recv, o_send, o_recv, dot_send, dot_recv,
    y_send, y_recv, dx_send, dx_recv, d_send, d_recv, z_send, z_recv, t_send, t_recv, x_send, x_recv,
    dot2_send, dot2_recv, sum_send, sum_recv, sum_free, stage_sems,
    *, rank, model_width
):
    rows, width = z.shape
    hidden = dgu.shape[1] // 2
    count = rate.shape[0]
    block = y_o.shape[0]
    tap_count = taps.shape[0]
    group, row, column = lax.axis_index("dp"), lax.axis_index("row"), lax.axis_index("col")
    row_size, col_size = lax.axis_size("row"), lax.axis_size("col")
    weights = fetch(
        (w_down_h, w_gate_h, w_up_h, w_out_h, w_x_h, w_z_h), (w_down, w_gate, w_up, w_out, w_x, w_z), w_sems
    )
    half = columns(column, block)
    sums = Sums()
    writers = {stage.shape[2]: Writer(stage, stage_sems.at[i]) for i, stage in enumerate((stage_d, stage_f, stage_e))}

    def total(number, grad, first_in, second_in, result):
        yield from plane_sum(
            grad, first_in, second_in, sum_send.at[number], sum_recv.at[number], sum_free.at[number]
        )
        if result is small_o:
            small_o[...] = grad[...].astype(f32)
        else:
            writers[grad.shape[1]].write(grad, result)

    def product(left, right, grad):
        size = grad.shape[0] // 4
        for start in range(0, grad.shape[0], size):
            grad[start : start + size, :] = over_rows(left[:, start : start + size], right[...]).astype(bf16)

    dg_all[:, columns(row, hidden)] = dgu[:, 0:hidden]
    du_all[:, columns(row, hidden)] = dgu[:, hidden:]
    greet("dp", "row", "col")
    dot_copies = spray("row", lambda k: dot, dot_in, dot_send, dot_recv)

    def first_work():
        product(hid_all, cg, g_down)
        sums.add(total(0, g_down, g_down_1, g_down_2, g_down_o))
        yield
        weights[0].wait()
        y_part[...] = matmul(hid_all[...], w_down[...])
        y_copy = swap("col", y_part, y_other, o_send.at[0], o_recv.at[0])
        yield
        wait_all(dot_copies)
        dot_own[...] = line_total(dot[...], dot_in)
        dot_copy = swap("col", dot_own, dot_other, o_send.at[2], o_recv.at[2])
        weights[1].wait()
        weights[2].wait()
        yield
        y_copy.wait()
        dot_copy.wait()
        y_own[...] = (h1[...] + (y_part[...] + y_other[...])).astype(bf16)

    run(line_gather("row", lanes(dg_all, hidden), g_send, g_recv), first_work(), pump=(sums, (0, 1, 1)))
    product(n2, dg_all, g_gate)
    sums.add(total(1, g_gate, g_gate_1, g_gate_2, g_gate_o))

    def second_work():
        own[...] = transposed(dg_all[...], w_gate[...])
        yield

    run(line_gather("row", lanes(du_all, hidden), u_send, u_recv), second_work(), pump=(sums, (1, 0, 1)))
    own[...] += transposed(du_all[...], w_up[...])
    copy = swap("col", own, other, o_send.at[1], o_recv.at[1])
    product(n2, du_all, g_up)
    sums.add(total(2, g_up, g_up_1, g_up_2, g_up_o))
    copy.wait()
    h1_now, s2_now = h1[...], s2[...]
    dn2 = own[...] + other[...]
    dots = column_form(dot_own[...] + dot_other[...])
    dh1_now = (
        cg[...].astype(f32)
        + s2_now * (as_row(gain2) * dn2)
        - h1_now * (s2_now * s2_now * dots / model_width)
    )
    dh1[...] = dh1_now
    dmix[...] = dh1_now.astype(bf16)
    gnorm2 = jnp.sum(dn2 * h1_now * s2_now, axis=0, keepdims=True)

    inner_x = xi[...]
    place_now = place[...]
    kept = {}

    def states():
        product(go_all, dmix, g_out)
        sums.add(total(3, g_out, g_out_1, g_out_2, g_out_o))
        w_step[...] = jnp.zeros_like(w_step)
        w_step[0:rank, :] = w_dt[...]
        xc = conv_sum(inner_x, place_now, taps[...], as_row(bias))
        sig_c = jax.nn.sigmoid(xc)
        u_low = (xc * sig_c).astype(bf16)
        u = u_low.astype(f32)
        u_s[...] = u
        step_low = proj[...].astype(bf16)
        pre = matmul(step_low, w_step[...]) + as_row(dt_bias)
        step_now = jax.nn.softplus(pre)
        step[...] = step_now
        gone[...] = jnp.where(place_now > 0.0, step_now, 1e30)
        drive[...] = step_now * u
        kept.update(xc=xc, sig_c=sig_c, u_low=u_low, u=u, step_low=step_low, pre=pre)
        yield from scan_states(proj, rank, gone, drive, rate[...], bb, hs)

    weights[3].wait()
    run(
        line_scatter(
            "row", lambda d: transposed(dmix[...], w_out[columns(d, width), :]), dgo, d_held, d_left, d_right,
            d_send, d_recv,
        ),
        states(),
        pump=(sums, (1, 1, 1)),
    )
    xc, sig_c, u_low, u = kept["xc"], kept["sig_c"], kept["u_low"], kept["u"]
    step_low, pre = kept["step_low"], kept["pre"]
    z_now = z[...]
    sig_z = jax.nn.sigmoid(z_now)
    d_z = (dgo[...] * yv[...] * (sig_z * (1.0 + z_now * (1.0 - sig_z)))).astype(bf16)
    mine = dz_all.at[:, columns(row, width)]
    mine[...] = d_z
    z_copies = []
    for k in range(1, row_size):
        copy = remote(mine, mine, z_send.at[k - 1], z_recv.at[k - 1], away("row", k))
        copy.start()
        z_copies.append(copy)
    dy = dgo[...] * (z_now * sig_z)
    dy_s[...] = dy
    dproj[...] = jnp.zeros_like(dproj)
    sums.pump(1)
    g_rate = scan_backward(
        proj, rank, rank + count, step, gone, drive, u_s, dy_s, rate[...], hs, bb, cb, pb, pc, du_s, dstep, dproj
    )
    d_pre = dstep[...] * jax.nn.sigmoid(pre)
    d_pre_low = d_pre.astype(bf16)
    dproj[...] += transposed(d_pre_low, w_step[...])
    sums.pump(1)
    total_of_sums(dproj, half_own, half_in, low_own, low_in, full, (t_send, t_recv))
    dproj_low = full[...].astype(bf16)
    du = du_s[...] + as_row(skip) * dy + transposed(dproj_low, w_xp[...])
    dxc = du * (sig_c * (1.0 + xc * (1.0 - sig_c)))
    taps_now = taps[...]
    d_inner = dxc * taps_now[tap_count - 1 : tap_count, :]
    masked = [dxc]
    for shift in range(1, tap_count):
        masked.append(jnp.where(place_now >= shift, dxc, 0.0))
        k = tap_count - 1 - shift
        d_inner = d_inner + pltpu.roll(masked[shift], rows - shift, 0) * taps_now[k : k + 1, :]
    d_inner = d_inner.astype(bf16)
    dxi_all[:, columns(row, width)] = d_inner

    def during():
        wait_all(z_copies)
        product(n1, dz_all, g_z)
        sums.add(total(4, g_z, g_z_1, g_z_2, g_z_o))
        dot_own[...] = rows_form(d_inner.astype(f32) * inner_x + d_z.astype(f32) * z_now)
        dot_copies = spray("row", lambda k: dot_own, dot_in, dot2_send, dot2_recv)
        small[0:RANK_LANES, :] = over_rows(dproj_low, u_low).astype(bf16)
        small[RANK_LANES : RANK_LANES + rank, :] = over_rows(step_low, d_pre_low)[0:rank, :].astype(bf16)
        yield
        wait_all(dot_copies)
        dot_sum[...] = line_total(dot_own[...], dot_in)
        dot_copy = swap("col", dot_sum, dot_other, o_send.at[3], o_recv.at[3])
        weights[4].wait()
        weights[5].wait()
        own[...] = transposed(dz_all[...], w_z[...])
        yield
        dot_copy.wait()

    run(line_gather("row", lanes(dxi_all, width), x_send, x_recv), during(), pump=(sums, (1, 1, 1)))
    own[...] += transposed(dxi_all[...], w_x[...])
    copy = swap("col", own, other, o_send.at[4], o_recv.at[4])
    product(n1, dxi_all, g_x)
    sums.add(total(5, g_x, g_x_1, g_x_2, g_x_o))
    copy.wait()
    dn1 = own[...] + other[...]
    s1_now = s1[...]
    xg_now = xg[...].astype(f32)
    dots = column_form(dot_sum[...] + dot_other[...])
    dx = dh1[...] + s1_now * (as_row(gain1) * dn1) - xg_now * (s1_now * s1_now * dots / model_width)
    dx_own[...] = dx.astype(bf16)
    dx_copies = plane_start(dx_own.at[half], dx_all, dx_send, dx_recv)
    y_copies = plane_start(y_own.at[half], y_all, y_send, y_recv)
    g_taps = [None] * tap_count
    for shift in range(tap_count):
        moved = pltpu.roll(inner_x, shift, 0) if shift else inner_x
        g_taps[tap_count - 1 - shift] = jnp.sum(masked[shift] * moved, axis=0, keepdims=True)
    pieces = [
        g_rate,
        *g_taps,
        jnp.sum(dxc, axis=0, keepdims=True),
        jnp.sum(d_pre, axis=0, keepdims=True),
        jnp.sum(dy * u, axis=0, keepdims=True),
        jnp.sum(dn1 * xg_now * s1_now, axis=0, keepdims=True),
        gnorm2,
    ]
    found = sum(piece.shape[0] for piece in pieces)
    pieces.append(jnp.zeros((small.shape[0] - RANK_LANES - rank - found, width), f32))
    small[RANK_LANES + rank :, :] = jnp.concatenate(pieces, axis=0).astype(bf16)
    sums.add(total(6, small, small_1, small_2, small_o))
    first = (group * col_size + column) * block
    wanted = owner_rows(lengths_row(lens), as_row(order), lens.shape[1], rows, block, first)
    sums.pump(2)
    plane_finish(dx_copies, dx_all, dx_send, dx_recv)
    dx_o[...] = pick_rows(wanted, dx_all[...])
    plane_finish(y_copies, y_all, y_send, y_recv)
    y_o[...] = pick_rows(wanted, y_all[...])
    sums.drain()
    for writer in writers.values():
        writer.finish()


VMEM_BYTES = 60 << 20
DMA = pltpu.SemaphoreType.DMA


def in_vmem(kernel, name, ident, outs, scratch, args, far=(), micros=50, far_outs=()):
    space = pl.BlockSpec(memory_space=pltpu.VMEM)
    anywhere = pl.BlockSpec(memory_space=pl.ANY)
    return pl.pallas_call(
        kernel,
        out_shape=tuple(jax.ShapeDtypeStruct(shape, kind) for shape, kind in [*outs, *far_outs]),
        in_specs=[space] * len(args) + [anywhere] * len(far),
        out_specs=tuple([space] * len(outs) + [anywhere] * len(far_outs)),
        scratch_shapes=scratch,
        compiler_params=pltpu.CompilerParams(
            collective_id=ident, has_side_effects=True, vmem_limit_bytes=VMEM_BYTES
        ),
        cost_estimate=pl.CostEstimate(flops=micros * 10**9, bytes_accessed=1 << 20, transcendentals=0),
        name=name,
    )(*args, *far)


def both(*shape):
    return [DMA(shape), DMA(shape)]


def on_pairs(
    x_in, lengths, seq_order, norm1_gain, w_in_x, w_in_z, conv_w, conv_b, w_xp, w_dt, dt_bias, a_log,
    skip_weight, w_out, norm2_gain, w_gate, w_up, w_down, cotangent,
):
    dp, rs = lax.axis_size("dp"), lax.axis_size("row")
    block, wide_d = x_in.shape
    rows = block * 2
    model_width = wide_d * rs
    width = conv_w.shape[0]
    hidden = w_gate.shape[1] // rs
    rank, count, taps = w_dt.shape[0], a_log.shape[1], conv_w.shape[1]
    conv_taps = conv_w.T
    rate = -jnp.exp(a_log).T
    vm = pltpu.VMEM
    tile = vm((128, count, 128), f32)
    big = vm((rows, width), f32)
    model = vm((rows, wide_d), f32)
    sums = [vm((8, rows), f32), vm((rs - 1, 8, rows), f32)]
    sums_scratch = [
        vm((rows // 2, RANK_LANES), f32),
        vm((rows // 2, RANK_LANES), f32),
        vm((rows // 2, RANK_LANES), bf16),
        vm((rs - 1, rows // 2, RANK_LANES), bf16),
    ]

    def weight(value):
        return vm(value.shape, value.dtype)

    def line(size, width):
        return [vm((size, rows, width), bf16)] * 3

    (xg, cg, n1, s1, place, xi, z, proj, yv, go_all, h1, s2, n2, hid_all, dgu, dot) = in_vmem(
        functools.partial(forward_kernel, model_width=model_width, rank=rank, count=count),
        "forward",
        0,
        [
            ((rows, wide_d), bf16), ((rows, wide_d), bf16), ((rows, wide_d), bf16), ((rows, 1), f32), ((rows, 1), f32),
            ((rows, width), f32), ((rows, width), f32), ((rows, RANK_LANES), f32), ((rows, width), f32),
            ((rows, rs * width), bf16), ((rows, wide_d), f32), ((rows, 1), f32), ((rows, wide_d), bf16),
            ((rows, rs * hidden), bf16), ((rows, 2 * hidden), bf16), ((8, rows), f32),
        ],
        [
            weight(w_in_x), weight(w_in_z), weight(w_out), weight(w_gate), weight(w_up), weight(w_down),
            vm((RANK_LANES, width), bf16),
            vm((2, dp, block, wide_d), bf16), vm((2, dp, block, wide_d), bf16), *sums, vm((rows, wide_d), bf16),
            *line(rs, width), vm((rs - 1, rows, width), bf16), vm((rs - 1, rows, width), bf16),
            vm((rows, RANK_LANES), f32), *sums_scratch, tile, tile, big, big, big,
            model, model, vm((rows, 2 * hidden), f32), *line(rs, 2 * hidden), vm((rows, hidden), f32), *line(rs, hidden),
            DMA((6,)), *both(dp), *both(dp), *both(rs - 1), *both(2, rs), *both(rs - 1), *both(rs + 1),
            *both(2, rs), *both(1), *both(rs - 1), *both(2, rs), *both(2, rs), *both(2, rs),
        ],
        (
            x_in, cotangent, lengths, seq_order, norm1_gain, conv_taps, conv_b, w_xp, w_dt, dt_bias, rate, skip_weight,
            norm2_gain,
        ),
        (w_in_x, w_in_z, w_out, w_gate, w_up, w_down),
        130,
    )

    def sizes(value, parts):
        return vm((2, value[0] // parts, value[1]), bf16)

    d_cols, f_cols, e_cols = (rs * hidden, wide_d), (wide_d, rs * hidden), (wide_d, rs * width)
    grads = (d_cols, f_cols, f_cols, (rs * width, wide_d), e_cols, e_cols, (2 * RANK_LANES, width))
    small, y_out, dx_out, g_down, g_gate, g_up, g_out, g_z, g_x = in_vmem(
        functools.partial(backward_kernel, rank=rank, model_width=model_width),
        "backward",
        1,
        [((2 * RANK_LANES, width), f32), ((block, wide_d), bf16), ((block, wide_d), bf16)],
        [
            weight(w_gate), weight(w_up), weight(w_down), weight(w_out), weight(w_in_x), weight(w_in_z),
            vm((RANK_LANES, width), bf16),
            vm((rows, rs * hidden), bf16), vm((rows, rs * hidden), bf16),
            vm((rows, rs * width), bf16), vm((rows, rs * width), bf16),
            model, vm((rows, wide_d), bf16), vm((rows, wide_d), bf16), vm((rows, wide_d), bf16),
            vm((2, dp, block, wide_d), bf16), vm((2, dp, block, wide_d), bf16),
            model, model, model, model, vm((rs - 1, 8, rows), f32), vm((8, rows), f32), vm((8, rows), f32),
            vm((8, rows), f32), big, *line(rs, width),
            vm((rows + 1, count, width), f32), tile, tile, tile, tile,
            big, big, big, big, big, big, big, vm((rows, RANK_LANES), f32), *sums_scratch, vm((rows, RANK_LANES), f32),
            *[vm(value, bf16) for value in grads], *[sizes(value, 4) for value in grads],
            *[sizes(value, 8) for value in grads],
            vm((2, rs * hidden // 8, wide_d), f32), vm((2, wide_d // 8, rs * hidden), f32),
            vm((2, wide_d // 8, rs * width), f32),
            DMA((6,)), *both(2, rs), *both(2, rs), *both(5), *both(rs - 1), *both(dp), *both(dp), *both(2, rs),
            *both(rs - 1), *both(rs + 1), *both(2, rs), *both(rs - 1), *both(len(grads), 5, 2),
            pltpu.SemaphoreType.REGULAR((len(grads), 2)), DMA((3, 2)),
        ],
        (
            lengths, seq_order, dgu, dot, norm2_gain, cg, h1, s2, hid_all, go_all, n1, n2,
            z, yv, xi, proj, place, conv_taps, conv_b, w_xp, w_dt, dt_bias, rate, skip_weight, xg, s1, norm1_gain,
        ),
        (w_gate, w_up, w_down, w_out, w_in_x, w_in_z),
        150,
        [(value, f32) for value in grads[:-1]],
    )
    at = RANK_LANES + rank
    return (
        y_out,
        dx_out,
        small[at + count + taps + 3],
        g_x,
        g_z,
        small[at + count : at + count + taps].T,
        small[at + count + taps],
        small[:RANK_LANES].T,
        small[RANK_LANES:at],
        small[at + count + taps + 1],
        small[at : at + count].T,
        small[at + count + taps + 2],
        g_out,
        small[at + count + taps + 4],
        g_gate,
        g_up,
        g_down,
    )


def on_device(
    x_in,
    lengths,
    seq_order,
    norm1_gain,
    w_in_x,
    w_in_z,
    conv_w,
    conv_b,
    w_xp,
    w_dt,
    dt_bias,
    a_log,
    skip_weight,
    w_out,
    norm2_gain,
    w_gate,
    w_up,
    w_down,
    cotangent,
):
    rows_in, width_row = x_in.shape
    row_devices = lax.axis_size("row")
    col_devices = lax.axis_size("col")
    group_rows = rows_in * col_devices
    model_width = width_row * row_devices
    rank_cols = w_dt.shape[0]
    state_count = a_log.shape[1]
    channels = conv_w.shape[0]
    ff_cols = w_gate.shape[1]
    my_group = lax.axis_index("dp")
    my_column = lax.axis_index("col")
    source, position_all = layout(lengths, seq_order, group_rows)
    my_source = lax.dynamic_index_in_dim(source, my_group, 0, keepdims=False)
    position = lax.dynamic_index_in_dim(position_all, my_group, 0, keepdims=False)
    slice_source = lax.dynamic_slice_in_dim(my_source, my_column * rows_in, rows_in, 0)

    def row_total(values):
        return lax.psum(values, "row")

    def token_rows(values):
        return lax.all_gather(values, "col", axis=0, tiled=True)

    def row_pieces(values):
        return lax.all_gather(values, "row", axis=0, tiled=True)

    def col_reduce(term_fn):
        return lax.psum_scatter(
            term_fn(jnp.int32(0), lax.axis_size("col") * rows_in),
            "col",
            scatter_dimension=0,
            tiled=True,
        )

    def row_reduce(term_fn, keep_rows):
        return lax.psum_scatter(
            term_fn(jnp.int32(0), lax.axis_size("row") * keep_rows),
            "row",
            scatter_dimension=0,
            tiled=True,
        )

    def projection_total(values):
        return lax.psum(values, ("row", "col"))

    blank_rows = jnp.zeros((rows_in, width_row), jnp.bfloat16)
    pieces = (
        lax.all_gather(x_in, ("dp", "col"), axis=0, tiled=True),
        lax.all_gather(cotangent, ("dp", "col"), axis=0, tiled=True),
    )
    row_count = pieces[0].shape[0]
    offset = slice_source
    inside = ((offset >= 0) & (offset < row_count))[:, None]
    index = jnp.clip(offset, 0, row_count - 1)
    x_rows = jnp.where(inside, jnp.take(pieces[0], index, axis=0), blank_rows)
    cot_rows = jnp.where(inside, jnp.take(pieces[1], index, axis=0), blank_rows)
    x_val = x_rows.astype(jnp.float32)
    scale_one = lax.rsqrt(row_total(jnp.sum(x_val * x_val, axis=1)) / model_width + epsilon)
    normed_one = (x_val * scale_one[:, None] * norm1_gain[None, :]).astype(jnp.bfloat16)
    normed_all = token_rows(normed_one)

    def inner_term(begin_row, row_count):
        return jnp.concatenate(
            [contract(w_in_x, normed_all, 0, 1), contract(w_in_z, normed_all, 0, 1)], axis=1
        )

    inner = row_reduce(inner_term, channels)
    inner_x = inner[:, :group_rows]
    inner_z = inner[:, group_rows:]

    def conv_part(values, kernel, kernel_bias):
        return convolve(values, kernel, kernel_bias, position)

    conv_out, conv_pull = jax.vjp(conv_part, inner_x, conv_w, conv_b)
    u_low = conv_out.astype(jnp.bfloat16)
    u_val = u_low.astype(jnp.float32)
    projected = projection_total(contract(w_xp, u_low, 0, 0))
    step_low = projected[:rank_cols].astype(jnp.bfloat16)
    pre_step = contract(w_dt, step_low, 0, 0) + dt_bias[:, None]
    step_size = jax.nn.softplus(pre_step)

    decay_rate = -jnp.exp(a_log).T
    proj_rows = projected.T
    u_rows = u_val.T
    step_rows = step_size.T
    gone_rows = jnp.where(position[:, None] > 0, step_rows, 1e30)
    drive_rows = step_rows * u_rows
    at_b, at_c = rank_cols, rank_cols + state_count
    scanned = scan_alone(proj_rows, step_rows, gone_rows, drive_rows, decay_rate, at_b, at_c)
    mixer_y = scanned.T + skip_weight[:, None] * u_val
    gated = mixer_y * jax.nn.silu(inner_z)
    gated_low = gated.astype(jnp.bfloat16)
    gated_all = row_pieces(gated_low)

    def mix_term(begin_row, row_count):
        return contract(gated_all, w_out, 0, 0)

    first_sum = x_val + col_reduce(mix_term)
    scale_two = lax.rsqrt(row_total(jnp.sum(first_sum * first_sum, axis=1)) / model_width + epsilon)
    normed_two = (first_sum * scale_two[:, None] * norm2_gain[None, :]).astype(jnp.bfloat16)
    normed_rows = token_rows(normed_two)

    def ffn_term(begin_row, row_count):
        return jnp.concatenate(
            [
                jnp.dot(normed_rows, w_gate, preferred_element_type=jnp.float32),
                jnp.dot(normed_rows, w_up, preferred_element_type=jnp.float32),
            ],
            axis=1,
        )

    gate_up = row_reduce(ffn_term, group_rows // row_devices)
    gate_val = gate_up[:, :ff_cols]
    up_val = gate_up[:, ff_cols:]
    hidden = (jax.nn.silu(gate_val) * up_val).astype(jnp.bfloat16)
    hidden_all = row_pieces(hidden)

    def down_term(begin_row, row_count):
        return jnp.dot(hidden_all, w_down, preferred_element_type=jnp.float32)

    second_sum = first_sum + col_reduce(down_term)
    out_low = second_sum.astype(jnp.bfloat16)
    back_down_all = token_rows(cot_rows)
    grad_down = contract(hidden_all, back_down_all, 0, 0)

    def hidden_term(begin_row, row_count):
        return contract(back_down_all, w_down, 1, 1)

    d_hidden = row_reduce(hidden_term, group_rows // row_devices)
    d_gate = (d_hidden * up_val * silu_slope(gate_val)).astype(jnp.bfloat16)
    d_up = (d_hidden * jax.nn.silu(gate_val)).astype(jnp.bfloat16)
    d_gate_up_all = row_pieces(jnp.concatenate([d_gate, d_up], axis=1))
    grad_gate = contract(normed_rows, d_gate_up_all[:, :ff_cols], 0, 0)
    grad_up = contract(normed_rows, d_gate_up_all[:, ff_cols:], 0, 0)

    def norm_two_term(begin_row, row_count):
        return contract(d_gate_up_all[:, :ff_cols], w_gate, 1, 1) + contract(
            d_gate_up_all[:, ff_cols:], w_up, 1, 1
        )

    d_normed_two = col_reduce(norm_two_term)
    cot_val = cot_rows.astype(jnp.float32)
    weighted_two = d_normed_two * norm2_gain[None, :]
    grad_norm_two = jnp.sum(d_normed_two * first_sum * scale_two[:, None], axis=0)
    dot_two = row_total(jnp.sum(weighted_two * first_sum, axis=1))
    d_first = (
        cot_val
        + scale_two[:, None] * weighted_two
        - first_sum * (scale_two**3 * dot_two / model_width)[:, None]
    )
    d_mix_all = token_rows(d_first.astype(jnp.bfloat16))
    grad_out = contract(gated_all, d_mix_all, 1, 0)

    def gated_term(begin_row, row_count):
        return contract(w_out, d_mix_all, 1, 1)

    d_gated = row_reduce(gated_term, channels)
    d_inner_z = d_gated * mixer_y * silu_slope(inner_z)
    d_mixer = d_gated * jax.nn.silu(inner_z)
    d_u_rows, d_step_rows, d_proj_rows, grad_rate_rows = adjoint_alone(
        proj_rows, step_rows, gone_rows, drive_rows, u_rows, d_mixer.T, decay_rate, at_b, at_c
    )
    d_u_mix = d_u_rows.T + skip_weight[:, None] * d_mixer
    d_step = d_step_rows.T
    d_enter = d_proj_rows.T[at_b:at_c]
    d_leave = d_proj_rows.T[at_c:]
    grad_rate = grad_rate_rows.T
    grad_skip = jnp.sum(d_mixer * u_val, axis=1)
    d_pre = d_step * jax.nn.sigmoid(pre_step)
    grad_step_bias = jnp.sum(d_pre, axis=1)
    d_pre_low = d_pre.astype(jnp.bfloat16)
    grad_step_w = contract(step_low, d_pre_low, 1, 1)
    d_projected = projection_total(
        jnp.concatenate(
            [jnp.dot(w_dt, d_pre_low, preferred_element_type=jnp.float32), d_enter, d_leave], axis=0
        )
    )
    d_proj_low = d_projected.astype(jnp.bfloat16)
    grad_proj_w = contract(u_low, d_proj_low, 1, 1)
    d_u_all = d_u_mix + jnp.dot(w_xp, d_proj_low, preferred_element_type=jnp.float32)
    d_inner_x, grad_kernel, grad_kernel_bias = conv_pull(d_u_all)
    d_inner_all = row_pieces(
        jnp.concatenate([d_inner_x.astype(jnp.bfloat16), d_inner_z.astype(jnp.bfloat16)], axis=1)
    )
    grad_in_x = contract(normed_all, d_inner_all[:, :group_rows], 0, 1)
    grad_in_z = contract(normed_all, d_inner_all[:, group_rows:], 0, 1)

    def norm_one_term(begin_row, row_count):
        piece_x = lax.dynamic_slice_in_dim(d_inner_all, begin_row, row_count, 1)
        piece_z = lax.dynamic_slice_in_dim(d_inner_all, group_rows, row_count, 1)
        return contract(piece_x, w_in_x, 0, 1) + contract(piece_z, w_in_z, 0, 1)

    d_normed_one = col_reduce(norm_one_term)
    weighted_one = d_normed_one * norm1_gain[None, :]
    grad_norm_one = jnp.sum(d_normed_one * x_val * scale_one[:, None], axis=0)
    dot_one = row_total(jnp.sum(weighted_one * x_val, axis=1))
    d_input = (
        d_first
        + scale_one[:, None] * weighted_one
        - x_val * (scale_one**3 * dot_one / model_width)[:, None]
    )
    d_input_low = d_input.astype(jnp.bfloat16)
    grad_norm_one, grad_norm_two = lax.psum((grad_norm_one, grad_norm_two), ("dp", "col"))
    (
        grad_in_x,
        grad_in_z,
        grad_kernel,
        grad_kernel_bias,
        grad_proj_w,
        grad_step_w,
        grad_step_bias,
        grad_rate,
        grad_skip,
        grad_out,
        grad_gate,
        grad_up,
        grad_down,
    ) = (
        lax.psum(grad_in_x.astype(jnp.bfloat16), "dp").astype(jnp.float32),
        lax.psum(grad_in_z.astype(jnp.bfloat16), "dp").astype(jnp.float32),
        lax.psum(grad_kernel.astype(jnp.bfloat16), "dp").astype(jnp.float32),
        lax.psum(grad_kernel_bias.astype(jnp.bfloat16), "dp").astype(jnp.float32),
        lax.psum(grad_proj_w.astype(jnp.bfloat16), "dp").astype(jnp.float32),
        lax.psum(grad_step_w.astype(jnp.bfloat16), "dp").astype(jnp.float32),
        lax.psum(grad_step_bias.astype(jnp.bfloat16), "dp").astype(jnp.float32),
        lax.psum(grad_rate.astype(jnp.bfloat16), "dp").astype(jnp.float32),
        lax.psum(grad_skip.astype(jnp.bfloat16), "dp").astype(jnp.float32),
        lax.psum(grad_out.astype(jnp.bfloat16), "dp").astype(jnp.float32),
        lax.psum(grad_gate.astype(jnp.bfloat16), "dp").astype(jnp.float32),
        lax.psum(grad_up.astype(jnp.bfloat16), "dp").astype(jnp.float32),
        lax.psum(grad_down.astype(jnp.bfloat16), "dp").astype(jnp.float32),
    )
    payload = jnp.concatenate([out_low, d_input_low], axis=1)
    tokens_all = lengths.shape[0] * group_rows
    owner = (
        jnp.zeros((tokens_all,), jnp.int32)
        .at[source.reshape(-1)]
        .set(jnp.arange(tokens_all, dtype=jnp.int32))
    )
    my_rows = lax.dynamic_slice_in_dim(
        owner, (my_group * col_devices + my_column) * rows_in, rows_in, 0
    )
    pieces = lax.all_gather(payload, ("dp", "col"), axis=0, tiled=True)
    row_count = pieces.shape[0]
    offset = my_rows
    inside = ((offset >= 0) & (offset < row_count))[:, None]
    returned = jnp.where(
        inside,
        jnp.take(pieces, jnp.clip(offset, 0, row_count - 1), axis=0),
        jnp.zeros_like(payload),
    )
    y_out = returned[:, :width_row]
    dx_out = returned[:, width_row:]
    return (
        y_out,
        dx_out,
        grad_norm_one,
        grad_in_x,
        grad_in_z,
        grad_kernel,
        grad_kernel_bias,
        grad_proj_w,
        grad_step_w,
        grad_step_bias,
        grad_rate,
        grad_skip,
        grad_out,
        grad_norm_two,
        grad_gate,
        grad_up,
        grad_down,
    )


def solution(mesh):
    placed = (
        P(("dp", "col"), "row"),
        P(),
        P(),
        P("row"),
        P("row", "col"),
        P("row", "col"),
        P(("col", "row"), None),
        P(("col", "row")),
        P(("col", "row"), None),
        P(None, ("col", "row")),
        P(("col", "row")),
        P(("col", "row"), None),
        P(("col", "row")),
        P("col", "row"),
        P("row"),
        P("row", "col"),
        P("row", "col"),
        P("col", "row"),
        P(("dp", "col"), "row"),
    )
    paired = mesh.shape["col"] == 2 and mesh.shape["dp"] == 4
    return jax.shard_map(
        on_pairs if paired else on_device,
        mesh=mesh,
        in_specs=placed,
        out_specs=(
            P(("dp", "col"), "row"),
            P(("dp", "col"), "row"),
            P("row"),
            P("row", "col"),
            P("row", "col"),
            P(("col", "row"), None),
            P(("col", "row")),
            P(("col", "row"), None),
            P(None, ("col", "row")),
            P(("col", "row")),
            P(("col", "row"), None),
            P(("col", "row")),
            P("col", "row"),
            P("row"),
            P("row", "col"),
            P("row", "col"),
            P("col", "row"),
        ),
        check_vma=False,
    )
```

```python
import functools

import jax
import jax.numpy as jnp
from jax import lax
from jax.experimental import pallas as pl
from jax.experimental.pallas import tpu as pltpu
from jax.sharding import PartitionSpec as P

epsilon = 1e-05


def layout(lengths, seq_order, group_rows):
    flat_lengths = lengths.reshape(-1)
    total_seqs = flat_lengths.shape[0]
    slot_length = jnp.take(flat_lengths, seq_order)
    input_start = jnp.cumsum(slot_length) - slot_length
    slot_of = (
        jnp.zeros((total_seqs,), jnp.int32)
        .at[seq_order]
        .set(jnp.arange(total_seqs, dtype=jnp.int32))
    )
    seq_input = jnp.take(input_start, slot_of).reshape(lengths.shape)
    group_start = jnp.cumsum(lengths, axis=1) - lengths
    places = jnp.arange(group_rows, dtype=jnp.int32)
    member = (
        jnp.sum((places[None, :, None] >= group_start[:, None, :]).astype(jnp.int32), axis=2) - 1
    )
    begin_at = jnp.take_along_axis(group_start, member, axis=1)
    within = places[None, :] - begin_at
    source = jnp.take_along_axis(seq_input, member, axis=1) + within
    return (source, within)


def silu_slope(values):
    sigmoid_v = jax.nn.sigmoid(values)
    return sigmoid_v * (1.0 + values * (1.0 - sigmoid_v))


def contract(left, right, left_dim, right_dim):
    return lax.dot_general(
        left, right, (((left_dim,), (right_dim,)), ((), ())), preferred_element_type=jnp.float32
    )


def convolve(inner_x, kernel, kernel_bias, places):
    tap_count = kernel.shape[1]
    conv_sum = kernel_bias[:, None] + inner_x * kernel[:, tap_count - 1][:, None]
    for shift_by in range(1, tap_count):
        shifted = jnp.pad(inner_x, ((0, 0), (shift_by, 0)))[:, :-shift_by]
        conv_sum = (
            conv_sum
            + shifted
            * (places >= shift_by).astype(jnp.float32)[None, :]
            * kernel[:, tap_count - 1 - shift_by][:, None]
        )
    return jax.nn.silu(conv_sum)


MESH = pl.DeviceIdType.MESH
f32 = jnp.float32
bf16 = jnp.bfloat16


def remote(src, dst, send, recv, where):
    return pltpu.make_async_remote_copy(
        src_ref=src, dst_ref=dst, send_sem=send, recv_sem=recv, device_id=where, device_id_type=MESH
    )


def away(axis, offset):
    return {axis: lax.rem(lax.axis_index(axis) + offset, lax.axis_size(axis))}


def greet(*axes):
    barrier = pltpu.get_barrier_semaphore()
    total = 0
    for axis in axes:
        for offset in range(1, lax.axis_size(axis)):
            pl.semaphore_signal(barrier, inc=1, device_id=away(axis, offset), device_id_type=MESH)
            total += 1
    pl.semaphore_wait(barrier, total)


def matmul(left, right):
    return jnp.dot(left, right, preferred_element_type=f32)


def silu(values):
    return values * jax.nn.sigmoid(values)


def rows_form(values):
    ones = jnp.ones((8, values.shape[1]), f32)
    return lax.dot_general(
        ones,
        values,
        (((1,), (1,)), ((), ())),
        precision=lax.Precision.HIGHEST,
        preferred_element_type=f32,
    )


def column_form(row_values):
    return jnp.transpose(row_values)[:, 0:1]


class Line:
    def __init__(self, axis, send, recv):
        self.axis, self.send, self.recv = axis, send, recv
        self.size = lax.axis_size(axis)
        self.me = lax.axis_index(axis)

    def right(self, src, dst, d):
        return remote(
            src, dst, self.send.at[0, d], self.recv.at[0, d], {self.axis: jnp.minimum(self.me + 1, self.size - 1)}
        )

    def left(self, src, dst, d):
        return remote(
            src, dst, self.send.at[1, d], self.recv.at[1, d], {self.axis: jnp.maximum(self.me - 1, 0)}
        )


def line_gather(axis, slot_of, send, recv):
    line = Line(axis, send, recv)
    size, me = line.size, line.me
    last = size - 1

    def go_right(s):
        slot = jnp.maximum(me - s, 0)
        return (me - s >= 0) & (me < last), line.right(slot_of(slot), slot_of(slot), slot)

    def go_left(s):
        slot = jnp.minimum(me + s, last)
        return (me + s <= last) & (me > 0), line.left(slot_of(slot), slot_of(slot), slot)

    for s in range(last):
        for valid, copy in (go_right(s), go_left(s)):
            pl.when(valid)(copy.start)
        yield
        slot = jnp.maximum(me - 1 - s, 0)
        pl.when(me - 1 - s >= 0)(line.right(slot_of(slot), slot_of(slot), slot).wait_recv)
        slot = jnp.minimum(me + 1 + s, last)
        pl.when(me + 1 + s <= last)(line.left(slot_of(slot), slot_of(slot), slot).wait_recv)
    yield
    for s in range(last):
        for valid, copy in (go_right(s), go_left(s)):
            pl.when(valid)(copy.wait_send)


def line_scatter(axis, block_of, out, held, from_left, from_right, send, recv):
    line = Line(axis, send, recv)
    size, me = line.size, line.me
    last = size - 1

    def right_at(t):
        d = jnp.clip(last - t + me, 0, last)
        return (t >= me) & (me < last), d, line.right(held.at[d], from_left.at[d], d)

    def left_at(t):
        d = jnp.clip(t - (last - me), 0, last)
        return (t >= last - me) & (me > 0), d, line.left(held.at[d], from_right.at[d], d)

    def pass_on(valid, first, d, copy, arrived):
        @pl.when(valid)
        def _():
            part = block_of(d)

            @pl.when(jnp.logical_not(first))
            def _():
                copy.wait_recv()
                held[d] = (part + arrived[d].astype(f32)).astype(held.dtype)

            @pl.when(first)
            def _():
                held[d] = part.astype(held.dtype)

            copy.start()

    for t in range(last):
        valid, d, copy = right_at(t)
        pass_on(valid, me == 0, d, copy, from_left)
        valid, d, copy = left_at(t)
        pass_on(valid, me == last, d, copy, from_right)
        if t == 0:
            out[...] = block_of(me)
        yield
    yield

    @pl.when(me > 0)
    def _():
        line.right(held.at[me], from_left.at[me], me).wait_recv()
        out[...] += from_left[me].astype(f32)

    @pl.when(me < last)
    def _():
        line.left(held.at[me], from_right.at[me], me).wait_recv()
        out[...] += from_right[me].astype(f32)

    for t in range(last):
        for valid, _, copy in (right_at(t), left_at(t)):
            pl.when(valid)(copy.wait_send)


def halves(rows):
    return [pl.ds(0, rows // 2), pl.ds(rows // 2, rows // 2)]


def gather_halves(axis, ref, size, send, recv):
    flows = []
    for h, at in enumerate(halves(ref.shape[0])):

        def slot_of(d, at=at):
            return ref.at[at, pl.ds(pl.multiple_of(d * size, size), size)]

        flows.append(line_gather(axis, slot_of, send.at[h], recv.at[h]))
    return flows


def scatter_halves(axis, block_of, out, held, from_left, from_right, send, recv):
    flows = []
    for h, at in enumerate(halves(out.shape[0])):
        flows.append(
            line_scatter(
                axis,
                functools.partial(block_of, at=at),
                out.at[at, :],
                held.at[:, at, :],
                from_left.at[:, at, :],
                from_right.at[:, at, :],
                send.at[h],
                recv.at[h],
            )
        )
    return flows


def run(*flows, pump=None):
    flows = list(flows)
    turn = 0
    while flows:
        flows = [flow for flow in flows if next(flow, flows) is not flows]
        if pump is not None and turn < len(pump[1]):
            pump[0].pump(pump[1][turn])
        turn += 1


def lanes(ref, size):
    return lambda d: ref.at[:, pl.ds(pl.multiple_of(d * size, size), size)]


def fetch(sources, targets, sems):
    copies = [pltpu.make_async_copy(s, t, sems.at[i]) for i, (s, t) in enumerate(zip(sources, targets))]
    for copy in copies:
        copy.start()
    return copies


def as_row(ref):
    return ref[...].reshape(1, ref.shape[0])


def lengths_row(lens):
    groups, per_group = lens.shape
    values = lens[...].astype(f32)
    at = lax.broadcasted_iota(jnp.int32, (per_group, groups * per_group), 1)
    inner = lax.broadcasted_iota(jnp.int32, (per_group, groups * per_group), 0)
    total = jnp.zeros((1, groups * per_group), f32)
    for g in range(groups):
        place = jnp.where(at == inner + g * per_group, 1.0, 0.0)
        total = total + jnp.dot(
            values[g : g + 1, :], place, precision=lax.Precision.HIGHEST, preferred_element_type=f32
        )
    return total


def spray(axis, src_of, dst, send, recv, base=0):
    copies = []
    for k in range(1, lax.axis_size(axis)):
        copy = remote(src_of(k), dst.at[k - 1], send.at[base + k - 1], recv.at[base + k - 1], away(axis, k))
        copy.start()
        copies.append(copy)
    return copies


def wait_all(copies):
    for copy in copies:
        copy.wait()


def swap(axis, src, dst, send, recv):
    copy = remote(src, dst, send, recv, away(axis, 1))
    copy.start()
    return copy


def sequence_rows(lens_row, order_row, per_group):
    count = lens_row.shape[1]
    ri = lax.broadcasted_iota(jnp.int32, (count, count), 0)
    ci = lax.broadcasted_iota(jnp.int32, (count, count), 1)
    lens_f = lens_row

    def to_column(row):
        return jnp.sum(jnp.where(ri == ci, row, 0.0), axis=1, keepdims=True)

    order_col = to_column(order_row.astype(f32)).astype(jnp.int32)
    lens_col = to_column(lens_f)
    pick = order_row == ri
    pick_t = order_col == ci
    slot_col = jnp.sum(jnp.where(pick_t, lens_f, 0.0), axis=1, keepdims=True)
    slot_row = jnp.sum(jnp.where(pick, lens_col, 0.0), axis=0, keepdims=True)
    start_col = jnp.sum(jnp.where(ci < ri, slot_row, 0.0), axis=1, keepdims=True)
    input_row = jnp.sum(jnp.where(pick_t, start_col, 0.0), axis=0, keepdims=True)
    same = (ri // per_group) == (ci // per_group)
    group_row = jnp.sum(jnp.where((ri < ci) & same, lens_col, 0.0), axis=0, keepdims=True)
    return lens_f, input_row, group_row


def place_rows(lens_row, order_row, per_group, group_rows, group):
    lens_f, input_row, group_row = sequence_rows(lens_row, order_row, per_group)
    count = lens_row.shape[1]
    rows = lax.broadcasted_iota(jnp.int32, (group_rows, count), 0).astype(f32)
    mine = (lax.broadcasted_iota(jnp.int32, (group_rows, count), 1) // per_group) == group
    inside = (rows >= group_row) & (rows < group_row + lens_f) & mine
    within = jnp.sum(jnp.where(inside, rows - group_row, 0.0), axis=1, keepdims=True)
    begin = jnp.sum(jnp.where(inside, input_row, 0.0), axis=1, keepdims=True)
    return begin + within, within


def owner_rows(lens_row, order_row, per_group, group_rows, block_rows, first):
    lens_f, input_row, group_row = sequence_rows(lens_row, order_row, per_group)
    count = lens_row.shape[1]
    rows = (lax.broadcasted_iota(jnp.int32, (block_rows, count), 0) + first).astype(f32)
    base = (lax.broadcasted_iota(jnp.int32, (block_rows, count), 1) // per_group) * group_rows
    inside = (rows >= input_row) & (rows < input_row + lens_f)
    found = jnp.where(inside, base.astype(f32) + group_row + rows - input_row, 0.0)
    return jnp.sum(found, axis=1, keepdims=True)


def plane_origin(rows, dp_size, col_size, block_rows):
    at = lax.broadcasted_iota(jnp.int32, (rows, dp_size * col_size * block_rows), 1)
    block = at // block_rows
    group = lax.rem(block, dp_size)
    column = block // dp_size
    return ((group * col_size + column) * block_rows + lax.rem(at, block_rows)).astype(f32)


def pick_rows(wanted, held):
    col_size, dp_size, block_rows, width = held.shape
    total = col_size * dp_size * block_rows
    chosen = wanted == plane_origin(wanted.shape[0], dp_size, col_size, block_rows)
    chosen = jnp.where(chosen, 1.0, 0.0).astype(bf16)
    return matmul(chosen, held.reshape(total, width)).astype(bf16)


def plane_start(src, held, send, recv):
    me, column = lax.axis_index("dp"), lax.axis_index("col")
    held[column, me] = src[...]
    copies = []
    for k in range(1, lax.axis_size("dp")):
        copy = remote(src, held.at[column, me], send.at[k], recv.at[k], away("dp", k))
        copy.start()
        copies.append(copy)
    return copies


def plane_finish(copies, held, send, recv):
    column = lax.axis_index("col")
    for copy in copies:
        copy.wait_recv()
    copy = swap("col", held.at[column], held.at[column], send.at[0], recv.at[0])
    copy.wait_recv()
    for one in copies + [copy]:
        one.wait_send()


def total_of_sums(part, half_own, half_in, low_own, low_in, full, sems):
    send, recv = sems
    rows = part.shape[0] // 2
    column = lax.axis_index("col")
    mine = pl.ds(pl.multiple_of(column * rows, rows), rows)
    other = pl.ds(pl.multiple_of((1 - column) * rows, rows), rows)
    half_own[...] = part[other, :]
    copy = swap("col", half_own, half_in, send.at[0], recv.at[0])
    yield
    copy.wait()
    low_own[...] = (part[mine, :] + half_in[...]).astype(bf16)
    copies = spray("row", lambda k: low_own, low_in, send, recv, 1)
    yield
    wait_all(copies)
    total = low_own[...].astype(f32)
    for k in range(low_in.shape[0]):
        total = total + low_in[k].astype(f32)
    full[mine, :] = total
    copy = swap("col", full.at[mine], full.at[mine], send.at[4], recv.at[4])
    yield
    copy.wait()


def lanes_like(tile, width):
    if tile.shape[-1] == width:
        return tile
    return jnp.concatenate([tile] * (width // tile.shape[-1]), axis=-1)


def lane_mask(count, lanes, first):
    lane = lax.broadcasted_iota(jnp.int32, (count, lanes), 1)
    return lane == lax.broadcasted_iota(jnp.int32, (count, lanes), 0) + first


def spread(values, first, count, wide):
    rows, lanes = values.shape
    chosen = jnp.where(lane_mask(count, lanes, first)[None], values[:, None, :], 0.0)
    chosen = chosen.reshape(rows * count, lanes)
    high = chosen.astype(bf16)
    rest = (chosen - high.astype(f32)).astype(bf16)
    ones = jnp.ones((lanes, wide), bf16)
    return matmul(high, ones) + matmul(rest, ones)


def lane_sums(values, first, lanes):
    rows, count, wide = values.shape
    flat = values.reshape(rows * count, wide)
    high = flat.astype(bf16)
    rest = (flat - high.astype(f32)).astype(bf16)
    ones = jnp.ones((wide, lanes), bf16)
    sums = (matmul(high, ones) + matmul(rest, ones)).reshape(rows, count, lanes)
    return jnp.sum(jnp.where(lane_mask(count, lanes, first)[None], sums, 0.0), axis=1)


def scan_forward(proj, b_at, c_at, gone_step, drive, rate, bb, cb, y):
    rows, width = drive.shape
    count = rate.shape[0]
    piece, _, wide = bb.shape
    state = jnp.zeros((count, width), f32)
    for start in range(0, rows, piece):
        values = proj[start : start + piece, :]
        bb[...] = spread(values, b_at, count, wide).reshape(bb.shape)
        cb[...] = spread(values, c_at, count, wide).reshape(cb.shape)

        def eight(k, state):
            inner = pl.multiple_of(k * 8, 8)
            base = pl.multiple_of(start + k * 8, 8)
            gone = gone_step[pl.ds(base, 8), :]
            driven = drive[pl.ds(base, 8), :]
            found = []
            for i in range(8):
                decay = jnp.exp(gone[i : i + 1, :] * rate)
                state = decay * state + driven[i : i + 1, :] * lanes_like(bb[inner + i], width)
                found.append(jnp.sum(state * lanes_like(cb[inner + i], width), axis=0, keepdims=True))
            y[pl.ds(base, 8), :] = jnp.concatenate(found, axis=0)
            return state

        state = lax.fori_loop(0, piece // 8, eight, state)
        yield


def scan_states(proj, b_at, gone_step, drive, rate, bb, hs):
    rows, width = drive.shape
    count = rate.shape[0]
    piece, _, wide = bb.shape
    hs[0] = jnp.zeros((count, width), f32)
    for start in range(0, rows, piece):
        bb[...] = spread(proj[start : start + piece, :], b_at, count, wide).reshape(bb.shape)

        def eight(k, state):
            inner = pl.multiple_of(k * 8, 8)
            base = pl.multiple_of(start + k * 8, 8)
            gone = gone_step[pl.ds(base, 8), :]
            driven = drive[pl.ds(base, 8), :]
            for i in range(8):
                decay = jnp.exp(gone[i : i + 1, :] * rate)
                state = decay * state + driven[i : i + 1, :] * lanes_like(bb[inner + i], width)
                hs[base + i + 1] = state
            return state

        lax.fori_loop(0, piece // 8, eight, hs[start])
        yield


def scan_backward(
    proj, b_at, c_at, step, gone_step, drive, inner_u, dy, rate, hs, bb, cb, pb, pc, du, dstep, dproj
):
    rows, width = drive.shape
    count = rate.shape[0]
    piece, _, wide = bb.shape

    def fold(values):
        total = values[:, 0:wide]
        for j in range(1, width // wide):
            total = total + values[:, j * wide : (j + 1) * wide]
        return total

    def part(start, carry):
        values = proj[start : start + piece, :]
        bb[...] = spread(values, b_at, count, wide).reshape(bb.shape)
        cb[...] = spread(values, c_at, count, wide).reshape(cb.shape)

        def eight(k, carry):
            later, total = carry
            inner = pl.multiple_of((piece // 8 - 1 - k) * 8, 8)
            base = pl.multiple_of(start + inner, 8)
            step8 = step[pl.ds(base, 8), :]
            gone8 = gone_step[pl.ds(base, 8), :]
            drive8 = drive[pl.ds(base, 8), :]
            u8 = inner_u[pl.ds(base, 8), :]
            dy8 = dy[pl.ds(base, 8), :]
            by_b = [None] * 8
            by_rate = [None] * 8
            for i in reversed(range(8)):
                dy_row = dy8[i : i + 1, :]
                lam = lanes_like(cb[inner + i], width) * dy_row + later
                later = jnp.exp(gone8[i : i + 1, :] * rate) * lam
                kept = later * hs[base + i]
                total = total + kept * step8[i : i + 1, :]
                by_b[i] = jnp.sum(lam * lanes_like(bb[inner + i], width), axis=0, keepdims=True)
                by_rate[i] = jnp.sum(kept * rate, axis=0, keepdims=True)
                pb[inner + i] = fold(lam * drive8[i : i + 1, :])
                pc[inner + i] = fold(hs[base + i + 1] * dy_row)
            by_b = jnp.concatenate(by_b, axis=0)
            by_rate = jnp.concatenate(by_rate, axis=0)
            du[pl.ds(base, 8), :] = by_b * step8
            dstep[pl.ds(base, 8), :] = by_rate + by_b * u8
            return later, total

        carry = lax.fori_loop(0, piece // 8, eight, carry)
        dproj[start : start + piece, :] += lane_sums(pb[...], b_at, dproj.shape[1]) + lane_sums(
            pc[...], c_at, dproj.shape[1]
        )
        return carry

    blank = jnp.zeros((count, width), f32)
    carry = (blank, blank)
    for start in reversed(range(0, rows, piece)):
        carry = part(start, carry)
        yield
    return carry[1] * rate


RANK_LANES = 128


def scan_kernel(proj, gone, drive, rate, y, bb, cb, *, b_at, c_at):
    run(scan_forward(proj, b_at, c_at, gone, drive, rate[...], bb, cb, y))


def adjoint_kernel(
    proj, step, gone, drive, inner_u, dy, rate, du, dstep, dproj, drate, bb, cb, hs, pb, pc, *, b_at, c_at
):
    run(scan_states(proj, b_at, gone, drive, rate[...], bb, hs))
    dproj[...] = jnp.zeros_like(dproj)
    kept = {}

    def adjoint():
        kept["rate"] = yield from scan_backward(
            proj, b_at, c_at, step, gone, drive, inner_u, dy, rate[...], hs, bb, cb, pb, pc, du, dstep, dproj
        )

    run(adjoint())
    drate[...] = kept["rate"]


def scan_sizes(rows, width, count):
    wide = 128 if width % 128 == 0 else width
    piece = min(128, rows)
    return pltpu.VMEM((piece, count, wide), f32)


def scan_alone(proj, gone, drive, rate, b_at, c_at):
    rows, width = drive.shape
    block = scan_sizes(rows, width, rate.shape[0])
    return pl.pallas_call(
        functools.partial(scan_kernel, b_at=b_at, c_at=c_at),
        out_shape=jax.ShapeDtypeStruct((rows, width), f32),
        scratch_shapes=[block, block],
        compiler_params=pltpu.CompilerParams(vmem_limit_bytes=VMEM_BYTES),
        name="scan_states",
    )(proj, gone, drive, rate)


def adjoint_alone(proj, step, gone, drive, inner_u, dy, rate, b_at, c_at):
    rows, width = step.shape
    count = rate.shape[0]
    block = scan_sizes(rows, width, count)
    shape = jax.ShapeDtypeStruct
    return pl.pallas_call(
        functools.partial(adjoint_kernel, b_at=b_at, c_at=c_at),
        out_shape=(
            shape((rows, width), f32),
            shape((rows, width), f32),
            shape(proj.shape, f32),
            shape((count, width), f32),
        ),
        scratch_shapes=[
            block,
            block,
            pltpu.VMEM((rows + 1, count, width), f32),
            block,
            block,
        ],
        compiler_params=pltpu.CompilerParams(vmem_limit_bytes=VMEM_BYTES),
        name="scan_adjoint",
    )(proj, step, gone, drive, inner_u, dy, rate)


PUMPS = ((0, 1, 1), (1, 0, 1), 0, (1, 1, 1), (1, 1), (0, 0, 0), (1, 1, 1), 0, 2)


def conv_sum(inner_x, place, taps, bias):
    count = taps.shape[0]
    total = bias + inner_x * taps[count - 1 : count, :]
    for shift in range(1, count):
        moved = jnp.where(place >= shift, pltpu.roll(inner_x, shift, 0), 0.0)
        total = total + moved * taps[count - 1 - shift : count - shift, :]
    return total


def transposed(left, right):
    return lax.dot_general(left, right, (((1,), (1,)), ((), ())), preferred_element_type=f32)


def over_rows(left, right):
    return lax.dot_general(left, right, (((0,), (0,)), ((), ())), preferred_element_type=f32)


def columns(d, size):
    return pl.ds(pl.multiple_of(d * size, size), size)


def line_total(own, arrived):
    total = own
    for k in range(arrived.shape[0]):
        total = total + arrived[k]
    return total


def forward_kernel(
    x, cot, lens, order, gain1, taps, bias, w_xp, w_dt, dt_bias, a_log, skip, gain2,
    w_x_h, w_z_h, w_out_h, w_gate_h, w_up_h, w_down_h,
    xg_o, cg_o, n1_o, s1_o, place_o, xi_o, z_o, proj_o, yv_o, go_all, h1_o, s2_o, n2_o, hid_all, dgu_o, dot_o,
    w_x, w_z, w_out, w_gate, w_up, w_down, w_step, rate,
    x_all, c_all, sum_own, sum_in, low, xi_held, xi_left, xi_right, z_held, z_left, z_right,
    part_s, half_own, half_in, low_own, low_in, bb, cb, step, gone, drive,
    own, other, gu, gu_held, gu_left, gu_right, dhid, h_held, h_left, h_right,
    w_sems, x_send, x_recv, c_send, c_recv, sum_send, sum_recv, xi_send, xi_recv, z_send, z_recv, t_send, t_recv,
    go_send, go_recv, o_send, o_recv, sum2_send, sum2_recv, gu_send, gu_recv, h_send, h_recv, hid_send, hid_recv,
    *, model_width, rank, count
):
    rows, width = xi_o.shape
    hidden = dgu_o.shape[1] // 2
    group, row = lax.axis_index("dp"), lax.axis_index("row")
    row_size = lax.axis_size("row")
    weights = fetch(
        (w_x_h, w_z_h, w_out_h, w_gate_h, w_up_h, w_down_h), (w_x, w_z, w_out, w_gate, w_up, w_down), w_sems
    )
    greet("dp", "row", "col")
    x_copies = plane_start(x, x_all, x_send, x_recv)
    lens_row = lengths_row(lens)
    source, place = place_rows(lens_row, as_row(order), lens.shape[1], rows, group)
    place_o[...] = place
    w_step[...] = jnp.zeros_like(w_step)
    w_step[0:rank, :] = w_dt[...]
    plane_finish(x_copies, x_all, x_send, x_recv)
    c_copies = plane_start(cot, c_all, c_send, c_recv)
    xg_low = pick_rows(source, x_all[...])
    xg_o[...] = xg_low
    xg = xg_low.astype(f32)
    gain1_now = as_row(gain1)
    low[...] = (xg * gain1_now).astype(bf16)
    weights[0].wait()
    kept = {}

    def during_xi():
        sum_own[...] = rows_form(xg * xg)
        sum_copies = spray("row", lambda k: sum_own, sum_in, sum_send, sum_recv)
        rate[...] = -jnp.exp(a_log[...])
        yield
        wait_all(sum_copies)
        kept["s1"] = column_form(lax.rsqrt(line_total(sum_own[...], sum_in) / model_width + epsilon))
        s1_o[...] = kept["s1"]

    run(
        *scatter_halves(
            "row", lambda d, at: matmul(low[at, :], w_x[:, columns(d, width)]), xi_o, xi_held, xi_left, xi_right,
            xi_send, xi_recv,
        ),
        during_xi(),
    )
    s1 = kept["s1"]
    inner_x = xi_o[...] * s1
    xi_o[...] = inner_x
    u_low = silu(conv_sum(inner_x, place, taps[...], as_row(bias))).astype(bf16)
    u = u_low.astype(f32)
    part_s[...] = matmul(u_low, w_xp[...])

    z_flows = scatter_halves(
        "row", lambda d, at: matmul(low[at, :], w_z[:, columns(d, width)]), z_o, z_held, z_left, z_right, z_send, z_recv
    )

    def mix():
        yield from total_of_sums(part_s, half_own, half_in, low_own, low_in, proj_o, (t_send, t_recv))
        pre = matmul(proj_o[...].astype(bf16), w_step[...]) + as_row(dt_bias)
        step_now = jax.nn.softplus(pre)
        step[...] = step_now
        gone[...] = jnp.where(place > 0.0, step_now, 1e30)
        drive[...] = step_now * u
        yield from scan_forward(proj_o, rank, rank + count, gone, drive, rate[...], bb, cb, yv_o)

    mixing = mix()
    next(mixing)
    next(mixing)
    weights[1].wait()
    run(*z_flows, mixing)
    yv = yv_o[...] + as_row(skip) * u
    yv_o[...] = yv
    z = z_o[...] * s1
    z_o[...] = z
    go_all[:, columns(row, width)] = (yv * silu(z)).astype(bf16)

    def during_gather():
        n1_o[...] = (xg * s1 * gain1_now).astype(bf16)
        plane_finish(c_copies, c_all, c_send, c_recv)
        cg_o[...] = pick_rows(source, c_all[...])
        yield

    run(*gather_halves("row", go_all, width, go_send, go_recv), during_gather())
    weights[2].wait()
    own[...] = matmul(go_all[...], w_out[...])
    copy = swap("col", own, other, o_send.at[0], o_recv.at[0])
    weights[3].wait()
    weights[4].wait()
    copy.wait()
    h1 = xg + (own[...] + other[...])
    h1_o[...] = h1
    gain2_now = as_row(gain2)
    low[...] = (h1 * gain2_now).astype(bf16)

    def gate_up(d, at):
        side = columns(d, hidden)
        return jnp.concatenate([matmul(low[at, :], w_gate[:, side]), matmul(low[at, :], w_up[:, side])], axis=1)

    def during_scatter():
        sum_own[...] = rows_form(h1 * h1)
        sum_copies = spray("row", lambda k: sum_own, sum_in, sum2_send, sum2_recv)
        yield
        wait_all(sum_copies)
        s2 = column_form(lax.rsqrt(line_total(sum_own[...], sum_in) / model_width + epsilon))
        s2_o[...] = s2
        n2_o[...] = (h1 * s2 * gain2_now).astype(bf16)

    run(
        *scatter_halves("row", gate_up, gu, gu_held, gu_left, gu_right, gu_send, gu_recv),
        during_scatter(),
    )
    s2 = s2_o[...]
    gate = gu[:, 0:hidden] * s2
    up = gu[:, hidden:] * s2
    sig = jax.nn.sigmoid(gate)
    act = gate * sig
    hid_all[:, columns(row, hidden)] = (act * up).astype(bf16)
    weights[5].wait()
    run(
        *gather_halves("row", hid_all, hidden, hid_send, hid_recv),
        *scatter_halves(
            "row", lambda d, at: transposed(cg_o[at, :], w_down[columns(d, hidden), :]), dhid, h_held, h_left, h_right,
            h_send, h_recv,
        ),
    )
    d_hid = dhid[...]
    d_gate = (d_hid * up * (sig * (1.0 + gate * (1.0 - sig)))).astype(bf16)
    d_up = (d_hid * act).astype(bf16)
    dgu_o[:, 0:hidden] = d_gate
    dgu_o[:, hidden:] = d_up
    dot_o[...] = rows_form(d_gate.astype(f32) * gate + d_up.astype(f32) * up)


def add_rows(target, base, source, rows):
    def piece(j, _):
        at = pl.ds(pl.multiple_of(base + j * 16, 16), 16)
        found = target[at, :].astype(f32) + source[pl.ds(pl.multiple_of(j * 16, 16), 16), :].astype(f32)
        target[at, :] = found.astype(target.dtype)
        return 0

    lax.fori_loop(0, rows // 16, piece, 0)


def plane_sum(grad, first_in, second_in, send, recv, free):
    quarter = grad.shape[0] // 4
    eighth = quarter // 2
    me = lax.axis_index("dp")
    bits = (lax.rem(me, 2), me // 2)
    partners = ({"dp": me + 1 - 2 * bits[0]}, {"dp": me + 2 - 4 * bits[1]})

    def rows(ref, start, count):
        return ref.at[pl.ds(pl.multiple_of(start, 16), count), :]

    class Half:
        def __init__(self, h):
            near, far = bits[h], bits[1 - h]
            self.free, self.mate, self.first = free.at[h], partners[h], first_in.at[h]
            base = h * 2 * quarter
            self.kept = base + near * quarter
            self.own = self.kept + far * eighth
            self.rest = self.kept + (1 - far) * eighth
            self.rest_in = (1 - far) * eighth
            across = base + (1 - near) * quarter
            self.second = second_in.at[h]

            def copy(stage, src, dst, to):
                return remote(src, dst, send.at[stage, h], recv.at[stage, h], to)

            mate, other = partners[h], partners[1 - h]
            own, rest = rows(grad, self.own, eighth), rows(grad, self.rest, eighth)
            there = (rows(grad, across + far * eighth, eighth), rows(grad, across + (1 - far) * eighth, eighth))
            back = rows(self.first, self.rest_in, eighth)
            self.out = (
                copy(0, rows(grad, across, quarter), self.first, mate),
                copy(1, rest, self.second, other),
                copy(2, own, rows(self.first, far * eighth, eighth), other),
                copy(3, own, own, mate),
                copy(4, rest, rest, mate),
            )
            self.back = (
                None,
                None,
                copy(2, back, back, other),
                copy(3, there[0], there[0], mate),
                copy(4, there[1], there[1], mate),
            )

    halves = (Half(0), Half(1))
    for half in halves:
        half.out[0].start()
    yield
    for half in halves:
        half.out[0].wait_recv()
        add_rows(grad, half.kept, half.first, quarter)
        half.out[1].start()
        half.out[0].wait_send()
        pl.semaphore_signal(half.free, inc=1, device_id=half.mate, device_id_type=MESH)
    yield
    for half in halves:
        half.out[1].wait_recv()
        add_rows(grad, half.own, half.second, eighth)
        half.out[2].start()
        pl.semaphore_wait(half.free, 1)
        half.out[3].start()
    yield
    for half in halves:
        half.back[2].wait_recv()
        half.out[1].wait_send()
        grad[pl.ds(pl.multiple_of(half.rest, 16), eighth), :] = half.first[
            pl.ds(pl.multiple_of(half.rest_in, 16), eighth), :
        ]
        half.out[4].start()
    yield
    for half in halves:
        half.back[3].wait_recv()
        half.back[4].wait_recv()
        for copy in half.out[2:]:
            copy.wait_send()


class Sums:
    def __init__(self):
        self.active = []

    def add(self, flow):
        next(flow)
        self.active.append(flow)

    def pump(self, count=1):
        for _ in range(count):
            if self.active:
                flow = self.active.pop(0)
                if next(flow, self) is not self:
                    self.active.append(flow)

    def drain(self):
        while self.active:
            self.pump()


def backward_kernel(
    lens, order, dgu, dot, gain2, cg, h1, s2, hid_all, go_all, n1, n2,
    z, yv, xi, proj, place, taps, bias, w_xp, w_dt, dt_bias, a_log, skip, xg, s1, gain1,
    w_gate_h, w_up_h, w_down_h, w_out_h, w_x_h, w_z_h,
    y_o, dx_o, small_o, g_down_o, g_gate_o, g_up_o, g_out_o, g_z_o, g_x_o,
    w_gate, w_up, w_down, w_out, w_x, w_z, w_step, rate,
    dg_all, du_all, dz_all, dxi_all, dh1, dmix, y_own, dx_own, y_all, dx_all,
    own, other, y_part, y_other, dot_in, dot_own, dot_sum, dot_other,
    dgo, d_held, d_left, d_right,
    hs, bb, cb, pb, pc, step, gone, drive, u_s, dy_s, du_s, dstep, dproj,
    half_own, half_in, low_own, low_in, full,
    g_down, g_gate, g_up, g_out, g_z, g_x, small,
    g_down_1, g_gate_1, g_up_1, g_out_1, g_z_1, g_x_1, small_1,
    g_down_2, g_gate_2, g_up_2, g_out_2, g_z_2, g_x_2, small_2,
    w_sems, g_send, g_recv, u_send, u_recv, o_send, o_recv, dot_send, dot_recv,
    y_send, y_recv, dx_send, dx_recv, d_send, d_recv, z_send, z_recv, t_send, t_recv, x_send, x_recv,
    dot2_send, dot2_recv, sum_send, sum_recv, sum_free, write_sems,
    *, rank, model_width
):
    rows, width = z.shape
    hidden = dgu.shape[1] // 2
    count = rate.shape[0]
    block = y_o.shape[0]
    tap_count = taps.shape[0]
    group, row, column = lax.axis_index("dp"), lax.axis_index("row"), lax.axis_index("col")
    row_size, col_size = lax.axis_size("row"), lax.axis_size("col")
    weights = fetch(
        (w_down_h, w_gate_h, w_up_h, w_out_h, w_x_h, w_z_h), (w_down, w_gate, w_up, w_out, w_x, w_z), w_sems
    )
    half = columns(column, block)
    sums = Sums()
    writes = []

    def total(number, grad, first_in, second_in, result):
        yield from plane_sum(
            grad, first_in, second_in, sum_send.at[number], sum_recv.at[number], sum_free.at[number]
        )
        write = pltpu.make_async_copy(grad, result, write_sems.at[number])
        write.start()
        writes.append(write)

    def product(left, right, grad):
        size = grad.shape[0] // 4
        for start in range(0, grad.shape[0], size):
            grad[start : start + size, :] = over_rows(left[:, start : start + size], right[...]).astype(bf16)

    dg_all[:, columns(row, hidden)] = dgu[:, 0:hidden]
    du_all[:, columns(row, hidden)] = dgu[:, hidden:]
    greet("dp", "row", "col")
    dot_copies = spray("row", lambda k: dot, dot_in, dot_send, dot_recv)

    def first_work():
        product(hid_all, cg, g_down)
        sums.add(total(0, g_down, g_down_1, g_down_2, g_down_o))
        yield
        weights[0].wait()
        y_part[...] = matmul(hid_all[...], w_down[...])
        y_copy = swap("col", y_part, y_other, o_send.at[0], o_recv.at[0])
        yield
        wait_all(dot_copies)
        dot_own[...] = line_total(dot[...], dot_in)
        dot_copy = swap("col", dot_own, dot_other, o_send.at[2], o_recv.at[2])
        weights[1].wait()
        weights[2].wait()
        yield
        y_copy.wait()
        dot_copy.wait()
        y_own[...] = (h1[...] + (y_part[...] + y_other[...])).astype(bf16)

    run(*gather_halves("row", dg_all, hidden, g_send, g_recv), first_work(), pump=(sums, PUMPS[0]))
    product(n2, dg_all, g_gate)
    sums.add(total(1, g_gate, g_gate_1, g_gate_2, g_gate_o))

    def second_work():
        own[...] = transposed(dg_all[...], w_gate[...])
        yield

    run(*gather_halves("row", du_all, hidden, u_send, u_recv), second_work(), pump=(sums, PUMPS[1]))
    own[...] += transposed(du_all[...], w_up[...])
    copy = swap("col", own, other, o_send.at[1], o_recv.at[1])
    product(n2, du_all, g_up)
    sums.add(total(2, g_up, g_up_1, g_up_2, g_up_o))
    sums.pump(PUMPS[2])
    copy.wait()
    h1_now, s2_now = h1[...], s2[...]
    dn2 = own[...] + other[...]
    dots = column_form(dot_own[...] + dot_other[...])
    dh1_now = (
        cg[...].astype(f32)
        + s2_now * (as_row(gain2) * dn2)
        - h1_now * (s2_now * s2_now * dots / model_width)
    )
    dh1[...] = dh1_now
    dmix[...] = dh1_now.astype(bf16)
    gnorm2 = jnp.sum(dn2 * h1_now * s2_now, axis=0, keepdims=True)

    inner_x = xi[...]
    place_now = place[...]
    kept = {}

    def states():
        product(go_all, dmix, g_out)
        sums.add(total(3, g_out, g_out_1, g_out_2, g_out_o))
        w_step[...] = jnp.zeros_like(w_step)
        w_step[0:rank, :] = w_dt[...]
        rate[...] = -jnp.exp(a_log[...])
        xc = conv_sum(inner_x, place_now, taps[...], as_row(bias))
        sig_c = jax.nn.sigmoid(xc)
        u_low = (xc * sig_c).astype(bf16)
        u = u_low.astype(f32)
        u_s[...] = u
        step_low = proj[...].astype(bf16)
        pre = matmul(step_low, w_step[...]) + as_row(dt_bias)
        step_now = jax.nn.softplus(pre)
        step[...] = step_now
        gone[...] = jnp.where(place_now > 0.0, step_now, 1e30)
        drive[...] = step_now * u
        kept.update(xc=xc, sig_c=sig_c, u_low=u_low, u=u, step_low=step_low, pre=pre)
        yield from scan_states(proj, rank, gone, drive, rate[...], bb, hs)

    weights[3].wait()
    run(
        *scatter_halves(
            "row", lambda d, at: transposed(dmix[at, :], w_out[columns(d, width), :]), dgo, d_held, d_left, d_right,
            d_send, d_recv,
        ),
        states(),
        pump=(sums, PUMPS[3]),
    )
    xc, sig_c, u_low, u = kept["xc"], kept["sig_c"], kept["u_low"], kept["u"]
    step_low, pre = kept["step_low"], kept["pre"]
    z_now = z[...]
    sig_z = jax.nn.sigmoid(z_now)
    d_z = (dgo[...] * yv[...] * (sig_z * (1.0 + z_now * (1.0 - sig_z)))).astype(bf16)
    mine = dz_all.at[:, columns(row, width)]
    mine[...] = d_z
    z_copies = []
    for k in range(1, row_size):
        copy = remote(mine, mine, z_send.at[k - 1], z_recv.at[k - 1], away("row", k))
        copy.start()
        z_copies.append(copy)
    dy = dgo[...] * (z_now * sig_z)
    dy_s[...] = dy
    dproj[...] = jnp.zeros_like(dproj)

    def adjoint():
        kept["rate"] = yield from scan_backward(
            proj, rank, rank + count, step, gone, drive, u_s, dy_s, rate[...], hs, bb, cb, pb, pc, du_s, dstep, dproj
        )

    run(adjoint(), pump=(sums, PUMPS[4]))
    g_rate = kept["rate"]
    d_pre = dstep[...] * jax.nn.sigmoid(pre)
    d_pre_low = d_pre.astype(bf16)
    dproj[...] += transposed(d_pre_low, w_step[...])

    def during_sums():
        yield
        wait_all(z_copies)
        product(n1, dz_all, g_z)
        sums.add(total(4, g_z, g_z_1, g_z_2, g_z_o))

    run(
        total_of_sums(dproj, half_own, half_in, low_own, low_in, full, (t_send, t_recv)),
        during_sums(),
        pump=(sums, PUMPS[5]),
    )
    dproj_low = full[...].astype(bf16)
    du = du_s[...] + as_row(skip) * dy + transposed(dproj_low, w_xp[...])
    dxc = du * (sig_c * (1.0 + xc * (1.0 - sig_c)))
    taps_now = taps[...]
    d_inner = dxc * taps_now[tap_count - 1 : tap_count, :]
    masked = [dxc]
    for shift in range(1, tap_count):
        masked.append(jnp.where(place_now >= shift, dxc, 0.0))
        k = tap_count - 1 - shift
        d_inner = d_inner + pltpu.roll(masked[shift], rows - shift, 0) * taps_now[k : k + 1, :]
    d_inner = d_inner.astype(bf16)
    dxi_all[:, columns(row, width)] = d_inner

    def during():
        dot_own[...] = rows_form(d_inner.astype(f32) * inner_x + d_z.astype(f32) * z_now)
        dot_copies = spray("row", lambda k: dot_own, dot_in, dot2_send, dot2_recv)
        small[0:RANK_LANES, :] = over_rows(dproj_low, u_low).astype(bf16)
        small[RANK_LANES : RANK_LANES + rank, :] = over_rows(step_low, d_pre_low)[0:rank, :].astype(bf16)
        yield
        wait_all(dot_copies)
        dot_sum[...] = line_total(dot_own[...], dot_in)
        dot_copy = swap("col", dot_sum, dot_other, o_send.at[3], o_recv.at[3])
        weights[4].wait()
        weights[5].wait()
        own[...] = transposed(dz_all[...], w_z[...])
        yield
        dot_copy.wait()

    run(*gather_halves("row", dxi_all, width, x_send, x_recv), during(), pump=(sums, PUMPS[6]))
    own[...] += transposed(dxi_all[...], w_x[...])
    copy = swap("col", own, other, o_send.at[4], o_recv.at[4])
    product(n1, dxi_all, g_x)
    sums.add(total(5, g_x, g_x_1, g_x_2, g_x_o))
    sums.pump(PUMPS[7])
    copy.wait()
    dn1 = own[...] + other[...]
    s1_now = s1[...]
    xg_now = xg[...].astype(f32)
    dots = column_form(dot_sum[...] + dot_other[...])
    dx = dh1[...] + s1_now * (as_row(gain1) * dn1) - xg_now * (s1_now * s1_now * dots / model_width)
    dx_own[...] = dx.astype(bf16)
    dx_copies = plane_start(dx_own.at[half], dx_all, dx_send, dx_recv)
    y_copies = plane_start(y_own.at[half], y_all, y_send, y_recv)
    g_taps = [None] * tap_count
    for shift in range(tap_count):
        moved = pltpu.roll(inner_x, shift, 0) if shift else inner_x
        g_taps[tap_count - 1 - shift] = jnp.sum(masked[shift] * moved, axis=0, keepdims=True)
    pieces = [
        g_rate,
        *g_taps,
        jnp.sum(dxc, axis=0, keepdims=True),
        jnp.sum(d_pre, axis=0, keepdims=True),
        jnp.sum(dy * u, axis=0, keepdims=True),
        jnp.sum(dn1 * xg_now * s1_now, axis=0, keepdims=True),
        gnorm2,
    ]
    found = sum(piece.shape[0] for piece in pieces)
    pieces.append(jnp.zeros((small.shape[0] - RANK_LANES - rank - found, width), f32))
    small[RANK_LANES + rank :, :] = jnp.concatenate(pieces, axis=0).astype(bf16)
    sums.add(total(6, small, small_1, small_2, small_o))
    first = (group * col_size + column) * block
    wanted = owner_rows(lengths_row(lens), as_row(order), lens.shape[1], rows, block, first)
    sums.pump(PUMPS[8])
    plane_finish(dx_copies, dx_all, dx_send, dx_recv)
    dx_o[...] = pick_rows(wanted, dx_all[...])
    plane_finish(y_copies, y_all, y_send, y_recv)
    y_o[...] = pick_rows(wanted, y_all[...])
    sums.drain()
    for write in writes:
        write.wait()


def finish_kernel(
    y, dx, small, down, gate, up, out, z, x,
    y_o, dx_o, norm1_o, z_o, x_o, taps_o, bias_o, w_xp_o, w_dt_o, dt_bias_o, rate_o, skip_o, out_o, norm2_o, gate_o,
    up_o, down_o,
    *, rank
):
    for source, target in ((z, z_o), (x, x_o), (out, out_o), (gate, gate_o), (up, up_o), (down, down_o)):
        target[...] = source[...].astype(f32)

    @pl.when(pl.program_id(0) == 0)
    def _():
        y_o[...] = y[...]
        dx_o[...] = dx[...]
        values = small[...].astype(f32)
        w_xp_o[...] = jnp.transpose(values[0:RANK_LANES, :])
        w_dt_o[...] = values[RANK_LANES : RANK_LANES + rank, :]
        at = RANK_LANES + rank
        for target in (rate_o, taps_o):
            target[...] = values[at : at + target.shape[0], :]
            at += target.shape[0]
        for target in (bias_o, dt_bias_o, skip_o, norm1_o, norm2_o):
            target[...] = values[at : at + 1, :].reshape(target.shape)
            at += 1


VMEM_BYTES = 60 << 20
DMA = pltpu.SemaphoreType.DMA


def in_vmem(kernel, name, ident, outs, scratch, args, far=(), micros=50, far_outs=()):
    space = pl.BlockSpec(memory_space=pltpu.VMEM)
    anywhere = pl.BlockSpec(memory_space=pl.ANY)
    return pl.pallas_call(
        kernel,
        out_shape=tuple(jax.ShapeDtypeStruct(shape, kind) for shape, kind in [*outs, *far_outs]),
        in_specs=[space] * len(args) + [anywhere] * len(far),
        out_specs=tuple([space] * len(outs) + [anywhere] * len(far_outs)),
        scratch_shapes=scratch,
        compiler_params=pltpu.CompilerParams(
            collective_id=ident, has_side_effects=True, vmem_limit_bytes=VMEM_BYTES
        ),
        cost_estimate=pl.CostEstimate(flops=micros * 10**9, bytes_accessed=1 << 20, transcendentals=0),
        name=name,
    )(*args, *far)


def both(*shape):
    return [DMA(shape), DMA(shape)]


def on_pairs(
    x_in, lengths, seq_order, norm1_gain, w_in_x, w_in_z, conv_w, conv_b, w_xp, w_dt, dt_bias, a_log,
    skip_weight, w_out, norm2_gain, w_gate, w_up, w_down, cotangent,
):
    dp, rs = lax.axis_size("dp"), lax.axis_size("row")
    block, wide_d = x_in.shape
    rows = block * 2
    model_width = wide_d * rs
    width = conv_w.shape[0]
    hidden = w_gate.shape[1] // rs
    rank, count, taps = w_dt.shape[0], a_log.shape[1], conv_w.shape[1]
    conv_taps = conv_w.T
    rates = a_log.T
    vm = pltpu.VMEM
    tile = vm((128, count, 128), f32)
    big = vm((rows, width), f32)
    model = vm((rows, wide_d), f32)
    sums = [vm((8, rows), f32), vm((rs - 1, 8, rows), f32)]
    sums_scratch = [
        vm((rows // 2, RANK_LANES), f32),
        vm((rows // 2, RANK_LANES), f32),
        vm((rows // 2, RANK_LANES), bf16),
        vm((rs - 1, rows // 2, RANK_LANES), bf16),
    ]

    def weight(value):
        return vm(value.shape, value.dtype)

    def line(size, width):
        return [vm((size, rows, width), bf16)] * 3

    (xg, cg, n1, s1, place, xi, z, proj, yv, go_all, h1, s2, n2, hid_all, dgu, dot) = in_vmem(
        functools.partial(forward_kernel, model_width=model_width, rank=rank, count=count),
        "forward",
        0,
        [
            ((rows, wide_d), bf16), ((rows, wide_d), bf16), ((rows, wide_d), bf16), ((rows, 1), f32), ((rows, 1), f32),
            ((rows, width), f32), ((rows, width), f32), ((rows, RANK_LANES), f32), ((rows, width), f32),
            ((rows, rs * width), bf16), ((rows, wide_d), f32), ((rows, 1), f32), ((rows, wide_d), bf16),
            ((rows, rs * hidden), bf16), ((rows, 2 * hidden), bf16), ((8, rows), f32),
        ],
        [
            weight(w_in_x), weight(w_in_z), weight(w_out), weight(w_gate), weight(w_up), weight(w_down),
            vm((RANK_LANES, width), bf16), vm((count, width), f32),
            vm((2, dp, block, wide_d), bf16), vm((2, dp, block, wide_d), bf16), *sums, vm((rows, wide_d), bf16),
            *line(rs, width), *line(rs, width),
            vm((rows, RANK_LANES), f32), *sums_scratch, tile, tile, big, big, big,
            model, model, vm((rows, 2 * hidden), f32), *line(rs, 2 * hidden), vm((rows, hidden), f32), *line(rs, hidden),
            DMA((6,)), *both(dp), *both(dp), *both(rs - 1), *both(2, 2, rs), *both(2, 2, rs), *both(rs + 1),
            *both(2, 2, rs), *both(1), *both(rs - 1), *both(2, 2, rs), *both(2, 2, rs), *both(2, 2, rs),
        ],
        (
            x_in, cotangent, lengths, seq_order, norm1_gain, conv_taps, conv_b, w_xp, w_dt, dt_bias, rates, skip_weight,
            norm2_gain,
        ),
        (w_in_x, w_in_z, w_out, w_gate, w_up, w_down),
        130,
    )

    def sizes(value, parts):
        return vm((2, value[0] // parts, value[1]), bf16)

    d_cols, f_cols, e_cols = (rs * hidden, wide_d), (wide_d, rs * hidden), (wide_d, rs * width)
    grads = (d_cols, f_cols, f_cols, (rs * width, wide_d), e_cols, e_cols, (2 * RANK_LANES, width))
    returned = in_vmem(
        functools.partial(backward_kernel, rank=rank, model_width=model_width),
        "backward",
        1,
        [((block, wide_d), bf16), ((block, wide_d), bf16)],
        [
            weight(w_gate), weight(w_up), weight(w_down), weight(w_out), weight(w_in_x), weight(w_in_z),
            vm((RANK_LANES, width), bf16), vm((count, width), f32),
            vm((rows, rs * hidden), bf16), vm((rows, rs * hidden), bf16),
            vm((rows, rs * width), bf16), vm((rows, rs * width), bf16),
            model, vm((rows, wide_d), bf16), vm((rows, wide_d), bf16), vm((rows, wide_d), bf16),
            vm((2, dp, block, wide_d), bf16), vm((2, dp, block, wide_d), bf16),
            model, model, model, model, vm((rs - 1, 8, rows), f32), vm((8, rows), f32), vm((8, rows), f32),
            vm((8, rows), f32), big, *line(rs, width),
            vm((rows + 1, count, width), f32), tile, tile, tile, tile,
            big, big, big, big, big, big, big, vm((rows, RANK_LANES), f32), *sums_scratch, vm((rows, RANK_LANES), f32),
            *[vm(value, bf16) for value in grads], *[sizes(value, 4) for value in grads],
            *[sizes(value, 8) for value in grads],
            DMA((6,)), *both(2, 2, rs), *both(2, 2, rs), *both(5), *both(rs - 1), *both(dp), *both(dp), *both(2, 2, rs),
            *both(rs - 1), *both(rs + 1), *both(2, 2, rs), *both(rs - 1), *both(len(grads), 5, 2),
            pltpu.SemaphoreType.REGULAR((len(grads), 2)), DMA((len(grads),)),
        ],
        (
            lengths, seq_order, dgu, dot, norm2_gain, cg, h1, s2, hid_all, go_all, n1, n2,
            z, yv, xi, proj, place, conv_taps, conv_b, w_xp, w_dt, dt_bias, rates, skip_weight, xg, s1, norm1_gain,
        ),
        (w_gate, w_up, w_down, w_out, w_in_x, w_in_z),
        150,
        [(value, bf16) for value in (grads[-1], *grads[:-1])],
    )
    steps = 8

    def pieces(value):
        return pl.BlockSpec((value[0] // steps, value[1]), lambda i: (i, 0))

    def whole(*shape):
        return pl.BlockSpec(shape, lambda i: (0,) * len(shape))

    rows_spec = whole(block, wide_d)
    shape = jax.ShapeDtypeStruct
    outs = (
        (rows_spec, (block, wide_d), bf16), (rows_spec, (block, wide_d), bf16), (whole(wide_d), (wide_d,), f32),
        (pieces(e_cols), e_cols, f32), (pieces(e_cols), e_cols, f32), (whole(taps, width), (taps, width), f32),
        (whole(width), (width,), f32), (whole(width, RANK_LANES), (width, RANK_LANES), f32),
        (whole(rank, width), (rank, width), f32), (whole(width), (width,), f32),
        (whole(count, width), (count, width), f32), (whole(width), (width,), f32), (pieces(grads[3]), grads[3], f32),
        (whole(wide_d), (wide_d,), f32), (pieces(f_cols), f_cols, f32), (pieces(f_cols), f_cols, f32),
        (pieces(d_cols), d_cols, f32),
    )
    results = pl.pallas_call(
        functools.partial(finish_kernel, rank=rank),
        grid=(steps,),
        in_specs=[rows_spec, rows_spec, whole(2 * RANK_LANES, width), *[pieces(value) for value in grads[:-1]]],
        out_specs=tuple(spec for spec, _, _ in outs),
        out_shape=tuple(shape(size, kind) for _, size, kind in outs),
        compiler_params=pltpu.CompilerParams(vmem_limit_bytes=VMEM_BYTES),
        name="finish",
    )(*returned)
    (y_out, dx_out, norm1, g_z, g_x, g_taps, g_bias, g_xp, g_dt, g_dt_bias, g_rate, g_skip, g_out, norm2, g_gate, g_up,
     g_down) = results
    return (
        y_out, dx_out, norm1, g_x, g_z, g_taps.T, g_bias, g_xp, g_dt, g_dt_bias, g_rate.T, g_skip, g_out, norm2,
        g_gate, g_up, g_down,
    )


def on_device(
    x_in,
    lengths,
    seq_order,
    norm1_gain,
    w_in_x,
    w_in_z,
    conv_w,
    conv_b,
    w_xp,
    w_dt,
    dt_bias,
    a_log,
    skip_weight,
    w_out,
    norm2_gain,
    w_gate,
    w_up,
    w_down,
    cotangent,
):
    rows_in, width_row = x_in.shape
    row_devices = lax.axis_size("row")
    col_devices = lax.axis_size("col")
    group_rows = rows_in * col_devices
    model_width = width_row * row_devices
    rank_cols = w_dt.shape[0]
    state_count = a_log.shape[1]
    channels = conv_w.shape[0]
    ff_cols = w_gate.shape[1]
    my_group = lax.axis_index("dp")
    my_column = lax.axis_index("col")
    source, position_all = layout(lengths, seq_order, group_rows)
    my_source = lax.dynamic_index_in_dim(source, my_group, 0, keepdims=False)
    position = lax.dynamic_index_in_dim(position_all, my_group, 0, keepdims=False)
    slice_source = lax.dynamic_slice_in_dim(my_source, my_column * rows_in, rows_in, 0)

    def row_total(values):
        return lax.psum(values, "row")

    def token_rows(values):
        return lax.all_gather(values, "col", axis=0, tiled=True)

    def row_pieces(values):
        return lax.all_gather(values, "row", axis=0, tiled=True)

    def col_reduce(term_fn):
        return lax.psum_scatter(
            term_fn(jnp.int32(0), lax.axis_size("col") * rows_in),
            "col",
            scatter_dimension=0,
            tiled=True,
        )

    def row_reduce(term_fn, keep_rows):
        return lax.psum_scatter(
            term_fn(jnp.int32(0), lax.axis_size("row") * keep_rows),
            "row",
            scatter_dimension=0,
            tiled=True,
        )

    def projection_total(values):
        return lax.psum(values, ("row", "col"))

    blank_rows = jnp.zeros((rows_in, width_row), jnp.bfloat16)
    pieces = (
        lax.all_gather(x_in, ("dp", "col"), axis=0, tiled=True),
        lax.all_gather(cotangent, ("dp", "col"), axis=0, tiled=True),
    )
    row_count = pieces[0].shape[0]
    offset = slice_source
    inside = ((offset >= 0) & (offset < row_count))[:, None]
    index = jnp.clip(offset, 0, row_count - 1)
    x_rows = jnp.where(inside, jnp.take(pieces[0], index, axis=0), blank_rows)
    cot_rows = jnp.where(inside, jnp.take(pieces[1], index, axis=0), blank_rows)
    x_val = x_rows.astype(jnp.float32)
    scale_one = lax.rsqrt(row_total(jnp.sum(x_val * x_val, axis=1)) / model_width + epsilon)
    normed_one = (x_val * scale_one[:, None] * norm1_gain[None, :]).astype(jnp.bfloat16)
    normed_all = token_rows(normed_one)

    def inner_term(begin_row, row_count):
        return jnp.concatenate(
            [contract(w_in_x, normed_all, 0, 1), contract(w_in_z, normed_all, 0, 1)], axis=1
        )

    inner = row_reduce(inner_term, channels)
    inner_x = inner[:, :group_rows]
    inner_z = inner[:, group_rows:]

    def conv_part(values, kernel, kernel_bias):
        return convolve(values, kernel, kernel_bias, position)

    conv_out, conv_pull = jax.vjp(conv_part, inner_x, conv_w, conv_b)
    u_low = conv_out.astype(jnp.bfloat16)
    u_val = u_low.astype(jnp.float32)
    projected = projection_total(contract(w_xp, u_low, 0, 0))
    step_low = projected[:rank_cols].astype(jnp.bfloat16)
    pre_step = contract(w_dt, step_low, 0, 0) + dt_bias[:, None]
    step_size = jax.nn.softplus(pre_step)

    decay_rate = -jnp.exp(a_log).T
    proj_rows = projected.T
    u_rows = u_val.T
    step_rows = step_size.T
    gone_rows = jnp.where(position[:, None] > 0, step_rows, 1e30)
    drive_rows = step_rows * u_rows
    at_b, at_c = rank_cols, rank_cols + state_count
    scanned = scan_alone(proj_rows, gone_rows, drive_rows, decay_rate, at_b, at_c)
    mixer_y = scanned.T + skip_weight[:, None] * u_val
    gated = mixer_y * jax.nn.silu(inner_z)
    gated_low = gated.astype(jnp.bfloat16)
    gated_all = row_pieces(gated_low)

    def mix_term(begin_row, row_count):
        return contract(gated_all, w_out, 0, 0)

    first_sum = x_val + col_reduce(mix_term)
    scale_two = lax.rsqrt(row_total(jnp.sum(first_sum * first_sum, axis=1)) / model_width + epsilon)
    normed_two = (first_sum * scale_two[:, None] * norm2_gain[None, :]).astype(jnp.bfloat16)
    normed_rows = token_rows(normed_two)

    def ffn_term(begin_row, row_count):
        return jnp.concatenate(
            [
                jnp.dot(normed_rows, w_gate, preferred_element_type=jnp.float32),
                jnp.dot(normed_rows, w_up, preferred_element_type=jnp.float32),
            ],
            axis=1,
        )

    gate_up = row_reduce(ffn_term, group_rows // row_devices)
    gate_val = gate_up[:, :ff_cols]
    up_val = gate_up[:, ff_cols:]
    hidden = (jax.nn.silu(gate_val) * up_val).astype(jnp.bfloat16)
    hidden_all = row_pieces(hidden)

    def down_term(begin_row, row_count):
        return jnp.dot(hidden_all, w_down, preferred_element_type=jnp.float32)

    second_sum = first_sum + col_reduce(down_term)
    out_low = second_sum.astype(jnp.bfloat16)
    back_down_all = token_rows(cot_rows)
    grad_down = contract(hidden_all, back_down_all, 0, 0)

    def hidden_term(begin_row, row_count):
        return contract(back_down_all, w_down, 1, 1)

    d_hidden = row_reduce(hidden_term, group_rows // row_devices)
    d_gate = (d_hidden * up_val * silu_slope(gate_val)).astype(jnp.bfloat16)
    d_up = (d_hidden * jax.nn.silu(gate_val)).astype(jnp.bfloat16)
    d_gate_up_all = row_pieces(jnp.concatenate([d_gate, d_up], axis=1))
    grad_gate = contract(normed_rows, d_gate_up_all[:, :ff_cols], 0, 0)
    grad_up = contract(normed_rows, d_gate_up_all[:, ff_cols:], 0, 0)

    def norm_two_term(begin_row, row_count):
        return contract(d_gate_up_all[:, :ff_cols], w_gate, 1, 1) + contract(
            d_gate_up_all[:, ff_cols:], w_up, 1, 1
        )

    d_normed_two = col_reduce(norm_two_term)
    cot_val = cot_rows.astype(jnp.float32)
    weighted_two = d_normed_two * norm2_gain[None, :]
    grad_norm_two = jnp.sum(d_normed_two * first_sum * scale_two[:, None], axis=0)
    dot_two = row_total(jnp.sum(weighted_two * first_sum, axis=1))
    d_first = (
        cot_val
        + scale_two[:, None] * weighted_two
        - first_sum * (scale_two**3 * dot_two / model_width)[:, None]
    )
    d_mix_all = token_rows(d_first.astype(jnp.bfloat16))
    grad_out = contract(gated_all, d_mix_all, 1, 0)

    def gated_term(begin_row, row_count):
        return contract(w_out, d_mix_all, 1, 1)

    d_gated = row_reduce(gated_term, channels)
    d_inner_z = d_gated * mixer_y * silu_slope(inner_z)
    d_mixer = d_gated * jax.nn.silu(inner_z)
    d_u_rows, d_step_rows, d_proj_rows, grad_rate_rows = adjoint_alone(
        proj_rows, step_rows, gone_rows, drive_rows, u_rows, d_mixer.T, decay_rate, at_b, at_c
    )
    d_u_mix = d_u_rows.T + skip_weight[:, None] * d_mixer
    d_step = d_step_rows.T
    d_enter = d_proj_rows.T[at_b:at_c]
    d_leave = d_proj_rows.T[at_c:]
    grad_rate = grad_rate_rows.T
    grad_skip = jnp.sum(d_mixer * u_val, axis=1)
    d_pre = d_step * jax.nn.sigmoid(pre_step)
    grad_step_bias = jnp.sum(d_pre, axis=1)
    d_pre_low = d_pre.astype(jnp.bfloat16)
    grad_step_w = contract(step_low, d_pre_low, 1, 1)
    d_projected = projection_total(
        jnp.concatenate(
            [jnp.dot(w_dt, d_pre_low, preferred_element_type=jnp.float32), d_enter, d_leave], axis=0
        )
    )
    d_proj_low = d_projected.astype(jnp.bfloat16)
    grad_proj_w = contract(u_low, d_proj_low, 1, 1)
    d_u_all = d_u_mix + jnp.dot(w_xp, d_proj_low, preferred_element_type=jnp.float32)
    d_inner_x, grad_kernel, grad_kernel_bias = conv_pull(d_u_all)
    d_inner_all = row_pieces(
        jnp.concatenate([d_inner_x.astype(jnp.bfloat16), d_inner_z.astype(jnp.bfloat16)], axis=1)
    )
    grad_in_x = contract(normed_all, d_inner_all[:, :group_rows], 0, 1)
    grad_in_z = contract(normed_all, d_inner_all[:, group_rows:], 0, 1)

    def norm_one_term(begin_row, row_count):
        piece_x = lax.dynamic_slice_in_dim(d_inner_all, begin_row, row_count, 1)
        piece_z = lax.dynamic_slice_in_dim(d_inner_all, group_rows, row_count, 1)
        return contract(piece_x, w_in_x, 0, 1) + contract(piece_z, w_in_z, 0, 1)

    d_normed_one = col_reduce(norm_one_term)
    weighted_one = d_normed_one * norm1_gain[None, :]
    grad_norm_one = jnp.sum(d_normed_one * x_val * scale_one[:, None], axis=0)
    dot_one = row_total(jnp.sum(weighted_one * x_val, axis=1))
    d_input = (
        d_first
        + scale_one[:, None] * weighted_one
        - x_val * (scale_one**3 * dot_one / model_width)[:, None]
    )
    d_input_low = d_input.astype(jnp.bfloat16)
    grad_norm_one, grad_norm_two = lax.psum((grad_norm_one, grad_norm_two), ("dp", "col"))
    (
        grad_in_x,
        grad_in_z,
        grad_kernel,
        grad_kernel_bias,
        grad_proj_w,
        grad_step_w,
        grad_step_bias,
        grad_rate,
        grad_skip,
        grad_out,
        grad_gate,
        grad_up,
        grad_down,
    ) = (
        lax.psum(grad_in_x.astype(jnp.bfloat16), "dp").astype(jnp.float32),
        lax.psum(grad_in_z.astype(jnp.bfloat16), "dp").astype(jnp.float32),
        lax.psum(grad_kernel.astype(jnp.bfloat16), "dp").astype(jnp.float32),
        lax.psum(grad_kernel_bias.astype(jnp.bfloat16), "dp").astype(jnp.float32),
        lax.psum(grad_proj_w.astype(jnp.bfloat16), "dp").astype(jnp.float32),
        lax.psum(grad_step_w.astype(jnp.bfloat16), "dp").astype(jnp.float32),
        lax.psum(grad_step_bias.astype(jnp.bfloat16), "dp").astype(jnp.float32),
        lax.psum(grad_rate.astype(jnp.bfloat16), "dp").astype(jnp.float32),
        lax.psum(grad_skip.astype(jnp.bfloat16), "dp").astype(jnp.float32),
        lax.psum(grad_out.astype(jnp.bfloat16), "dp").astype(jnp.float32),
        lax.psum(grad_gate.astype(jnp.bfloat16), "dp").astype(jnp.float32),
        lax.psum(grad_up.astype(jnp.bfloat16), "dp").astype(jnp.float32),
        lax.psum(grad_down.astype(jnp.bfloat16), "dp").astype(jnp.float32),
    )
    payload = jnp.concatenate([out_low, d_input_low], axis=1)
    tokens_all = lengths.shape[0] * group_rows
    owner = (
        jnp.zeros((tokens_all,), jnp.int32)
        .at[source.reshape(-1)]
        .set(jnp.arange(tokens_all, dtype=jnp.int32))
    )
    my_rows = lax.dynamic_slice_in_dim(
        owner, (my_group * col_devices + my_column) * rows_in, rows_in, 0
    )
    pieces = lax.all_gather(payload, ("dp", "col"), axis=0, tiled=True)
    row_count = pieces.shape[0]
    offset = my_rows
    inside = ((offset >= 0) & (offset < row_count))[:, None]
    returned = jnp.where(
        inside,
        jnp.take(pieces, jnp.clip(offset, 0, row_count - 1), axis=0),
        jnp.zeros_like(payload),
    )
    y_out = returned[:, :width_row]
    dx_out = returned[:, width_row:]
    return (
        y_out,
        dx_out,
        grad_norm_one,
        grad_in_x,
        grad_in_z,
        grad_kernel,
        grad_kernel_bias,
        grad_proj_w,
        grad_step_w,
        grad_step_bias,
        grad_rate,
        grad_skip,
        grad_out,
        grad_norm_two,
        grad_gate,
        grad_up,
        grad_down,
    )


def solution(mesh):
    placed = (
        P(("dp", "col"), "row"),
        P(),
        P(),
        P("row"),
        P("row", "col"),
        P("row", "col"),
        P(("col", "row"), None),
        P(("col", "row")),
        P(("col", "row"), None),
        P(None, ("col", "row")),
        P(("col", "row")),
        P(("col", "row"), None),
        P(("col", "row")),
        P("col", "row"),
        P("row"),
        P("row", "col"),
        P("row", "col"),
        P("col", "row"),
        P(("dp", "col"), "row"),
    )
    paired = mesh.shape["col"] == 2 and mesh.shape["dp"] == 4
    return jax.shard_map(
        on_pairs if paired else on_device,
        mesh=mesh,
        in_specs=placed,
        out_specs=(
            P(("dp", "col"), "row"),
            P(("dp", "col"), "row"),
            P("row"),
            P("row", "col"),
            P("row", "col"),
            P(("col", "row"), None),
            P(("col", "row")),
            P(("col", "row"), None),
            P(None, ("col", "row")),
            P(("col", "row")),
            P(("col", "row"), None),
            P(("col", "row")),
            P("col", "row"),
            P("row"),
            P("row", "col"),
            P("row", "col"),
            P("col", "row"),
        ),
        check_vma=False,
    )
```

```python
import functools

import jax
import jax.numpy as jnp
from jax import lax
from jax.experimental import pallas as pl
from jax.experimental.pallas import tpu as pltpu
from jax.sharding import PartitionSpec as P

epsilon = 1e-05


def layout(lengths, seq_order, group_rows):
    flat_lengths = lengths.reshape(-1)
    total_seqs = flat_lengths.shape[0]
    slot_length = jnp.take(flat_lengths, seq_order)
    input_start = jnp.cumsum(slot_length) - slot_length
    slot_of = (
        jnp.zeros((total_seqs,), jnp.int32)
        .at[seq_order]
        .set(jnp.arange(total_seqs, dtype=jnp.int32))
    )
    seq_input = jnp.take(input_start, slot_of).reshape(lengths.shape)
    group_start = jnp.cumsum(lengths, axis=1) - lengths
    places = jnp.arange(group_rows, dtype=jnp.int32)
    member = (
        jnp.sum((places[None, :, None] >= group_start[:, None, :]).astype(jnp.int32), axis=2) - 1
    )
    begin_at = jnp.take_along_axis(group_start, member, axis=1)
    within = places[None, :] - begin_at
    source = jnp.take_along_axis(seq_input, member, axis=1) + within
    return (source, within)


def silu_slope(values):
    sigmoid_v = jax.nn.sigmoid(values)
    return sigmoid_v * (1.0 + values * (1.0 - sigmoid_v))


def contract(left, right, left_dim, right_dim):
    return lax.dot_general(
        left, right, (((left_dim,), (right_dim,)), ((), ())), preferred_element_type=jnp.float32
    )


def convolve(inner_x, kernel, kernel_bias, places):
    tap_count = kernel.shape[1]
    conv_sum = kernel_bias[:, None] + inner_x * kernel[:, tap_count - 1][:, None]
    for shift_by in range(1, tap_count):
        shifted = jnp.pad(inner_x, ((0, 0), (shift_by, 0)))[:, :-shift_by]
        conv_sum = (
            conv_sum
            + shifted
            * (places >= shift_by).astype(jnp.float32)[None, :]
            * kernel[:, tap_count - 1 - shift_by][:, None]
        )
    return jax.nn.silu(conv_sum)


MESH = pl.DeviceIdType.MESH
f32 = jnp.float32
bf16 = jnp.bfloat16


def remote(src, dst, send, recv, where):
    return pltpu.make_async_remote_copy(
        src_ref=src, dst_ref=dst, send_sem=send, recv_sem=recv, device_id=where, device_id_type=MESH
    )


def away(axis, offset):
    return {axis: lax.rem(lax.axis_index(axis) + offset, lax.axis_size(axis))}


def greet(*axes):
    barrier = pltpu.get_barrier_semaphore()
    total = 0
    for axis in axes:
        for offset in range(1, lax.axis_size(axis)):
            pl.semaphore_signal(barrier, inc=1, device_id=away(axis, offset), device_id_type=MESH)
            total += 1
    return lambda: pl.semaphore_wait(barrier, total)


class Late:
    def __init__(self, names, sources, targets, sems):
        self.targets = dict(zip(names, targets))
        self.waiting = {}
        for i, (name, source, target) in enumerate(zip(names, sources, targets)):
            self.waiting[name] = pltpu.make_async_copy(source, target, sems.at[i])
            self.waiting[name].start()

    def __call__(self, name):
        if name in self.waiting:
            self.waiting.pop(name).wait()
        return self.targets[name]


class Leave:
    def __init__(self, names, sources, targets, sems):
        self.copies = {
            name: pltpu.make_async_copy(source, target, sems.at[i])
            for i, (name, source, target) in enumerate(zip(names, sources, targets))
        }

    def __call__(self, *names):
        for name in names:
            self.copies[name].start()

    def finish(self):
        for copy in self.copies.values():
            copy.wait()


def matmul(left, right):
    return jnp.dot(left, right, preferred_element_type=f32)


def silu(values):
    return values * jax.nn.sigmoid(values)


def rows_form(values):
    ones = jnp.ones((8, values.shape[1]), f32)
    return lax.dot_general(
        ones,
        values,
        (((1,), (1,)), ((), ())),
        precision=lax.Precision.HIGHEST,
        preferred_element_type=f32,
    )


def column_form(row_values):
    return jnp.transpose(row_values)[:, 0:1]


class Line:
    def __init__(self, axis, send, recv):
        self.axis, self.send, self.recv = axis, send, recv
        self.size = lax.axis_size(axis)
        self.me = lax.axis_index(axis)

    def right(self, src, dst, d):
        return remote(
            src, dst, self.send.at[0, d], self.recv.at[0, d], {self.axis: jnp.minimum(self.me + 1, self.size - 1)}
        )

    def left(self, src, dst, d):
        return remote(
            src, dst, self.send.at[1, d], self.recv.at[1, d], {self.axis: jnp.maximum(self.me - 1, 0)}
        )


def line_gather(axis, slot_of, send, recv):
    line = Line(axis, send, recv)
    size, me = line.size, line.me
    last = size - 1

    def go_right(s):
        slot = jnp.maximum(me - s, 0)
        return (me - s >= 0) & (me < last), line.right(slot_of(slot), slot_of(slot), slot)

    def go_left(s):
        slot = jnp.minimum(me + s, last)
        return (me + s <= last) & (me > 0), line.left(slot_of(slot), slot_of(slot), slot)

    for s in range(last):
        for valid, copy in (go_right(s), go_left(s)):
            pl.when(valid)(copy.start)
        yield
        slot = jnp.maximum(me - 1 - s, 0)
        pl.when(me - 1 - s >= 0)(line.right(slot_of(slot), slot_of(slot), slot).wait_recv)
        slot = jnp.minimum(me + 1 + s, last)
        pl.when(me + 1 + s <= last)(line.left(slot_of(slot), slot_of(slot), slot).wait_recv)
    yield
    for s in range(last):
        for valid, copy in (go_right(s), go_left(s)):
            pl.when(valid)(copy.wait_send)


def line_scatter(axis, block_of, out, held, from_left, from_right, send, recv):
    line = Line(axis, send, recv)
    size, me = line.size, line.me
    last = size - 1

    def right_at(t):
        d = jnp.clip(last - t + me, 0, last)
        return (t >= me) & (me < last), d, line.right(held.at[d], from_left.at[d], d)

    def left_at(t):
        d = jnp.clip(t - (last - me), 0, last)
        return (t >= last - me) & (me > 0), d, line.left(held.at[d], from_right.at[d], d)

    def pass_on(valid, first, d, copy, arrived):
        @pl.when(valid)
        def _():
            part = block_of(d)

            @pl.when(jnp.logical_not(first))
            def _():
                copy.wait_recv()
                held[d] = (part + arrived[d].astype(f32)).astype(held.dtype)

            @pl.when(first)
            def _():
                held[d] = part.astype(held.dtype)

            copy.start()

    for t in range(last):
        valid, d, copy = right_at(t)
        pass_on(valid, me == 0, d, copy, from_left)
        valid, d, copy = left_at(t)
        pass_on(valid, me == last, d, copy, from_right)
        if t == 0:
            out[...] = block_of(me)
        yield
    yield

    @pl.when(me > 0)
    def _():
        line.right(held.at[me], from_left.at[me], me).wait_recv()
        out[...] += from_left[me].astype(f32)

    @pl.when(me < last)
    def _():
        line.left(held.at[me], from_right.at[me], me).wait_recv()
        out[...] += from_right[me].astype(f32)

    for t in range(last):
        for valid, _, copy in (right_at(t), left_at(t)):
            pl.when(valid)(copy.wait_send)


def halves(rows):
    return [pl.ds(0, rows // 2), pl.ds(rows // 2, rows // 2)]


def gather_halves(axis, ref, size, send, recv):
    flows = []
    for h, at in enumerate(halves(ref.shape[0])):

        def slot_of(d, at=at):
            return ref.at[at, pl.ds(pl.multiple_of(d * size, size), size)]

        flows.append(line_gather(axis, slot_of, send.at[h], recv.at[h]))
    return flows


def scatter_halves(axis, block_of, out, held, from_left, from_right, send, recv):
    flows = []
    for h, at in enumerate(halves(out.shape[0])):
        flows.append(
            line_scatter(
                axis,
                functools.partial(block_of, at=at),
                out.at[at, :],
                held.at[:, at, :],
                from_left.at[:, at, :],
                from_right.at[:, at, :],
                send.at[h],
                recv.at[h],
            )
        )
    return flows


def run(*flows, pump=None):
    flows = list(flows)
    turn = 0
    while flows:
        flows = [flow for flow in flows if next(flow, flows) is not flows]
        if pump is not None and turn < len(pump[1]):
            pump[0].pump(pump[1][turn])
        turn += 1


def lanes(ref, size):
    return lambda d: ref.at[:, pl.ds(pl.multiple_of(d * size, size), size)]


def fetch(sources, targets, sems):
    copies = [pltpu.make_async_copy(s, t, sems.at[i]) for i, (s, t) in enumerate(zip(sources, targets))]
    for copy in copies:
        copy.start()
    return copies


def as_row(ref):
    return ref[...].reshape(1, ref.shape[0])


def lengths_row(lens):
    groups, per_group = lens.shape
    values = lens[...].astype(f32)
    at = lax.broadcasted_iota(jnp.int32, (per_group, groups * per_group), 1)
    inner = lax.broadcasted_iota(jnp.int32, (per_group, groups * per_group), 0)
    total = jnp.zeros((1, groups * per_group), f32)
    for g in range(groups):
        place = jnp.where(at == inner + g * per_group, 1.0, 0.0)
        total = total + jnp.dot(
            values[g : g + 1, :], place, precision=lax.Precision.HIGHEST, preferred_element_type=f32
        )
    return total


def spray(axis, src_of, dst, send, recv, base=0):
    copies = []
    for k in range(1, lax.axis_size(axis)):
        copy = remote(src_of(k), dst.at[k - 1], send.at[base + k - 1], recv.at[base + k - 1], away(axis, k))
        copy.start()
        copies.append(copy)
    return copies


def wait_all(copies):
    for copy in copies:
        copy.wait()


def swap(axis, src, dst, send, recv):
    copy = remote(src, dst, send, recv, away(axis, 1))
    copy.start()
    return copy


def sequence_rows(lens_row, order_row, per_group):
    count = lens_row.shape[1]
    ri = lax.broadcasted_iota(jnp.int32, (count, count), 0)
    ci = lax.broadcasted_iota(jnp.int32, (count, count), 1)
    lens_f = lens_row

    def to_column(row):
        return jnp.sum(jnp.where(ri == ci, row, 0.0), axis=1, keepdims=True)

    order_col = to_column(order_row.astype(f32)).astype(jnp.int32)
    lens_col = to_column(lens_f)
    pick = order_row == ri
    pick_t = order_col == ci
    slot_col = jnp.sum(jnp.where(pick_t, lens_f, 0.0), axis=1, keepdims=True)
    slot_row = jnp.sum(jnp.where(pick, lens_col, 0.0), axis=0, keepdims=True)
    start_col = jnp.sum(jnp.where(ci < ri, slot_row, 0.0), axis=1, keepdims=True)
    input_row = jnp.sum(jnp.where(pick_t, start_col, 0.0), axis=0, keepdims=True)
    same = (ri // per_group) == (ci // per_group)
    group_row = jnp.sum(jnp.where((ri < ci) & same, lens_col, 0.0), axis=0, keepdims=True)
    return lens_f, input_row, group_row


def place_rows(lens_row, order_row, per_group, group_rows, group):
    lens_f, input_row, group_row = sequence_rows(lens_row, order_row, per_group)
    count = lens_row.shape[1]
    rows = lax.broadcasted_iota(jnp.int32, (group_rows, count), 0).astype(f32)
    mine = (lax.broadcasted_iota(jnp.int32, (group_rows, count), 1) // per_group) == group
    inside = (rows >= group_row) & (rows < group_row + lens_f) & mine
    within = jnp.sum(jnp.where(inside, rows - group_row, 0.0), axis=1, keepdims=True)
    begin = jnp.sum(jnp.where(inside, input_row, 0.0), axis=1, keepdims=True)
    return begin + within, within


def owner_rows(lens_row, order_row, per_group, group_rows, block_rows, first):
    lens_f, input_row, group_row = sequence_rows(lens_row, order_row, per_group)
    count = lens_row.shape[1]
    rows = (lax.broadcasted_iota(jnp.int32, (block_rows, count), 0) + first).astype(f32)
    base = (lax.broadcasted_iota(jnp.int32, (block_rows, count), 1) // per_group) * group_rows
    inside = (rows >= input_row) & (rows < input_row + lens_f)
    found = jnp.where(inside, base.astype(f32) + group_row + rows - input_row, 0.0)
    return jnp.sum(found, axis=1, keepdims=True)


def plane_origin(rows, dp_size, col_size, block_rows):
    at = lax.broadcasted_iota(jnp.int32, (rows, dp_size * col_size * block_rows), 1)
    block = at // block_rows
    group = lax.rem(block, dp_size)
    column = block // dp_size
    return ((group * col_size + column) * block_rows + lax.rem(at, block_rows)).astype(f32)


def pick_rows(wanted, held):
    col_size, dp_size, block_rows, width = held.shape
    total = col_size * dp_size * block_rows
    chosen = wanted == plane_origin(wanted.shape[0], dp_size, col_size, block_rows)
    chosen = jnp.where(chosen, 1.0, 0.0).astype(bf16)
    return matmul(chosen, held.reshape(total, width)).astype(bf16)


def plane_start(src, held, send, recv):
    me, column = lax.axis_index("dp"), lax.axis_index("col")
    held[column, me] = src[...]
    copies = []
    for k in range(1, lax.axis_size("dp")):
        copy = remote(src, held.at[column, me], send.at[k], recv.at[k], away("dp", k))
        copy.start()
        copies.append(copy)
    return copies


def plane_finish(copies, held, send, recv):
    column = lax.axis_index("col")
    for copy in copies:
        copy.wait_recv()
    copy = swap("col", held.at[column], held.at[column], send.at[0], recv.at[0])
    copy.wait_recv()
    for one in copies + [copy]:
        one.wait_send()


def total_of_sums(part, half_own, half_in, low_own, low_in, full, sems):
    send, recv = sems
    rows = part.shape[0] // 2
    column = lax.axis_index("col")
    mine = pl.ds(pl.multiple_of(column * rows, rows), rows)
    other = pl.ds(pl.multiple_of((1 - column) * rows, rows), rows)
    half_own[...] = part[other, :]
    copy = swap("col", half_own, half_in, send.at[0], recv.at[0])
    yield
    copy.wait()
    low_own[...] = (part[mine, :] + half_in[...]).astype(bf16)
    copies = spray("row", lambda k: low_own, low_in, send, recv, 1)
    yield
    wait_all(copies)
    total = low_own[...].astype(f32)
    for k in range(low_in.shape[0]):
        total = total + low_in[k].astype(f32)
    full[mine, :] = total
    copy = swap("col", full.at[mine], full.at[mine], send.at[4], recv.at[4])
    yield
    copy.wait()


def lanes_like(tile, width):
    if tile.shape[-1] == width:
        return tile
    return jnp.concatenate([tile] * (width // tile.shape[-1]), axis=-1)


def lane_mask(count, lanes, first):
    lane = lax.broadcasted_iota(jnp.int32, (count, lanes), 1)
    return lane == lax.broadcasted_iota(jnp.int32, (count, lanes), 0) + first


def spread(values, first, count, wide):
    rows, lanes = values.shape
    chosen = jnp.where(lane_mask(count, lanes, first)[None], values[:, None, :], 0.0)
    chosen = chosen.reshape(rows * count, lanes)
    high = chosen.astype(bf16)
    rest = (chosen - high.astype(f32)).astype(bf16)
    ones = jnp.ones((lanes, wide), bf16)
    return matmul(high, ones) + matmul(rest, ones)


def lane_sums(values, first, lanes):
    rows, count, wide = values.shape
    flat = values.reshape(rows * count, wide)
    high = flat.astype(bf16)
    rest = (flat - high.astype(f32)).astype(bf16)
    ones = jnp.ones((wide, lanes), bf16)
    sums = (matmul(high, ones) + matmul(rest, ones)).reshape(rows, count, lanes)
    return jnp.sum(jnp.where(lane_mask(count, lanes, first)[None], sums, 0.0), axis=1)


def scan_forward(proj, b_at, c_at, gone_step, drive, rate, bb, cb, y):
    rows, width = drive.shape
    count = rate.shape[0]
    piece, _, wide = bb.shape
    state = jnp.zeros((count, width), f32)
    for start in range(0, rows, piece):
        values = proj[start : start + piece, :]
        bb[...] = spread(values, b_at, count, wide).reshape(bb.shape)
        cb[...] = spread(values, c_at, count, wide).reshape(cb.shape)

        def eight(k, state):
            inner = pl.multiple_of(k * 8, 8)
            base = pl.multiple_of(start + k * 8, 8)
            gone = gone_step[pl.ds(base, 8), :]
            driven = drive[pl.ds(base, 8), :]
            found = []
            for i in range(8):
                decay = jnp.exp(gone[i : i + 1, :] * rate)
                state = decay * state + driven[i : i + 1, :] * lanes_like(bb[inner + i], width)
                found.append(jnp.sum(state * lanes_like(cb[inner + i], width), axis=0, keepdims=True))
            y[pl.ds(base, 8), :] = jnp.concatenate(found, axis=0)
            return state

        state = lax.fori_loop(0, piece // 8, eight, state)
        yield


def scan_states(proj, b_at, gone_step, drive, rate, bb, hs):
    rows, width = drive.shape
    count = rate.shape[0]
    piece, _, wide = bb.shape
    hs[0] = jnp.zeros((count, width), f32)
    for start in range(0, rows, piece):
        bb[...] = spread(proj[start : start + piece, :], b_at, count, wide).reshape(bb.shape)

        def eight(k, state):
            inner = pl.multiple_of(k * 8, 8)
            base = pl.multiple_of(start + k * 8, 8)
            gone = gone_step[pl.ds(base, 8), :]
            driven = drive[pl.ds(base, 8), :]
            for i in range(8):
                decay = jnp.exp(gone[i : i + 1, :] * rate)
                state = decay * state + driven[i : i + 1, :] * lanes_like(bb[inner + i], width)
                hs[base + i + 1] = state
            return state

        lax.fori_loop(0, piece // 8, eight, hs[start])
        yield


def scan_backward(
    proj, b_at, c_at, step, gone_step, drive, inner_u, dy, rate, hs, bb, cb, pb, pc, du, dstep, dproj
):
    rows, width = drive.shape
    count = rate.shape[0]
    piece, _, wide = bb.shape

    def fold(values):
        total = values[:, 0:wide]
        for j in range(1, width // wide):
            total = total + values[:, j * wide : (j + 1) * wide]
        return total

    def part(start, carry):
        values = proj[start : start + piece, :]
        bb[...] = spread(values, b_at, count, wide).reshape(bb.shape)
        cb[...] = spread(values, c_at, count, wide).reshape(cb.shape)

        def eight(k, carry):
            later, total = carry
            inner = pl.multiple_of((piece // 8 - 1 - k) * 8, 8)
            base = pl.multiple_of(start + inner, 8)
            step8 = step[pl.ds(base, 8), :]
            gone8 = gone_step[pl.ds(base, 8), :]
            drive8 = drive[pl.ds(base, 8), :]
            u8 = inner_u[pl.ds(base, 8), :]
            dy8 = dy[pl.ds(base, 8), :]
            by_b = [None] * 8
            by_rate = [None] * 8
            for i in reversed(range(8)):
                dy_row = dy8[i : i + 1, :]
                lam = lanes_like(cb[inner + i], width) * dy_row + later
                later = jnp.exp(gone8[i : i + 1, :] * rate) * lam
                kept = later * hs[base + i]
                total = total + kept * step8[i : i + 1, :]
                by_b[i] = jnp.sum(lam * lanes_like(bb[inner + i], width), axis=0, keepdims=True)
                by_rate[i] = jnp.sum(kept * rate, axis=0, keepdims=True)
                pb[inner + i] = fold(lam * drive8[i : i + 1, :])
                pc[inner + i] = fold(hs[base + i + 1] * dy_row)
            by_b = jnp.concatenate(by_b, axis=0)
            by_rate = jnp.concatenate(by_rate, axis=0)
            du[pl.ds(base, 8), :] = by_b * step8
            dstep[pl.ds(base, 8), :] = by_rate + by_b * u8
            return later, total

        carry = lax.fori_loop(0, piece // 8, eight, carry)
        dproj[start : start + piece, :] += lane_sums(pb[...], b_at, dproj.shape[1]) + lane_sums(
            pc[...], c_at, dproj.shape[1]
        )
        return carry

    blank = jnp.zeros((count, width), f32)
    carry = (blank, blank)
    for start in reversed(range(0, rows, piece)):
        carry = part(start, carry)
        yield
    return carry[1] * rate


RANK_LANES = 128


def scan_kernel(proj, gone, drive, rate, y, bb, cb, *, b_at, c_at):
    run(scan_forward(proj, b_at, c_at, gone, drive, rate[...], bb, cb, y))


def adjoint_kernel(
    proj, step, gone, drive, inner_u, dy, rate, du, dstep, dproj, drate, bb, cb, hs, pb, pc, *, b_at, c_at
):
    run(scan_states(proj, b_at, gone, drive, rate[...], bb, hs))
    dproj[...] = jnp.zeros_like(dproj)
    kept = {}

    def adjoint():
        kept["rate"] = yield from scan_backward(
            proj, b_at, c_at, step, gone, drive, inner_u, dy, rate[...], hs, bb, cb, pb, pc, du, dstep, dproj
        )

    run(adjoint())
    drate[...] = kept["rate"]


def scan_sizes(rows, width, count):
    wide = 128 if width % 128 == 0 else width
    piece = min(128, rows)
    return pltpu.VMEM((piece, count, wide), f32)


def scan_alone(proj, gone, drive, rate, b_at, c_at):
    rows, width = drive.shape
    block = scan_sizes(rows, width, rate.shape[0])
    return pl.pallas_call(
        functools.partial(scan_kernel, b_at=b_at, c_at=c_at),
        out_shape=jax.ShapeDtypeStruct((rows, width), f32),
        scratch_shapes=[block, block],
        compiler_params=pltpu.CompilerParams(vmem_limit_bytes=VMEM_BYTES),
        name="scan_states",
    )(proj, gone, drive, rate)


def adjoint_alone(proj, step, gone, drive, inner_u, dy, rate, b_at, c_at):
    rows, width = step.shape
    count = rate.shape[0]
    block = scan_sizes(rows, width, count)
    shape = jax.ShapeDtypeStruct
    return pl.pallas_call(
        functools.partial(adjoint_kernel, b_at=b_at, c_at=c_at),
        out_shape=(
            shape((rows, width), f32),
            shape((rows, width), f32),
            shape(proj.shape, f32),
            shape((count, width), f32),
        ),
        scratch_shapes=[
            block,
            block,
            pltpu.VMEM((rows + 1, count, width), f32),
            block,
            block,
        ],
        compiler_params=pltpu.CompilerParams(vmem_limit_bytes=VMEM_BYTES),
        name="scan_adjoint",
    )(proj, step, gone, drive, inner_u, dy, rate)


PUMPS = ((0, 1, 1), (1, 0, 1), 0, (1, 2, 1), (1, 1), (0, 0, 0), (2, 2, 1), 0, 2)


def conv_sum(inner_x, place, taps, bias):
    count = taps.shape[0]
    total = bias + inner_x * taps[count - 1 : count, :]
    for shift in range(1, count):
        moved = jnp.where(place >= shift, pltpu.roll(inner_x, shift, 0), 0.0)
        total = total + moved * taps[count - 1 - shift : count - shift, :]
    return total


def transposed(left, right):
    return lax.dot_general(left, right, (((1,), (1,)), ((), ())), preferred_element_type=f32)


def over_rows(left, right):
    return lax.dot_general(left, right, (((0,), (0,)), ((), ())), preferred_element_type=f32)


def columns(d, size):
    return pl.ds(pl.multiple_of(d * size, size), size)


def line_total(own, arrived):
    total = own
    for k in range(arrived.shape[0]):
        total = total + arrived[k]
    return total


def forward_kernel(
    x, cot, lens, order, gain1, taps, bias, w_xp, w_dt, dt_bias, a_log, skip, gain2,
    w_x_h, w_z_h, w_out_h, w_gate_h, w_up_h, w_down_h,
    xg_o, cg_o, n1_o, s1_o, place_o, xi_o, z_o, proj_o, yv_o, go_all, h1_o, s2_o, n2_o, hid_all, dgu_o, dot_o, n1_mates, n2_mates, cg_mates,
    w_x, w_z, w_out, w_gate, w_up, w_down, w_step, rate,
    x_all, c_all, sum_own, sum_in, low, xi_held, xi_left, xi_right, z_held, z_left, z_right,
    part_s, half_own, half_in, low_own, low_in, bb, cb, step, gone, drive,
    own, other, gu, gu_held, gu_left, gu_right, dhid, h_held, h_left, h_right,
    w_sems, x_send, x_recv, c_send, c_recv, sum_send, sum_recv, xi_send, xi_recv, z_send, z_recv, t_send, t_recv,
    go_send, go_recv, o_send, o_recv, sum2_send, sum2_recv, gu_send, gu_recv, h_send, h_recv, hid_send, hid_recv, m_send, m_recv,
    *, model_width, rank, count, leave
):
    rows, width = xi_o.shape
    hidden = dgu_o.shape[1] // 2
    group, row = lax.axis_index("dp"), lax.axis_index("row")
    row_size = lax.axis_size("row")
    weights = fetch(
        (w_x_h, w_z_h, w_out_h, w_gate_h, w_up_h, w_down_h), (w_x, w_z, w_out, w_gate, w_up, w_down), w_sems
    )
    met = greet("dp", "row", "col")
    w_step[...] = jnp.zeros_like(w_step)
    w_step[0:rank, :] = w_dt[...]
    met()
    x_copies = plane_start(x, x_all, x_send, x_recv)
    lens_row = lengths_row(lens)
    source, place = place_rows(lens_row, as_row(order), lens.shape[1], rows, group)
    place_o[...] = place
    plane_finish(x_copies, x_all, x_send, x_recv)
    c_copies = plane_start(cot, c_all, c_send, c_recv)
    xg_low = pick_rows(source, x_all[...])
    xg_o[...] = xg_low
    xg = xg_low.astype(f32)
    gain1_now = as_row(gain1)
    low[...] = (xg * gain1_now).astype(bf16)
    weights[0].wait()
    kept = {}

    def during_xi():
        sum_own[...] = rows_form(xg * xg)
        sum_copies = spray("row", lambda k: sum_own, sum_in, sum_send, sum_recv)
        rate[...] = -jnp.exp(a_log[...])
        yield
        wait_all(sum_copies)
        kept["s1"] = column_form(lax.rsqrt(line_total(sum_own[...], sum_in) / model_width + epsilon))
        s1_o[...] = kept["s1"]
        leave("xg", "s1", "place")

    run(
        *scatter_halves(
            "row", lambda d, at: matmul(low[at, :], w_x[:, columns(d, width)]), xi_o, xi_held, xi_left, xi_right,
            xi_send, xi_recv,
        ),
        during_xi(),
    )
    s1 = kept["s1"]
    inner_x = xi_o[...] * s1
    xi_o[...] = inner_x
    u_low = silu(conv_sum(inner_x, place, taps[...], as_row(bias))).astype(bf16)
    u = u_low.astype(f32)
    part_s[...] = matmul(u_low, w_xp[...])

    z_flows = scatter_halves(
        "row", lambda d, at: matmul(low[at, :], w_z[:, columns(d, width)]), z_o, z_held, z_left, z_right, z_send, z_recv
    )

    def mix():
        yield from total_of_sums(part_s, half_own, half_in, low_own, low_in, proj_o, (t_send, t_recv))
        pre = matmul(proj_o[...].astype(bf16), w_step[...]) + as_row(dt_bias)
        step_now = jax.nn.softplus(pre)
        step[...] = step_now
        gone[...] = jnp.where(place > 0.0, step_now, 1e30)
        drive[...] = step_now * u
        yield from scan_forward(proj_o, rank, rank + count, gone, drive, rate[...], bb, cb, yv_o)

    mixing = mix()
    next(mixing)
    next(mixing)
    weights[1].wait()
    run(*z_flows, mixing)
    yv = yv_o[...] + as_row(skip) * u
    yv_o[...] = yv
    z = z_o[...] * s1
    z_o[...] = z
    go_all[:, columns(row, width)] = (yv * silu(z)).astype(bf16)

    def during_gather():
        n1_o[...] = (xg * s1 * gain1_now).astype(bf16)
        kept["mates"] = to_mates(n1_o, n1_mates, m_send.at[0], m_recv.at[0])
        plane_finish(c_copies, c_all, c_send, c_recv)
        cg_o[...] = pick_rows(source, c_all[...])
        kept["mates"] += to_mates(cg_o, cg_mates, m_send.at[1], m_recv.at[1])
        yield

    run(*gather_halves("row", go_all, width, go_send, go_recv), during_gather())
    weights[2].wait()
    own[...] = matmul(go_all[...], w_out[...])
    copy = swap("col", own, other, o_send.at[0], o_recv.at[0])
    weights[3].wait()
    weights[4].wait()
    copy.wait()
    h1 = xg + (own[...] + other[...])
    h1_o[...] = h1
    gain2_now = as_row(gain2)
    low[...] = (h1 * gain2_now).astype(bf16)

    def gate_up(d, at):
        side = columns(d, hidden)
        return jnp.concatenate([matmul(low[at, :], w_gate[:, side]), matmul(low[at, :], w_up[:, side])], axis=1)

    def during_scatter():
        sum_own[...] = rows_form(h1 * h1)
        sum_copies = spray("row", lambda k: sum_own, sum_in, sum2_send, sum2_recv)
        yield
        wait_all(sum_copies)
        s2 = column_form(lax.rsqrt(line_total(sum_own[...], sum_in) / model_width + epsilon))
        s2_o[...] = s2
        n2_o[...] = (h1 * s2 * gain2_now).astype(bf16)
        leave("n1", "cg", "xi", "z", "proj", "yv", "go_all", "h1", "s2", "n2")
        kept["mates"] += to_mates(n2_o, n2_mates, m_send.at[2], m_recv.at[2])

    run(
        *scatter_halves("row", gate_up, gu, gu_held, gu_left, gu_right, gu_send, gu_recv),
        during_scatter(),
    )
    s2 = s2_o[...]
    gate = gu[:, 0:hidden] * s2
    up = gu[:, hidden:] * s2
    sig = jax.nn.sigmoid(gate)
    act = gate * sig
    hid_all[:, columns(row, hidden)] = (act * up).astype(bf16)
    weights[5].wait()
    run(
        *gather_halves("row", hid_all, hidden, hid_send, hid_recv),
        *scatter_halves(
            "row", lambda d, at: transposed(cg_o[at, :], w_down[columns(d, hidden), :]), dhid, h_held, h_left, h_right,
            h_send, h_recv,
        ),
    )
    d_hid = dhid[...]
    d_gate = (d_hid * up * (sig * (1.0 + gate * (1.0 - sig)))).astype(bf16)
    d_up = (d_hid * act).astype(bf16)
    dgu_o[:, 0:hidden] = d_gate
    dgu_o[:, hidden:] = d_up
    dot_o[...] = rows_form(d_gate.astype(f32) * gate + d_up.astype(f32) * up)
    wait_all(kept["mates"])
    leave("hid_all", "dgu", "dot", "n1_mates", "n2_mates", "cg_mates")
    leave.finish()


def dp_bits():
    me = lax.axis_index("dp")
    return lax.rem(me, 2), me // 2


def dp_mates():
    me = lax.axis_index("dp")
    along_x, along_y = dp_bits()
    return {"dp": me + 1 - 2 * along_x}, {"dp": me + 2 - 4 * along_y}


def to_mates(src, dst, send, recv):
    copies = [remote(src, dst.at[h], send.at[h], recv.at[h], mate) for h, mate in enumerate(dp_mates())]
    for copy in copies:
        copy.start()
    return copies


def pair_sum(grad, sent, fixed, fixed_mates, by_rows, sent_in, second_in, third_in, send, recv):
    quarter = sent.shape[1] // 4
    eighth = (quarter if by_rows else grad.shape[0]) // 2
    bits, mates = dp_bits(), dp_mates()

    def side(h, near):
        return pl.ds(pl.multiple_of((2 * h + near) * quarter, quarter), quarter)

    def view(h, near, far):
        if by_rows:
            return grad.at[pl.ds(pl.multiple_of((2 * h + near) * quarter + far * eighth, eighth), eighth), :]
        return grad.at[pl.ds(pl.multiple_of(far * eighth, eighth), eighth), side(h, near)]

    class Half:
        def __init__(self, h):
            near, far = bits[h], bits[1 - h]
            mate, other = mates[h], mates[1 - h]

            def copy(stage, src, dst, to):
                return remote(src, dst, send.at[stage, h], recv.at[stage, h], to)

            self.h, self.near = h, near
            self.own, self.rest = view(h, near, far), view(h, near, 1 - far)
            there = view(h, 1 - near, far), view(h, 1 - near, 1 - far)
            self.out = (
                copy(0, sent.at[:, side(h, 1 - near)], sent_in.at[h], mate),
                copy(1, self.rest, second_in.at[h], other),
                copy(2, self.own, third_in.at[h], other),
                copy(3, self.own, self.own, mate),
                copy(4, self.rest, self.rest, mate),
            )
            self.back = (copy(3, there[0], there[0], mate), copy(4, there[1], there[1], mate))

        def product(self):
            mine, mates_part = sent[:, side(self.h, self.near)], sent_in[self.h]
            if by_rows:
                found = over_rows(mine, fixed[...]) + over_rows(mates_part, fixed_mates[self.h])
                grad[side(self.h, self.near), :] = found.astype(bf16)
            else:
                found = over_rows(fixed[...], mine) + over_rows(fixed_mates[self.h], mates_part)
                grad[:, side(self.h, self.near)] = found.astype(bf16)

    both_halves = (Half(0), Half(1))
    for half in both_halves:
        half.out[0].start()
    yield
    for half in both_halves:
        half.out[0].wait_recv()
        half.product()
        half.out[1].start()
    yield
    for half in both_halves:
        half.out[1].wait_recv()
        add_view(half.own, second_in.at[half.h], eighth)
        half.out[2].start()
        half.out[3].start()
    yield
    for half in both_halves:
        half.out[2].wait_recv()
        half.out[1].wait_send()
        half.rest[...] = third_in[half.h]
        half.out[4].start()
    yield
    for half in both_halves:
        for copy in half.back:
            copy.wait_recv()
        for stage in (0, 2, 3, 4):
            half.out[stage].wait_send()


def add_view(target, source, rows):
    def piece(j, _):
        at = pl.ds(pl.multiple_of(j * 16, 16), 16)
        target[at, :] = (target[at, :].astype(f32) + source[at, :].astype(f32)).astype(bf16)
        return 0

    lax.fori_loop(0, rows // 16, piece, 0)


def add_rows(target, base, source, rows):
    def piece(j, _):
        at = pl.ds(pl.multiple_of(base + j * 16, 16), 16)
        found = target[at, :].astype(f32) + source[pl.ds(pl.multiple_of(j * 16, 16), 16), :].astype(f32)
        target[at, :] = found.astype(target.dtype)
        return 0

    lax.fori_loop(0, rows // 16, piece, 0)


def plane_sum(grad, first_in, second_in, send, recv, free):
    quarter = grad.shape[0] // 4
    eighth = quarter // 2
    bits, partners = dp_bits(), dp_mates()

    def rows(ref, start, count):
        return ref.at[pl.ds(pl.multiple_of(start, 16), count), :]

    class Half:
        def __init__(self, h):
            near, far = bits[h], bits[1 - h]
            self.free, self.mate, self.first = free.at[h], partners[h], first_in.at[h]
            base = h * 2 * quarter
            self.kept = base + near * quarter
            self.own = self.kept + far * eighth
            self.rest = self.kept + (1 - far) * eighth
            self.rest_in = (1 - far) * eighth
            across = base + (1 - near) * quarter
            self.second = second_in.at[h]

            def copy(stage, src, dst, to):
                return remote(src, dst, send.at[stage, h], recv.at[stage, h], to)

            mate, other = partners[h], partners[1 - h]
            own, rest = rows(grad, self.own, eighth), rows(grad, self.rest, eighth)
            there = (rows(grad, across + far * eighth, eighth), rows(grad, across + (1 - far) * eighth, eighth))
            back = rows(self.first, self.rest_in, eighth)
            self.out = (
                copy(0, rows(grad, across, quarter), self.first, mate),
                copy(1, rest, self.second, other),
                copy(2, own, rows(self.first, far * eighth, eighth), other),
                copy(3, own, own, mate),
                copy(4, rest, rest, mate),
            )
            self.back = (
                None,
                None,
                copy(2, back, back, other),
                copy(3, there[0], there[0], mate),
                copy(4, there[1], there[1], mate),
            )

    halves = (Half(0), Half(1))
    for half in halves:
        half.out[0].start()
    yield
    for half in halves:
        half.out[0].wait_recv()
        add_rows(grad, half.kept, half.first, quarter)
        half.out[1].start()
        half.out[0].wait_send()
        pl.semaphore_signal(half.free, inc=1, device_id=half.mate, device_id_type=MESH)
    yield
    for half in halves:
        half.out[1].wait_recv()
        add_rows(grad, half.own, half.second, eighth)
        half.out[2].start()
        pl.semaphore_wait(half.free, 1)
        half.out[3].start()
    yield
    for half in halves:
        half.back[2].wait_recv()
        half.out[1].wait_send()
        grad[pl.ds(pl.multiple_of(half.rest, 16), eighth), :] = half.first[
            pl.ds(pl.multiple_of(half.rest_in, 16), eighth), :
        ]
        half.out[4].start()
    yield
    for half in halves:
        half.back[3].wait_recv()
        half.back[4].wait_recv()
        for copy in half.out[2:]:
            copy.wait_send()


class Sums:
    def __init__(self):
        self.active = []

    def add(self, flow):
        next(flow)
        self.active.append(flow)

    def pump(self, count=1):
        for _ in range(count):
            if self.active:
                flow = self.active.pop(0)
                if next(flow, self) is not self:
                    self.active.append(flow)

    def drain(self):
        while self.active:
            self.pump()


def backward_kernel(
    lens, order, gain2, taps, bias, w_xp, w_dt, dt_bias, a_log, skip, gain1,
    w_gate_h, w_up_h, w_down_h, w_out_h, w_x_h, w_z_h,
    y_o, dx_o, small_o, g_down_o, g_gate_o, g_up_o, g_z_o, g_x_o, g_out_o,
    w_gate, w_up, w_down, w_out, w_x, w_z, w_step, rate,
    dg_all, du_all, dz_all, dxi_all, dh1, dmix, y_own, dx_own, y_all, dx_all,
    own, other, y_part, y_other, dot_in, dot_own, dot_sum, dot_other,
    dgo, d_held, d_left, d_right,
    hs, bb, cb, pb, pc, step, gone, drive, u_s, dy_s, du_s, dstep, dproj,
    half_own, half_in, low_own, low_in, full,
    g_down, g_gate, g_up, g_z, g_x, g_out, small,
    g_down_1, g_gate_1, g_up_1, g_z_1, g_x_1, g_out_1, small_1,
    g_down_2, g_gate_2, g_up_2, g_z_2, g_x_2, g_out_2, small_2,
    g_down_3, g_gate_3, g_up_3, g_z_3, g_x_3,
    w_sems, g_send, g_recv, u_send, u_recv, o_send, o_recv, dot_send, dot_recv,
    y_send, y_recv, dx_send, dx_recv, d_send, d_recv, z_send, z_recv, t_send, t_recv, x_send, x_recv,
    dot2_send, dot2_recv, sum_send, sum_recv, sum_free, write_sems,
    *, rank, model_width, late
):
    rows, width = dgo.shape
    count = rate.shape[0]
    block = y_o.shape[0]
    tap_count = taps.shape[0]
    group, row, column = lax.axis_index("dp"), lax.axis_index("row"), lax.axis_index("col")
    row_size, col_size = lax.axis_size("row"), lax.axis_size("col")
    weights = fetch(
        (w_down_h, w_gate_h, w_up_h, w_out_h, w_x_h, w_z_h), (w_down, w_gate, w_up, w_out, w_x, w_z), w_sems
    )
    half = columns(column, block)
    sums = Sums()
    writes = []

    def write(number, grad, result):
        copy = pltpu.make_async_copy(grad, result, write_sems.at[number])
        copy.start()
        writes.append(copy)

    def total(number, grad, first_in, second_in, result):
        yield from plane_sum(
            grad, first_in, second_in, sum_send.at[number], sum_recv.at[number], sum_free.at[number]
        )
        write(number, grad, result)

    def pair(number, grad, sent, fixed, fixed_mates, by_rows, ins, result):
        yield from pair_sum(
            grad, sent, fixed, fixed_mates, by_rows, *ins, sum_send.at[number], sum_recv.at[number]
        )
        write(number, grad, result)

    def product(left, right, grad):
        size = grad.shape[0] // 4
        for start in range(0, grad.shape[0], size):
            grad[start : start + size, :] = over_rows(left[:, start : start + size], right[...]).astype(bf16)

    met = greet("dp", "row", "col")
    dgu = late("dgu")
    hidden = dgu.shape[1] // 2
    dg_all[:, columns(row, hidden)] = dgu[:, 0:hidden]
    du_all[:, columns(row, hidden)] = dgu[:, hidden:]
    dot, hid_all, cg, cg_mates = late("dot"), late("hid_all"), late("cg"), late("cg_mates")
    met()
    dot_copies = spray("row", lambda k: dot, dot_in, dot_send, dot_recv)

    def first_work():
        sums.add(pair(0, g_down, hid_all, cg, cg_mates, True, (g_down_1, g_down_2, g_down_3), g_down_o))
        yield
        weights[0].wait()
        y_part[...] = matmul(hid_all[...], w_down[...])
        y_copy = swap("col", y_part, y_other, o_send.at[0], o_recv.at[0])
        yield
        wait_all(dot_copies)
        dot_own[...] = line_total(dot[...], dot_in)
        dot_copy = swap("col", dot_own, dot_other, o_send.at[2], o_recv.at[2])
        weights[1].wait()
        weights[2].wait()
        yield
        y_copy.wait()
        dot_copy.wait()
        y_own[...] = (late("h1")[...] + (y_part[...] + y_other[...])).astype(bf16)

    run(*gather_halves("row", dg_all, hidden, g_send, g_recv), first_work(), pump=(sums, PUMPS[0]))
    n2, n2_mates = late("n2"), late("n2_mates")
    sums.add(pair(1, g_gate, dg_all, n2, n2_mates, False, (g_gate_1, g_gate_2, g_gate_3), g_gate_o))

    def second_work():
        own[...] = transposed(dg_all[...], w_gate[...])
        yield

    run(*gather_halves("row", du_all, hidden, u_send, u_recv), second_work(), pump=(sums, PUMPS[1]))
    own[...] += transposed(du_all[...], w_up[...])
    copy = swap("col", own, other, o_send.at[1], o_recv.at[1])
    sums.add(pair(2, g_up, du_all, n2, n2_mates, False, (g_up_1, g_up_2, g_up_3), g_up_o))
    sums.pump(PUMPS[2])
    copy.wait()
    h1_now, s2_now = late("h1")[...], late("s2")[...]
    dn2 = own[...] + other[...]
    dots = column_form(dot_own[...] + dot_other[...])
    dh1_now = (
        cg[...].astype(f32)
        + s2_now * (as_row(gain2) * dn2)
        - h1_now * (s2_now * s2_now * dots / model_width)
    )
    dh1[...] = dh1_now
    dmix[...] = dh1_now.astype(bf16)
    gnorm2 = jnp.sum(dn2 * h1_now * s2_now, axis=0, keepdims=True)

    inner_x = late("xi")[...]
    place_now = late("place")[...]
    proj = late("proj")
    kept = {}

    def states():
        go_all = late("go_all")
        product(go_all, dmix, g_out)
        sums.add(total(5, g_out, g_out_1, g_out_2, g_out_o))
        w_step[...] = jnp.zeros_like(w_step)
        w_step[0:rank, :] = w_dt[...]
        rate[...] = -jnp.exp(a_log[...])
        xc = conv_sum(inner_x, place_now, taps[...], as_row(bias))
        sig_c = jax.nn.sigmoid(xc)
        u_low = (xc * sig_c).astype(bf16)
        u = u_low.astype(f32)
        u_s[...] = u
        step_low = proj[...].astype(bf16)
        pre = matmul(step_low, w_step[...]) + as_row(dt_bias)
        step_now = jax.nn.softplus(pre)
        step[...] = step_now
        gone[...] = jnp.where(place_now > 0.0, step_now, 1e30)
        drive[...] = step_now * u
        kept.update(xc=xc, sig_c=sig_c, u_low=u_low, u=u, step_low=step_low, pre=pre)
        yield from scan_states(proj, rank, gone, drive, rate[...], bb, hs)

    weights[3].wait()
    run(
        *scatter_halves(
            "row", lambda d, at: transposed(dmix[at, :], w_out[columns(d, width), :]), dgo, d_held, d_left, d_right,
            d_send, d_recv,
        ),
        states(),
        pump=(sums, PUMPS[3]),
    )
    xc, sig_c, u_low, u = kept["xc"], kept["sig_c"], kept["u_low"], kept["u"]
    step_low, pre = kept["step_low"], kept["pre"]
    z_now = late("z")[...]
    sig_z = jax.nn.sigmoid(z_now)
    d_z = (dgo[...] * late("yv")[...] * (sig_z * (1.0 + z_now * (1.0 - sig_z)))).astype(bf16)
    mine = dz_all.at[:, columns(row, width)]
    mine[...] = d_z
    z_copies = []
    for k in range(1, row_size):
        copy = remote(mine, mine, z_send.at[k - 1], z_recv.at[k - 1], away("row", k))
        copy.start()
        z_copies.append(copy)
    dy = dgo[...] * (z_now * sig_z)
    dy_s[...] = dy
    dproj[...] = jnp.zeros_like(dproj)

    def adjoint():
        kept["rate"] = yield from scan_backward(
            proj, rank, rank + count, step, gone, drive, u_s, dy_s, rate[...], hs, bb, cb, pb, pc, du_s, dstep, dproj
        )

    run(adjoint(), pump=(sums, PUMPS[4]))
    g_rate = kept["rate"]
    d_pre = dstep[...] * jax.nn.sigmoid(pre)
    d_pre_low = d_pre.astype(bf16)
    dproj[...] += transposed(d_pre_low, w_step[...])

    def during_sums():
        yield
        wait_all(z_copies)
        sums.add(pair(3, g_z, dz_all, late("n1"), late("n1_mates"), False, (g_z_1, g_z_2, g_z_3), g_z_o))

    run(
        total_of_sums(dproj, half_own, half_in, low_own, low_in, full, (t_send, t_recv)),
        during_sums(),
        pump=(sums, PUMPS[5]),
    )
    dproj_low = full[...].astype(bf16)
    du = du_s[...] + as_row(skip) * dy + transposed(dproj_low, w_xp[...])
    dxc = du * (sig_c * (1.0 + xc * (1.0 - sig_c)))
    taps_now = taps[...]
    d_inner = dxc * taps_now[tap_count - 1 : tap_count, :]
    masked = [dxc]
    for shift in range(1, tap_count):
        masked.append(jnp.where(place_now >= shift, dxc, 0.0))
        k = tap_count - 1 - shift
        d_inner = d_inner + pltpu.roll(masked[shift], rows - shift, 0) * taps_now[k : k + 1, :]
    d_inner = d_inner.astype(bf16)
    dxi_all[:, columns(row, width)] = d_inner

    def during():
        dot_own[...] = rows_form(d_inner.astype(f32) * inner_x + d_z.astype(f32) * z_now)
        dot_copies = spray("row", lambda k: dot_own, dot_in, dot2_send, dot2_recv)
        small[0:RANK_LANES, :] = over_rows(dproj_low, u_low).astype(bf16)
        small[RANK_LANES : RANK_LANES + rank, :] = over_rows(step_low, d_pre_low)[0:rank, :].astype(bf16)
        yield
        wait_all(dot_copies)
        dot_sum[...] = line_total(dot_own[...], dot_in)
        dot_copy = swap("col", dot_sum, dot_other, o_send.at[3], o_recv.at[3])
        weights[4].wait()
        weights[5].wait()
        own[...] = transposed(dz_all[...], w_z[...])
        yield
        dot_copy.wait()

    run(*gather_halves("row", dxi_all, width, x_send, x_recv), during(), pump=(sums, PUMPS[6]))
    own[...] += transposed(dxi_all[...], w_x[...])
    copy = swap("col", own, other, o_send.at[4], o_recv.at[4])
    sums.add(pair(4, g_x, dxi_all, late("n1"), late("n1_mates"), False, (g_x_1, g_x_2, g_x_3), g_x_o))
    sums.pump(PUMPS[7])
    copy.wait()
    dn1 = own[...] + other[...]
    s1_now = late("s1")[...]
    xg_now = late("xg")[...].astype(f32)
    dots = column_form(dot_sum[...] + dot_other[...])
    dx = dh1[...] + s1_now * (as_row(gain1) * dn1) - xg_now * (s1_now * s1_now * dots / model_width)
    dx_own[...] = dx.astype(bf16)
    dx_copies = plane_start(dx_own.at[half], dx_all, dx_send, dx_recv)
    y_copies = plane_start(y_own.at[half], y_all, y_send, y_recv)
    g_taps = [None] * tap_count
    for shift in range(tap_count):
        moved = pltpu.roll(inner_x, shift, 0) if shift else inner_x
        g_taps[tap_count - 1 - shift] = jnp.sum(masked[shift] * moved, axis=0, keepdims=True)
    pieces = [
        g_rate,
        *g_taps,
        jnp.sum(dxc, axis=0, keepdims=True),
        jnp.sum(d_pre, axis=0, keepdims=True),
        jnp.sum(dy * u, axis=0, keepdims=True),
        jnp.sum(dn1 * xg_now * s1_now, axis=0, keepdims=True),
        gnorm2,
    ]
    found = sum(piece.shape[0] for piece in pieces)
    pieces.append(jnp.zeros((small.shape[0] - RANK_LANES - rank - found, width), f32))
    small[RANK_LANES + rank :, :] = jnp.concatenate(pieces, axis=0).astype(bf16)
    sums.add(total(6, small, small_1, small_2, small_o))
    first = (group * col_size + column) * block
    wanted = owner_rows(lengths_row(lens), as_row(order), lens.shape[1], rows, block, first)
    sums.pump(PUMPS[8])
    plane_finish(dx_copies, dx_all, dx_send, dx_recv)
    dx_o[...] = pick_rows(wanted, dx_all[...])
    plane_finish(y_copies, y_all, y_send, y_recv)
    y_o[...] = pick_rows(wanted, y_all[...])
    sums.drain()
    for write in writes:
        write.wait()


def finish_kernel(
    y, dx, small,
    y_o, dx_o, norm1_o, taps_o, bias_o, w_xp_o, w_dt_o, dt_bias_o, rate_o, skip_o, norm2_o,
    z_o, x_o, out_o, down_o, gate_o, up_o,
    *, rank, late, leave
):
    for name, target in (("z", z_o), ("x", x_o), ("out", out_o), ("down", down_o), ("gate", gate_o), ("up", up_o)):
        target[...] = late(name)[...].astype(f32)
        leave(name)
    y_o[...] = y[...]
    dx_o[...] = dx[...]
    values = small[...].astype(f32)
    w_xp_o[...] = jnp.transpose(values[0:RANK_LANES, :])
    w_dt_o[...] = values[RANK_LANES : RANK_LANES + rank, :]
    at = RANK_LANES + rank
    for target in (rate_o, taps_o):
        target[...] = values[at : at + target.shape[0], :]
        at += target.shape[0]
    for target in (bias_o, dt_bias_o, skip_o, norm1_o, norm2_o):
        target[...] = values[at : at + 1, :].reshape(target.shape)
        at += 1
    leave.finish()


VMEM_BYTES = 60 << 20
DMA = pltpu.SemaphoreType.DMA


def in_vmem(kernel, name, ident, outs, scratch, args, far=(), far_outs=(), late=None, leave=None):
    late, leave = late or {}, leave or {}
    space = pl.BlockSpec(memory_space=pltpu.VMEM)
    anywhere = pl.BlockSpec(memory_space=pl.ANY)
    heads, tails, before, after = len(args) + len(far), len(outs) + len(far_outs), len(late), len(leave)

    def whole(*refs):
        at = [0]

        def take(count):
            at[0] += count
            return refs[at[0] - count : at[0]]

        head, sources, tail, targets = take(heads), take(before), take(tails), take(after)
        middle = take(len(scratch))
        keywords = {}
        if late:
            held = take(before)
            keywords["late"] = Late(list(late), sources, held, take(1)[0])
        held = take(after)
        if leave:
            keywords["leave"] = Leave(list(leave), held, targets, take(1)[0])
        kernel(*head, *tail, *held, *middle, **keywords)

    own = list(scratch)
    if late:
        own += [pltpu.VMEM(value.shape, value.dtype) for value in late.values()] + [DMA((before,))]
    if leave:
        own += [pltpu.VMEM(shape, kind) for shape, kind in leave.values()] + [DMA((after,))]
    return pl.pallas_call(
        whole,
        out_shape=tuple(jax.ShapeDtypeStruct(shape, kind) for shape, kind in [*outs, *far_outs, *leave.values()]),
        in_specs=[space] * len(args) + [anywhere] * (len(far) + before),
        out_specs=tuple([space] * len(outs) + [anywhere] * (len(far_outs) + after)),
        scratch_shapes=own,
        compiler_params=pltpu.CompilerParams(
            collective_id=ident, has_side_effects=ident is not None, vmem_limit_bytes=VMEM_BYTES
        ),
        name=name,
    )(*args, *far, *late.values())


def both(*shape):
    return [DMA(shape), DMA(shape)]


def on_pairs(
    x_in, lengths, seq_order, norm1_gain, w_in_x, w_in_z, conv_w, conv_b, w_xp, w_dt, dt_bias, a_log,
    skip_weight, w_out, norm2_gain, w_gate, w_up, w_down, cotangent,
):
    dp, rs = lax.axis_size("dp"), lax.axis_size("row")
    block, wide_d = x_in.shape
    rows = block * 2
    model_width = wide_d * rs
    width = conv_w.shape[0]
    hidden = w_gate.shape[1] // rs
    rank, count, taps = w_dt.shape[0], a_log.shape[1], conv_w.shape[1]
    conv_taps = conv_w.T
    rates = a_log.T
    vm = pltpu.VMEM
    tile = vm((128, count, 128), f32)
    big = vm((rows, width), f32)
    model = vm((rows, wide_d), f32)
    sums = [vm((8, rows), f32), vm((rs - 1, 8, rows), f32)]
    sums_scratch = [
        vm((rows // 2, RANK_LANES), f32),
        vm((rows // 2, RANK_LANES), f32),
        vm((rows // 2, RANK_LANES), bf16),
        vm((rs - 1, rows // 2, RANK_LANES), bf16),
    ]

    def weight(value):
        return vm(value.shape, value.dtype)

    def line(size, width):
        return [vm((size, rows, width), bf16)] * 3

    leave = {
        "xg": ((rows, wide_d), bf16), "cg": ((rows, wide_d), bf16), "n1": ((rows, wide_d), bf16),
        "s1": ((rows, 1), f32), "place": ((rows, 1), f32), "xi": ((rows, width), f32), "z": ((rows, width), f32),
        "proj": ((rows, RANK_LANES), f32), "yv": ((rows, width), f32), "go_all": ((rows, rs * width), bf16),
        "h1": ((rows, wide_d), f32), "s2": ((rows, 1), f32), "n2": ((rows, wide_d), bf16),
        "hid_all": ((rows, rs * hidden), bf16), "dgu": ((rows, 2 * hidden), bf16), "dot": ((8, rows), f32),
        "n1_mates": ((2, rows, wide_d), bf16), "n2_mates": ((2, rows, wide_d), bf16),
        "cg_mates": ((2, rows, wide_d), bf16),
    }
    passed = in_vmem(
        functools.partial(forward_kernel, model_width=model_width, rank=rank, count=count),
        "forward",
        0,
        [],
        [
            weight(w_in_x), weight(w_in_z), weight(w_out), weight(w_gate), weight(w_up), weight(w_down),
            vm((RANK_LANES, width), bf16), vm((count, width), f32),
            vm((2, dp, block, wide_d), bf16), vm((2, dp, block, wide_d), bf16), *sums, vm((rows, wide_d), bf16),
            *line(rs, width), *line(rs, width),
            vm((rows, RANK_LANES), f32), *sums_scratch, tile, tile, big, big, big,
            model, model, vm((rows, 2 * hidden), f32), *line(rs, 2 * hidden), vm((rows, hidden), f32), *line(rs, hidden),
            DMA((6,)), *both(dp), *both(dp), *both(rs - 1), *both(2, 2, rs), *both(2, 2, rs), *both(rs + 1),
            *both(2, 2, rs), *both(1), *both(rs - 1), *both(2, 2, rs), *both(2, 2, rs), *both(2, 2, rs), *both(3, 2),
        ],
        (
            x_in, cotangent, lengths, seq_order, norm1_gain, conv_taps, conv_b, w_xp, w_dt, dt_bias, rates, skip_weight,
            norm2_gain,
        ),
        (w_in_x, w_in_z, w_out, w_gate, w_up, w_down),
        leave=leave,
    )
    passed = dict(zip(leave, passed))
    first = ("dgu", "dot", "hid_all", "cg", "cg_mates", "n2", "n2_mates")
    late = {name: passed[name] for name in (*first, *(name for name in passed if name not in first))}

    def sizes(value, parts):
        return vm((2, value[0] // parts, value[1]), bf16)

    def eighths(value):
        return vm((2, value[0] // 8, value[1]) if value == d_cols else (2, value[0] // 2, value[1] // 4), bf16)

    d_cols, f_cols, e_cols = (rs * hidden, wide_d), (wide_d, rs * hidden), (wide_d, rs * width)
    grads = (d_cols, f_cols, f_cols, e_cols, e_cols, (rs * width, wide_d), (2 * RANK_LANES, width))
    returned = in_vmem(
        functools.partial(backward_kernel, rank=rank, model_width=model_width),
        "backward",
        1,
        [((block, wide_d), bf16), ((block, wide_d), bf16)],
        [
            weight(w_gate), weight(w_up), weight(w_down), weight(w_out), weight(w_in_x), weight(w_in_z),
            vm((RANK_LANES, width), bf16), vm((count, width), f32),
            vm((rows, rs * hidden), bf16), vm((rows, rs * hidden), bf16),
            vm((rows, rs * width), bf16), vm((rows, rs * width), bf16),
            model, vm((rows, wide_d), bf16), vm((rows, wide_d), bf16), vm((rows, wide_d), bf16),
            vm((2, dp, block, wide_d), bf16), vm((2, dp, block, wide_d), bf16),
            model, model, model, model, vm((rs - 1, 8, rows), f32), vm((8, rows), f32), vm((8, rows), f32),
            vm((8, rows), f32), big, *line(rs, width),
            vm((rows + 1, count, width), f32), tile, tile, tile, tile,
            big, big, big, big, big, big, big, vm((rows, RANK_LANES), f32), *sums_scratch, vm((rows, RANK_LANES), f32),
            *[vm(value, bf16) for value in grads],
            *[vm((2, rows, max(value) // 4), bf16) for value in grads[:5]], *[sizes(value, 4) for value in grads[5:]],
            *[eighths(value) for value in grads[:5]], *[sizes(value, 8) for value in grads[5:]],
            *[eighths(value) for value in grads[:5]],
            DMA((6,)), *both(2, 2, rs), *both(2, 2, rs), *both(5), *both(rs - 1), *both(dp), *both(dp), *both(2, 2, rs),
            *both(rs - 1), *both(rs + 1), *both(2, 2, rs), *both(rs - 1), *both(len(grads), 5, 2),
            pltpu.SemaphoreType.REGULAR((len(grads), 2)), DMA((len(grads),)),
        ],
        (
            lengths, seq_order, norm2_gain, conv_taps, conv_b, w_xp, w_dt, dt_bias, rates, skip_weight, norm1_gain,
        ),
        (w_gate, w_up, w_down, w_out, w_in_x, w_in_z),
        [(value, bf16) for value in (grads[-1], *grads[:-1])],
        late,
    )
    y_part, dx_part, small, *summed = returned
    names = ("down", "gate", "up", "z", "x", "out")
    order = (3, 4, 5, 0, 1, 2)
    y_out, dx_out, norm1, g_taps, g_bias, g_xp, g_dt, g_dt_bias, g_rate, g_skip, norm2, *wide = in_vmem(
        functools.partial(finish_kernel, rank=rank),
        "finish",
        None,
        [
            ((block, wide_d), bf16), ((block, wide_d), bf16), ((wide_d,), f32), ((taps, width), f32), ((width,), f32),
            ((width, RANK_LANES), f32), ((rank, width), f32), ((width,), f32), ((count, width), f32), ((width,), f32),
            ((wide_d,), f32),
        ],
        [],
        (y_part, dx_part, small),
        late={names[i]: summed[i] for i in order},
        leave={names[i]: (grads[i], f32) for i in order},
    )
    g_z, g_x, g_out, g_down, g_gate, g_up = wide
    return (
        y_out, dx_out, norm1, g_x, g_z, g_taps.T, g_bias, g_xp, g_dt, g_dt_bias, g_rate.T, g_skip, g_out, norm2,
        g_gate, g_up, g_down,
    )


def on_device(
    x_in,
    lengths,
    seq_order,
    norm1_gain,
    w_in_x,
    w_in_z,
    conv_w,
    conv_b,
    w_xp,
    w_dt,
    dt_bias,
    a_log,
    skip_weight,
    w_out,
    norm2_gain,
    w_gate,
    w_up,
    w_down,
    cotangent,
):
    rows_in, width_row = x_in.shape
    row_devices = lax.axis_size("row")
    col_devices = lax.axis_size("col")
    group_rows = rows_in * col_devices
    model_width = width_row * row_devices
    rank_cols = w_dt.shape[0]
    state_count = a_log.shape[1]
    channels = conv_w.shape[0]
    ff_cols = w_gate.shape[1]
    my_group = lax.axis_index("dp")
    my_column = lax.axis_index("col")
    source, position_all = layout(lengths, seq_order, group_rows)
    my_source = lax.dynamic_index_in_dim(source, my_group, 0, keepdims=False)
    position = lax.dynamic_index_in_dim(position_all, my_group, 0, keepdims=False)
    slice_source = lax.dynamic_slice_in_dim(my_source, my_column * rows_in, rows_in, 0)

    def row_total(values):
        return lax.psum(values, "row")

    def token_rows(values):
        return lax.all_gather(values, "col", axis=0, tiled=True)

    def row_pieces(values):
        return lax.all_gather(values, "row", axis=0, tiled=True)

    def col_reduce(term_fn):
        return lax.psum_scatter(
            term_fn(jnp.int32(0), lax.axis_size("col") * rows_in),
            "col",
            scatter_dimension=0,
            tiled=True,
        )

    def row_reduce(term_fn, keep_rows):
        return lax.psum_scatter(
            term_fn(jnp.int32(0), lax.axis_size("row") * keep_rows),
            "row",
            scatter_dimension=0,
            tiled=True,
        )

    def projection_total(values):
        return lax.psum(values, ("row", "col"))

    blank_rows = jnp.zeros((rows_in, width_row), jnp.bfloat16)
    pieces = (
        lax.all_gather(x_in, ("dp", "col"), axis=0, tiled=True),
        lax.all_gather(cotangent, ("dp", "col"), axis=0, tiled=True),
    )
    row_count = pieces[0].shape[0]
    offset = slice_source
    inside = ((offset >= 0) & (offset < row_count))[:, None]
    index = jnp.clip(offset, 0, row_count - 1)
    x_rows = jnp.where(inside, jnp.take(pieces[0], index, axis=0), blank_rows)
    cot_rows = jnp.where(inside, jnp.take(pieces[1], index, axis=0), blank_rows)
    x_val = x_rows.astype(jnp.float32)
    scale_one = lax.rsqrt(row_total(jnp.sum(x_val * x_val, axis=1)) / model_width + epsilon)
    normed_one = (x_val * scale_one[:, None] * norm1_gain[None, :]).astype(jnp.bfloat16)
    normed_all = token_rows(normed_one)

    def inner_term(begin_row, row_count):
        return jnp.concatenate(
            [contract(w_in_x, normed_all, 0, 1), contract(w_in_z, normed_all, 0, 1)], axis=1
        )

    inner = row_reduce(inner_term, channels)
    inner_x = inner[:, :group_rows]
    inner_z = inner[:, group_rows:]

    def conv_part(values, kernel, kernel_bias):
        return convolve(values, kernel, kernel_bias, position)

    conv_out, conv_pull = jax.vjp(conv_part, inner_x, conv_w, conv_b)
    u_low = conv_out.astype(jnp.bfloat16)
    u_val = u_low.astype(jnp.float32)
    projected = projection_total(contract(w_xp, u_low, 0, 0))
    step_low = projected[:rank_cols].astype(jnp.bfloat16)
    pre_step = contract(w_dt, step_low, 0, 0) + dt_bias[:, None]
    step_size = jax.nn.softplus(pre_step)

    decay_rate = -jnp.exp(a_log).T
    proj_rows = projected.T
    u_rows = u_val.T
    step_rows = step_size.T
    gone_rows = jnp.where(position[:, None] > 0, step_rows, 1e30)
    drive_rows = step_rows * u_rows
    at_b, at_c = rank_cols, rank_cols + state_count
    scanned = scan_alone(proj_rows, gone_rows, drive_rows, decay_rate, at_b, at_c)
    mixer_y = scanned.T + skip_weight[:, None] * u_val
    gated = mixer_y * jax.nn.silu(inner_z)
    gated_low = gated.astype(jnp.bfloat16)
    gated_all = row_pieces(gated_low)

    def mix_term(begin_row, row_count):
        return contract(gated_all, w_out, 0, 0)

    first_sum = x_val + col_reduce(mix_term)
    scale_two = lax.rsqrt(row_total(jnp.sum(first_sum * first_sum, axis=1)) / model_width + epsilon)
    normed_two = (first_sum * scale_two[:, None] * norm2_gain[None, :]).astype(jnp.bfloat16)
    normed_rows = token_rows(normed_two)

    def ffn_term(begin_row, row_count):
        return jnp.concatenate(
            [
                jnp.dot(normed_rows, w_gate, preferred_element_type=jnp.float32),
                jnp.dot(normed_rows, w_up, preferred_element_type=jnp.float32),
            ],
            axis=1,
        )

    gate_up = row_reduce(ffn_term, group_rows // row_devices)
    gate_val = gate_up[:, :ff_cols]
    up_val = gate_up[:, ff_cols:]
    hidden = (jax.nn.silu(gate_val) * up_val).astype(jnp.bfloat16)
    hidden_all = row_pieces(hidden)

    def down_term(begin_row, row_count):
        return jnp.dot(hidden_all, w_down, preferred_element_type=jnp.float32)

    second_sum = first_sum + col_reduce(down_term)
    out_low = second_sum.astype(jnp.bfloat16)
    back_down_all = token_rows(cot_rows)
    grad_down = contract(hidden_all, back_down_all, 0, 0)

    def hidden_term(begin_row, row_count):
        return contract(back_down_all, w_down, 1, 1)

    d_hidden = row_reduce(hidden_term, group_rows // row_devices)
    d_gate = (d_hidden * up_val * silu_slope(gate_val)).astype(jnp.bfloat16)
    d_up = (d_hidden * jax.nn.silu(gate_val)).astype(jnp.bfloat16)
    d_gate_up_all = row_pieces(jnp.concatenate([d_gate, d_up], axis=1))
    grad_gate = contract(normed_rows, d_gate_up_all[:, :ff_cols], 0, 0)
    grad_up = contract(normed_rows, d_gate_up_all[:, ff_cols:], 0, 0)

    def norm_two_term(begin_row, row_count):
        return contract(d_gate_up_all[:, :ff_cols], w_gate, 1, 1) + contract(
            d_gate_up_all[:, ff_cols:], w_up, 1, 1
        )

    d_normed_two = col_reduce(norm_two_term)
    cot_val = cot_rows.astype(jnp.float32)
    weighted_two = d_normed_two * norm2_gain[None, :]
    grad_norm_two = jnp.sum(d_normed_two * first_sum * scale_two[:, None], axis=0)
    dot_two = row_total(jnp.sum(weighted_two * first_sum, axis=1))
    d_first = (
        cot_val
        + scale_two[:, None] * weighted_two
        - first_sum * (scale_two**3 * dot_two / model_width)[:, None]
    )
    d_mix_all = token_rows(d_first.astype(jnp.bfloat16))
    grad_out = contract(gated_all, d_mix_all, 1, 0)

    def gated_term(begin_row, row_count):
        return contract(w_out, d_mix_all, 1, 1)

    d_gated = row_reduce(gated_term, channels)
    d_inner_z = d_gated * mixer_y * silu_slope(inner_z)
    d_mixer = d_gated * jax.nn.silu(inner_z)
    d_u_rows, d_step_rows, d_proj_rows, grad_rate_rows = adjoint_alone(
        proj_rows, step_rows, gone_rows, drive_rows, u_rows, d_mixer.T, decay_rate, at_b, at_c
    )
    d_u_mix = d_u_rows.T + skip_weight[:, None] * d_mixer
    d_step = d_step_rows.T
    d_enter = d_proj_rows.T[at_b:at_c]
    d_leave = d_proj_rows.T[at_c:]
    grad_rate = grad_rate_rows.T
    grad_skip = jnp.sum(d_mixer * u_val, axis=1)
    d_pre = d_step * jax.nn.sigmoid(pre_step)
    grad_step_bias = jnp.sum(d_pre, axis=1)
    d_pre_low = d_pre.astype(jnp.bfloat16)
    grad_step_w = contract(step_low, d_pre_low, 1, 1)
    d_projected = projection_total(
        jnp.concatenate(
            [jnp.dot(w_dt, d_pre_low, preferred_element_type=jnp.float32), d_enter, d_leave], axis=0
        )
    )
    d_proj_low = d_projected.astype(jnp.bfloat16)
    grad_proj_w = contract(u_low, d_proj_low, 1, 1)
    d_u_all = d_u_mix + jnp.dot(w_xp, d_proj_low, preferred_element_type=jnp.float32)
    d_inner_x, grad_kernel, grad_kernel_bias = conv_pull(d_u_all)
    d_inner_all = row_pieces(
        jnp.concatenate([d_inner_x.astype(jnp.bfloat16), d_inner_z.astype(jnp.bfloat16)], axis=1)
    )
    grad_in_x = contract(normed_all, d_inner_all[:, :group_rows], 0, 1)
    grad_in_z = contract(normed_all, d_inner_all[:, group_rows:], 0, 1)

    def norm_one_term(begin_row, row_count):
        piece_x = lax.dynamic_slice_in_dim(d_inner_all, begin_row, row_count, 1)
        piece_z = lax.dynamic_slice_in_dim(d_inner_all, group_rows, row_count, 1)
        return contract(piece_x, w_in_x, 0, 1) + contract(piece_z, w_in_z, 0, 1)

    d_normed_one = col_reduce(norm_one_term)
    weighted_one = d_normed_one * norm1_gain[None, :]
    grad_norm_one = jnp.sum(d_normed_one * x_val * scale_one[:, None], axis=0)
    dot_one = row_total(jnp.sum(weighted_one * x_val, axis=1))
    d_input = (
        d_first
        + scale_one[:, None] * weighted_one
        - x_val * (scale_one**3 * dot_one / model_width)[:, None]
    )
    d_input_low = d_input.astype(jnp.bfloat16)
    grad_norm_one, grad_norm_two = lax.psum((grad_norm_one, grad_norm_two), ("dp", "col"))
    (
        grad_in_x,
        grad_in_z,
        grad_kernel,
        grad_kernel_bias,
        grad_proj_w,
        grad_step_w,
        grad_step_bias,
        grad_rate,
        grad_skip,
        grad_out,
        grad_gate,
        grad_up,
        grad_down,
    ) = (
        lax.psum(grad_in_x.astype(jnp.bfloat16), "dp").astype(jnp.float32),
        lax.psum(grad_in_z.astype(jnp.bfloat16), "dp").astype(jnp.float32),
        lax.psum(grad_kernel.astype(jnp.bfloat16), "dp").astype(jnp.float32),
        lax.psum(grad_kernel_bias.astype(jnp.bfloat16), "dp").astype(jnp.float32),
        lax.psum(grad_proj_w.astype(jnp.bfloat16), "dp").astype(jnp.float32),
        lax.psum(grad_step_w.astype(jnp.bfloat16), "dp").astype(jnp.float32),
        lax.psum(grad_step_bias.astype(jnp.bfloat16), "dp").astype(jnp.float32),
        lax.psum(grad_rate.astype(jnp.bfloat16), "dp").astype(jnp.float32),
        lax.psum(grad_skip.astype(jnp.bfloat16), "dp").astype(jnp.float32),
        lax.psum(grad_out.astype(jnp.bfloat16), "dp").astype(jnp.float32),
        lax.psum(grad_gate.astype(jnp.bfloat16), "dp").astype(jnp.float32),
        lax.psum(grad_up.astype(jnp.bfloat16), "dp").astype(jnp.float32),
        lax.psum(grad_down.astype(jnp.bfloat16), "dp").astype(jnp.float32),
    )
    payload = jnp.concatenate([out_low, d_input_low], axis=1)
    tokens_all = lengths.shape[0] * group_rows
    owner = (
        jnp.zeros((tokens_all,), jnp.int32)
        .at[source.reshape(-1)]
        .set(jnp.arange(tokens_all, dtype=jnp.int32))
    )
    my_rows = lax.dynamic_slice_in_dim(
        owner, (my_group * col_devices + my_column) * rows_in, rows_in, 0
    )
    pieces = lax.all_gather(payload, ("dp", "col"), axis=0, tiled=True)
    row_count = pieces.shape[0]
    offset = my_rows
    inside = ((offset >= 0) & (offset < row_count))[:, None]
    returned = jnp.where(
        inside,
        jnp.take(pieces, jnp.clip(offset, 0, row_count - 1), axis=0),
        jnp.zeros_like(payload),
    )
    y_out = returned[:, :width_row]
    dx_out = returned[:, width_row:]
    return (
        y_out,
        dx_out,
        grad_norm_one,
        grad_in_x,
        grad_in_z,
        grad_kernel,
        grad_kernel_bias,
        grad_proj_w,
        grad_step_w,
        grad_step_bias,
        grad_rate,
        grad_skip,
        grad_out,
        grad_norm_two,
        grad_gate,
        grad_up,
        grad_down,
    )


def solution(mesh):
    placed = (
        P(("dp", "col"), "row"),
        P(),
        P(),
        P("row"),
        P("row", "col"),
        P("row", "col"),
        P(("col", "row"), None),
        P(("col", "row")),
        P(("col", "row"), None),
        P(None, ("col", "row")),
        P(("col", "row")),
        P(("col", "row"), None),
        P(("col", "row")),
        P("col", "row"),
        P("row"),
        P("row", "col"),
        P("row", "col"),
        P("col", "row"),
        P(("dp", "col"), "row"),
    )
    paired = mesh.shape["col"] == 2 and mesh.shape["dp"] == 4
    return jax.shard_map(
        on_pairs if paired else on_device,
        mesh=mesh,
        in_specs=placed,
        out_specs=(
            P(("dp", "col"), "row"),
            P(("dp", "col"), "row"),
            P("row"),
            P("row", "col"),
            P("row", "col"),
            P(("col", "row"), None),
            P(("col", "row")),
            P(("col", "row"), None),
            P(None, ("col", "row")),
            P(("col", "row")),
            P(("col", "row"), None),
            P(("col", "row")),
            P("col", "row"),
            P("row"),
            P("row", "col"),
            P("row", "col"),
            P("col", "row"),
        ),
        check_vma=False,
    )
```

```python
import functools

import jax
import jax.numpy as jnp
from jax import lax
from jax.experimental import pallas as pl
from jax.experimental.pallas import tpu as pltpu
from jax.sharding import PartitionSpec as P

epsilon = 1e-05


def layout(lengths, seq_order, group_rows):
    flat_lengths = lengths.reshape(-1)
    total_seqs = flat_lengths.shape[0]
    slot_length = jnp.take(flat_lengths, seq_order)
    input_start = jnp.cumsum(slot_length) - slot_length
    slot_of = (
        jnp.zeros((total_seqs,), jnp.int32)
        .at[seq_order]
        .set(jnp.arange(total_seqs, dtype=jnp.int32))
    )
    seq_input = jnp.take(input_start, slot_of).reshape(lengths.shape)
    group_start = jnp.cumsum(lengths, axis=1) - lengths
    places = jnp.arange(group_rows, dtype=jnp.int32)
    member = (
        jnp.sum((places[None, :, None] >= group_start[:, None, :]).astype(jnp.int32), axis=2) - 1
    )
    begin_at = jnp.take_along_axis(group_start, member, axis=1)
    within = places[None, :] - begin_at
    source = jnp.take_along_axis(seq_input, member, axis=1) + within
    return (source, within)


def silu_slope(values):
    sigmoid_v = jax.nn.sigmoid(values)
    return sigmoid_v * (1.0 + values * (1.0 - sigmoid_v))


def contract(left, right, left_dim, right_dim):
    return lax.dot_general(
        left, right, (((left_dim,), (right_dim,)), ((), ())), preferred_element_type=jnp.float32
    )


def convolve(inner_x, kernel, kernel_bias, places):
    tap_count = kernel.shape[1]
    conv_sum = kernel_bias[:, None] + inner_x * kernel[:, tap_count - 1][:, None]
    for shift_by in range(1, tap_count):
        shifted = jnp.pad(inner_x, ((0, 0), (shift_by, 0)))[:, :-shift_by]
        conv_sum = (
            conv_sum
            + shifted
            * (places >= shift_by).astype(jnp.float32)[None, :]
            * kernel[:, tap_count - 1 - shift_by][:, None]
        )
    return jax.nn.silu(conv_sum)


MESH = pl.DeviceIdType.MESH
f32 = jnp.float32
bf16 = jnp.bfloat16


def remote(src, dst, send, recv, where):
    return pltpu.make_async_remote_copy(
        src_ref=src, dst_ref=dst, send_sem=send, recv_sem=recv, device_id=where, device_id_type=MESH
    )


def away(axis, offset):
    return {axis: lax.rem(lax.axis_index(axis) + offset, lax.axis_size(axis))}


def greet(*axes):
    barrier = pltpu.get_barrier_semaphore()
    total = 0
    for axis in axes:
        for offset in range(1, lax.axis_size(axis)):
            pl.semaphore_signal(barrier, inc=1, device_id=away(axis, offset), device_id_type=MESH)
            total += 1
    return lambda: pl.semaphore_wait(barrier, total)


class Late:
    def __init__(self, names, sources, targets, sems):
        self.targets = dict(zip(names, targets))
        self.waiting = {}
        for i, (name, source, target) in enumerate(zip(names, sources, targets)):
            self.waiting[name] = pltpu.make_async_copy(source, target, sems.at[i])
            self.waiting[name].start()

    def __call__(self, name):
        if name in self.waiting:
            self.waiting.pop(name).wait()
        return self.targets[name]


class Leave:
    def __init__(self, names, sources, targets, sems):
        self.copies = {
            name: pltpu.make_async_copy(source, target, sems.at[i])
            for i, (name, source, target) in enumerate(zip(names, sources, targets))
        }

    def __call__(self, *names):
        for name in names:
            self.copies[name].start()

    def finish(self):
        for copy in self.copies.values():
            copy.wait()


def matmul(left, right):
    return jnp.dot(left, right, preferred_element_type=f32)


def silu(values):
    return values * jax.nn.sigmoid(values)


def rows_form(values):
    ones = jnp.ones((8, values.shape[1]), f32)
    return lax.dot_general(
        ones,
        values,
        (((1,), (1,)), ((), ())),
        precision=lax.Precision.HIGHEST,
        preferred_element_type=f32,
    )


def column_form(row_values):
    return jnp.transpose(row_values)[:, 0:1]


class Line:
    def __init__(self, axis, send, recv):
        self.axis, self.send, self.recv = axis, send, recv
        self.size = lax.axis_size(axis)
        self.me = lax.axis_index(axis)

    def right(self, src, dst, d):
        return remote(
            src, dst, self.send.at[0, d], self.recv.at[0, d], {self.axis: jnp.minimum(self.me + 1, self.size - 1)}
        )

    def left(self, src, dst, d):
        return remote(
            src, dst, self.send.at[1, d], self.recv.at[1, d], {self.axis: jnp.maximum(self.me - 1, 0)}
        )


def line_gather(axis, slot_of, send, recv):
    line = Line(axis, send, recv)
    size, me = line.size, line.me
    last = size - 1

    def go_right(s):
        slot = jnp.maximum(me - s, 0)
        return (me - s >= 0) & (me < last), line.right(slot_of(slot), slot_of(slot), slot)

    def go_left(s):
        slot = jnp.minimum(me + s, last)
        return (me + s <= last) & (me > 0), line.left(slot_of(slot), slot_of(slot), slot)

    for s in range(last):
        for valid, copy in (go_right(s), go_left(s)):
            pl.when(valid)(copy.start)
        yield
        slot = jnp.maximum(me - 1 - s, 0)
        pl.when(me - 1 - s >= 0)(line.right(slot_of(slot), slot_of(slot), slot).wait_recv)
        slot = jnp.minimum(me + 1 + s, last)
        pl.when(me + 1 + s <= last)(line.left(slot_of(slot), slot_of(slot), slot).wait_recv)
    yield
    for s in range(last):
        for valid, copy in (go_right(s), go_left(s)):
            pl.when(valid)(copy.wait_send)


def line_scatter(axis, block_of, out, held, from_left, from_right, send, recv, slots=False):
    line = Line(axis, send, recv)
    size, me = line.size, line.me
    last = size - 1

    def right_at(t):
        d = jnp.clip(last - t + me, 0, last)
        return (t >= me) & (me < last), d, line.right(held.at[d], from_left.at[d], d)

    def left_at(t):
        d = jnp.clip(t - (last - me), 0, last)
        return (t >= last - me) & (me > 0), d, line.left(held.at[d], from_right.at[d], d)

    def made(d, slot):
        return block_of(d, slot) if slots else block_of(d)

    def pass_on(valid, first, d, copy, arrived, slot):
        @pl.when(valid)
        def _():
            part = made(d, slot)

            @pl.when(jnp.logical_not(first))
            def _():
                copy.wait_recv()
                held[d] = (part + arrived[d].astype(f32)).astype(held.dtype)

            @pl.when(first)
            def _():
                held[d] = part.astype(held.dtype)

            copy.start()

    for t in range(last):
        valid, d, copy = right_at(t)
        pass_on(valid, me == 0, d, copy, from_left, 0)
        valid, d, copy = left_at(t)
        pass_on(valid, me == last, d, copy, from_right, 1)
        if t == 0:
            out[...] = made(me, 2)
        yield
    yield

    @pl.when(me > 0)
    def _():
        line.right(held.at[me], from_left.at[me], me).wait_recv()
        out[...] += from_left[me].astype(f32)

    @pl.when(me < last)
    def _():
        line.left(held.at[me], from_right.at[me], me).wait_recv()
        out[...] += from_right[me].astype(f32)

    for t in range(last):
        for valid, _, copy in (right_at(t), left_at(t)):
            pl.when(valid)(copy.wait_send)


def halves(rows):
    return [pl.ds(0, rows // 2), pl.ds(rows // 2, rows // 2)]


def gather_halves(axis, ref, size, send, recv):
    flows = []
    for h, at in enumerate(halves(ref.shape[0])):

        def slot_of(d, at=at):
            return ref.at[at, pl.ds(pl.multiple_of(d * size, size), size)]

        flows.append(line_gather(axis, slot_of, send.at[h], recv.at[h]))
    return flows


def scatter_halves(axis, block_of, out, held, from_left, from_right, send, recv):
    flows = []
    for h, at in enumerate(halves(out.shape[0])):
        flows.append(
            line_scatter(
                axis,
                functools.partial(block_of, at=at),
                out.at[at, :],
                held.at[:, at, :],
                from_left.at[:, at, :],
                from_right.at[:, at, :],
                send.at[h],
                recv.at[h],
            )
        )
    return flows


def run(*flows, pump=None):
    flows = list(flows)
    turn = 0
    while flows:
        flows = [flow for flow in flows if next(flow, flows) is not flows]
        if pump is not None and turn < len(pump[1]):
            pump[0].pump(pump[1][turn])
        turn += 1


def lanes(ref, size):
    return lambda d: ref.at[:, pl.ds(pl.multiple_of(d * size, size), size)]


def fetch(sources, targets, sems):
    copies = [pltpu.make_async_copy(s, t, sems.at[i]) for i, (s, t) in enumerate(zip(sources, targets))]
    for copy in copies:
        copy.start()
    return copies


def as_row(ref):
    return ref[...].reshape(1, ref.shape[0])


def lengths_row(lens):
    groups, per_group = lens.shape
    values = lens[...].astype(f32)
    at = lax.broadcasted_iota(jnp.int32, (per_group, groups * per_group), 1)
    inner = lax.broadcasted_iota(jnp.int32, (per_group, groups * per_group), 0)
    total = jnp.zeros((1, groups * per_group), f32)
    for g in range(groups):
        place = jnp.where(at == inner + g * per_group, 1.0, 0.0)
        total = total + jnp.dot(
            values[g : g + 1, :], place, precision=lax.Precision.HIGHEST, preferred_element_type=f32
        )
    return total


def spray(axis, src_of, dst, send, recv, base=0):
    copies = []
    for k in range(1, lax.axis_size(axis)):
        copy = remote(src_of(k), dst.at[k - 1], send.at[base + k - 1], recv.at[base + k - 1], away(axis, k))
        copy.start()
        copies.append(copy)
    return copies


def wait_all(copies):
    for copy in copies:
        copy.wait()


def swap(axis, src, dst, send, recv):
    copy = remote(src, dst, send, recv, away(axis, 1))
    copy.start()
    return copy


def sequence_rows(lens_row, order_row, per_group):
    count = lens_row.shape[1]
    ri = lax.broadcasted_iota(jnp.int32, (count, count), 0)
    ci = lax.broadcasted_iota(jnp.int32, (count, count), 1)
    lens_f = lens_row

    def to_column(row):
        return jnp.sum(jnp.where(ri == ci, row, 0.0), axis=1, keepdims=True)

    order_col = to_column(order_row.astype(f32)).astype(jnp.int32)
    lens_col = to_column(lens_f)
    pick = order_row == ri
    pick_t = order_col == ci
    slot_col = jnp.sum(jnp.where(pick_t, lens_f, 0.0), axis=1, keepdims=True)
    slot_row = jnp.sum(jnp.where(pick, lens_col, 0.0), axis=0, keepdims=True)
    start_col = jnp.sum(jnp.where(ci < ri, slot_row, 0.0), axis=1, keepdims=True)
    input_row = jnp.sum(jnp.where(pick_t, start_col, 0.0), axis=0, keepdims=True)
    same = (ri // per_group) == (ci // per_group)
    group_row = jnp.sum(jnp.where((ri < ci) & same, lens_col, 0.0), axis=0, keepdims=True)
    return lens_f, input_row, group_row


def place_rows(lens_row, order_row, per_group, group_rows, group):
    lens_f, input_row, group_row = sequence_rows(lens_row, order_row, per_group)
    count = lens_row.shape[1]
    rows = lax.broadcasted_iota(jnp.int32, (group_rows, count), 0).astype(f32)
    mine = (lax.broadcasted_iota(jnp.int32, (group_rows, count), 1) // per_group) == group
    inside = (rows >= group_row) & (rows < group_row + lens_f) & mine
    within = jnp.sum(jnp.where(inside, rows - group_row, 0.0), axis=1, keepdims=True)
    begin = jnp.sum(jnp.where(inside, input_row, 0.0), axis=1, keepdims=True)
    return begin + within, within


def owner_rows(lens_row, order_row, per_group, group_rows, block_rows, first):
    lens_f, input_row, group_row = sequence_rows(lens_row, order_row, per_group)
    count = lens_row.shape[1]
    rows = (lax.broadcasted_iota(jnp.int32, (block_rows, count), 0) + first).astype(f32)
    base = (lax.broadcasted_iota(jnp.int32, (block_rows, count), 1) // per_group) * group_rows
    inside = (rows >= input_row) & (rows < input_row + lens_f)
    found = jnp.where(inside, base.astype(f32) + group_row + rows - input_row, 0.0)
    return jnp.sum(found, axis=1, keepdims=True)


def plane_origin(rows, dp_size, col_size, block_rows):
    at = lax.broadcasted_iota(jnp.int32, (rows, dp_size * col_size * block_rows), 1)
    block = at // block_rows
    group = lax.rem(block, dp_size)
    column = block // dp_size
    return ((group * col_size + column) * block_rows + lax.rem(at, block_rows)).astype(f32)


def pick_rows(wanted, held):
    col_size, dp_size, block_rows, width = held.shape
    total = col_size * dp_size * block_rows
    chosen = wanted == plane_origin(wanted.shape[0], dp_size, col_size, block_rows)
    chosen = jnp.where(chosen, 1.0, 0.0).astype(bf16)
    return matmul(chosen, held.reshape(total, width)).astype(bf16)


def plane_start(src, held, send, recv):
    me, column = lax.axis_index("dp"), lax.axis_index("col")
    held[column, me] = src[...]
    copies = []
    for k in range(1, lax.axis_size("dp")):
        copy = remote(src, held.at[column, me], send.at[k], recv.at[k], away("dp", k))
        copy.start()
        copies.append(copy)
    return copies


def plane_swap(copies, held, send, recv):
    column = lax.axis_index("col")
    for copy in copies:
        copy.wait_recv()
    return swap("col", held.at[column], held.at[column], send.at[0], recv.at[0])


def plane_wait(copies, last):
    last.wait_recv()
    for copy in [*copies, last]:
        copy.wait_send()


def plane_finish(copies, held, send, recv):
    plane_wait(copies, plane_swap(copies, held, send, recv))


def total_of_sums(part, half_own, half_in, low_own, low_in, full, sems):
    send, recv = sems
    rows = part.shape[0] // 2
    column = lax.axis_index("col")
    mine = pl.ds(pl.multiple_of(column * rows, rows), rows)
    other = pl.ds(pl.multiple_of((1 - column) * rows, rows), rows)
    half_own[...] = part[other, :]
    copy = swap("col", half_own, half_in, send.at[0], recv.at[0])
    yield
    copy.wait()
    low_own[...] = (part[mine, :] + half_in[...]).astype(bf16)
    copies = spray("row", lambda k: low_own, low_in, send, recv, 1)
    yield
    wait_all(copies)
    total = low_own[...].astype(f32)
    for k in range(low_in.shape[0]):
        total = total + low_in[k].astype(f32)
    full[mine, :] = total
    copy = swap("col", full.at[mine], full.at[mine], send.at[4], recv.at[4])
    yield
    copy.wait()


def lanes_like(tile, width):
    if tile.shape[-1] == width:
        return tile
    return jnp.concatenate([tile] * (width // tile.shape[-1]), axis=-1)


def lane_mask(count, lanes, first):
    lane = lax.broadcasted_iota(jnp.int32, (count, lanes), 1)
    return lane == lax.broadcasted_iota(jnp.int32, (count, lanes), 0) + first


def spread(values, first, count, wide):
    rows, lanes = values.shape
    chosen = jnp.where(lane_mask(count, lanes, first)[None], values[:, None, :], 0.0)
    chosen = chosen.reshape(rows * count, lanes)
    high = chosen.astype(bf16)
    rest = (chosen - high.astype(f32)).astype(bf16)
    ones = jnp.ones((lanes, wide), bf16)
    return matmul(high, ones) + matmul(rest, ones)


def lane_sums(values, first, lanes):
    rows, count, wide = values.shape
    flat = values.reshape(rows * count, wide)
    high = flat.astype(bf16)
    rest = (flat - high.astype(f32)).astype(bf16)
    ones = jnp.ones((wide, lanes), bf16)
    sums = (matmul(high, ones) + matmul(rest, ones)).reshape(rows, count, lanes)
    return jnp.sum(jnp.where(lane_mask(count, lanes, first)[None], sums, 0.0), axis=1)


def scan_forward(proj, b_at, c_at, gone_step, drive, rate, bb, cb, y):
    rows, width = drive.shape
    count = rate.shape[0]
    piece, _, wide = bb.shape
    state = jnp.zeros((count, width), f32)
    for start in range(0, rows, piece):
        values = proj[start : start + piece, :]
        bb[...] = spread(values, b_at, count, wide).reshape(bb.shape)
        cb[...] = spread(values, c_at, count, wide).reshape(cb.shape)

        def eight(k, state):
            inner = pl.multiple_of(k * 8, 8)
            base = pl.multiple_of(start + k * 8, 8)
            gone = gone_step[pl.ds(base, 8), :]
            driven = drive[pl.ds(base, 8), :]
            found = []
            for i in range(8):
                decay = jnp.exp(gone[i : i + 1, :] * rate)
                state = decay * state + driven[i : i + 1, :] * lanes_like(bb[inner + i], width)
                found.append(jnp.sum(state * lanes_like(cb[inner + i], width), axis=0, keepdims=True))
            y[pl.ds(base, 8), :] = jnp.concatenate(found, axis=0)
            return state

        state = lax.fori_loop(0, piece // 8, eight, state)
        yield


def scan_states(proj, b_at, gone_step, drive, rate, bb, hs):
    rows, width = drive.shape
    count = rate.shape[0]
    piece, _, wide = bb.shape
    hs[0] = jnp.zeros((count, width), f32)
    for start in range(0, rows, piece):
        bb[...] = spread(proj[start : start + piece, :], b_at, count, wide).reshape(bb.shape)

        def eight(k, state):
            inner = pl.multiple_of(k * 8, 8)
            base = pl.multiple_of(start + k * 8, 8)
            gone = gone_step[pl.ds(base, 8), :]
            driven = drive[pl.ds(base, 8), :]
            for i in range(8):
                decay = jnp.exp(gone[i : i + 1, :] * rate)
                state = decay * state + driven[i : i + 1, :] * lanes_like(bb[inner + i], width)
                hs[base + i + 1] = state
            return state

        lax.fori_loop(0, piece // 8, eight, hs[start])
        yield


def scan_backward(
    proj, b_at, c_at, step, gone_step, drive, inner_u, dy, rate, hs, bb, cb, pb, pc, du, dstep, dproj
):
    rows, width = drive.shape
    count = rate.shape[0]
    piece, _, wide = bb.shape

    def fold(values):
        total = values[:, 0:wide]
        for j in range(1, width // wide):
            total = total + values[:, j * wide : (j + 1) * wide]
        return total

    def part(start, carry):
        values = proj[start : start + piece, :]
        bb[...] = spread(values, b_at, count, wide).reshape(bb.shape)
        cb[...] = spread(values, c_at, count, wide).reshape(cb.shape)

        def eight(k, carry):
            later, total = carry
            inner = pl.multiple_of((piece // 8 - 1 - k) * 8, 8)
            base = pl.multiple_of(start + inner, 8)
            step8 = step[pl.ds(base, 8), :]
            gone8 = gone_step[pl.ds(base, 8), :]
            drive8 = drive[pl.ds(base, 8), :]
            u8 = inner_u[pl.ds(base, 8), :]
            dy8 = dy[pl.ds(base, 8), :]
            by_b = [None] * 8
            by_rate = [None] * 8
            for i in reversed(range(8)):
                dy_row = dy8[i : i + 1, :]
                lam = lanes_like(cb[inner + i], width) * dy_row + later
                later = jnp.exp(gone8[i : i + 1, :] * rate) * lam
                kept = later * hs[base + i]
                total = total + kept * step8[i : i + 1, :]
                by_b[i] = jnp.sum(lam * lanes_like(bb[inner + i], width), axis=0, keepdims=True)
                by_rate[i] = jnp.sum(kept * rate, axis=0, keepdims=True)
                pb[inner + i] = fold(lam * drive8[i : i + 1, :])
                pc[inner + i] = fold(hs[base + i + 1] * dy_row)
            by_b = jnp.concatenate(by_b, axis=0)
            by_rate = jnp.concatenate(by_rate, axis=0)
            du[pl.ds(base, 8), :] = by_b * step8
            dstep[pl.ds(base, 8), :] = by_rate + by_b * u8
            return later, total

        carry = lax.fori_loop(0, piece // 8, eight, carry)
        dproj[start : start + piece, :] += lane_sums(pb[...], b_at, dproj.shape[1]) + lane_sums(
            pc[...], c_at, dproj.shape[1]
        )
        return carry

    blank = jnp.zeros((count, width), f32)
    carry = (blank, blank)
    for start in reversed(range(0, rows, piece)):
        carry = part(start, carry)
        yield
    return carry[1] * rate


RANK_LANES = 128


def scan_kernel(proj, gone, drive, rate, y, bb, cb, *, b_at, c_at):
    run(scan_forward(proj, b_at, c_at, gone, drive, rate[...], bb, cb, y))


def adjoint_kernel(
    proj, step, gone, drive, inner_u, dy, rate, du, dstep, dproj, drate, bb, cb, hs, pb, pc, *, b_at, c_at
):
    run(scan_states(proj, b_at, gone, drive, rate[...], bb, hs))
    dproj[...] = jnp.zeros_like(dproj)
    kept = {}

    def adjoint():
        kept["rate"] = yield from scan_backward(
            proj, b_at, c_at, step, gone, drive, inner_u, dy, rate[...], hs, bb, cb, pb, pc, du, dstep, dproj
        )

    run(adjoint())
    drate[...] = kept["rate"]


def scan_sizes(rows, width, count):
    wide = 128 if width % 128 == 0 else width
    piece = min(128, rows)
    return pltpu.VMEM((piece, count, wide), f32)


def scan_alone(proj, gone, drive, rate, b_at, c_at):
    rows, width = drive.shape
    block = scan_sizes(rows, width, rate.shape[0])
    return pl.pallas_call(
        functools.partial(scan_kernel, b_at=b_at, c_at=c_at),
        out_shape=jax.ShapeDtypeStruct((rows, width), f32),
        scratch_shapes=[block, block],
        compiler_params=pltpu.CompilerParams(vmem_limit_bytes=VMEM_BYTES),
        name="scan_states",
    )(proj, gone, drive, rate)


def adjoint_alone(proj, step, gone, drive, inner_u, dy, rate, b_at, c_at):
    rows, width = step.shape
    count = rate.shape[0]
    block = scan_sizes(rows, width, count)
    shape = jax.ShapeDtypeStruct
    return pl.pallas_call(
        functools.partial(adjoint_kernel, b_at=b_at, c_at=c_at),
        out_shape=(
            shape((rows, width), f32),
            shape((rows, width), f32),
            shape(proj.shape, f32),
            shape((count, width), f32),
        ),
        scratch_shapes=[
            block,
            block,
            pltpu.VMEM((rows + 1, count, width), f32),
            block,
            block,
        ],
        compiler_params=pltpu.CompilerParams(vmem_limit_bytes=VMEM_BYTES),
        name="scan_adjoint",
    )(proj, step, gone, drive, inner_u, dy, rate)


PUMPS = ((0, 1, 1), (1, 0, 1), 0, (1, 2, 1), (1, 1), (0, 0, 0), (2, 2, 1), 0, 2)


def conv_sum(inner_x, place, taps, bias):
    count = taps.shape[0]
    total = bias + inner_x * taps[count - 1 : count, :]
    for shift in range(1, count):
        moved = jnp.where(place >= shift, pltpu.roll(inner_x, shift, 0), 0.0)
        total = total + moved * taps[count - 1 - shift : count - shift, :]
    return total


def transposed(left, right):
    return lax.dot_general(left, right, (((1,), (1,)), ((), ())), preferred_element_type=f32)


def over_rows(left, right):
    return lax.dot_general(left, right, (((0,), (0,)), ((), ())), preferred_element_type=f32)


def columns(d, size):
    return pl.ds(pl.multiple_of(d * size, size), size)


def line_total(own, arrived):
    total = own
    for k in range(arrived.shape[0]):
        total = total + arrived[k]
    return total


def forward_kernel(
    x, cot, lens, order, gain1, taps, bias, w_xp, w_dt, dt_bias, a_log, skip, gain2,
    w_x_h, w_z_h, w_out_h, w_gate_h, w_up_h, w_down_h,
    xg_o, cg_o, n1_o, s1_o, place_o, xi_o, z_o, proj_o, yv_o, go_all, h1_o, s2_o, n2_o, hid_all, dgu_o, dot_o, n1_mates, n2_mates, cg_mates, go_mates, hid_mates,
    w_x, w_z, w_out, w_gate, w_up, w_down, w_step, rate,
    x_all, c_all, sum_own, sum_in, low, xi_held, xi_left, xi_right, z_held, z_left, z_right,
    part_s, half_own, half_in, low_own, low_in, bb, cb, step, gone, drive,
    own, other, gu, gu_part, gu_held, gu_left, gu_right, dhid, h_held, h_left, h_right,
    w_sems, x_send, x_recv, c_send, c_recv, sum_send, sum_recv, xi_send, xi_recv, z_send, z_recv, t_send, t_recv,
    go_send, go_recv, o_send, o_recv, sum2_send, sum2_recv, gu_send, gu_recv, h_send, h_recv, hid_send, hid_recv, m_send, m_recv,
    *, model_width, rank, count, leave
):
    rows, width = xi_o.shape
    hidden = dgu_o.shape[1] // 2
    group, row = lax.axis_index("dp"), lax.axis_index("row")
    row_size = lax.axis_size("row")
    weights = fetch(
        (w_x_h, w_z_h, w_out_h, w_gate_h, w_up_h, w_down_h), (w_x, w_z, w_out, w_gate, w_up, w_down), w_sems
    )
    met = greet("dp", "row", "col")
    w_step[...] = jnp.zeros_like(w_step)
    w_step[0:rank, :] = w_dt[...]
    met()
    x_copies = plane_start(x, x_all, x_send, x_recv)
    lens_row = lengths_row(lens)
    source, place = place_rows(lens_row, as_row(order), lens.shape[1], rows, group)
    place_o[...] = place
    plane_finish(x_copies, x_all, x_send, x_recv)
    c_copies = plane_start(cot, c_all, c_send, c_recv)
    xg_low = pick_rows(source, x_all[...])
    xg_o[...] = xg_low
    xg = xg_low.astype(f32)
    gain1_now = as_row(gain1)
    low[...] = (xg * gain1_now).astype(bf16)
    weights[0].wait()
    kept = {}

    def during_xi():
        sum_own[...] = rows_form(xg * xg)
        sum_copies = spray("row", lambda k: sum_own, sum_in, sum_send, sum_recv)
        rate[...] = -jnp.exp(a_log[...])
        yield
        wait_all(sum_copies)
        kept["s1"] = column_form(lax.rsqrt(line_total(sum_own[...], sum_in) / model_width + epsilon))
        s1_o[...] = kept["s1"]
        leave("xg", "s1", "place")
        kept["cot"] = plane_swap(c_copies, c_all, c_send, c_recv)

    run(
        *scatter_halves(
            "row", lambda d, at: matmul(low[at, :], w_x[:, columns(d, width)]), xi_o, xi_held, xi_left, xi_right,
            xi_send, xi_recv,
        ),
        during_xi(),
    )
    weights[1].wait()
    z_flows = scatter_halves(
        "row", lambda d, at: matmul(low[at, :], w_z[:, columns(d, width)]), z_o, z_held, z_left, z_right, z_send, z_recv
    )
    for flow in z_flows:
        next(flow)
    s1 = kept["s1"]
    inner_x = xi_o[...] * s1
    xi_o[...] = inner_x
    u_low = silu(conv_sum(inner_x, place, taps[...], as_row(bias))).astype(bf16)
    u = u_low.astype(f32)
    part_s[...] = matmul(u_low, w_xp[...])

    def mix():
        yield from total_of_sums(part_s, half_own, half_in, low_own, low_in, proj_o, (t_send, t_recv))
        pre = matmul(proj_o[...].astype(bf16), w_step[...]) + as_row(dt_bias)
        step_now = jax.nn.softplus(pre)
        step[...] = step_now
        gone[...] = jnp.where(place > 0.0, step_now, 1e30)
        drive[...] = step_now * u
        yield from scan_forward(proj_o, rank, rank + count, gone, drive, rate[...], bb, cb, yv_o)

    mixing = mix()
    next(mixing)
    plane_wait(c_copies, kept["cot"])
    cg_o[...] = pick_rows(source, c_all[...])
    kept["mates"] = to_mates(cg_o, cg_mates, m_send.at[1], m_recv.at[1])
    next(mixing)
    run(*z_flows, mixing)
    yv = yv_o[...] + as_row(skip) * u
    yv_o[...] = yv
    z = z_o[...] * s1
    z_o[...] = z
    go_all[:, columns(row, width)] = (yv * silu(z)).astype(bf16)

    def during_gather():
        n1_o[...] = (xg * s1 * gain1_now).astype(bf16)
        kept["mates"] += to_mates(n1_o, n1_mates, m_send.at[0], m_recv.at[0])
        yield

    weights[5].wait()
    run(
        *gather_halves("row", go_all, width, go_send, go_recv),
        *scatter_halves(
            "row", lambda d, at: transposed(cg_o[at, :], w_down[columns(d, hidden), :]), dhid, h_held, h_left, h_right,
            h_send, h_recv,
        ),
        during_gather(),
    )
    kept["mates"] += quarters_to_mates(go_all, go_mates, m_send.at[3], m_recv.at[3])
    weights[2].wait()
    own[...] = matmul(go_all[...], w_out[...])
    copy = swap("col", own, other, o_send.at[0], o_recv.at[0])
    weights[3].wait()
    weights[4].wait()
    copy.wait()
    h1 = xg + (own[...] + other[...])
    h1_o[...] = h1
    gain2_now = as_row(gain2)
    low[...] = (h1 * gain2_now).astype(bf16)

    def gate_up_flows(first):
        rows_now, size = rows // 2, rows // 4

        def block_of(d, slot, part):
            side = columns(d, hidden)
            if part == 0:
                left = low[first : first + rows_now, :]
                gu_part[slot, :, 0:hidden] = matmul(left, w_gate[:, side])
                gu_part[slot, :, hidden:] = matmul(left, w_up[:, side])
            return gu_part[slot, part * size : (part + 1) * size, :]

        flows = []
        for part in range(2):
            at = pl.ds(first + part * size, size)
            number = first // size + part
            flows.append(
                line_scatter(
                    "row", functools.partial(block_of, part=part), gu.at[at, :], gu_held.at[:, at, :],
                    gu_left.at[:, at, :], gu_right.at[:, at, :], gu_send.at[number], gu_recv.at[number], slots=True,
                )
            )
        return flows

    def hid_flows(first, count):
        size = rows // 2 // count
        flows = []
        for part in range(count):
            at = pl.ds(first + part * size, size)

            def slot_of(d, at=at):
                return hid_all.at[at, columns(d, hidden)]

            number = first // (rows // 4) + part
            flows.append(line_gather("row", slot_of, hid_send.at[number], hid_recv.at[number]))
        return flows

    def activate(first):
        at = slice(first, first + rows // 2)
        s2 = s2_o[at, :]
        gate, up = gu[at, 0:hidden] * s2, gu[at, hidden:] * s2
        gu[at, 0:hidden], gu[at, hidden:] = gate, up
        sig = jax.nn.sigmoid(gate)
        act = gate * sig
        hid_all[at, columns(row, hidden)] = (act * up).astype(bf16)
        d_hid = dhid[at, :]
        dgu_o[at, 0:hidden] = (d_hid * up * (sig * (1.0 + gate * (1.0 - sig)))).astype(bf16)
        dgu_o[at, hidden:] = (d_hid * act).astype(bf16)

    def during_scatter():
        sum_own[...] = rows_form(h1 * h1)
        sum_copies = spray("row", lambda k: sum_own, sum_in, sum2_send, sum2_recv)
        yield
        wait_all(sum_copies)
        s2 = column_form(lax.rsqrt(line_total(sum_own[...], sum_in) / model_width + epsilon))
        s2_o[...] = s2
        n2_o[...] = (h1 * s2 * gain2_now).astype(bf16)
        leave("n1", "cg", "xi", "z", "proj", "yv", "go_all", "h1", "s2", "n2")
        kept["mates"] += to_mates(n2_o, n2_mates, m_send.at[2], m_recv.at[2])

    def dots():
        yield
        dot_o[...] = rows_form(dgu_o[...].astype(f32) * gu[...])

    run(*gate_up_flows(0), during_scatter())
    activate(0)
    run(*gate_up_flows(rows // 2), *hid_flows(0, 1))
    activate(rows // 2)
    top, bottom = pl.ds(0, rows // 2), pl.ds(rows // 2, rows // 2)
    kept["mates"] += quarters_to_mates(hid_all, hid_mates, m_send.at[4], m_recv.at[4], top)
    run(*hid_flows(rows // 2, 2), dots())
    kept["mates"] += quarters_to_mates(hid_all, hid_mates, m_send.at[5], m_recv.at[5], bottom)
    leave("hid_all", "dgu", "dot")
    wait_all(kept["mates"])
    leave("hid_mates", "n1_mates", "n2_mates", "cg_mates", "go_mates")
    leave.finish()


def dp_bits():
    me = lax.axis_index("dp")
    return lax.rem(me, 2), me // 2


def dp_mates():
    me = lax.axis_index("dp")
    along_x, along_y = dp_bits()
    return {"dp": me + 1 - 2 * along_x}, {"dp": me + 2 - 4 * along_y}


def to_mates(src, dst, send, recv):
    copies = [remote(src, dst.at[h], send.at[h], recv.at[h], mate) for h, mate in enumerate(dp_mates())]
    for copy in copies:
        copy.start()
    return copies


def quarters_to_mates(ref, dst, send, recv, rows=None):
    size = ref.shape[1] // 4
    at = pl.ds(0, ref.shape[0]) if rows is None else rows
    copies = []
    for h, (near, mate) in enumerate(zip(dp_bits(), dp_mates())):
        side = pl.ds(pl.multiple_of((2 * h + 1 - near) * size, size), size)
        copies.append(remote(ref.at[at, side], dst.at[h, at, :], send.at[h], recv.at[h], mate))
        copies[-1].start()
    return copies


def pair_sum(grad, sent, fixed, fixed_mates, by_rows, sent_in, second_in, third_in, send, recv, swapped="sent"):
    quarter = sent.shape[1] // 4
    eighth = (quarter if by_rows else grad.shape[0]) // 2
    bits, mates = dp_bits(), dp_mates()

    def side(h, near):
        return pl.ds(pl.multiple_of((2 * h + near) * quarter, quarter), quarter)

    def view(h, near, far):
        if by_rows:
            return grad.at[pl.ds(pl.multiple_of((2 * h + near) * quarter + far * eighth, eighth), eighth), :]
        return grad.at[pl.ds(pl.multiple_of(far * eighth, eighth), eighth), side(h, near)]

    class Half:
        def __init__(self, h):
            near, far = bits[h], bits[1 - h]
            mate, other = mates[h], mates[1 - h]

            def copy(stage, src, dst, to):
                return remote(src, dst, send.at[stage, h], recv.at[stage, h], to)

            self.h, self.near = h, near
            self.own, self.rest = view(h, near, far), view(h, near, 1 - far)
            there = view(h, 1 - near, far), view(h, 1 - near, 1 - far)
            first = None
            if swapped == "fixed":
                first = copy(0, fixed, fixed_mates.at[h], mate)
            elif swapped == "sent":
                first = copy(0, sent.at[:, side(h, 1 - near)], sent_in.at[h], mate)
            self.out = (
                first,
                copy(1, self.rest, second_in.at[h], other),
                copy(2, self.own, third_in.at[h], other),
                copy(3, self.own, self.own, mate),
                copy(4, self.rest, self.rest, mate),
            )
            self.back = (copy(3, there[0], there[0], mate), copy(4, there[1], there[1], mate))

        def product(self):
            mine, mates_part = sent[:, side(self.h, self.near)], sent_in[self.h]
            if by_rows:
                found = over_rows(mine, fixed[...]) + over_rows(mates_part, fixed_mates[self.h])
                grad[side(self.h, self.near), :] = found.astype(bf16)
            else:
                found = over_rows(fixed[...], mine) + over_rows(fixed_mates[self.h], mates_part)
                grad[:, side(self.h, self.near)] = found.astype(bf16)

    both_halves = (Half(0), Half(1))
    if swapped:
        for half in both_halves:
            half.out[0].start()
        yield
    for half in both_halves:
        if swapped:
            half.out[0].wait_recv()
        half.product()
        half.out[1].start()
    yield
    for half in both_halves:
        half.out[1].wait_recv()
        add_view(half.own, second_in.at[half.h], eighth)
        half.out[2].start()
        half.out[3].start()
    yield
    for half in both_halves:
        half.out[2].wait_recv()
        half.out[1].wait_send()
        half.rest[...] = third_in[half.h]
        half.out[4].start()
    yield
    for half in both_halves:
        for copy in half.back:
            copy.wait_recv()
        for stage in (0, 2, 3, 4) if swapped else (2, 3, 4):
            half.out[stage].wait_send()


def add_view(target, source, rows):
    def piece(j, _):
        at = pl.ds(pl.multiple_of(j * 16, 16), 16)
        target[at, :] = (target[at, :].astype(f32) + source[at, :].astype(f32)).astype(bf16)
        return 0

    lax.fori_loop(0, rows // 16, piece, 0)


def add_rows(target, base, source, rows):
    def piece(j, _):
        at = pl.ds(pl.multiple_of(base + j * 16, 16), 16)
        found = target[at, :].astype(f32) + source[pl.ds(pl.multiple_of(j * 16, 16), 16), :].astype(f32)
        target[at, :] = found.astype(target.dtype)
        return 0

    lax.fori_loop(0, rows // 16, piece, 0)


def plane_sum(grad, first_in, second_in, send, recv, free):
    quarter = grad.shape[0] // 4
    eighth = quarter // 2
    bits, partners = dp_bits(), dp_mates()

    def rows(ref, start, count):
        return ref.at[pl.ds(pl.multiple_of(start, 16), count), :]

    class Half:
        def __init__(self, h):
            near, far = bits[h], bits[1 - h]
            self.free, self.mate, self.first = free.at[h], partners[h], first_in.at[h]
            base = h * 2 * quarter
            self.kept = base + near * quarter
            self.own = self.kept + far * eighth
            self.rest = self.kept + (1 - far) * eighth
            self.rest_in = (1 - far) * eighth
            across = base + (1 - near) * quarter
            self.second = second_in.at[h]

            def copy(stage, src, dst, to):
                return remote(src, dst, send.at[stage, h], recv.at[stage, h], to)

            mate, other = partners[h], partners[1 - h]
            own, rest = rows(grad, self.own, eighth), rows(grad, self.rest, eighth)
            there = (rows(grad, across + far * eighth, eighth), rows(grad, across + (1 - far) * eighth, eighth))
            back = rows(self.first, self.rest_in, eighth)
            self.out = (
                copy(0, rows(grad, across, quarter), self.first, mate),
                copy(1, rest, self.second, other),
                copy(2, own, rows(self.first, far * eighth, eighth), other),
                copy(3, own, own, mate),
                copy(4, rest, rest, mate),
            )
            self.back = (
                None,
                None,
                copy(2, back, back, other),
                copy(3, there[0], there[0], mate),
                copy(4, there[1], there[1], mate),
            )

    halves = (Half(0), Half(1))
    for half in halves:
        half.out[0].start()
    yield
    for half in halves:
        half.out[0].wait_recv()
        add_rows(grad, half.kept, half.first, quarter)
        half.out[1].start()
        half.out[0].wait_send()
        pl.semaphore_signal(half.free, inc=1, device_id=half.mate, device_id_type=MESH)
    yield
    for half in halves:
        half.out[1].wait_recv()
        add_rows(grad, half.own, half.second, eighth)
        half.out[2].start()
        pl.semaphore_wait(half.free, 1)
        half.out[3].start()
    yield
    for half in halves:
        half.back[2].wait_recv()
        half.out[1].wait_send()
        grad[pl.ds(pl.multiple_of(half.rest, 16), eighth), :] = half.first[
            pl.ds(pl.multiple_of(half.rest_in, 16), eighth), :
        ]
        half.out[4].start()
    yield
    for half in halves:
        half.back[3].wait_recv()
        half.back[4].wait_recv()
        for copy in half.out[2:]:
            copy.wait_send()


class Sums:
    def __init__(self):
        self.active = []

    def add(self, flow):
        next(flow)
        self.active.append(flow)

    def pump(self, count=1):
        for _ in range(count):
            if self.active:
                flow = self.active.pop(0)
                if next(flow, self) is not self:
                    self.active.append(flow)

    def drain(self):
        while self.active:
            self.pump()


def backward_kernel(
    lens, order, gain2, taps, bias, w_xp, w_dt, dt_bias, a_log, skip, gain1,
    w_gate_h, w_up_h, w_down_h, w_out_h, w_x_h, w_z_h,
    y_o, dx_o, small_o, g_down_o, g_gate_o, g_up_o, g_z_o, g_x_o, g_out_o,
    w_gate, w_up, w_down, w_out, w_x, w_z, w_step, rate,
    dg_all, du_all, dz_all, dxi_all, dh1, dmix, y_own, dx_own, y_all, dx_all,
    own, other, y_part, y_other, dot_in, dot_own, dot_sum, dot_other,
    dgo, d_held, d_left, d_right,
    hs, bb, cb, pb, pc, step, gone, drive, u_s, dy_s, du_s, dstep, dproj,
    half_own, half_in, low_own, low_in, full,
    g_down, g_gate, g_up, g_z, g_x, g_out, small,
    g_gate_1, g_up_1, g_z_1, g_x_1, small_1,
    g_down_2, g_gate_2, g_up_2, g_z_2, g_x_2, g_out_2, small_2,
    g_down_3, g_gate_3, g_up_3, g_z_3, g_x_3, g_out_3, dmix_mates,
    w_sems, g_send, g_recv, u_send, u_recv, o_send, o_recv, dot_send, dot_recv,
    y_send, y_recv, dx_send, dx_recv, d_send, d_recv, z_send, z_recv, t_send, t_recv, x_send, x_recv,
    dot2_send, dot2_recv, sum_send, sum_recv, sum_free, write_sems,
    *, rank, model_width, late
):
    rows, width = dgo.shape
    count = rate.shape[0]
    block = y_o.shape[0]
    tap_count = taps.shape[0]
    group, row, column = lax.axis_index("dp"), lax.axis_index("row"), lax.axis_index("col")
    row_size, col_size = lax.axis_size("row"), lax.axis_size("col")
    weights = fetch(
        (w_down_h, w_gate_h, w_up_h, w_out_h, w_x_h, w_z_h), (w_down, w_gate, w_up, w_out, w_x, w_z), w_sems
    )
    half = columns(column, block)
    sums = Sums()
    writes = []

    def write(number, grad, result):
        copy = pltpu.make_async_copy(grad, result, write_sems.at[number])
        copy.start()
        writes.append(copy)

    def total(number, grad, first_in, second_in, result):
        yield from plane_sum(
            grad, first_in, second_in, sum_send.at[number], sum_recv.at[number], sum_free.at[number]
        )
        write(number, grad, result)

    def pair(number, grad, sent, fixed, fixed_mates, by_rows, ins, result, swapped="sent"):
        yield from pair_sum(
            grad, sent, fixed, fixed_mates, by_rows, *ins, sum_send.at[number], sum_recv.at[number], swapped
        )
        write(number, grad, result)

    met = greet("dp", "row", "col")
    dgu = late("dgu")
    hidden = dgu.shape[1] // 2
    dg_all[:, columns(row, hidden)] = dgu[:, 0:hidden]
    du_all[:, columns(row, hidden)] = dgu[:, hidden:]
    dot, hid_all, cg, cg_mates = late("dot"), late("hid_all"), late("cg"), late("cg_mates")
    hid_mates = late("hid_mates")
    met()
    dot_copies = spray("row", lambda k: dot, dot_in, dot_send, dot_recv)

    def first_work():
        sums.add(pair(0, g_down, hid_all, cg, cg_mates, True, (hid_mates, g_down_2, g_down_3), g_down_o, None))
        yield
        weights[0].wait()
        y_part[...] = matmul(hid_all[...], w_down[...])
        y_copy = swap("col", y_part, y_other, o_send.at[0], o_recv.at[0])
        yield
        wait_all(dot_copies)
        dot_own[...] = line_total(dot[...], dot_in)
        dot_copy = swap("col", dot_own, dot_other, o_send.at[2], o_recv.at[2])
        weights[1].wait()
        weights[2].wait()
        yield
        y_copy.wait()
        dot_copy.wait()
        y_own[...] = (late("h1")[...] + (y_part[...] + y_other[...])).astype(bf16)

    run(*gather_halves("row", dg_all, hidden, g_send, g_recv), first_work(), pump=(sums, PUMPS[0]))
    n2, n2_mates = late("n2"), late("n2_mates")
    sums.add(pair(1, g_gate, dg_all, n2, n2_mates, False, (g_gate_1, g_gate_2, g_gate_3), g_gate_o))

    def second_work():
        own[...] = transposed(dg_all[...], w_gate[...])
        yield

    run(*gather_halves("row", du_all, hidden, u_send, u_recv), second_work(), pump=(sums, PUMPS[1]))
    own[...] += transposed(du_all[...], w_up[...])
    copy = swap("col", own, other, o_send.at[1], o_recv.at[1])
    sums.add(pair(2, g_up, du_all, n2, n2_mates, False, (g_up_1, g_up_2, g_up_3), g_up_o))
    sums.pump(PUMPS[2])
    copy.wait()
    h1_now, s2_now = late("h1")[...], late("s2")[...]
    dn2 = own[...] + other[...]
    dots = column_form(dot_own[...] + dot_other[...])
    dh1_now = (
        cg[...].astype(f32)
        + s2_now * (as_row(gain2) * dn2)
        - h1_now * (s2_now * s2_now * dots / model_width)
    )
    dh1[...] = dh1_now
    dmix[...] = dh1_now.astype(bf16)
    gnorm2 = jnp.sum(dn2 * h1_now * s2_now, axis=0, keepdims=True)

    inner_x = late("xi")[...]
    place_now = late("place")[...]
    proj = late("proj")
    kept = {}

    def states():
        go_all = late("go_all")
        sums.add(
            pair(5, g_out, go_all, dmix, dmix_mates, True, (late("go_mates"), g_out_2, g_out_3), g_out_o, "fixed")
        )
        w_step[...] = jnp.zeros_like(w_step)
        w_step[0:rank, :] = w_dt[...]
        rate[...] = -jnp.exp(a_log[...])
        xc = conv_sum(inner_x, place_now, taps[...], as_row(bias))
        sig_c = jax.nn.sigmoid(xc)
        u_low = (xc * sig_c).astype(bf16)
        u = u_low.astype(f32)
        u_s[...] = u
        step_low = proj[...].astype(bf16)
        pre = matmul(step_low, w_step[...]) + as_row(dt_bias)
        step_now = jax.nn.softplus(pre)
        step[...] = step_now
        gone[...] = jnp.where(place_now > 0.0, step_now, 1e30)
        drive[...] = step_now * u
        kept.update(xc=xc, sig_c=sig_c, u_low=u_low, u=u, step_low=step_low, pre=pre)
        yield from scan_states(proj, rank, gone, drive, rate[...], bb, hs)

    weights[3].wait()
    run(
        *scatter_halves(
            "row", lambda d, at: transposed(dmix[at, :], w_out[columns(d, width), :]), dgo, d_held, d_left, d_right,
            d_send, d_recv,
        ),
        states(),
        pump=(sums, PUMPS[3]),
    )
    xc, sig_c, u_low, u = kept["xc"], kept["sig_c"], kept["u_low"], kept["u"]
    step_low, pre = kept["step_low"], kept["pre"]
    z_now = late("z")[...]
    sig_z = jax.nn.sigmoid(z_now)
    d_z = (dgo[...] * late("yv")[...] * (sig_z * (1.0 + z_now * (1.0 - sig_z)))).astype(bf16)
    mine = dz_all.at[:, columns(row, width)]
    mine[...] = d_z
    z_copies = []
    for k in range(1, row_size):
        copy = remote(mine, mine, z_send.at[k - 1], z_recv.at[k - 1], away("row", k))
        copy.start()
        z_copies.append(copy)
    dy = dgo[...] * (z_now * sig_z)
    dy_s[...] = dy
    dproj[...] = jnp.zeros_like(dproj)

    def adjoint():
        kept["rate"] = yield from scan_backward(
            proj, rank, rank + count, step, gone, drive, u_s, dy_s, rate[...], hs, bb, cb, pb, pc, du_s, dstep, dproj
        )

    run(adjoint(), pump=(sums, PUMPS[4]))
    g_rate = kept["rate"]
    d_pre = dstep[...] * jax.nn.sigmoid(pre)
    d_pre_low = d_pre.astype(bf16)
    dproj[...] += transposed(d_pre_low, w_step[...])

    def during_sums():
        yield
        wait_all(z_copies)
        sums.add(pair(3, g_z, dz_all, late("n1"), late("n1_mates"), False, (g_z_1, g_z_2, g_z_3), g_z_o))

    run(
        total_of_sums(dproj, half_own, half_in, low_own, low_in, full, (t_send, t_recv)),
        during_sums(),
        pump=(sums, PUMPS[5]),
    )
    dproj_low = full[...].astype(bf16)
    du = du_s[...] + as_row(skip) * dy + transposed(dproj_low, w_xp[...])
    dxc = du * (sig_c * (1.0 + xc * (1.0 - sig_c)))
    taps_now = taps[...]
    d_inner = dxc * taps_now[tap_count - 1 : tap_count, :]
    masked = [dxc]
    for shift in range(1, tap_count):
        masked.append(jnp.where(place_now >= shift, dxc, 0.0))
        k = tap_count - 1 - shift
        d_inner = d_inner + pltpu.roll(masked[shift], rows - shift, 0) * taps_now[k : k + 1, :]
    d_inner = d_inner.astype(bf16)
    dxi_all[:, columns(row, width)] = d_inner

    def during():
        dot_own[...] = rows_form(d_inner.astype(f32) * inner_x + d_z.astype(f32) * z_now)
        dot_copies = spray("row", lambda k: dot_own, dot_in, dot2_send, dot2_recv)
        small[0:RANK_LANES, :] = over_rows(dproj_low, u_low).astype(bf16)
        small[RANK_LANES : RANK_LANES + rank, :] = over_rows(step_low, d_pre_low)[0:rank, :].astype(bf16)
        yield
        wait_all(dot_copies)
        dot_sum[...] = line_total(dot_own[...], dot_in)
        dot_copy = swap("col", dot_sum, dot_other, o_send.at[3], o_recv.at[3])
        weights[4].wait()
        weights[5].wait()
        own[...] = transposed(dz_all[...], w_z[...])
        yield
        dot_copy.wait()

    run(*gather_halves("row", dxi_all, width, x_send, x_recv), during(), pump=(sums, PUMPS[6]))
    own[...] += transposed(dxi_all[...], w_x[...])
    copy = swap("col", own, other, o_send.at[4], o_recv.at[4])
    sums.add(pair(4, g_x, dxi_all, late("n1"), late("n1_mates"), False, (g_x_1, g_x_2, g_x_3), g_x_o))
    sums.pump(PUMPS[7])
    copy.wait()
    dn1 = own[...] + other[...]
    s1_now = late("s1")[...]
    xg_now = late("xg")[...].astype(f32)
    dots = column_form(dot_sum[...] + dot_other[...])
    dx = dh1[...] + s1_now * (as_row(gain1) * dn1) - xg_now * (s1_now * s1_now * dots / model_width)
    dx_own[...] = dx.astype(bf16)
    dx_copies = plane_start(dx_own.at[half], dx_all, dx_send, dx_recv)
    y_copies = plane_start(y_own.at[half], y_all, y_send, y_recv)
    g_taps = [None] * tap_count
    for shift in range(tap_count):
        moved = pltpu.roll(inner_x, shift, 0) if shift else inner_x
        g_taps[tap_count - 1 - shift] = jnp.sum(masked[shift] * moved, axis=0, keepdims=True)
    pieces = [
        g_rate,
        *g_taps,
        jnp.sum(dxc, axis=0, keepdims=True),
        jnp.sum(d_pre, axis=0, keepdims=True),
        jnp.sum(dy * u, axis=0, keepdims=True),
        jnp.sum(dn1 * xg_now * s1_now, axis=0, keepdims=True),
        gnorm2,
    ]
    found = sum(piece.shape[0] for piece in pieces)
    pieces.append(jnp.zeros((small.shape[0] - RANK_LANES - rank - found, width), f32))
    small[RANK_LANES + rank :, :] = jnp.concatenate(pieces, axis=0).astype(bf16)
    sums.add(total(6, small, small_1, small_2, small_o))
    first = (group * col_size + column) * block
    wanted = owner_rows(lengths_row(lens), as_row(order), lens.shape[1], rows, block, first)
    sums.pump(PUMPS[8])
    plane_finish(dx_copies, dx_all, dx_send, dx_recv)
    dx_o[...] = pick_rows(wanted, dx_all[...])
    plane_finish(y_copies, y_all, y_send, y_recv)
    y_o[...] = pick_rows(wanted, y_all[...])
    sums.drain()
    for write in writes:
        write.wait()


def finish_kernel(
    y, dx, small,
    y_o, dx_o, norm1_o, taps_o, bias_o, w_xp_o, w_dt_o, dt_bias_o, rate_o, skip_o, norm2_o,
    z_o, x_o, out_o, down_o, gate_o, up_o,
    *, rank, late, leave
):
    for name, target in (("z", z_o), ("x", x_o), ("out", out_o), ("down", down_o), ("gate", gate_o), ("up", up_o)):
        target[...] = late(name)[...].astype(f32)
        leave(name)
    y_o[...] = y[...]
    dx_o[...] = dx[...]
    values = small[...].astype(f32)
    w_xp_o[...] = jnp.transpose(values[0:RANK_LANES, :])
    w_dt_o[...] = values[RANK_LANES : RANK_LANES + rank, :]
    at = RANK_LANES + rank
    for target in (rate_o, taps_o):
        target[...] = values[at : at + target.shape[0], :]
        at += target.shape[0]
    for target in (bias_o, dt_bias_o, skip_o, norm1_o, norm2_o):
        target[...] = values[at : at + 1, :].reshape(target.shape)
        at += 1
    leave.finish()


VMEM_BYTES = 60 << 20
DMA = pltpu.SemaphoreType.DMA


def in_vmem(kernel, name, ident, outs, scratch, args, far=(), far_outs=(), late=None, leave=None):
    late, leave = late or {}, leave or {}
    space = pl.BlockSpec(memory_space=pltpu.VMEM)
    anywhere = pl.BlockSpec(memory_space=pl.ANY)
    heads, tails, before, after = len(args) + len(far), len(outs) + len(far_outs), len(late), len(leave)

    def whole(*refs):
        at = [0]

        def take(count):
            at[0] += count
            return refs[at[0] - count : at[0]]

        head, sources, tail, targets = take(heads), take(before), take(tails), take(after)
        middle = take(len(scratch))
        keywords = {}
        if late:
            held = take(before)
            keywords["late"] = Late(list(late), sources, held, take(1)[0])
        held = take(after)
        if leave:
            keywords["leave"] = Leave(list(leave), held, targets, take(1)[0])
        kernel(*head, *tail, *held, *middle, **keywords)

    own = list(scratch)
    if late:
        own += [pltpu.VMEM(value.shape, value.dtype) for value in late.values()] + [DMA((before,))]
    if leave:
        own += [pltpu.VMEM(shape, kind) for shape, kind in leave.values()] + [DMA((after,))]
    return pl.pallas_call(
        whole,
        out_shape=tuple(jax.ShapeDtypeStruct(shape, kind) for shape, kind in [*outs, *far_outs, *leave.values()]),
        in_specs=[space] * len(args) + [anywhere] * (len(far) + before),
        out_specs=tuple([space] * len(outs) + [anywhere] * (len(far_outs) + after)),
        scratch_shapes=own,
        compiler_params=pltpu.CompilerParams(
            collective_id=ident, has_side_effects=ident is not None, vmem_limit_bytes=VMEM_BYTES
        ),
        name=name,
    )(*args, *far, *late.values())


def both(*shape):
    return [DMA(shape), DMA(shape)]


def on_pairs(
    x_in, lengths, seq_order, norm1_gain, w_in_x, w_in_z, conv_w, conv_b, w_xp, w_dt, dt_bias, a_log,
    skip_weight, w_out, norm2_gain, w_gate, w_up, w_down, cotangent,
):
    dp, rs = lax.axis_size("dp"), lax.axis_size("row")
    block, wide_d = x_in.shape
    rows = block * 2
    model_width = wide_d * rs
    width = conv_w.shape[0]
    hidden = w_gate.shape[1] // rs
    rank, count, taps = w_dt.shape[0], a_log.shape[1], conv_w.shape[1]
    conv_taps = conv_w.T
    rates = a_log.T
    vm = pltpu.VMEM
    tile = vm((128, count, 128), f32)
    big = vm((rows, width), f32)
    model = vm((rows, wide_d), f32)
    sums = [vm((8, rows), f32), vm((rs - 1, 8, rows), f32)]
    sums_scratch = [
        vm((rows // 2, RANK_LANES), f32),
        vm((rows // 2, RANK_LANES), f32),
        vm((rows // 2, RANK_LANES), bf16),
        vm((rs - 1, rows // 2, RANK_LANES), bf16),
    ]

    def weight(value):
        return vm(value.shape, value.dtype)

    def line(size, width):
        return [vm((size, rows, width), bf16)] * 3

    leave = {
        "xg": ((rows, wide_d), bf16), "cg": ((rows, wide_d), bf16), "n1": ((rows, wide_d), bf16),
        "s1": ((rows, 1), f32), "place": ((rows, 1), f32), "xi": ((rows, width), f32), "z": ((rows, width), f32),
        "proj": ((rows, RANK_LANES), f32), "yv": ((rows, width), f32), "go_all": ((rows, rs * width), bf16),
        "h1": ((rows, wide_d), f32), "s2": ((rows, 1), f32), "n2": ((rows, wide_d), bf16),
        "hid_all": ((rows, rs * hidden), bf16), "dgu": ((rows, 2 * hidden), bf16), "dot": ((8, rows), f32),
        "n1_mates": ((2, rows, wide_d), bf16), "n2_mates": ((2, rows, wide_d), bf16),
        "cg_mates": ((2, rows, wide_d), bf16), "go_mates": ((2, rows, width), bf16),
        "hid_mates": ((2, rows, hidden), bf16),
    }
    passed = in_vmem(
        functools.partial(forward_kernel, model_width=model_width, rank=rank, count=count),
        "forward",
        0,
        [],
        [
            weight(w_in_x), weight(w_in_z), weight(w_out), weight(w_gate), weight(w_up), weight(w_down),
            vm((RANK_LANES, width), bf16), vm((count, width), f32),
            vm((2, dp, block, wide_d), bf16), vm((2, dp, block, wide_d), bf16), *sums, vm((rows, wide_d), bf16),
            *line(rs, width), *line(rs, width),
            vm((rows, RANK_LANES), f32), *sums_scratch, tile, tile, big, big, big,
            model, model, vm((rows, 2 * hidden), f32), vm((3, rows // 2, 2 * hidden), f32), *line(rs, 2 * hidden), vm((rows, hidden), f32), *line(rs, hidden),
            DMA((6,)), *both(dp), *both(dp), *both(rs - 1), *both(2, 2, rs), *both(2, 2, rs), *both(rs + 1),
            *both(2, 2, rs), *both(1), *both(rs - 1), *both(4, 2, rs), *both(2, 2, rs), *both(4, 2, rs), *both(6, 2),
        ],
        (
            x_in, cotangent, lengths, seq_order, norm1_gain, conv_taps, conv_b, w_xp, w_dt, dt_bias, rates, skip_weight,
            norm2_gain,
        ),
        (w_in_x, w_in_z, w_out, w_gate, w_up, w_down),
        leave=leave,
    )
    passed = dict(zip(leave, passed))
    first = ("dgu", "dot", "hid_all", "hid_mates", "cg", "cg_mates", "n2", "n2_mates")
    late = {name: passed[name] for name in (*first, *(name for name in passed if name not in first))}

    def sizes(value, parts):
        return vm((2, value[0] // parts, value[1]), bf16)

    def eighths(value):
        return vm((2, value[0] // 8, value[1]) if value in (d_cols, grads[5]) else (2, value[0] // 2, value[1] // 4), bf16)

    d_cols, f_cols, e_cols = (rs * hidden, wide_d), (wide_d, rs * hidden), (wide_d, rs * width)
    grads = (d_cols, f_cols, f_cols, e_cols, e_cols, (rs * width, wide_d), (2 * RANK_LANES, width))
    returned = in_vmem(
        functools.partial(backward_kernel, rank=rank, model_width=model_width),
        "backward",
        1,
        [((block, wide_d), bf16), ((block, wide_d), bf16)],
        [
            weight(w_gate), weight(w_up), weight(w_down), weight(w_out), weight(w_in_x), weight(w_in_z),
            vm((RANK_LANES, width), bf16), vm((count, width), f32),
            vm((rows, rs * hidden), bf16), vm((rows, rs * hidden), bf16),
            vm((rows, rs * width), bf16), vm((rows, rs * width), bf16),
            model, vm((rows, wide_d), bf16), vm((rows, wide_d), bf16), vm((rows, wide_d), bf16),
            vm((2, dp, block, wide_d), bf16), vm((2, dp, block, wide_d), bf16),
            model, model, model, model, vm((rs - 1, 8, rows), f32), vm((8, rows), f32), vm((8, rows), f32),
            vm((8, rows), f32), big, *line(rs, width),
            vm((rows + 1, count, width), f32), tile, tile, tile, tile,
            big, big, big, big, big, big, big, vm((rows, RANK_LANES), f32), *sums_scratch, vm((rows, RANK_LANES), f32),
            *[vm(value, bf16) for value in grads],
            *[vm((2, rows, max(value) // 4), bf16) for value in grads[1:5]], sizes(grads[6], 4),
            *[eighths(value) for value in grads[:6]], sizes(grads[6], 8),
            *[eighths(value) for value in grads[:6]], vm((2, rows, wide_d), bf16),
            DMA((6,)), *both(2, 2, rs), *both(2, 2, rs), *both(5), *both(rs - 1), *both(dp), *both(dp), *both(2, 2, rs),
            *both(rs - 1), *both(rs + 1), *both(2, 2, rs), *both(rs - 1), *both(len(grads), 5, 2),
            pltpu.SemaphoreType.REGULAR((len(grads), 2)), DMA((len(grads),)),
        ],
        (
            lengths, seq_order, norm2_gain, conv_taps, conv_b, w_xp, w_dt, dt_bias, rates, skip_weight, norm1_gain,
        ),
        (w_gate, w_up, w_down, w_out, w_in_x, w_in_z),
        [(value, bf16) for value in (grads[-1], *grads[:-1])],
        late,
    )
    y_part, dx_part, small, *summed = returned
    names = ("down", "gate", "up", "z", "x", "out")
    order = (3, 4, 5, 0, 1, 2)
    y_out, dx_out, norm1, g_taps, g_bias, g_xp, g_dt, g_dt_bias, g_rate, g_skip, norm2, *wide = in_vmem(
        functools.partial(finish_kernel, rank=rank),
        "finish",
        None,
        [
            ((block, wide_d), bf16), ((block, wide_d), bf16), ((wide_d,), f32), ((taps, width), f32), ((width,), f32),
            ((width, RANK_LANES), f32), ((rank, width), f32), ((width,), f32), ((count, width), f32), ((width,), f32),
            ((wide_d,), f32),
        ],
        [],
        (y_part, dx_part, small),
        late={names[i]: summed[i] for i in order},
        leave={names[i]: (grads[i], f32) for i in order},
    )
    g_z, g_x, g_out, g_down, g_gate, g_up = wide
    return (
        y_out, dx_out, norm1, g_x, g_z, g_taps.T, g_bias, g_xp, g_dt, g_dt_bias, g_rate.T, g_skip, g_out, norm2,
        g_gate, g_up, g_down,
    )


def on_device(
    x_in,
    lengths,
    seq_order,
    norm1_gain,
    w_in_x,
    w_in_z,
    conv_w,
    conv_b,
    w_xp,
    w_dt,
    dt_bias,
    a_log,
    skip_weight,
    w_out,
    norm2_gain,
    w_gate,
    w_up,
    w_down,
    cotangent,
):
    rows_in, width_row = x_in.shape
    row_devices = lax.axis_size("row")
    col_devices = lax.axis_size("col")
    group_rows = rows_in * col_devices
    model_width = width_row * row_devices
    rank_cols = w_dt.shape[0]
    state_count = a_log.shape[1]
    channels = conv_w.shape[0]
    ff_cols = w_gate.shape[1]
    my_group = lax.axis_index("dp")
    my_column = lax.axis_index("col")
    source, position_all = layout(lengths, seq_order, group_rows)
    my_source = lax.dynamic_index_in_dim(source, my_group, 0, keepdims=False)
    position = lax.dynamic_index_in_dim(position_all, my_group, 0, keepdims=False)
    slice_source = lax.dynamic_slice_in_dim(my_source, my_column * rows_in, rows_in, 0)

    def row_total(values):
        return lax.psum(values, "row")

    def token_rows(values):
        return lax.all_gather(values, "col", axis=0, tiled=True)

    def row_pieces(values):
        return lax.all_gather(values, "row", axis=0, tiled=True)

    def col_reduce(term_fn):
        return lax.psum_scatter(
            term_fn(jnp.int32(0), lax.axis_size("col") * rows_in),
            "col",
            scatter_dimension=0,
            tiled=True,
        )

    def row_reduce(term_fn, keep_rows):
        return lax.psum_scatter(
            term_fn(jnp.int32(0), lax.axis_size("row") * keep_rows),
            "row",
            scatter_dimension=0,
            tiled=True,
        )

    def projection_total(values):
        return lax.psum(values, ("row", "col"))

    blank_rows = jnp.zeros((rows_in, width_row), jnp.bfloat16)
    pieces = (
        lax.all_gather(x_in, ("dp", "col"), axis=0, tiled=True),
        lax.all_gather(cotangent, ("dp", "col"), axis=0, tiled=True),
    )
    row_count = pieces[0].shape[0]
    offset = slice_source
    inside = ((offset >= 0) & (offset < row_count))[:, None]
    index = jnp.clip(offset, 0, row_count - 1)
    x_rows = jnp.where(inside, jnp.take(pieces[0], index, axis=0), blank_rows)
    cot_rows = jnp.where(inside, jnp.take(pieces[1], index, axis=0), blank_rows)
    x_val = x_rows.astype(jnp.float32)
    scale_one = lax.rsqrt(row_total(jnp.sum(x_val * x_val, axis=1)) / model_width + epsilon)
    normed_one = (x_val * scale_one[:, None] * norm1_gain[None, :]).astype(jnp.bfloat16)
    normed_all = token_rows(normed_one)

    def inner_term(begin_row, row_count):
        return jnp.concatenate(
            [contract(w_in_x, normed_all, 0, 1), contract(w_in_z, normed_all, 0, 1)], axis=1
        )

    inner = row_reduce(inner_term, channels)
    inner_x = inner[:, :group_rows]
    inner_z = inner[:, group_rows:]

    def conv_part(values, kernel, kernel_bias):
        return convolve(values, kernel, kernel_bias, position)

    conv_out, conv_pull = jax.vjp(conv_part, inner_x, conv_w, conv_b)
    u_low = conv_out.astype(jnp.bfloat16)
    u_val = u_low.astype(jnp.float32)
    projected = projection_total(contract(w_xp, u_low, 0, 0))
    step_low = projected[:rank_cols].astype(jnp.bfloat16)
    pre_step = contract(w_dt, step_low, 0, 0) + dt_bias[:, None]
    step_size = jax.nn.softplus(pre_step)

    decay_rate = -jnp.exp(a_log).T
    proj_rows = projected.T
    u_rows = u_val.T
    step_rows = step_size.T
    gone_rows = jnp.where(position[:, None] > 0, step_rows, 1e30)
    drive_rows = step_rows * u_rows
    at_b, at_c = rank_cols, rank_cols + state_count
    scanned = scan_alone(proj_rows, gone_rows, drive_rows, decay_rate, at_b, at_c)
    mixer_y = scanned.T + skip_weight[:, None] * u_val
    gated = mixer_y * jax.nn.silu(inner_z)
    gated_low = gated.astype(jnp.bfloat16)
    gated_all = row_pieces(gated_low)

    def mix_term(begin_row, row_count):
        return contract(gated_all, w_out, 0, 0)

    first_sum = x_val + col_reduce(mix_term)
    scale_two = lax.rsqrt(row_total(jnp.sum(first_sum * first_sum, axis=1)) / model_width + epsilon)
    normed_two = (first_sum * scale_two[:, None] * norm2_gain[None, :]).astype(jnp.bfloat16)
    normed_rows = token_rows(normed_two)

    def ffn_term(begin_row, row_count):
        return jnp.concatenate(
            [
                jnp.dot(normed_rows, w_gate, preferred_element_type=jnp.float32),
                jnp.dot(normed_rows, w_up, preferred_element_type=jnp.float32),
            ],
            axis=1,
        )

    gate_up = row_reduce(ffn_term, group_rows // row_devices)
    gate_val = gate_up[:, :ff_cols]
    up_val = gate_up[:, ff_cols:]
    hidden = (jax.nn.silu(gate_val) * up_val).astype(jnp.bfloat16)
    hidden_all = row_pieces(hidden)

    def down_term(begin_row, row_count):
        return jnp.dot(hidden_all, w_down, preferred_element_type=jnp.float32)

    second_sum = first_sum + col_reduce(down_term)
    out_low = second_sum.astype(jnp.bfloat16)
    back_down_all = token_rows(cot_rows)
    grad_down = contract(hidden_all, back_down_all, 0, 0)

    def hidden_term(begin_row, row_count):
        return contract(back_down_all, w_down, 1, 1)

    d_hidden = row_reduce(hidden_term, group_rows // row_devices)
    d_gate = (d_hidden * up_val * silu_slope(gate_val)).astype(jnp.bfloat16)
    d_up = (d_hidden * jax.nn.silu(gate_val)).astype(jnp.bfloat16)
    d_gate_up_all = row_pieces(jnp.concatenate([d_gate, d_up], axis=1))
    grad_gate = contract(normed_rows, d_gate_up_all[:, :ff_cols], 0, 0)
    grad_up = contract(normed_rows, d_gate_up_all[:, ff_cols:], 0, 0)

    def norm_two_term(begin_row, row_count):
        return contract(d_gate_up_all[:, :ff_cols], w_gate, 1, 1) + contract(
            d_gate_up_all[:, ff_cols:], w_up, 1, 1
        )

    d_normed_two = col_reduce(norm_two_term)
    cot_val = cot_rows.astype(jnp.float32)
    weighted_two = d_normed_two * norm2_gain[None, :]
    grad_norm_two = jnp.sum(d_normed_two * first_sum * scale_two[:, None], axis=0)
    dot_two = row_total(jnp.sum(weighted_two * first_sum, axis=1))
    d_first = (
        cot_val
        + scale_two[:, None] * weighted_two
        - first_sum * (scale_two**3 * dot_two / model_width)[:, None]
    )
    d_mix_all = token_rows(d_first.astype(jnp.bfloat16))
    grad_out = contract(gated_all, d_mix_all, 1, 0)

    def gated_term(begin_row, row_count):
        return contract(w_out, d_mix_all, 1, 1)

    d_gated = row_reduce(gated_term, channels)
    d_inner_z = d_gated * mixer_y * silu_slope(inner_z)
    d_mixer = d_gated * jax.nn.silu(inner_z)
    d_u_rows, d_step_rows, d_proj_rows, grad_rate_rows = adjoint_alone(
        proj_rows, step_rows, gone_rows, drive_rows, u_rows, d_mixer.T, decay_rate, at_b, at_c
    )
    d_u_mix = d_u_rows.T + skip_weight[:, None] * d_mixer
    d_step = d_step_rows.T
    d_enter = d_proj_rows.T[at_b:at_c]
    d_leave = d_proj_rows.T[at_c:]
    grad_rate = grad_rate_rows.T
    grad_skip = jnp.sum(d_mixer * u_val, axis=1)
    d_pre = d_step * jax.nn.sigmoid(pre_step)
    grad_step_bias = jnp.sum(d_pre, axis=1)
    d_pre_low = d_pre.astype(jnp.bfloat16)
    grad_step_w = contract(step_low, d_pre_low, 1, 1)
    d_projected = projection_total(
        jnp.concatenate(
            [jnp.dot(w_dt, d_pre_low, preferred_element_type=jnp.float32), d_enter, d_leave], axis=0
        )
    )
    d_proj_low = d_projected.astype(jnp.bfloat16)
    grad_proj_w = contract(u_low, d_proj_low, 1, 1)
    d_u_all = d_u_mix + jnp.dot(w_xp, d_proj_low, preferred_element_type=jnp.float32)
    d_inner_x, grad_kernel, grad_kernel_bias = conv_pull(d_u_all)
    d_inner_all = row_pieces(
        jnp.concatenate([d_inner_x.astype(jnp.bfloat16), d_inner_z.astype(jnp.bfloat16)], axis=1)
    )
    grad_in_x = contract(normed_all, d_inner_all[:, :group_rows], 0, 1)
    grad_in_z = contract(normed_all, d_inner_all[:, group_rows:], 0, 1)

    def norm_one_term(begin_row, row_count):
        piece_x = lax.dynamic_slice_in_dim(d_inner_all, begin_row, row_count, 1)
        piece_z = lax.dynamic_slice_in_dim(d_inner_all, group_rows, row_count, 1)
        return contract(piece_x, w_in_x, 0, 1) + contract(piece_z, w_in_z, 0, 1)

    d_normed_one = col_reduce(norm_one_term)
    weighted_one = d_normed_one * norm1_gain[None, :]
    grad_norm_one = jnp.sum(d_normed_one * x_val * scale_one[:, None], axis=0)
    dot_one = row_total(jnp.sum(weighted_one * x_val, axis=1))
    d_input = (
        d_first
        + scale_one[:, None] * weighted_one
        - x_val * (scale_one**3 * dot_one / model_width)[:, None]
    )
    d_input_low = d_input.astype(jnp.bfloat16)
    grad_norm_one, grad_norm_two = lax.psum((grad_norm_one, grad_norm_two), ("dp", "col"))
    (
        grad_in_x,
        grad_in_z,
        grad_kernel,
        grad_kernel_bias,
        grad_proj_w,
        grad_step_w,
        grad_step_bias,
        grad_rate,
        grad_skip,
        grad_out,
        grad_gate,
        grad_up,
        grad_down,
    ) = (
        lax.psum(grad_in_x.astype(jnp.bfloat16), "dp").astype(jnp.float32),
        lax.psum(grad_in_z.astype(jnp.bfloat16), "dp").astype(jnp.float32),
        lax.psum(grad_kernel.astype(jnp.bfloat16), "dp").astype(jnp.float32),
        lax.psum(grad_kernel_bias.astype(jnp.bfloat16), "dp").astype(jnp.float32),
        lax.psum(grad_proj_w.astype(jnp.bfloat16), "dp").astype(jnp.float32),
        lax.psum(grad_step_w.astype(jnp.bfloat16), "dp").astype(jnp.float32),
        lax.psum(grad_step_bias.astype(jnp.bfloat16), "dp").astype(jnp.float32),
        lax.psum(grad_rate.astype(jnp.bfloat16), "dp").astype(jnp.float32),
        lax.psum(grad_skip.astype(jnp.bfloat16), "dp").astype(jnp.float32),
        lax.psum(grad_out.astype(jnp.bfloat16), "dp").astype(jnp.float32),
        lax.psum(grad_gate.astype(jnp.bfloat16), "dp").astype(jnp.float32),
        lax.psum(grad_up.astype(jnp.bfloat16), "dp").astype(jnp.float32),
        lax.psum(grad_down.astype(jnp.bfloat16), "dp").astype(jnp.float32),
    )
    payload = jnp.concatenate([out_low, d_input_low], axis=1)
    tokens_all = lengths.shape[0] * group_rows
    owner = (
        jnp.zeros((tokens_all,), jnp.int32)
        .at[source.reshape(-1)]
        .set(jnp.arange(tokens_all, dtype=jnp.int32))
    )
    my_rows = lax.dynamic_slice_in_dim(
        owner, (my_group * col_devices + my_column) * rows_in, rows_in, 0
    )
    pieces = lax.all_gather(payload, ("dp", "col"), axis=0, tiled=True)
    row_count = pieces.shape[0]
    offset = my_rows
    inside = ((offset >= 0) & (offset < row_count))[:, None]
    returned = jnp.where(
        inside,
        jnp.take(pieces, jnp.clip(offset, 0, row_count - 1), axis=0),
        jnp.zeros_like(payload),
    )
    y_out = returned[:, :width_row]
    dx_out = returned[:, width_row:]
    return (
        y_out,
        dx_out,
        grad_norm_one,
        grad_in_x,
        grad_in_z,
        grad_kernel,
        grad_kernel_bias,
        grad_proj_w,
        grad_step_w,
        grad_step_bias,
        grad_rate,
        grad_skip,
        grad_out,
        grad_norm_two,
        grad_gate,
        grad_up,
        grad_down,
    )


def solution(mesh):
    placed = (
        P(("dp", "col"), "row"),
        P(),
        P(),
        P("row"),
        P("row", "col"),
        P("row", "col"),
        P(("col", "row"), None),
        P(("col", "row")),
        P(("col", "row"), None),
        P(None, ("col", "row")),
        P(("col", "row")),
        P(("col", "row"), None),
        P(("col", "row")),
        P("col", "row"),
        P("row"),
        P("row", "col"),
        P("row", "col"),
        P("col", "row"),
        P(("dp", "col"), "row"),
    )
    paired = mesh.shape["col"] == 2 and mesh.shape["dp"] == 4
    return jax.shard_map(
        on_pairs if paired else on_device,
        mesh=mesh,
        in_specs=placed,
        out_specs=(
            P(("dp", "col"), "row"),
            P(("dp", "col"), "row"),
            P("row"),
            P("row", "col"),
            P("row", "col"),
            P(("col", "row"), None),
            P(("col", "row")),
            P(("col", "row"), None),
            P(None, ("col", "row")),
            P(("col", "row")),
            P(("col", "row"), None),
            P(("col", "row")),
            P("col", "row"),
            P("row"),
            P("row", "col"),
            P("row", "col"),
            P("col", "row"),
        ),
        check_vma=False,
    )
```

```python
import functools

import jax
import jax.numpy as jnp
from jax import lax
from jax.experimental import pallas as pl
from jax.experimental.pallas import tpu as pltpu
from jax.sharding import PartitionSpec as P

epsilon = 1e-05


def layout(lengths, seq_order, group_rows):
    flat_lengths = lengths.reshape(-1)
    total_seqs = flat_lengths.shape[0]
    slot_length = jnp.take(flat_lengths, seq_order)
    input_start = jnp.cumsum(slot_length) - slot_length
    slot_of = (
        jnp.zeros((total_seqs,), jnp.int32)
        .at[seq_order]
        .set(jnp.arange(total_seqs, dtype=jnp.int32))
    )
    seq_input = jnp.take(input_start, slot_of).reshape(lengths.shape)
    group_start = jnp.cumsum(lengths, axis=1) - lengths
    places = jnp.arange(group_rows, dtype=jnp.int32)
    member = (
        jnp.sum((places[None, :, None] >= group_start[:, None, :]).astype(jnp.int32), axis=2) - 1
    )
    begin_at = jnp.take_along_axis(group_start, member, axis=1)
    within = places[None, :] - begin_at
    source = jnp.take_along_axis(seq_input, member, axis=1) + within
    return (source, within)


def silu_slope(values):
    sigmoid_v = jax.nn.sigmoid(values)
    return sigmoid_v * (1.0 + values * (1.0 - sigmoid_v))


def contract(left, right, left_dim, right_dim):
    return lax.dot_general(
        left, right, (((left_dim,), (right_dim,)), ((), ())), preferred_element_type=jnp.float32
    )


def convolve(inner_x, kernel, kernel_bias, places):
    tap_count = kernel.shape[1]
    conv_sum = kernel_bias[:, None] + inner_x * kernel[:, tap_count - 1][:, None]
    for shift_by in range(1, tap_count):
        shifted = jnp.pad(inner_x, ((0, 0), (shift_by, 0)))[:, :-shift_by]
        conv_sum = (
            conv_sum
            + shifted
            * (places >= shift_by).astype(jnp.float32)[None, :]
            * kernel[:, tap_count - 1 - shift_by][:, None]
        )
    return jax.nn.silu(conv_sum)


MESH = pl.DeviceIdType.MESH
f32 = jnp.float32
bf16 = jnp.bfloat16


def remote(src, dst, send, recv, where):
    return pltpu.make_async_remote_copy(
        src_ref=src, dst_ref=dst, send_sem=send, recv_sem=recv, device_id=where, device_id_type=MESH
    )


def away(axis, offset):
    return {axis: lax.rem(lax.axis_index(axis) + offset, lax.axis_size(axis))}


def greet(*axes):
    barrier = pltpu.get_barrier_semaphore()
    total = 0
    for axis in axes:
        for offset in range(1, lax.axis_size(axis)):
            pl.semaphore_signal(barrier, inc=1, device_id=away(axis, offset), device_id_type=MESH)
            total += 1
    return lambda: pl.semaphore_wait(barrier, total)


class Late:
    def __init__(self, names, sources, targets, sems):
        self.targets = dict(zip(names, targets))
        self.waiting = {}
        for i, (name, source, target) in enumerate(zip(names, sources, targets)):
            self.waiting[name] = pltpu.make_async_copy(source, target, sems.at[i])
            self.waiting[name].start()

    def __call__(self, name):
        if name in self.waiting:
            self.waiting.pop(name).wait()
        return self.targets[name]


class Leave:
    def __init__(self, names, sources, targets, sems):
        self.copies = {
            name: pltpu.make_async_copy(source, target, sems.at[i])
            for i, (name, source, target) in enumerate(zip(names, sources, targets))
        }

    def __call__(self, *names):
        for name in names:
            self.copies[name].start()

    def finish(self):
        for copy in self.copies.values():
            copy.wait()


def matmul(left, right):
    return jnp.dot(left, right, preferred_element_type=f32)


def silu(values):
    return values * jax.nn.sigmoid(values)


def rows_form(values):
    ones = jnp.ones((8, values.shape[1]), f32)
    return lax.dot_general(
        ones,
        values,
        (((1,), (1,)), ((), ())),
        precision=lax.Precision.HIGHEST,
        preferred_element_type=f32,
    )


def column_form(row_values):
    return jnp.transpose(row_values)[:, 0:1]


class Line:
    def __init__(self, axis, send, recv):
        self.axis, self.send, self.recv = axis, send, recv
        self.size = lax.axis_size(axis)
        self.me = lax.axis_index(axis)

    def right(self, src, dst, d):
        return remote(
            src, dst, self.send.at[0, d], self.recv.at[0, d], {self.axis: jnp.minimum(self.me + 1, self.size - 1)}
        )

    def left(self, src, dst, d):
        return remote(
            src, dst, self.send.at[1, d], self.recv.at[1, d], {self.axis: jnp.maximum(self.me - 1, 0)}
        )


def line_gather(axis, slot_of, send, recv):
    line = Line(axis, send, recv)
    size, me = line.size, line.me
    last = size - 1

    def go_right(s):
        slot = jnp.maximum(me - s, 0)
        return (me - s >= 0) & (me < last), line.right(slot_of(slot), slot_of(slot), slot)

    def go_left(s):
        slot = jnp.minimum(me + s, last)
        return (me + s <= last) & (me > 0), line.left(slot_of(slot), slot_of(slot), slot)

    for s in range(last):
        for valid, copy in (go_right(s), go_left(s)):
            pl.when(valid)(copy.start)
        yield
        slot = jnp.maximum(me - 1 - s, 0)
        pl.when(me - 1 - s >= 0)(line.right(slot_of(slot), slot_of(slot), slot).wait_recv)
        slot = jnp.minimum(me + 1 + s, last)
        pl.when(me + 1 + s <= last)(line.left(slot_of(slot), slot_of(slot), slot).wait_recv)
    yield
    for s in range(last):
        for valid, copy in (go_right(s), go_left(s)):
            pl.when(valid)(copy.wait_send)


def line_scatter(axis, block_of, out, held, from_left, from_right, send, recv, slots=False):
    line = Line(axis, send, recv)
    size, me = line.size, line.me
    last = size - 1

    def right_at(t):
        d = jnp.clip(last - t + me, 0, last)
        return (t >= me) & (me < last), d, line.right(held.at[d], from_left.at[d], d)

    def left_at(t):
        d = jnp.clip(t - (last - me), 0, last)
        return (t >= last - me) & (me > 0), d, line.left(held.at[d], from_right.at[d], d)

    def made(d, slot):
        return block_of(d, slot) if slots else block_of(d)

    def pass_on(valid, first, d, copy, arrived, slot):
        @pl.when(valid)
        def _():
            part = made(d, slot)

            @pl.when(jnp.logical_not(first))
            def _():
                copy.wait_recv()
                held[d] = (part + arrived[d].astype(f32)).astype(held.dtype)

            @pl.when(first)
            def _():
                held[d] = part.astype(held.dtype)

            copy.start()

    for t in range(last):
        valid, d, copy = right_at(t)
        pass_on(valid, me == 0, d, copy, from_left, 0)
        valid, d, copy = left_at(t)
        pass_on(valid, me == last, d, copy, from_right, 1)
        if t == 0:
            out[...] = made(me, 2)
        yield
    yield

    @pl.when(me > 0)
    def _():
        line.right(held.at[me], from_left.at[me], me).wait_recv()
        out[...] += from_left[me].astype(f32)

    @pl.when(me < last)
    def _():
        line.left(held.at[me], from_right.at[me], me).wait_recv()
        out[...] += from_right[me].astype(f32)

    for t in range(last):
        for valid, _, copy in (right_at(t), left_at(t)):
            pl.when(valid)(copy.wait_send)


def halves(rows):
    return [pl.ds(0, rows // 2), pl.ds(rows // 2, rows // 2)]


def gather_halves(axis, ref, size, send, recv):
    flows = []
    for h, at in enumerate(halves(ref.shape[0])):

        def slot_of(d, at=at):
            return ref.at[at, pl.ds(pl.multiple_of(d * size, size), size)]

        flows.append(line_gather(axis, slot_of, send.at[h], recv.at[h]))
    return flows


def scatter_halves(axis, block_of, out, held, from_left, from_right, send, recv):
    flows = []
    for h, at in enumerate(halves(out.shape[0])):
        flows.append(
            line_scatter(
                axis,
                functools.partial(block_of, at=at),
                out.at[at, :],
                held.at[:, at, :],
                from_left.at[:, at, :],
                from_right.at[:, at, :],
                send.at[h],
                recv.at[h],
            )
        )
    return flows


def run(*flows, pump=None):
    flows = list(flows)
    turn = 0
    while flows:
        flows = [flow for flow in flows if next(flow, flows) is not flows]
        if pump is not None and turn < len(pump[1]):
            pump[0].pump(pump[1][turn])
        turn += 1


def lanes(ref, size):
    return lambda d: ref.at[:, pl.ds(pl.multiple_of(d * size, size), size)]


def fetch(sources, targets, sems):
    copies = [pltpu.make_async_copy(s, t, sems.at[i]) for i, (s, t) in enumerate(zip(sources, targets))]
    for copy in copies:
        copy.start()
    return copies


def as_row(ref):
    return ref[...].reshape(1, ref.shape[0])


def lengths_row(lens):
    groups, per_group = lens.shape
    values = lens[...].astype(f32)
    at = lax.broadcasted_iota(jnp.int32, (per_group, groups * per_group), 1)
    inner = lax.broadcasted_iota(jnp.int32, (per_group, groups * per_group), 0)
    total = jnp.zeros((1, groups * per_group), f32)
    for g in range(groups):
        place = jnp.where(at == inner + g * per_group, 1.0, 0.0)
        total = total + jnp.dot(
            values[g : g + 1, :], place, precision=lax.Precision.HIGHEST, preferred_element_type=f32
        )
    return total


def spray(axis, src_of, dst, send, recv, base=0):
    copies = []
    for k in range(1, lax.axis_size(axis)):
        copy = remote(src_of(k), dst.at[k - 1], send.at[base + k - 1], recv.at[base + k - 1], away(axis, k))
        copy.start()
        copies.append(copy)
    return copies


def wait_all(copies):
    for copy in copies:
        copy.wait()


def swap(axis, src, dst, send, recv):
    copy = remote(src, dst, send, recv, away(axis, 1))
    copy.start()
    return copy


def sequence_rows(lens_row, order_row, per_group):
    count = lens_row.shape[1]
    ri = lax.broadcasted_iota(jnp.int32, (count, count), 0)
    ci = lax.broadcasted_iota(jnp.int32, (count, count), 1)
    lens_f = lens_row

    def to_column(row):
        return jnp.sum(jnp.where(ri == ci, row, 0.0), axis=1, keepdims=True)

    order_col = to_column(order_row.astype(f32)).astype(jnp.int32)
    lens_col = to_column(lens_f)
    pick = order_row == ri
    pick_t = order_col == ci
    slot_col = jnp.sum(jnp.where(pick_t, lens_f, 0.0), axis=1, keepdims=True)
    slot_row = jnp.sum(jnp.where(pick, lens_col, 0.0), axis=0, keepdims=True)
    start_col = jnp.sum(jnp.where(ci < ri, slot_row, 0.0), axis=1, keepdims=True)
    input_row = jnp.sum(jnp.where(pick_t, start_col, 0.0), axis=0, keepdims=True)
    same = (ri // per_group) == (ci // per_group)
    group_row = jnp.sum(jnp.where((ri < ci) & same, lens_col, 0.0), axis=0, keepdims=True)
    return lens_f, input_row, group_row


def place_rows(lens_row, order_row, per_group, group_rows, group):
    lens_f, input_row, group_row = sequence_rows(lens_row, order_row, per_group)
    count = lens_row.shape[1]
    rows = lax.broadcasted_iota(jnp.int32, (group_rows, count), 0).astype(f32)
    mine = (lax.broadcasted_iota(jnp.int32, (group_rows, count), 1) // per_group) == group
    inside = (rows >= group_row) & (rows < group_row + lens_f) & mine
    within = jnp.sum(jnp.where(inside, rows - group_row, 0.0), axis=1, keepdims=True)
    begin = jnp.sum(jnp.where(inside, input_row, 0.0), axis=1, keepdims=True)
    return begin + within, within


def owner_rows(lens_row, order_row, per_group, group_rows, block_rows, first):
    lens_f, input_row, group_row = sequence_rows(lens_row, order_row, per_group)
    count = lens_row.shape[1]
    rows = (lax.broadcasted_iota(jnp.int32, (block_rows, count), 0) + first).astype(f32)
    base = (lax.broadcasted_iota(jnp.int32, (block_rows, count), 1) // per_group) * group_rows
    inside = (rows >= input_row) & (rows < input_row + lens_f)
    found = jnp.where(inside, base.astype(f32) + group_row + rows - input_row, 0.0)
    return jnp.sum(found, axis=1, keepdims=True)


def plane_origin(rows, dp_size, col_size, block_rows):
    at = lax.broadcasted_iota(jnp.int32, (rows, dp_size * col_size * block_rows), 1)
    block = at // block_rows
    group = lax.rem(block, dp_size)
    column = block // dp_size
    return ((group * col_size + column) * block_rows + lax.rem(at, block_rows)).astype(f32)


def pick_rows(wanted, held):
    col_size, dp_size, block_rows, width = held.shape
    total = col_size * dp_size * block_rows
    chosen = wanted == plane_origin(wanted.shape[0], dp_size, col_size, block_rows)
    chosen = jnp.where(chosen, 1.0, 0.0).astype(bf16)
    return matmul(chosen, held.reshape(total, width)).astype(bf16)


def plane_start(src, held, send, recv):
    me, column = lax.axis_index("dp"), lax.axis_index("col")
    held[column, me] = src[...]
    copies = []
    for k in range(1, lax.axis_size("dp")):
        copy = remote(src, held.at[column, me], send.at[k], recv.at[k], away("dp", k))
        copy.start()
        copies.append(copy)
    return copies


def plane_swap(copies, held, send, recv):
    column = lax.axis_index("col")
    for copy in copies:
        copy.wait_recv()
    return swap("col", held.at[column], held.at[column], send.at[0], recv.at[0])


def plane_wait(copies, last):
    last.wait_recv()
    for copy in [*copies, last]:
        copy.wait_send()


def plane_finish(copies, held, send, recv):
    plane_wait(copies, plane_swap(copies, held, send, recv))


def total_of_sums(part, half_own, half_in, low_own, low_in, full, sems):
    send, recv = sems
    rows = part.shape[0] // 2
    column = lax.axis_index("col")
    mine = pl.ds(pl.multiple_of(column * rows, rows), rows)
    other = pl.ds(pl.multiple_of((1 - column) * rows, rows), rows)
    half_own[...] = part[other, :]
    copy = swap("col", half_own, half_in, send.at[0], recv.at[0])
    yield
    copy.wait()
    low_own[...] = (part[mine, :] + half_in[...]).astype(bf16)
    copies = spray("row", lambda k: low_own, low_in, send, recv, 1)
    yield
    wait_all(copies)
    total = low_own[...].astype(f32)
    for k in range(low_in.shape[0]):
        total = total + low_in[k].astype(f32)
    full[mine, :] = total
    copy = swap("col", full.at[mine], full.at[mine], send.at[4], recv.at[4])
    yield
    copy.wait()


def lanes_like(tile, width):
    if tile.shape[-1] == width:
        return tile
    return jnp.concatenate([tile] * (width // tile.shape[-1]), axis=-1)


def lane_mask(count, lanes, first):
    lane = lax.broadcasted_iota(jnp.int32, (count, lanes), 1)
    return lane == lax.broadcasted_iota(jnp.int32, (count, lanes), 0) + first


def spread(values, first, count, wide):
    rows, lanes = values.shape
    chosen = jnp.where(lane_mask(count, lanes, first)[None], values[:, None, :], 0.0)
    chosen = chosen.reshape(rows * count, lanes)
    high = chosen.astype(bf16)
    rest = (chosen - high.astype(f32)).astype(bf16)
    ones = jnp.ones((lanes, wide), bf16)
    return matmul(high, ones) + matmul(rest, ones)


def spread_into(target, source, start, first, count):
    rows, _, wide = target.shape
    size = min(32, rows)

    def one(j, _):
        at = pl.ds(pl.multiple_of(start + j * size, size), size)
        found = spread(source[at, :], first, count, wide)
        target[pl.ds(pl.multiple_of(j * size, size), size)] = found.reshape(size, count, wide)
        return 0

    lax.fori_loop(0, rows // size, one, 0)


def add_lane_sums(target, start, sources):
    rows = sources[0][0].shape[0]
    size = min(32, rows)

    def one(j, _):
        inner = pl.ds(pl.multiple_of(j * size, size), size)
        at = pl.ds(pl.multiple_of(start + j * size, size), size)
        total = target[at, :]
        for source, first in sources:
            total = total + lane_sums(source[inner], first, target.shape[1])
        target[at, :] = total
        return 0

    lax.fori_loop(0, rows // size, one, 0)


def lane_sums(values, first, lanes):
    rows, count, wide = values.shape
    flat = values.reshape(rows * count, wide)
    high = flat.astype(bf16)
    rest = (flat - high.astype(f32)).astype(bf16)
    ones = jnp.ones((wide, lanes), bf16)
    sums = (matmul(high, ones) + matmul(rest, ones)).reshape(rows, count, lanes)
    return jnp.sum(jnp.where(lane_mask(count, lanes, first)[None], sums, 0.0), axis=1)


def scan_forward(proj, b_at, c_at, gone_step, drive, rate, bb, cb, y):
    rows, width = drive.shape
    count = rate.shape[0]
    piece, _, wide = bb.shape
    state = jnp.zeros((count, width), f32)
    for start in range(0, rows, piece):
        spread_into(bb, proj, start, b_at, count)
        spread_into(cb, proj, start, c_at, count)

        def eight(k, state):
            inner = pl.multiple_of(k * 8, 8)
            base = pl.multiple_of(start + k * 8, 8)
            gone = gone_step[pl.ds(base, 8), :]
            driven = drive[pl.ds(base, 8), :]
            found = []
            for i in range(8):
                decay = jnp.exp(gone[i : i + 1, :] * rate)
                state = decay * state + driven[i : i + 1, :] * lanes_like(bb[inner + i], width)
                found.append(jnp.sum(state * lanes_like(cb[inner + i], width), axis=0, keepdims=True))
            y[pl.ds(base, 8), :] = jnp.concatenate(found, axis=0)
            return state

        state = lax.fori_loop(0, piece // 8, eight, state)
        yield


def scan_states(proj, b_at, gone_step, drive, rate, bb, hs):
    rows, width = drive.shape
    count = rate.shape[0]
    piece, _, wide = bb.shape
    hs[0] = jnp.zeros((count, width), f32)
    for start in range(0, rows, piece):
        spread_into(bb, proj, start, b_at, count)

        def eight(k, state):
            inner = pl.multiple_of(k * 8, 8)
            base = pl.multiple_of(start + k * 8, 8)
            gone = gone_step[pl.ds(base, 8), :]
            driven = drive[pl.ds(base, 8), :]
            for i in range(8):
                decay = jnp.exp(gone[i : i + 1, :] * rate)
                state = decay * state + driven[i : i + 1, :] * lanes_like(bb[inner + i], width)
                hs[base + i + 1] = state
            return state

        lax.fori_loop(0, piece // 8, eight, hs[start])
        yield


def scan_backward(
    proj, b_at, c_at, step, gone_step, drive, inner_u, dy, rate, hs, bb, cb, pb, pc, du, dstep, dproj
):
    rows, width = drive.shape
    count = rate.shape[0]
    piece, _, wide = bb.shape

    def fold(values):
        total = values[:, 0:wide]
        for j in range(1, width // wide):
            total = total + values[:, j * wide : (j + 1) * wide]
        return total

    def part(start, carry):
        spread_into(bb, proj, start, b_at, count)
        spread_into(cb, proj, start, c_at, count)

        def eight(k, carry):
            later, total = carry
            inner = pl.multiple_of((piece // 8 - 1 - k) * 8, 8)
            base = pl.multiple_of(start + inner, 8)
            step8 = step[pl.ds(base, 8), :]
            gone8 = gone_step[pl.ds(base, 8), :]
            drive8 = drive[pl.ds(base, 8), :]
            u8 = inner_u[pl.ds(base, 8), :]
            dy8 = dy[pl.ds(base, 8), :]
            by_b = [None] * 8
            by_rate = [None] * 8
            for i in reversed(range(8)):
                dy_row = dy8[i : i + 1, :]
                lam = lanes_like(cb[inner + i], width) * dy_row + later
                later = jnp.exp(gone8[i : i + 1, :] * rate) * lam
                kept = later * hs[base + i]
                total = total + kept * step8[i : i + 1, :]
                by_b[i] = jnp.sum(lam * lanes_like(bb[inner + i], width), axis=0, keepdims=True)
                by_rate[i] = jnp.sum(kept * rate, axis=0, keepdims=True)
                pb[inner + i] = fold(lam * drive8[i : i + 1, :])
                pc[inner + i] = fold(hs[base + i + 1] * dy_row)
            by_b = jnp.concatenate(by_b, axis=0)
            by_rate = jnp.concatenate(by_rate, axis=0)
            du[pl.ds(base, 8), :] = by_b * step8
            dstep[pl.ds(base, 8), :] = by_rate + by_b * u8
            return later, total

        carry = lax.fori_loop(0, piece // 8, eight, carry)
        add_lane_sums(dproj, start, ((pb, b_at), (pc, c_at)))
        return carry

    blank = jnp.zeros((count, width), f32)
    carry = (blank, blank)
    for start in reversed(range(0, rows, piece)):
        carry = part(start, carry)
        yield
    return carry[1] * rate


RANK_LANES = 128


def scan_kernel(proj, gone, drive, rate, y, bb, cb, *, b_at, c_at):
    run(scan_forward(proj, b_at, c_at, gone, drive, rate[...], bb, cb, y))


def adjoint_kernel(
    proj, step, gone, drive, inner_u, dy, rate, du, dstep, dproj, drate, bb, cb, hs, pb, pc, *, b_at, c_at
):
    run(scan_states(proj, b_at, gone, drive, rate[...], bb, hs))
    dproj[...] = jnp.zeros_like(dproj)
    kept = {}

    def adjoint():
        kept["rate"] = yield from scan_backward(
            proj, b_at, c_at, step, gone, drive, inner_u, dy, rate[...], hs, bb, cb, pb, pc, du, dstep, dproj
        )

    run(adjoint())
    drate[...] = kept["rate"]


def scan_sizes(rows, width, count):
    wide = 128 if width % 128 == 0 else width
    piece = min(128, rows)
    return pltpu.VMEM((piece, count, wide), f32)


def scan_alone(proj, gone, drive, rate, b_at, c_at):
    rows, width = drive.shape
    block = scan_sizes(rows, width, rate.shape[0])
    return pl.pallas_call(
        functools.partial(scan_kernel, b_at=b_at, c_at=c_at),
        out_shape=jax.ShapeDtypeStruct((rows, width), f32),
        scratch_shapes=[block, block],
        compiler_params=pltpu.CompilerParams(vmem_limit_bytes=VMEM_BYTES),
        name="scan_states",
    )(proj, gone, drive, rate)


def adjoint_alone(proj, step, gone, drive, inner_u, dy, rate, b_at, c_at):
    rows, width = step.shape
    count = rate.shape[0]
    block = scan_sizes(rows, width, count)
    shape = jax.ShapeDtypeStruct
    return pl.pallas_call(
        functools.partial(adjoint_kernel, b_at=b_at, c_at=c_at),
        out_shape=(
            shape((rows, width), f32),
            shape((rows, width), f32),
            shape(proj.shape, f32),
            shape((count, width), f32),
        ),
        scratch_shapes=[
            block,
            block,
            pltpu.VMEM((rows + 1, count, width), f32),
            block,
            block,
        ],
        compiler_params=pltpu.CompilerParams(vmem_limit_bytes=VMEM_BYTES),
        name="scan_adjoint",
    )(proj, step, gone, drive, inner_u, dy, rate)


PUMPS = ((0, 1, 1), (1, 0, 1), 0, (1, 2, 1), (1, 1), (0, 0, 0), (2, 2, 1), 0, 2)


def conv_sum(inner_x, place, taps, bias):
    count = taps.shape[0]
    total = bias + inner_x * taps[count - 1 : count, :]
    for shift in range(1, count):
        moved = jnp.where(place >= shift, pltpu.roll(inner_x, shift, 0), 0.0)
        total = total + moved * taps[count - 1 - shift : count - shift, :]
    return total


def transposed(left, right):
    return lax.dot_general(left, right, (((1,), (1,)), ((), ())), preferred_element_type=f32)


def over_rows(left, right):
    return lax.dot_general(left, right, (((0,), (0,)), ((), ())), preferred_element_type=f32)


def columns(d, size):
    return pl.ds(pl.multiple_of(d * size, size), size)


def line_total(own, arrived):
    total = own
    for k in range(arrived.shape[0]):
        total = total + arrived[k]
    return total


def forward_kernel(
    x, cot, lens, order, gain1, taps, bias, w_xp, w_dt, dt_bias, a_log, skip, gain2,
    w_x_h, w_z_h, w_out_h, w_gate_h, w_up_h, w_down_h,
    xg_o, cg_o, n1_o, s1_o, place_o, xi_o, z_o, proj_o, yv_o, go_all, h1_o, s2_o, n2_o, hid_all, dgu_o, dot_o, n1_mates, n2_mates, cg_mates, go_mates, hid_mates,
    w_x, w_z, w_out, w_gate, w_up, w_down, w_step, rate,
    x_all, c_all, sum_own, sum_in, low, xi_held, xi_left, xi_right, z_held, z_left, z_right,
    part_s, half_own, half_in, low_own, low_in, bb, cb, step, gone, drive,
    own, other, gu, gu_part, gu_held, gu_left, gu_right, dhid, h_held, h_left, h_right,
    w_sems, x_send, x_recv, c_send, c_recv, sum_send, sum_recv, xi_send, xi_recv, z_send, z_recv, t_send, t_recv,
    go_send, go_recv, o_send, o_recv, sum2_send, sum2_recv, gu_send, gu_recv, h_send, h_recv, hid_send, hid_recv, m_send, m_recv,
    *, model_width, rank, count, leave
):
    rows, width = xi_o.shape
    hidden = dgu_o.shape[1] // 2
    group, row = lax.axis_index("dp"), lax.axis_index("row")
    row_size = lax.axis_size("row")
    weights = fetch(
        (w_x_h, w_z_h, w_out_h, w_gate_h, w_up_h, w_down_h), (w_x, w_z, w_out, w_gate, w_up, w_down), w_sems
    )
    met = greet("dp", "row", "col")
    w_step[...] = jnp.zeros_like(w_step)
    w_step[0:rank, :] = w_dt[...]
    met()
    x_copies = plane_start(x, x_all, x_send, x_recv)
    lens_row = lengths_row(lens)
    source, place = place_rows(lens_row, as_row(order), lens.shape[1], rows, group)
    place_o[...] = place
    plane_finish(x_copies, x_all, x_send, x_recv)
    c_copies = plane_start(cot, c_all, c_send, c_recv)
    xg_low = pick_rows(source, x_all[...])
    xg_o[...] = xg_low
    xg = xg_low.astype(f32)
    gain1_now = as_row(gain1)
    low[...] = (xg * gain1_now).astype(bf16)
    weights[0].wait()
    kept = {}

    def during_xi():
        sum_own[...] = rows_form(xg * xg)
        sum_copies = spray("row", lambda k: sum_own, sum_in, sum_send, sum_recv)
        rate[...] = -jnp.exp(a_log[...])
        yield
        wait_all(sum_copies)
        kept["s1"] = column_form(lax.rsqrt(line_total(sum_own[...], sum_in) / model_width + epsilon))
        s1_o[...] = kept["s1"]
        leave("xg", "s1", "place")
        kept["cot"] = plane_swap(c_copies, c_all, c_send, c_recv)

    run(
        *scatter_halves(
            "row", lambda d, at: matmul(low[at, :], w_x[:, columns(d, width)]), xi_o, xi_held, xi_left, xi_right,
            xi_send, xi_recv,
        ),
        during_xi(),
    )
    weights[1].wait()
    z_flows = scatter_halves(
        "row", lambda d, at: matmul(low[at, :], w_z[:, columns(d, width)]), z_o, z_held, z_left, z_right, z_send, z_recv
    )
    for flow in z_flows:
        next(flow)
    s1 = kept["s1"]
    inner_x = xi_o[...] * s1
    xi_o[...] = inner_x
    u_low = silu(conv_sum(inner_x, place, taps[...], as_row(bias))).astype(bf16)
    u = u_low.astype(f32)
    part_s[...] = matmul(u_low, w_xp[...])

    def mix():
        yield from total_of_sums(part_s, half_own, half_in, low_own, low_in, proj_o, (t_send, t_recv))
        pre = matmul(proj_o[...].astype(bf16), w_step[...]) + as_row(dt_bias)
        step_now = jax.nn.softplus(pre)
        step[...] = step_now
        gone[...] = jnp.where(place > 0.0, step_now, 1e30)
        drive[...] = step_now * u
        yield from scan_forward(proj_o, rank, rank + count, gone, drive, rate[...], bb, cb, yv_o)

    mixing = mix()
    next(mixing)
    plane_wait(c_copies, kept["cot"])
    cg_o[...] = pick_rows(source, c_all[...])
    kept["mates"] = to_mates(cg_o, cg_mates, m_send.at[1], m_recv.at[1])
    next(mixing)
    run(*z_flows, mixing)
    yv = yv_o[...] + as_row(skip) * u
    yv_o[...] = yv
    z = z_o[...] * s1
    z_o[...] = z
    go_all[:, columns(row, width)] = (yv * silu(z)).astype(bf16)

    def during_gather():
        n1_o[...] = (xg * s1 * gain1_now).astype(bf16)
        kept["mates"] += to_mates(n1_o, n1_mates, m_send.at[0], m_recv.at[0])
        yield

    weights[5].wait()
    run(
        *gather_halves("row", go_all, width, go_send, go_recv),
        *scatter_halves(
            "row", lambda d, at: transposed(cg_o[at, :], w_down[columns(d, hidden), :]), dhid, h_held, h_left, h_right,
            h_send, h_recv,
        ),
        during_gather(),
    )
    kept["mates"] += quarters_to_mates(go_all, go_mates, m_send.at[3], m_recv.at[3])
    weights[2].wait()
    own[...] = matmul(go_all[...], w_out[...])
    copy = swap("col", own, other, o_send.at[0], o_recv.at[0])
    weights[3].wait()
    weights[4].wait()
    copy.wait()
    h1 = xg + (own[...] + other[...])
    h1_o[...] = h1
    gain2_now = as_row(gain2)
    low[...] = (h1 * gain2_now).astype(bf16)

    def gate_up_flows(first):
        rows_now, size = rows // 2, rows // 4

        def block_of(d, slot, part):
            side = columns(d, hidden)
            if part == 0:
                left = low[first : first + rows_now, :]
                gu_part[slot, :, 0:hidden] = matmul(left, w_gate[:, side])
                gu_part[slot, :, hidden:] = matmul(left, w_up[:, side])
            return gu_part[slot, part * size : (part + 1) * size, :]

        flows = []
        for part in range(2):
            at = pl.ds(first + part * size, size)
            number = first // size + part
            flows.append(
                line_scatter(
                    "row", functools.partial(block_of, part=part), gu.at[at, :], gu_held.at[:, at, :],
                    gu_left.at[:, at, :], gu_right.at[:, at, :], gu_send.at[number], gu_recv.at[number], slots=True,
                )
            )
        return flows

    def hid_flows(first, count):
        size = rows // 2 // count
        flows = []
        for part in range(count):
            at = pl.ds(first + part * size, size)

            def slot_of(d, at=at):
                return hid_all.at[at, columns(d, hidden)]

            number = first // (rows // 4) + part
            flows.append(line_gather("row", slot_of, hid_send.at[number], hid_recv.at[number]))
        return flows

    def activate(first):
        at = slice(first, first + rows // 2)
        s2 = s2_o[at, :]
        gate, up = gu[at, 0:hidden] * s2, gu[at, hidden:] * s2
        gu[at, 0:hidden], gu[at, hidden:] = gate, up
        sig = jax.nn.sigmoid(gate)
        act = gate * sig
        hid_all[at, columns(row, hidden)] = (act * up).astype(bf16)
        d_hid = dhid[at, :]
        dgu_o[at, 0:hidden] = (d_hid * up * (sig * (1.0 + gate * (1.0 - sig)))).astype(bf16)
        dgu_o[at, hidden:] = (d_hid * act).astype(bf16)

    def during_scatter():
        sum_own[...] = rows_form(h1 * h1)
        sum_copies = spray("row", lambda k: sum_own, sum_in, sum2_send, sum2_recv)
        yield
        wait_all(sum_copies)
        s2 = column_form(lax.rsqrt(line_total(sum_own[...], sum_in) / model_width + epsilon))
        s2_o[...] = s2
        n2_o[...] = (h1 * s2 * gain2_now).astype(bf16)
        leave("n1", "cg", "xi", "z", "proj", "yv", "go_all", "h1", "s2", "n2")
        kept["mates"] += to_mates(n2_o, n2_mates, m_send.at[2], m_recv.at[2])

    def dots():
        yield
        dot_o[...] = rows_form(dgu_o[...].astype(f32) * gu[...])

    run(*gate_up_flows(0), during_scatter())
    activate(0)
    run(*gate_up_flows(rows // 2), *hid_flows(0, 1))
    activate(rows // 2)
    top, bottom = pl.ds(0, rows // 2), pl.ds(rows // 2, rows // 2)
    kept["mates"] += quarters_to_mates(hid_all, hid_mates, m_send.at[4], m_recv.at[4], top)
    run(*hid_flows(rows // 2, 2), dots())
    kept["mates"] += quarters_to_mates(hid_all, hid_mates, m_send.at[5], m_recv.at[5], bottom)
    leave("hid_all", "dgu", "dot")
    wait_all(kept["mates"])
    leave("hid_mates", "n1_mates", "n2_mates", "cg_mates", "go_mates")
    leave.finish()


def dp_bits():
    me = lax.axis_index("dp")
    return lax.rem(me, 2), me // 2


def dp_mates():
    me = lax.axis_index("dp")
    along_x, along_y = dp_bits()
    return {"dp": me + 1 - 2 * along_x}, {"dp": me + 2 - 4 * along_y}


def to_mates(src, dst, send, recv):
    copies = [remote(src, dst.at[h], send.at[h], recv.at[h], mate) for h, mate in enumerate(dp_mates())]
    for copy in copies:
        copy.start()
    return copies


def quarters_to_mates(ref, dst, send, recv, rows=None):
    size = ref.shape[1] // 4
    at = pl.ds(0, ref.shape[0]) if rows is None else rows
    copies = []
    for h, (near, mate) in enumerate(zip(dp_bits(), dp_mates())):
        side = pl.ds(pl.multiple_of((2 * h + 1 - near) * size, size), size)
        copies.append(remote(ref.at[at, side], dst.at[h, at, :], send.at[h], recv.at[h], mate))
        copies[-1].start()
    return copies


def pair_sum(grad, sent, fixed, fixed_mates, by_rows, sent_in, second_in, third_in, send, recv, swapped="sent"):
    quarter = sent.shape[1] // 4
    eighth = (quarter if by_rows else grad.shape[0]) // 2
    bits, mates = dp_bits(), dp_mates()

    def side(h, near):
        return pl.ds(pl.multiple_of((2 * h + near) * quarter, quarter), quarter)

    def view(h, near, far):
        if by_rows:
            return grad.at[pl.ds(pl.multiple_of((2 * h + near) * quarter + far * eighth, eighth), eighth), :]
        return grad.at[pl.ds(pl.multiple_of(far * eighth, eighth), eighth), side(h, near)]

    class Half:
        def __init__(self, h):
            near, far = bits[h], bits[1 - h]
            mate, other = mates[h], mates[1 - h]

            def copy(stage, src, dst, to):
                return remote(src, dst, send.at[stage, h], recv.at[stage, h], to)

            self.h, self.near = h, near
            self.own, self.rest = view(h, near, far), view(h, near, 1 - far)
            there = view(h, 1 - near, far), view(h, 1 - near, 1 - far)
            first = None
            if swapped == "fixed":
                first = copy(0, fixed, fixed_mates.at[h], mate)
            elif swapped == "sent":
                first = copy(0, sent.at[:, side(h, 1 - near)], sent_in.at[h], mate)
            self.out = (
                first,
                copy(1, self.rest, second_in.at[h], other),
                copy(2, self.own, third_in.at[h], other),
                copy(3, self.own, self.own, mate),
                copy(4, self.rest, self.rest, mate),
            )
            self.back = (copy(3, there[0], there[0], mate), copy(4, there[1], there[1], mate))

        def product(self):
            mine, mates_part = sent[:, side(self.h, self.near)], sent_in[self.h]
            if by_rows:
                found = over_rows(mine, fixed[...]) + over_rows(mates_part, fixed_mates[self.h])
                grad[side(self.h, self.near), :] = found.astype(bf16)
            else:
                found = over_rows(fixed[...], mine) + over_rows(fixed_mates[self.h], mates_part)
                grad[:, side(self.h, self.near)] = found.astype(bf16)

    both_halves = (Half(0), Half(1))
    if swapped:
        for half in both_halves:
            half.out[0].start()
        yield
    for half in both_halves:
        if swapped:
            half.out[0].wait_recv()
        half.product()
        half.out[1].start()
    yield
    for half in both_halves:
        half.out[1].wait_recv()
        add_view(half.own, second_in.at[half.h], eighth)
        half.out[2].start()
        half.out[3].start()
    yield
    for half in both_halves:
        half.out[2].wait_recv()
        half.out[1].wait_send()
        half.rest[...] = third_in[half.h]
        half.out[4].start()
    yield
    for half in both_halves:
        for copy in half.back:
            copy.wait_recv()
        for stage in (0, 2, 3, 4) if swapped else (2, 3, 4):
            half.out[stage].wait_send()


def add_view(target, source, rows):
    def piece(j, _):
        at = pl.ds(pl.multiple_of(j * 16, 16), 16)
        target[at, :] = (target[at, :].astype(f32) + source[at, :].astype(f32)).astype(bf16)
        return 0

    lax.fori_loop(0, rows // 16, piece, 0)


def add_rows(target, base, source, rows):
    def piece(j, _):
        at = pl.ds(pl.multiple_of(base + j * 16, 16), 16)
        found = target[at, :].astype(f32) + source[pl.ds(pl.multiple_of(j * 16, 16), 16), :].astype(f32)
        target[at, :] = found.astype(target.dtype)
        return 0

    lax.fori_loop(0, rows // 16, piece, 0)


def plane_sum(grad, first_in, second_in, send, recv, free):
    quarter = grad.shape[0] // 4
    eighth = quarter // 2
    bits, partners = dp_bits(), dp_mates()

    def rows(ref, start, count):
        return ref.at[pl.ds(pl.multiple_of(start, 16), count), :]

    class Half:
        def __init__(self, h):
            near, far = bits[h], bits[1 - h]
            self.free, self.mate, self.first = free.at[h], partners[h], first_in.at[h]
            base = h * 2 * quarter
            self.kept = base + near * quarter
            self.own = self.kept + far * eighth
            self.rest = self.kept + (1 - far) * eighth
            self.rest_in = (1 - far) * eighth
            across = base + (1 - near) * quarter
            self.second = second_in.at[h]

            def copy(stage, src, dst, to):
                return remote(src, dst, send.at[stage, h], recv.at[stage, h], to)

            mate, other = partners[h], partners[1 - h]
            own, rest = rows(grad, self.own, eighth), rows(grad, self.rest, eighth)
            there = (rows(grad, across + far * eighth, eighth), rows(grad, across + (1 - far) * eighth, eighth))
            back = rows(self.first, self.rest_in, eighth)
            self.out = (
                copy(0, rows(grad, across, quarter), self.first, mate),
                copy(1, rest, self.second, other),
                copy(2, own, rows(self.first, far * eighth, eighth), other),
                copy(3, own, own, mate),
                copy(4, rest, rest, mate),
            )
            self.back = (
                None,
                None,
                copy(2, back, back, other),
                copy(3, there[0], there[0], mate),
                copy(4, there[1], there[1], mate),
            )

    halves = (Half(0), Half(1))
    for half in halves:
        half.out[0].start()
    yield
    for half in halves:
        half.out[0].wait_recv()
        add_rows(grad, half.kept, half.first, quarter)
        half.out[1].start()
        half.out[0].wait_send()
        pl.semaphore_signal(half.free, inc=1, device_id=half.mate, device_id_type=MESH)
    yield
    for half in halves:
        half.out[1].wait_recv()
        add_rows(grad, half.own, half.second, eighth)
        half.out[2].start()
        pl.semaphore_wait(half.free, 1)
        half.out[3].start()
    yield
    for half in halves:
        half.back[2].wait_recv()
        half.out[1].wait_send()
        grad[pl.ds(pl.multiple_of(half.rest, 16), eighth), :] = half.first[
            pl.ds(pl.multiple_of(half.rest_in, 16), eighth), :
        ]
        half.out[4].start()
    yield
    for half in halves:
        half.back[3].wait_recv()
        half.back[4].wait_recv()
        for copy in half.out[2:]:
            copy.wait_send()


class Sums:
    def __init__(self):
        self.active = []

    def add(self, flow):
        next(flow)
        self.active.append(flow)

    def pump(self, count=1):
        for _ in range(count):
            if self.active:
                flow = self.active.pop(0)
                if next(flow, self) is not self:
                    self.active.append(flow)

    def drain(self):
        while self.active:
            self.pump()


def backward_kernel(
    lens, order, gain2, taps, bias, w_xp, w_dt, dt_bias, a_log, skip, gain1,
    w_gate_h, w_up_h, w_down_h, w_out_h, w_x_h, w_z_h,
    y_o, dx_o, small_o, g_down_o, g_gate_o, g_up_o, g_z_o, g_x_o, g_out_o,
    w_gate, w_up, w_down, w_out, w_x, w_z, w_step, rate,
    dg_all, du_all, dz_all, dxi_all, dh1, dmix, y_own, dx_own, y_all, dx_all,
    own, other, y_part, y_other, dot_in, dot_own, dot_sum, dot_other,
    dgo, d_held, d_left, d_right,
    hs, bb, cb, pb, pc, step, gone, drive, u_s, dy_s, du_s, dstep, dproj,
    half_own, half_in, low_own, low_in, full,
    g_down, g_gate, g_up, g_z, g_x, g_out, small,
    g_gate_1, g_up_1, g_z_1, g_x_1, small_1,
    g_down_2, g_gate_2, g_up_2, g_z_2, g_x_2, g_out_2, small_2,
    g_down_3, g_gate_3, g_up_3, g_z_3, g_x_3, g_out_3, dmix_mates,
    w_sems, g_send, g_recv, u_send, u_recv, o_send, o_recv, dot_send, dot_recv,
    y_send, y_recv, dx_send, dx_recv, d_send, d_recv, z_send, z_recv, t_send, t_recv, x_send, x_recv,
    dot2_send, dot2_recv, sum_send, sum_recv, sum_free, write_sems,
    *, rank, model_width, late
):
    rows, width = dgo.shape
    count = rate.shape[0]
    block = y_o.shape[0]
    tap_count = taps.shape[0]
    group, row, column = lax.axis_index("dp"), lax.axis_index("row"), lax.axis_index("col")
    row_size, col_size = lax.axis_size("row"), lax.axis_size("col")
    weights = fetch(
        (w_down_h, w_gate_h, w_up_h, w_out_h, w_x_h, w_z_h), (w_down, w_gate, w_up, w_out, w_x, w_z), w_sems
    )
    half = columns(column, block)
    sums = Sums()
    writes = []

    def write(number, grad, result):
        copy = pltpu.make_async_copy(grad, result, write_sems.at[number])
        copy.start()
        writes.append(copy)

    def total(number, grad, first_in, second_in, result):
        yield from plane_sum(
            grad, first_in, second_in, sum_send.at[number], sum_recv.at[number], sum_free.at[number]
        )
        write(number, grad, result)

    def pair(number, grad, sent, fixed, fixed_mates, by_rows, ins, result, swapped="sent"):
        yield from pair_sum(
            grad, sent, fixed, fixed_mates, by_rows, *ins, sum_send.at[number], sum_recv.at[number], swapped
        )
        write(number, grad, result)

    met = greet("dp", "row", "col")
    dgu = late("dgu")
    hidden = dgu.shape[1] // 2
    dg_all[:, columns(row, hidden)] = dgu[:, 0:hidden]
    du_all[:, columns(row, hidden)] = dgu[:, hidden:]
    dot, hid_all, cg, cg_mates = late("dot"), late("hid_all"), late("cg"), late("cg_mates")
    hid_mates = late("hid_mates")
    met()
    dot_copies = spray("row", lambda k: dot, dot_in, dot_send, dot_recv)

    def first_work():
        sums.add(pair(0, g_down, hid_all, cg, cg_mates, True, (hid_mates, g_down_2, g_down_3), g_down_o, None))
        yield
        weights[0].wait()
        y_part[...] = matmul(hid_all[...], w_down[...])
        y_copy = swap("col", y_part, y_other, o_send.at[0], o_recv.at[0])
        yield
        wait_all(dot_copies)
        dot_own[...] = line_total(dot[...], dot_in)
        dot_copy = swap("col", dot_own, dot_other, o_send.at[2], o_recv.at[2])
        weights[1].wait()
        weights[2].wait()
        yield
        y_copy.wait()
        dot_copy.wait()
        y_own[...] = (late("h1")[...] + (y_part[...] + y_other[...])).astype(bf16)

    run(*gather_halves("row", dg_all, hidden, g_send, g_recv), first_work(), pump=(sums, PUMPS[0]))
    n2, n2_mates = late("n2"), late("n2_mates")
    sums.add(pair(1, g_gate, dg_all, n2, n2_mates, False, (g_gate_1, g_gate_2, g_gate_3), g_gate_o))

    def second_work():
        own[...] = transposed(dg_all[...], w_gate[...])
        yield

    run(*gather_halves("row", du_all, hidden, u_send, u_recv), second_work(), pump=(sums, PUMPS[1]))
    own[...] += transposed(du_all[...], w_up[...])
    copy = swap("col", own, other, o_send.at[1], o_recv.at[1])
    sums.add(pair(2, g_up, du_all, n2, n2_mates, False, (g_up_1, g_up_2, g_up_3), g_up_o))
    sums.pump(PUMPS[2])
    copy.wait()
    h1_now, s2_now = late("h1")[...], late("s2")[...]
    dn2 = own[...] + other[...]
    dots = column_form(dot_own[...] + dot_other[...])
    dh1_now = (
        cg[...].astype(f32)
        + s2_now * (as_row(gain2) * dn2)
        - h1_now * (s2_now * s2_now * dots / model_width)
    )
    dh1[...] = dh1_now
    dmix[...] = dh1_now.astype(bf16)
    gnorm2 = jnp.sum(dn2 * h1_now * s2_now, axis=0, keepdims=True)

    inner_x = late("xi")[...]
    place_now = late("place")[...]
    proj = late("proj")
    kept = {}

    def states():
        go_all = late("go_all")
        sums.add(
            pair(5, g_out, go_all, dmix, dmix_mates, True, (late("go_mates"), g_out_2, g_out_3), g_out_o, "fixed")
        )
        w_step[...] = jnp.zeros_like(w_step)
        w_step[0:rank, :] = w_dt[...]
        rate[...] = -jnp.exp(a_log[...])
        xc = conv_sum(inner_x, place_now, taps[...], as_row(bias))
        sig_c = jax.nn.sigmoid(xc)
        u_low = (xc * sig_c).astype(bf16)
        u = u_low.astype(f32)
        u_s[...] = u
        step_low = proj[...].astype(bf16)
        pre = matmul(step_low, w_step[...]) + as_row(dt_bias)
        step_now = jax.nn.softplus(pre)
        step[...] = step_now
        gone[...] = jnp.where(place_now > 0.0, step_now, 1e30)
        drive[...] = step_now * u
        kept.update(xc=xc, sig_c=sig_c, u_low=u_low, u=u, step_low=step_low, pre=pre)
        yield from scan_states(proj, rank, gone, drive, rate[...], bb, hs)

    weights[3].wait()
    run(
        *scatter_halves(
            "row", lambda d, at: transposed(dmix[at, :], w_out[columns(d, width), :]), dgo, d_held, d_left, d_right,
            d_send, d_recv,
        ),
        states(),
        pump=(sums, PUMPS[3]),
    )
    xc, sig_c, u_low, u = kept["xc"], kept["sig_c"], kept["u_low"], kept["u"]
    step_low, pre = kept["step_low"], kept["pre"]
    z_now = late("z")[...]
    sig_z = jax.nn.sigmoid(z_now)
    d_z = (dgo[...] * late("yv")[...] * (sig_z * (1.0 + z_now * (1.0 - sig_z)))).astype(bf16)
    mine = dz_all.at[:, columns(row, width)]
    mine[...] = d_z
    z_copies = []
    for k in range(1, row_size):
        copy = remote(mine, mine, z_send.at[k - 1], z_recv.at[k - 1], away("row", k))
        copy.start()
        z_copies.append(copy)
    dy = dgo[...] * (z_now * sig_z)
    dy_s[...] = dy
    dproj[...] = jnp.zeros_like(dproj)

    def adjoint():
        kept["rate"] = yield from scan_backward(
            proj, rank, rank + count, step, gone, drive, u_s, dy_s, rate[...], hs, bb, cb, pb, pc, du_s, dstep, dproj
        )

    run(adjoint(), pump=(sums, PUMPS[4]))
    g_rate = kept["rate"]
    d_pre = dstep[...] * jax.nn.sigmoid(pre)
    d_pre_low = d_pre.astype(bf16)
    dproj[...] += transposed(d_pre_low, w_step[...])

    def during_sums():
        yield
        wait_all(z_copies)
        sums.add(pair(3, g_z, dz_all, late("n1"), late("n1_mates"), False, (g_z_1, g_z_2, g_z_3), g_z_o))

    run(
        total_of_sums(dproj, half_own, half_in, low_own, low_in, full, (t_send, t_recv)),
        during_sums(),
        pump=(sums, PUMPS[5]),
    )
    dproj_low = full[...].astype(bf16)
    du = du_s[...] + as_row(skip) * dy + transposed(dproj_low, w_xp[...])
    dxc = du * (sig_c * (1.0 + xc * (1.0 - sig_c)))
    taps_now = taps[...]
    d_inner = dxc * taps_now[tap_count - 1 : tap_count, :]
    masked = [dxc]
    for shift in range(1, tap_count):
        masked.append(jnp.where(place_now >= shift, dxc, 0.0))
        k = tap_count - 1 - shift
        d_inner = d_inner + pltpu.roll(masked[shift], rows - shift, 0) * taps_now[k : k + 1, :]
    d_inner = d_inner.astype(bf16)
    dxi_all[:, columns(row, width)] = d_inner

    def during():
        dot_own[...] = rows_form(d_inner.astype(f32) * inner_x + d_z.astype(f32) * z_now)
        dot_copies = spray("row", lambda k: dot_own, dot_in, dot2_send, dot2_recv)
        small[0:RANK_LANES, :] = over_rows(dproj_low, u_low).astype(bf16)
        small[RANK_LANES : RANK_LANES + rank, :] = over_rows(step_low, d_pre_low)[0:rank, :].astype(bf16)
        yield
        wait_all(dot_copies)
        dot_sum[...] = line_total(dot_own[...], dot_in)
        dot_copy = swap("col", dot_sum, dot_other, o_send.at[3], o_recv.at[3])
        weights[4].wait()
        weights[5].wait()
        own[...] = transposed(dz_all[...], w_z[...])
        yield
        dot_copy.wait()

    run(*gather_halves("row", dxi_all, width, x_send, x_recv), during(), pump=(sums, PUMPS[6]))
    own[...] += transposed(dxi_all[...], w_x[...])
    copy = swap("col", own, other, o_send.at[4], o_recv.at[4])
    sums.add(pair(4, g_x, dxi_all, late("n1"), late("n1_mates"), False, (g_x_1, g_x_2, g_x_3), g_x_o))
    sums.pump(PUMPS[7])
    copy.wait()
    dn1 = own[...] + other[...]
    s1_now = late("s1")[...]
    xg_now = late("xg")[...].astype(f32)
    dots = column_form(dot_sum[...] + dot_other[...])
    dx = dh1[...] + s1_now * (as_row(gain1) * dn1) - xg_now * (s1_now * s1_now * dots / model_width)
    dx_own[...] = dx.astype(bf16)
    dx_copies = plane_start(dx_own.at[half], dx_all, dx_send, dx_recv)
    y_copies = plane_start(y_own.at[half], y_all, y_send, y_recv)
    g_taps = [None] * tap_count
    for shift in range(tap_count):
        moved = pltpu.roll(inner_x, shift, 0) if shift else inner_x
        g_taps[tap_count - 1 - shift] = jnp.sum(masked[shift] * moved, axis=0, keepdims=True)
    pieces = [
        g_rate,
        *g_taps,
        jnp.sum(dxc, axis=0, keepdims=True),
        jnp.sum(d_pre, axis=0, keepdims=True),
        jnp.sum(dy * u, axis=0, keepdims=True),
        jnp.sum(dn1 * xg_now * s1_now, axis=0, keepdims=True),
        gnorm2,
    ]
    found = sum(piece.shape[0] for piece in pieces)
    pieces.append(jnp.zeros((small.shape[0] - RANK_LANES - rank - found, width), f32))
    small[RANK_LANES + rank :, :] = jnp.concatenate(pieces, axis=0).astype(bf16)
    sums.add(total(6, small, small_1, small_2, small_o))
    first = (group * col_size + column) * block
    wanted = owner_rows(lengths_row(lens), as_row(order), lens.shape[1], rows, block, first)
    sums.pump(PUMPS[8])
    plane_finish(dx_copies, dx_all, dx_send, dx_recv)
    dx_o[...] = pick_rows(wanted, dx_all[...])
    plane_finish(y_copies, y_all, y_send, y_recv)
    y_o[...] = pick_rows(wanted, y_all[...])
    sums.drain()
    for write in writes:
        write.wait()


def finish_kernel(
    y, dx, small, down, gate, up, z, x, out,
    y_o, dx_o, norm1_o, z_o, x_o, taps_o, bias_o, w_xp_o, w_dt_o, dt_bias_o, rate_o, skip_o, out_o, norm2_o, gate_o,
    up_o, down_o,
    *, rank
):
    for source, target in ((z, z_o), (x, x_o), (out, out_o), (gate, gate_o), (up, up_o), (down, down_o)):
        target[...] = source[...].astype(f32)

    @pl.when(pl.program_id(0) == 0)
    def _():
        y_o[...] = y[...]
        dx_o[...] = dx[...]
        values = small[...].astype(f32)
        w_xp_o[...] = jnp.transpose(values[0:RANK_LANES, :])
        w_dt_o[...] = values[RANK_LANES : RANK_LANES + rank, :]
        at = RANK_LANES + rank
        for target in (rate_o, taps_o):
            target[...] = values[at : at + target.shape[0], :]
            at += target.shape[0]
        for target in (bias_o, dt_bias_o, skip_o, norm1_o, norm2_o):
            target[...] = values[at : at + 1, :].reshape(target.shape)
            at += 1


VMEM_BYTES = 60 << 20
DMA = pltpu.SemaphoreType.DMA


def in_vmem(kernel, name, ident, outs, scratch, args, far=(), far_outs=(), late=None, leave=None):
    late, leave = late or {}, leave or {}
    space = pl.BlockSpec(memory_space=pltpu.VMEM)
    anywhere = pl.BlockSpec(memory_space=pl.ANY)
    heads, tails, before, after = len(args) + len(far), len(outs) + len(far_outs), len(late), len(leave)

    def whole(*refs):
        at = [0]

        def take(count):
            at[0] += count
            return refs[at[0] - count : at[0]]

        head, sources, tail, targets = take(heads), take(before), take(tails), take(after)
        middle = take(len(scratch))
        keywords = {}
        if late:
            held = take(before)
            keywords["late"] = Late(list(late), sources, held, take(1)[0])
        held = take(after)
        if leave:
            keywords["leave"] = Leave(list(leave), held, targets, take(1)[0])
        kernel(*head, *tail, *held, *middle, **keywords)

    own = list(scratch)
    if late:
        own += [pltpu.VMEM(value.shape, value.dtype) for value in late.values()] + [DMA((before,))]
    if leave:
        own += [pltpu.VMEM(shape, kind) for shape, kind in leave.values()] + [DMA((after,))]
    return pl.pallas_call(
        whole,
        out_shape=tuple(jax.ShapeDtypeStruct(shape, kind) for shape, kind in [*outs, *far_outs, *leave.values()]),
        in_specs=[space] * len(args) + [anywhere] * (len(far) + before),
        out_specs=tuple([space] * len(outs) + [anywhere] * (len(far_outs) + after)),
        scratch_shapes=own,
        compiler_params=pltpu.CompilerParams(
            collective_id=ident, has_side_effects=ident is not None, vmem_limit_bytes=VMEM_BYTES
        ),
        name=name,
    )(*args, *far, *late.values())


def both(*shape):
    return [DMA(shape), DMA(shape)]


def on_pairs(
    x_in, lengths, seq_order, norm1_gain, w_in_x, w_in_z, conv_w, conv_b, w_xp, w_dt, dt_bias, a_log,
    skip_weight, w_out, norm2_gain, w_gate, w_up, w_down, cotangent,
):
    dp, rs = lax.axis_size("dp"), lax.axis_size("row")
    block, wide_d = x_in.shape
    rows = block * 2
    model_width = wide_d * rs
    width = conv_w.shape[0]
    hidden = w_gate.shape[1] // rs
    rank, count, taps = w_dt.shape[0], a_log.shape[1], conv_w.shape[1]
    conv_taps = conv_w.T
    rates = a_log.T
    vm = pltpu.VMEM
    tile = vm((128, count, 128), f32)
    big = vm((rows, width), f32)
    model = vm((rows, wide_d), f32)
    sums = [vm((8, rows), f32), vm((rs - 1, 8, rows), f32)]
    sums_scratch = [
        vm((rows // 2, RANK_LANES), f32),
        vm((rows // 2, RANK_LANES), f32),
        vm((rows // 2, RANK_LANES), bf16),
        vm((rs - 1, rows // 2, RANK_LANES), bf16),
    ]

    def weight(value):
        return vm(value.shape, value.dtype)

    def line(size, width):
        return [vm((size, rows, width), bf16)] * 3

    leave = {
        "xg": ((rows, wide_d), bf16), "cg": ((rows, wide_d), bf16), "n1": ((rows, wide_d), bf16),
        "s1": ((rows, 1), f32), "place": ((rows, 1), f32), "xi": ((rows, width), f32), "z": ((rows, width), f32),
        "proj": ((rows, RANK_LANES), f32), "yv": ((rows, width), f32), "go_all": ((rows, rs * width), bf16),
        "h1": ((rows, wide_d), f32), "s2": ((rows, 1), f32), "n2": ((rows, wide_d), bf16),
        "hid_all": ((rows, rs * hidden), bf16), "dgu": ((rows, 2 * hidden), bf16), "dot": ((8, rows), f32),
        "n1_mates": ((2, rows, wide_d), bf16), "n2_mates": ((2, rows, wide_d), bf16),
        "cg_mates": ((2, rows, wide_d), bf16), "go_mates": ((2, rows, width), bf16),
        "hid_mates": ((2, rows, hidden), bf16),
    }
    passed = in_vmem(
        functools.partial(forward_kernel, model_width=model_width, rank=rank, count=count),
        "forward",
        0,
        [],
        [
            weight(w_in_x), weight(w_in_z), weight(w_out), weight(w_gate), weight(w_up), weight(w_down),
            vm((RANK_LANES, width), bf16), vm((count, width), f32),
            vm((2, dp, block, wide_d), bf16), vm((2, dp, block, wide_d), bf16), *sums, vm((rows, wide_d), bf16),
            *line(rs, width), *line(rs, width),
            vm((rows, RANK_LANES), f32), *sums_scratch, tile, tile, big, big, big,
            model, model, vm((rows, 2 * hidden), f32), vm((3, rows // 2, 2 * hidden), f32), *line(rs, 2 * hidden), vm((rows, hidden), f32), *line(rs, hidden),
            DMA((6,)), *both(dp), *both(dp), *both(rs - 1), *both(2, 2, rs), *both(2, 2, rs), *both(rs + 1),
            *both(2, 2, rs), *both(1), *both(rs - 1), *both(4, 2, rs), *both(2, 2, rs), *both(4, 2, rs), *both(6, 2),
        ],
        (
            x_in, cotangent, lengths, seq_order, norm1_gain, conv_taps, conv_b, w_xp, w_dt, dt_bias, rates, skip_weight,
            norm2_gain,
        ),
        (w_in_x, w_in_z, w_out, w_gate, w_up, w_down),
        leave=leave,
    )
    passed = dict(zip(leave, passed))
    first = ("dgu", "dot", "hid_all", "hid_mates", "cg", "cg_mates", "n2", "n2_mates")
    late = {name: passed[name] for name in (*first, *(name for name in passed if name not in first))}

    def sizes(value, parts):
        return vm((2, value[0] // parts, value[1]), bf16)

    def eighths(value):
        return vm((2, value[0] // 8, value[1]) if value in (d_cols, grads[5]) else (2, value[0] // 2, value[1] // 4), bf16)

    d_cols, f_cols, e_cols = (rs * hidden, wide_d), (wide_d, rs * hidden), (wide_d, rs * width)
    grads = (d_cols, f_cols, f_cols, e_cols, e_cols, (rs * width, wide_d), (2 * RANK_LANES, width))
    returned = in_vmem(
        functools.partial(backward_kernel, rank=rank, model_width=model_width),
        "backward",
        1,
        [((block, wide_d), bf16), ((block, wide_d), bf16)],
        [
            weight(w_gate), weight(w_up), weight(w_down), weight(w_out), weight(w_in_x), weight(w_in_z),
            vm((RANK_LANES, width), bf16), vm((count, width), f32),
            vm((rows, rs * hidden), bf16), vm((rows, rs * hidden), bf16),
            vm((rows, rs * width), bf16), vm((rows, rs * width), bf16),
            model, vm((rows, wide_d), bf16), vm((rows, wide_d), bf16), vm((rows, wide_d), bf16),
            vm((2, dp, block, wide_d), bf16), vm((2, dp, block, wide_d), bf16),
            model, model, model, model, vm((rs - 1, 8, rows), f32), vm((8, rows), f32), vm((8, rows), f32),
            vm((8, rows), f32), big, *line(rs, width),
            vm((rows + 1, count, width), f32), tile, tile, tile, tile,
            big, big, big, big, big, big, big, vm((rows, RANK_LANES), f32), *sums_scratch, vm((rows, RANK_LANES), f32),
            *[vm(value, bf16) for value in grads],
            *[vm((2, rows, max(value) // 4), bf16) for value in grads[1:5]], sizes(grads[6], 4),
            *[eighths(value) for value in grads[:6]], sizes(grads[6], 8),
            *[eighths(value) for value in grads[:6]], vm((2, rows, wide_d), bf16),
            DMA((6,)), *both(2, 2, rs), *both(2, 2, rs), *both(5), *both(rs - 1), *both(dp), *both(dp), *both(2, 2, rs),
            *both(rs - 1), *both(rs + 1), *both(2, 2, rs), *both(rs - 1), *both(len(grads), 5, 2),
            pltpu.SemaphoreType.REGULAR((len(grads), 2)), DMA((len(grads),)),
        ],
        (
            lengths, seq_order, norm2_gain, conv_taps, conv_b, w_xp, w_dt, dt_bias, rates, skip_weight, norm1_gain,
        ),
        (w_gate, w_up, w_down, w_out, w_in_x, w_in_z),
        [(value, bf16) for value in (grads[-1], *grads[:-1])],
        late,
    )
    steps = 2

    def pieces(value):
        return pl.BlockSpec((value[0] // steps, value[1]), lambda i: (i, 0))

    def whole(*shape):
        return pl.BlockSpec(shape, lambda i: (0,) * len(shape))

    rows_spec = whole(block, wide_d)
    shape = jax.ShapeDtypeStruct
    outs = (
        (rows_spec, (block, wide_d), bf16), (rows_spec, (block, wide_d), bf16), (whole(wide_d), (wide_d,), f32),
        (pieces(e_cols), e_cols, f32), (pieces(e_cols), e_cols, f32), (whole(taps, width), (taps, width), f32),
        (whole(width), (width,), f32), (whole(width, RANK_LANES), (width, RANK_LANES), f32),
        (whole(rank, width), (rank, width), f32), (whole(width), (width,), f32),
        (whole(count, width), (count, width), f32), (whole(width), (width,), f32), (pieces(grads[5]), grads[5], f32),
        (whole(wide_d), (wide_d,), f32), (pieces(f_cols), f_cols, f32), (pieces(f_cols), f_cols, f32),
        (pieces(d_cols), d_cols, f32),
    )
    results = pl.pallas_call(
        functools.partial(finish_kernel, rank=rank),
        grid=(steps,),
        in_specs=[rows_spec, rows_spec, whole(2 * RANK_LANES, width), *[pieces(value) for value in grads[:-1]]],
        out_specs=tuple(spec for spec, _, _ in outs),
        out_shape=tuple(shape(size, kind) for _, size, kind in outs),
        compiler_params=pltpu.CompilerParams(vmem_limit_bytes=VMEM_BYTES),
        name="finish",
    )(*returned)
    (y_out, dx_out, norm1, g_z, g_x, g_taps, g_bias, g_xp, g_dt, g_dt_bias, g_rate, g_skip, g_out, norm2, g_gate, g_up,
     g_down) = results
    return (
        y_out, dx_out, norm1, g_x, g_z, g_taps.T, g_bias, g_xp, g_dt, g_dt_bias, g_rate.T, g_skip, g_out, norm2,
        g_gate, g_up, g_down,
    )


def on_device(
    x_in,
    lengths,
    seq_order,
    norm1_gain,
    w_in_x,
    w_in_z,
    conv_w,
    conv_b,
    w_xp,
    w_dt,
    dt_bias,
    a_log,
    skip_weight,
    w_out,
    norm2_gain,
    w_gate,
    w_up,
    w_down,
    cotangent,
):
    rows_in, width_row = x_in.shape
    row_devices = lax.axis_size("row")
    col_devices = lax.axis_size("col")
    group_rows = rows_in * col_devices
    model_width = width_row * row_devices
    rank_cols = w_dt.shape[0]
    state_count = a_log.shape[1]
    channels = conv_w.shape[0]
    ff_cols = w_gate.shape[1]
    my_group = lax.axis_index("dp")
    my_column = lax.axis_index("col")
    source, position_all = layout(lengths, seq_order, group_rows)
    my_source = lax.dynamic_index_in_dim(source, my_group, 0, keepdims=False)
    position = lax.dynamic_index_in_dim(position_all, my_group, 0, keepdims=False)
    slice_source = lax.dynamic_slice_in_dim(my_source, my_column * rows_in, rows_in, 0)

    def row_total(values):
        return lax.psum(values, "row")

    def token_rows(values):
        return lax.all_gather(values, "col", axis=0, tiled=True)

    def row_pieces(values):
        return lax.all_gather(values, "row", axis=0, tiled=True)

    def col_reduce(term_fn):
        return lax.psum_scatter(
            term_fn(jnp.int32(0), lax.axis_size("col") * rows_in),
            "col",
            scatter_dimension=0,
            tiled=True,
        )

    def row_reduce(term_fn, keep_rows):
        return lax.psum_scatter(
            term_fn(jnp.int32(0), lax.axis_size("row") * keep_rows),
            "row",
            scatter_dimension=0,
            tiled=True,
        )

    def projection_total(values):
        return lax.psum(values, ("row", "col"))

    blank_rows = jnp.zeros((rows_in, width_row), jnp.bfloat16)
    pieces = (
        lax.all_gather(x_in, ("dp", "col"), axis=0, tiled=True),
        lax.all_gather(cotangent, ("dp", "col"), axis=0, tiled=True),
    )
    row_count = pieces[0].shape[0]
    offset = slice_source
    inside = ((offset >= 0) & (offset < row_count))[:, None]
    index = jnp.clip(offset, 0, row_count - 1)
    x_rows = jnp.where(inside, jnp.take(pieces[0], index, axis=0), blank_rows)
    cot_rows = jnp.where(inside, jnp.take(pieces[1], index, axis=0), blank_rows)
    x_val = x_rows.astype(jnp.float32)
    scale_one = lax.rsqrt(row_total(jnp.sum(x_val * x_val, axis=1)) / model_width + epsilon)
    normed_one = (x_val * scale_one[:, None] * norm1_gain[None, :]).astype(jnp.bfloat16)
    normed_all = token_rows(normed_one)

    def inner_term(begin_row, row_count):
        return jnp.concatenate(
            [contract(w_in_x, normed_all, 0, 1), contract(w_in_z, normed_all, 0, 1)], axis=1
        )

    inner = row_reduce(inner_term, channels)
    inner_x = inner[:, :group_rows]
    inner_z = inner[:, group_rows:]

    def conv_part(values, kernel, kernel_bias):
        return convolve(values, kernel, kernel_bias, position)

    conv_out, conv_pull = jax.vjp(conv_part, inner_x, conv_w, conv_b)
    u_low = conv_out.astype(jnp.bfloat16)
    u_val = u_low.astype(jnp.float32)
    projected = projection_total(contract(w_xp, u_low, 0, 0))
    step_low = projected[:rank_cols].astype(jnp.bfloat16)
    pre_step = contract(w_dt, step_low, 0, 0) + dt_bias[:, None]
    step_size = jax.nn.softplus(pre_step)

    decay_rate = -jnp.exp(a_log).T
    proj_rows = projected.T
    u_rows = u_val.T
    step_rows = step_size.T
    gone_rows = jnp.where(position[:, None] > 0, step_rows, 1e30)
    drive_rows = step_rows * u_rows
    at_b, at_c = rank_cols, rank_cols + state_count
    scanned = scan_alone(proj_rows, gone_rows, drive_rows, decay_rate, at_b, at_c)
    mixer_y = scanned.T + skip_weight[:, None] * u_val
    gated = mixer_y * jax.nn.silu(inner_z)
    gated_low = gated.astype(jnp.bfloat16)
    gated_all = row_pieces(gated_low)

    def mix_term(begin_row, row_count):
        return contract(gated_all, w_out, 0, 0)

    first_sum = x_val + col_reduce(mix_term)
    scale_two = lax.rsqrt(row_total(jnp.sum(first_sum * first_sum, axis=1)) / model_width + epsilon)
    normed_two = (first_sum * scale_two[:, None] * norm2_gain[None, :]).astype(jnp.bfloat16)
    normed_rows = token_rows(normed_two)

    def ffn_term(begin_row, row_count):
        return jnp.concatenate(
            [
                jnp.dot(normed_rows, w_gate, preferred_element_type=jnp.float32),
                jnp.dot(normed_rows, w_up, preferred_element_type=jnp.float32),
            ],
            axis=1,
        )

    gate_up = row_reduce(ffn_term, group_rows // row_devices)
    gate_val = gate_up[:, :ff_cols]
    up_val = gate_up[:, ff_cols:]
    hidden = (jax.nn.silu(gate_val) * up_val).astype(jnp.bfloat16)
    hidden_all = row_pieces(hidden)

    def down_term(begin_row, row_count):
        return jnp.dot(hidden_all, w_down, preferred_element_type=jnp.float32)

    second_sum = first_sum + col_reduce(down_term)
    out_low = second_sum.astype(jnp.bfloat16)
    back_down_all = token_rows(cot_rows)
    grad_down = contract(hidden_all, back_down_all, 0, 0)

    def hidden_term(begin_row, row_count):
        return contract(back_down_all, w_down, 1, 1)

    d_hidden = row_reduce(hidden_term, group_rows // row_devices)
    d_gate = (d_hidden * up_val * silu_slope(gate_val)).astype(jnp.bfloat16)
    d_up = (d_hidden * jax.nn.silu(gate_val)).astype(jnp.bfloat16)
    d_gate_up_all = row_pieces(jnp.concatenate([d_gate, d_up], axis=1))
    grad_gate = contract(normed_rows, d_gate_up_all[:, :ff_cols], 0, 0)
    grad_up = contract(normed_rows, d_gate_up_all[:, ff_cols:], 0, 0)

    def norm_two_term(begin_row, row_count):
        return contract(d_gate_up_all[:, :ff_cols], w_gate, 1, 1) + contract(
            d_gate_up_all[:, ff_cols:], w_up, 1, 1
        )

    d_normed_two = col_reduce(norm_two_term)
    cot_val = cot_rows.astype(jnp.float32)
    weighted_two = d_normed_two * norm2_gain[None, :]
    grad_norm_two = jnp.sum(d_normed_two * first_sum * scale_two[:, None], axis=0)
    dot_two = row_total(jnp.sum(weighted_two * first_sum, axis=1))
    d_first = (
        cot_val
        + scale_two[:, None] * weighted_two
        - first_sum * (scale_two**3 * dot_two / model_width)[:, None]
    )
    d_mix_all = token_rows(d_first.astype(jnp.bfloat16))
    grad_out = contract(gated_all, d_mix_all, 1, 0)

    def gated_term(begin_row, row_count):
        return contract(w_out, d_mix_all, 1, 1)

    d_gated = row_reduce(gated_term, channels)
    d_inner_z = d_gated * mixer_y * silu_slope(inner_z)
    d_mixer = d_gated * jax.nn.silu(inner_z)
    d_u_rows, d_step_rows, d_proj_rows, grad_rate_rows = adjoint_alone(
        proj_rows, step_rows, gone_rows, drive_rows, u_rows, d_mixer.T, decay_rate, at_b, at_c
    )
    d_u_mix = d_u_rows.T + skip_weight[:, None] * d_mixer
    d_step = d_step_rows.T
    d_enter = d_proj_rows.T[at_b:at_c]
    d_leave = d_proj_rows.T[at_c:]
    grad_rate = grad_rate_rows.T
    grad_skip = jnp.sum(d_mixer * u_val, axis=1)
    d_pre = d_step * jax.nn.sigmoid(pre_step)
    grad_step_bias = jnp.sum(d_pre, axis=1)
    d_pre_low = d_pre.astype(jnp.bfloat16)
    grad_step_w = contract(step_low, d_pre_low, 1, 1)
    d_projected = projection_total(
        jnp.concatenate(
            [jnp.dot(w_dt, d_pre_low, preferred_element_type=jnp.float32), d_enter, d_leave], axis=0
        )
    )
    d_proj_low = d_projected.astype(jnp.bfloat16)
    grad_proj_w = contract(u_low, d_proj_low, 1, 1)
    d_u_all = d_u_mix + jnp.dot(w_xp, d_proj_low, preferred_element_type=jnp.float32)
    d_inner_x, grad_kernel, grad_kernel_bias = conv_pull(d_u_all)
    d_inner_all = row_pieces(
        jnp.concatenate([d_inner_x.astype(jnp.bfloat16), d_inner_z.astype(jnp.bfloat16)], axis=1)
    )
    grad_in_x = contract(normed_all, d_inner_all[:, :group_rows], 0, 1)
    grad_in_z = contract(normed_all, d_inner_all[:, group_rows:], 0, 1)

    def norm_one_term(begin_row, row_count):
        piece_x = lax.dynamic_slice_in_dim(d_inner_all, begin_row, row_count, 1)
        piece_z = lax.dynamic_slice_in_dim(d_inner_all, group_rows, row_count, 1)
        return contract(piece_x, w_in_x, 0, 1) + contract(piece_z, w_in_z, 0, 1)

    d_normed_one = col_reduce(norm_one_term)
    weighted_one = d_normed_one * norm1_gain[None, :]
    grad_norm_one = jnp.sum(d_normed_one * x_val * scale_one[:, None], axis=0)
    dot_one = row_total(jnp.sum(weighted_one * x_val, axis=1))
    d_input = (
        d_first
        + scale_one[:, None] * weighted_one
        - x_val * (scale_one**3 * dot_one / model_width)[:, None]
    )
    d_input_low = d_input.astype(jnp.bfloat16)
    grad_norm_one, grad_norm_two = lax.psum((grad_norm_one, grad_norm_two), ("dp", "col"))
    (
        grad_in_x,
        grad_in_z,
        grad_kernel,
        grad_kernel_bias,
        grad_proj_w,
        grad_step_w,
        grad_step_bias,
        grad_rate,
        grad_skip,
        grad_out,
        grad_gate,
        grad_up,
        grad_down,
    ) = (
        lax.psum(grad_in_x.astype(jnp.bfloat16), "dp").astype(jnp.float32),
        lax.psum(grad_in_z.astype(jnp.bfloat16), "dp").astype(jnp.float32),
        lax.psum(grad_kernel.astype(jnp.bfloat16), "dp").astype(jnp.float32),
        lax.psum(grad_kernel_bias.astype(jnp.bfloat16), "dp").astype(jnp.float32),
        lax.psum(grad_proj_w.astype(jnp.bfloat16), "dp").astype(jnp.float32),
        lax.psum(grad_step_w.astype(jnp.bfloat16), "dp").astype(jnp.float32),
        lax.psum(grad_step_bias.astype(jnp.bfloat16), "dp").astype(jnp.float32),
        lax.psum(grad_rate.astype(jnp.bfloat16), "dp").astype(jnp.float32),
        lax.psum(grad_skip.astype(jnp.bfloat16), "dp").astype(jnp.float32),
        lax.psum(grad_out.astype(jnp.bfloat16), "dp").astype(jnp.float32),
        lax.psum(grad_gate.astype(jnp.bfloat16), "dp").astype(jnp.float32),
        lax.psum(grad_up.astype(jnp.bfloat16), "dp").astype(jnp.float32),
        lax.psum(grad_down.astype(jnp.bfloat16), "dp").astype(jnp.float32),
    )
    payload = jnp.concatenate([out_low, d_input_low], axis=1)
    tokens_all = lengths.shape[0] * group_rows
    owner = (
        jnp.zeros((tokens_all,), jnp.int32)
        .at[source.reshape(-1)]
        .set(jnp.arange(tokens_all, dtype=jnp.int32))
    )
    my_rows = lax.dynamic_slice_in_dim(
        owner, (my_group * col_devices + my_column) * rows_in, rows_in, 0
    )
    pieces = lax.all_gather(payload, ("dp", "col"), axis=0, tiled=True)
    row_count = pieces.shape[0]
    offset = my_rows
    inside = ((offset >= 0) & (offset < row_count))[:, None]
    returned = jnp.where(
        inside,
        jnp.take(pieces, jnp.clip(offset, 0, row_count - 1), axis=0),
        jnp.zeros_like(payload),
    )
    y_out = returned[:, :width_row]
    dx_out = returned[:, width_row:]
    return (
        y_out,
        dx_out,
        grad_norm_one,
        grad_in_x,
        grad_in_z,
        grad_kernel,
        grad_kernel_bias,
        grad_proj_w,
        grad_step_w,
        grad_step_bias,
        grad_rate,
        grad_skip,
        grad_out,
        grad_norm_two,
        grad_gate,
        grad_up,
        grad_down,
    )


def solution(mesh):
    placed = (
        P(("dp", "col"), "row"),
        P(),
        P(),
        P("row"),
        P("row", "col"),
        P("row", "col"),
        P(("col", "row"), None),
        P(("col", "row")),
        P(("col", "row"), None),
        P(None, ("col", "row")),
        P(("col", "row")),
        P(("col", "row"), None),
        P(("col", "row")),
        P("col", "row"),
        P("row"),
        P("row", "col"),
        P("row", "col"),
        P("col", "row"),
        P(("dp", "col"), "row"),
    )
    paired = mesh.shape["col"] == 2 and mesh.shape["dp"] == 4
    return jax.shard_map(
        on_pairs if paired else on_device,
        mesh=mesh,
        in_specs=placed,
        out_specs=(
            P(("dp", "col"), "row"),
            P(("dp", "col"), "row"),
            P("row"),
            P("row", "col"),
            P("row", "col"),
            P(("col", "row"), None),
            P(("col", "row")),
            P(("col", "row"), None),
            P(None, ("col", "row")),
            P(("col", "row")),
            P(("col", "row"), None),
            P(("col", "row")),
            P("col", "row"),
            P("row"),
            P("row", "col"),
            P("row", "col"),
            P("col", "row"),
        ),
        check_vma=False,
    )
```

```python
import functools

import jax
import jax.numpy as jnp
from jax import lax
from jax.experimental import pallas as pl
from jax.experimental.pallas import tpu as pltpu
from jax.sharding import PartitionSpec as P

epsilon = 1e-05


def layout(lengths, seq_order, group_rows):
    flat_lengths = lengths.reshape(-1)
    total_seqs = flat_lengths.shape[0]
    slot_length = jnp.take(flat_lengths, seq_order)
    input_start = jnp.cumsum(slot_length) - slot_length
    slot_of = (
        jnp.zeros((total_seqs,), jnp.int32)
        .at[seq_order]
        .set(jnp.arange(total_seqs, dtype=jnp.int32))
    )
    seq_input = jnp.take(input_start, slot_of).reshape(lengths.shape)
    group_start = jnp.cumsum(lengths, axis=1) - lengths
    places = jnp.arange(group_rows, dtype=jnp.int32)
    member = (
        jnp.sum((places[None, :, None] >= group_start[:, None, :]).astype(jnp.int32), axis=2) - 1
    )
    begin_at = jnp.take_along_axis(group_start, member, axis=1)
    within = places[None, :] - begin_at
    source = jnp.take_along_axis(seq_input, member, axis=1) + within
    return (source, within)


def silu_slope(values):
    sigmoid_v = jax.nn.sigmoid(values)
    return sigmoid_v * (1.0 + values * (1.0 - sigmoid_v))


def contract(left, right, left_dim, right_dim):
    return lax.dot_general(
        left, right, (((left_dim,), (right_dim,)), ((), ())), preferred_element_type=jnp.float32
    )


def convolve(inner_x, kernel, kernel_bias, places):
    tap_count = kernel.shape[1]
    conv_sum = kernel_bias[:, None] + inner_x * kernel[:, tap_count - 1][:, None]
    for shift_by in range(1, tap_count):
        shifted = jnp.pad(inner_x, ((0, 0), (shift_by, 0)))[:, :-shift_by]
        conv_sum = (
            conv_sum
            + shifted
            * (places >= shift_by).astype(jnp.float32)[None, :]
            * kernel[:, tap_count - 1 - shift_by][:, None]
        )
    return jax.nn.silu(conv_sum)


MESH = pl.DeviceIdType.MESH
f32 = jnp.float32
bf16 = jnp.bfloat16


def remote(src, dst, send, recv, where):
    return pltpu.make_async_remote_copy(
        src_ref=src, dst_ref=dst, send_sem=send, recv_sem=recv, device_id=where, device_id_type=MESH
    )


def away(axis, offset):
    return {axis: lax.rem(lax.axis_index(axis) + offset, lax.axis_size(axis))}


def greet(*axes):
    barrier = pltpu.get_barrier_semaphore()
    total = 0
    for axis in axes:
        for offset in range(1, lax.axis_size(axis)):
            pl.semaphore_signal(barrier, inc=1, device_id=away(axis, offset), device_id_type=MESH)
            total += 1
    return lambda: pl.semaphore_wait(barrier, total)


class Late:
    def __init__(self, names, sources, targets, sems):
        self.targets = dict(zip(names, targets))
        self.waiting = {}
        for i, (name, source, target) in enumerate(zip(names, sources, targets)):
            self.waiting[name] = pltpu.make_async_copy(source, target, sems.at[i])
            self.waiting[name].start()

    def __call__(self, name):
        if name in self.waiting:
            self.waiting.pop(name).wait()
        return self.targets[name]


class Leave:
    def __init__(self, names, sources, targets, sems):
        self.copies = {
            name: pltpu.make_async_copy(source, target, sems.at[i])
            for i, (name, source, target) in enumerate(zip(names, sources, targets))
        }

    def __call__(self, *names):
        for name in names:
            self.copies[name].start()

    def finish(self):
        for copy in self.copies.values():
            copy.wait()


def matmul(left, right):
    return jnp.dot(left, right, preferred_element_type=f32)


def silu(values):
    return values * jax.nn.sigmoid(values)


def rows_form(values):
    ones = jnp.ones((8, values.shape[1]), f32)
    return lax.dot_general(
        ones,
        values,
        (((1,), (1,)), ((), ())),
        precision=lax.Precision.HIGHEST,
        preferred_element_type=f32,
    )


def column_form(row_values):
    return jnp.transpose(row_values)[:, 0:1]


class Line:
    def __init__(self, axis, send, recv):
        self.axis, self.send, self.recv = axis, send, recv
        self.size = lax.axis_size(axis)
        self.me = lax.axis_index(axis)

    def right(self, src, dst, d):
        return remote(
            src, dst, self.send.at[0, d], self.recv.at[0, d], {self.axis: jnp.minimum(self.me + 1, self.size - 1)}
        )

    def left(self, src, dst, d):
        return remote(
            src, dst, self.send.at[1, d], self.recv.at[1, d], {self.axis: jnp.maximum(self.me - 1, 0)}
        )


def line_gather(axis, slot_of, send, recv):
    line = Line(axis, send, recv)
    size, me = line.size, line.me
    last = size - 1

    def go_right(s):
        slot = jnp.maximum(me - s, 0)
        return (me - s >= 0) & (me < last), line.right(slot_of(slot), slot_of(slot), slot)

    def go_left(s):
        slot = jnp.minimum(me + s, last)
        return (me + s <= last) & (me > 0), line.left(slot_of(slot), slot_of(slot), slot)

    for s in range(last):
        for valid, copy in (go_right(s), go_left(s)):
            pl.when(valid)(copy.start)
        yield
        slot = jnp.maximum(me - 1 - s, 0)
        pl.when(me - 1 - s >= 0)(line.right(slot_of(slot), slot_of(slot), slot).wait_recv)
        slot = jnp.minimum(me + 1 + s, last)
        pl.when(me + 1 + s <= last)(line.left(slot_of(slot), slot_of(slot), slot).wait_recv)
    yield
    for s in range(last):
        for valid, copy in (go_right(s), go_left(s)):
            pl.when(valid)(copy.wait_send)


def line_scatter(axis, block_of, out, held, from_left, from_right, send, recv, slots=False):
    line = Line(axis, send, recv)
    size, me = line.size, line.me
    last = size - 1

    def right_at(t):
        d = jnp.clip(last - t + me, 0, last)
        return (t >= me) & (me < last), d, line.right(held.at[d], from_left.at[d], d)

    def left_at(t):
        d = jnp.clip(t - (last - me), 0, last)
        return (t >= last - me) & (me > 0), d, line.left(held.at[d], from_right.at[d], d)

    def made(d, slot):
        return block_of(d, slot) if slots else block_of(d)

    def pass_on(valid, first, d, copy, arrived, slot):
        @pl.when(valid)
        def _():
            part = made(d, slot)

            @pl.when(jnp.logical_not(first))
            def _():
                copy.wait_recv()
                held[d] = (part + arrived[d].astype(f32)).astype(held.dtype)

            @pl.when(first)
            def _():
                held[d] = part.astype(held.dtype)

            copy.start()

    for t in range(last):
        valid, d, copy = right_at(t)
        pass_on(valid, me == 0, d, copy, from_left, 0)
        valid, d, copy = left_at(t)
        pass_on(valid, me == last, d, copy, from_right, 1)
        if t == 0:
            out[...] = made(me, 2)
        yield
    yield

    @pl.when(me > 0)
    def _():
        line.right(held.at[me], from_left.at[me], me).wait_recv()
        out[...] += from_left[me].astype(f32)

    @pl.when(me < last)
    def _():
        line.left(held.at[me], from_right.at[me], me).wait_recv()
        out[...] += from_right[me].astype(f32)

    for t in range(last):
        for valid, _, copy in (right_at(t), left_at(t)):
            pl.when(valid)(copy.wait_send)


def halves(rows):
    return [pl.ds(0, rows // 2), pl.ds(rows // 2, rows // 2)]


def gather_halves(axis, ref, size, send, recv):
    flows = []
    for h, at in enumerate(halves(ref.shape[0])):

        def slot_of(d, at=at):
            return ref.at[at, pl.ds(pl.multiple_of(d * size, size), size)]

        flows.append(line_gather(axis, slot_of, send.at[h], recv.at[h]))
    return flows


def scatter_halves(axis, block_of, out, held, from_left, from_right, send, recv):
    flows = []
    for h, at in enumerate(halves(out.shape[0])):
        flows.append(
            line_scatter(
                axis,
                functools.partial(block_of, at=at),
                out.at[at, :],
                held.at[:, at, :],
                from_left.at[:, at, :],
                from_right.at[:, at, :],
                send.at[h],
                recv.at[h],
            )
        )
    return flows


def run(*flows, pump=None):
    flows = list(flows)
    turn = 0
    while flows:
        flows = [flow for flow in flows if next(flow, flows) is not flows]
        if pump is not None and turn < len(pump[1]):
            pump[0].pump(pump[1][turn])
        turn += 1


def lanes(ref, size):
    return lambda d: ref.at[:, pl.ds(pl.multiple_of(d * size, size), size)]


def fetch(sources, targets, sems):
    copies = [pltpu.make_async_copy(s, t, sems.at[i]) for i, (s, t) in enumerate(zip(sources, targets))]
    for copy in copies:
        copy.start()
    return copies


def as_row(ref):
    return ref[...].reshape(1, ref.shape[0])


def lengths_row(lens):
    groups, per_group = lens.shape
    values = lens[...].astype(f32)
    at = lax.broadcasted_iota(jnp.int32, (per_group, groups * per_group), 1)
    inner = lax.broadcasted_iota(jnp.int32, (per_group, groups * per_group), 0)
    total = jnp.zeros((1, groups * per_group), f32)
    for g in range(groups):
        place = jnp.where(at == inner + g * per_group, 1.0, 0.0)
        total = total + jnp.dot(
            values[g : g + 1, :], place, precision=lax.Precision.HIGHEST, preferred_element_type=f32
        )
    return total


def spray(axis, src_of, dst, send, recv, base=0):
    copies = []
    for k in range(1, lax.axis_size(axis)):
        copy = remote(src_of(k), dst.at[k - 1], send.at[base + k - 1], recv.at[base + k - 1], away(axis, k))
        copy.start()
        copies.append(copy)
    return copies


def wait_all(copies):
    for copy in copies:
        copy.wait()


def swap(axis, src, dst, send, recv):
    copy = remote(src, dst, send, recv, away(axis, 1))
    copy.start()
    return copy


def sequence_rows(lens_row, order_row, per_group):
    count = lens_row.shape[1]
    ri = lax.broadcasted_iota(jnp.int32, (count, count), 0)
    ci = lax.broadcasted_iota(jnp.int32, (count, count), 1)
    lens_f = lens_row

    def to_column(row):
        return jnp.sum(jnp.where(ri == ci, row, 0.0), axis=1, keepdims=True)

    order_col = to_column(order_row.astype(f32)).astype(jnp.int32)
    lens_col = to_column(lens_f)
    pick = order_row == ri
    pick_t = order_col == ci
    slot_col = jnp.sum(jnp.where(pick_t, lens_f, 0.0), axis=1, keepdims=True)
    slot_row = jnp.sum(jnp.where(pick, lens_col, 0.0), axis=0, keepdims=True)
    start_col = jnp.sum(jnp.where(ci < ri, slot_row, 0.0), axis=1, keepdims=True)
    input_row = jnp.sum(jnp.where(pick_t, start_col, 0.0), axis=0, keepdims=True)
    same = (ri // per_group) == (ci // per_group)
    group_row = jnp.sum(jnp.where((ri < ci) & same, lens_col, 0.0), axis=0, keepdims=True)
    return lens_f, input_row, group_row


def place_rows(lens_row, order_row, per_group, group_rows, group):
    lens_f, input_row, group_row = sequence_rows(lens_row, order_row, per_group)
    count = lens_row.shape[1]
    rows = lax.broadcasted_iota(jnp.int32, (group_rows, count), 0).astype(f32)
    mine = (lax.broadcasted_iota(jnp.int32, (group_rows, count), 1) // per_group) == group
    inside = (rows >= group_row) & (rows < group_row + lens_f) & mine
    within = jnp.sum(jnp.where(inside, rows - group_row, 0.0), axis=1, keepdims=True)
    begin = jnp.sum(jnp.where(inside, input_row, 0.0), axis=1, keepdims=True)
    return begin + within, within


def owner_rows(lens_row, order_row, per_group, group_rows, block_rows, first):
    lens_f, input_row, group_row = sequence_rows(lens_row, order_row, per_group)
    count = lens_row.shape[1]
    rows = (lax.broadcasted_iota(jnp.int32, (block_rows, count), 0) + first).astype(f32)
    base = (lax.broadcasted_iota(jnp.int32, (block_rows, count), 1) // per_group) * group_rows
    inside = (rows >= input_row) & (rows < input_row + lens_f)
    found = jnp.where(inside, base.astype(f32) + group_row + rows - input_row, 0.0)
    return jnp.sum(found, axis=1, keepdims=True)


def plane_origin(rows, dp_size, col_size, block_rows):
    at = lax.broadcasted_iota(jnp.int32, (rows, dp_size * col_size * block_rows), 1)
    block = at // block_rows
    group = lax.rem(block, dp_size)
    column = block // dp_size
    return ((group * col_size + column) * block_rows + lax.rem(at, block_rows)).astype(f32)


def pick_rows(wanted, held):
    col_size, dp_size, block_rows, width = held.shape
    total = col_size * dp_size * block_rows
    chosen = wanted == plane_origin(wanted.shape[0], dp_size, col_size, block_rows)
    chosen = jnp.where(chosen, 1.0, 0.0).astype(bf16)
    return matmul(chosen, held.reshape(total, width)).astype(bf16)


def plane_start(src, held, send, recv):
    me, column = lax.axis_index("dp"), lax.axis_index("col")
    held[column, me] = src[...]
    copies = []
    for k in range(1, lax.axis_size("dp")):
        copy = remote(src, held.at[column, me], send.at[k], recv.at[k], away("dp", k))
        copy.start()
        copies.append(copy)
    return copies


def plane_swap(copies, held, send, recv):
    column = lax.axis_index("col")
    for copy in copies:
        copy.wait_recv()
    return swap("col", held.at[column], held.at[column], send.at[0], recv.at[0])


def plane_wait(copies, last):
    last.wait_recv()
    for copy in [*copies, last]:
        copy.wait_send()


def plane_finish(copies, held, send, recv):
    plane_wait(copies, plane_swap(copies, held, send, recv))


def total_of_sums(part, half_own, half_in, low_own, low_in, full, sems):
    send, recv = sems
    rows = part.shape[0] // 2
    column = lax.axis_index("col")
    mine = pl.ds(pl.multiple_of(column * rows, rows), rows)
    other = pl.ds(pl.multiple_of((1 - column) * rows, rows), rows)
    half_own[...] = part[other, :]
    copy = swap("col", half_own, half_in, send.at[0], recv.at[0])
    yield
    copy.wait()
    low_own[...] = (part[mine, :] + half_in[...]).astype(bf16)
    copies = spray("row", lambda k: low_own, low_in, send, recv, 1)
    yield
    wait_all(copies)
    total = low_own[...].astype(f32)
    for k in range(low_in.shape[0]):
        total = total + low_in[k].astype(f32)
    full[mine, :] = total
    copy = swap("col", full.at[mine], full.at[mine], send.at[4], recv.at[4])
    yield
    copy.wait()


def lanes_like(tile, width):
    if tile.shape[-1] == width:
        return tile
    return jnp.concatenate([tile] * (width // tile.shape[-1]), axis=-1)


def lane_mask(count, lanes, first):
    lane = lax.broadcasted_iota(jnp.int32, (count, lanes), 1)
    return lane == lax.broadcasted_iota(jnp.int32, (count, lanes), 0) + first


def spread(values, first, count, wide):
    rows, lanes = values.shape
    chosen = jnp.where(lane_mask(count, lanes, first)[None], values[:, None, :], 0.0)
    chosen = chosen.reshape(rows * count, lanes)
    high = chosen.astype(bf16)
    rest = (chosen - high.astype(f32)).astype(bf16)
    ones = jnp.ones((lanes, wide), bf16)
    return matmul(high, ones) + matmul(rest, ones)


def spread_into(target, source, start, first, count):
    rows, _, wide = target.shape
    size = min(32, rows)

    def one(j, _):
        at = pl.ds(pl.multiple_of(start + j * size, size), size)
        found = spread(source[at, :], first, count, wide)
        target[pl.ds(pl.multiple_of(j * size, size), size)] = found.reshape(size, count, wide)
        return 0

    lax.fori_loop(0, rows // size, one, 0)


def add_lane_sums(target, start, sources):
    rows = sources[0][0].shape[0]
    size = min(32, rows)

    def one(j, _):
        inner = pl.ds(pl.multiple_of(j * size, size), size)
        at = pl.ds(pl.multiple_of(start + j * size, size), size)
        total = target[at, :]
        for source, first in sources:
            total = total + lane_sums(source[inner], first, target.shape[1])
        target[at, :] = total
        return 0

    lax.fori_loop(0, rows // size, one, 0)


def lane_sums(values, first, lanes):
    rows, count, wide = values.shape
    flat = values.reshape(rows * count, wide)
    high = flat.astype(bf16)
    rest = (flat - high.astype(f32)).astype(bf16)
    ones = jnp.ones((wide, lanes), bf16)
    sums = (matmul(high, ones) + matmul(rest, ones)).reshape(rows, count, lanes)
    return jnp.sum(jnp.where(lane_mask(count, lanes, first)[None], sums, 0.0), axis=1)


def scan_forward(proj, b_at, c_at, gone_step, drive, rate, bb, cb, y):
    rows, width = drive.shape
    count = rate.shape[0]
    piece, _, wide = bb.shape
    state = jnp.zeros((count, width), f32)
    for start in range(0, rows, piece):
        spread_into(bb, proj, start, b_at, count)
        spread_into(cb, proj, start, c_at, count)

        def eight(k, state):
            inner = pl.multiple_of(k * 8, 8)
            base = pl.multiple_of(start + k * 8, 8)
            gone = gone_step[pl.ds(base, 8), :]
            driven = drive[pl.ds(base, 8), :]
            found = []
            for i in range(8):
                decay = jnp.exp(gone[i : i + 1, :] * rate)
                state = decay * state + driven[i : i + 1, :] * lanes_like(bb[inner + i], width)
                found.append(jnp.sum(state * lanes_like(cb[inner + i], width), axis=0, keepdims=True))
            y[pl.ds(base, 8), :] = jnp.concatenate(found, axis=0)
            return state

        state = lax.fori_loop(0, piece // 8, eight, state)
        yield


def scan_states(proj, b_at, gone_step, drive, rate, bb, hs):
    rows, width = drive.shape
    count = rate.shape[0]
    piece, _, wide = bb.shape
    hs[0] = jnp.zeros((count, width), f32)
    for start in range(0, rows, piece):
        spread_into(bb, proj, start, b_at, count)

        def eight(k, state):
            inner = pl.multiple_of(k * 8, 8)
            base = pl.multiple_of(start + k * 8, 8)
            gone = gone_step[pl.ds(base, 8), :]
            driven = drive[pl.ds(base, 8), :]
            for i in range(8):
                decay = jnp.exp(gone[i : i + 1, :] * rate)
                state = decay * state + driven[i : i + 1, :] * lanes_like(bb[inner + i], width)
                hs[base + i + 1] = state
            return state

        lax.fori_loop(0, piece // 8, eight, hs[start])
        yield


def scan_backward(
    proj, b_at, c_at, step, gone_step, drive, inner_u, dy, rate, hs, bb, cb, pb, pc, du, dstep, dproj
):
    rows, width = drive.shape
    count = rate.shape[0]
    piece, _, wide = bb.shape

    def fold(values):
        total = values[:, 0:wide]
        for j in range(1, width // wide):
            total = total + values[:, j * wide : (j + 1) * wide]
        return total

    def part(start, carry):
        spread_into(bb, proj, start, b_at, count)
        spread_into(cb, proj, start, c_at, count)

        def eight(k, carry):
            later, total = carry
            inner = pl.multiple_of((piece // 8 - 1 - k) * 8, 8)
            base = pl.multiple_of(start + inner, 8)
            step8 = step[pl.ds(base, 8), :]
            gone8 = gone_step[pl.ds(base, 8), :]
            drive8 = drive[pl.ds(base, 8), :]
            u8 = inner_u[pl.ds(base, 8), :]
            dy8 = dy[pl.ds(base, 8), :]
            by_b = [None] * 8
            by_rate = [None] * 8
            for i in reversed(range(8)):
                dy_row = dy8[i : i + 1, :]
                lam = lanes_like(cb[inner + i], width) * dy_row + later
                later = jnp.exp(gone8[i : i + 1, :] * rate) * lam
                kept = later * hs[base + i]
                total = total + kept * step8[i : i + 1, :]
                by_b[i] = jnp.sum(lam * lanes_like(bb[inner + i], width), axis=0, keepdims=True)
                by_rate[i] = jnp.sum(kept * rate, axis=0, keepdims=True)
                pb[inner + i] = fold(lam * drive8[i : i + 1, :])
                pc[inner + i] = fold(hs[base + i + 1] * dy_row)
            by_b = jnp.concatenate(by_b, axis=0)
            by_rate = jnp.concatenate(by_rate, axis=0)
            du[pl.ds(base, 8), :] = by_b * step8
            dstep[pl.ds(base, 8), :] = by_rate + by_b * u8
            return later, total

        carry = lax.fori_loop(0, piece // 8, eight, carry)
        add_lane_sums(dproj, start, ((pb, b_at), (pc, c_at)))
        return carry

    blank = jnp.zeros((count, width), f32)
    carry = (blank, blank)
    for start in reversed(range(0, rows, piece)):
        carry = part(start, carry)
        yield
    return carry[1] * rate


RANK_LANES = 128


def scan_kernel(proj, gone, drive, rate, y, bb, cb, *, b_at, c_at):
    run(scan_forward(proj, b_at, c_at, gone, drive, rate[...], bb, cb, y))


def adjoint_kernel(
    proj, step, gone, drive, inner_u, dy, rate, du, dstep, dproj, drate, bb, cb, hs, pb, pc, *, b_at, c_at
):
    run(scan_states(proj, b_at, gone, drive, rate[...], bb, hs))
    dproj[...] = jnp.zeros_like(dproj)
    kept = {}

    def adjoint():
        kept["rate"] = yield from scan_backward(
            proj, b_at, c_at, step, gone, drive, inner_u, dy, rate[...], hs, bb, cb, pb, pc, du, dstep, dproj
        )

    run(adjoint())
    drate[...] = kept["rate"]


def scan_sizes(rows, width, count):
    wide = 128 if width % 128 == 0 else width
    piece = min(128, rows)
    return pltpu.VMEM((piece, count, wide), f32)


def scan_alone(proj, gone, drive, rate, b_at, c_at):
    rows, width = drive.shape
    block = scan_sizes(rows, width, rate.shape[0])
    return pl.pallas_call(
        functools.partial(scan_kernel, b_at=b_at, c_at=c_at),
        out_shape=jax.ShapeDtypeStruct((rows, width), f32),
        scratch_shapes=[block, block],
        compiler_params=pltpu.CompilerParams(vmem_limit_bytes=VMEM_BYTES),
        name="scan_states",
    )(proj, gone, drive, rate)


def adjoint_alone(proj, step, gone, drive, inner_u, dy, rate, b_at, c_at):
    rows, width = step.shape
    count = rate.shape[0]
    block = scan_sizes(rows, width, count)
    shape = jax.ShapeDtypeStruct
    return pl.pallas_call(
        functools.partial(adjoint_kernel, b_at=b_at, c_at=c_at),
        out_shape=(
            shape((rows, width), f32),
            shape((rows, width), f32),
            shape(proj.shape, f32),
            shape((count, width), f32),
        ),
        scratch_shapes=[
            block,
            block,
            pltpu.VMEM((rows + 1, count, width), f32),
            block,
            block,
        ],
        compiler_params=pltpu.CompilerParams(vmem_limit_bytes=VMEM_BYTES),
        name="scan_adjoint",
    )(proj, step, gone, drive, inner_u, dy, rate)


PUMPS = ((0, 1, 1), (1, 1, 1), 0, (1, 2, 1), (1, 1), (0, 0, 0), (2, 2, 1), 0, 2)


def conv_sum(inner_x, place, taps, bias):
    count = taps.shape[0]
    total = bias + inner_x * taps[count - 1 : count, :]
    for shift in range(1, count):
        moved = jnp.where(place >= shift, pltpu.roll(inner_x, shift, 0), 0.0)
        total = total + moved * taps[count - 1 - shift : count - shift, :]
    return total


def transposed(left, right):
    return lax.dot_general(left, right, (((1,), (1,)), ((), ())), preferred_element_type=f32)


def over_rows(left, right):
    return lax.dot_general(left, right, (((0,), (0,)), ((), ())), preferred_element_type=f32)


def columns(d, size):
    return pl.ds(pl.multiple_of(d * size, size), size)


def line_total(own, arrived):
    total = own
    for k in range(arrived.shape[0]):
        total = total + arrived[k]
    return total


def forward_kernel(
    x, cot, lens, order, gain1, taps, bias, w_xp, w_dt, dt_bias, a_log, skip, gain2,
    w_x_h, w_z_h, w_out_h, w_gate_h, w_up_h, w_down_h,
    xg_o, cg_o, n1_o, s1_o, place_o, xi_o, z_o, proj_o, yv_o, go_all, h1_o, s2_o, n2_o, hid_all, dgu_o, dot_o, n1_mates, n2_mates, cg_mates, go_mates, hid_mates,
    w_x, w_z, w_out, w_gate, w_up, w_down, w_step, rate,
    x_all, c_all, sum_own, sum_in, low, xi_held, xi_left, xi_right, z_held, z_left, z_right,
    part_s, half_own, half_in, low_own, low_in, bb, cb, step, gone, drive,
    own, other, gu, gu_part, gu_held, gu_left, gu_right, dhid, h_held, h_left, h_right,
    w_sems, x_send, x_recv, c_send, c_recv, sum_send, sum_recv, xi_send, xi_recv, z_send, z_recv, t_send, t_recv,
    go_send, go_recv, o_send, o_recv, sum2_send, sum2_recv, gu_send, gu_recv, h_send, h_recv, hid_send, hid_recv, m_send, m_recv,
    *, model_width, rank, count, leave
):
    rows, width = xi_o.shape
    hidden = dgu_o.shape[1] // 2
    group, row = lax.axis_index("dp"), lax.axis_index("row")
    row_size = lax.axis_size("row")
    weights = fetch(
        (w_x_h, w_z_h, w_out_h, w_gate_h, w_up_h, w_down_h), (w_x, w_z, w_out, w_gate, w_up, w_down), w_sems
    )
    met = greet("dp", "row", "col")
    w_step[...] = jnp.zeros_like(w_step)
    w_step[0:rank, :] = w_dt[...]
    met()
    x_copies = plane_start(x, x_all, x_send, x_recv)
    lens_row = lengths_row(lens)
    source, place = place_rows(lens_row, as_row(order), lens.shape[1], rows, group)
    place_o[...] = place
    plane_finish(x_copies, x_all, x_send, x_recv)
    c_copies = plane_start(cot, c_all, c_send, c_recv)
    xg_low = pick_rows(source, x_all[...])
    xg_o[...] = xg_low
    xg = xg_low.astype(f32)
    gain1_now = as_row(gain1)
    low[...] = (xg * gain1_now).astype(bf16)
    weights[0].wait()
    kept = {}

    def during_xi():
        sum_own[...] = rows_form(xg * xg)
        sum_copies = spray("row", lambda k: sum_own, sum_in, sum_send, sum_recv)
        rate[...] = -jnp.exp(a_log[...])
        yield
        wait_all(sum_copies)
        kept["s1"] = column_form(lax.rsqrt(line_total(sum_own[...], sum_in) / model_width + epsilon))
        s1_o[...] = kept["s1"]
        leave("xg", "s1", "place")
        kept["cot"] = plane_swap(c_copies, c_all, c_send, c_recv)

    run(
        *scatter_halves(
            "row", lambda d, at: matmul(low[at, :], w_x[:, columns(d, width)]), xi_o, xi_held, xi_left, xi_right,
            xi_send, xi_recv,
        ),
        during_xi(),
    )
    weights[1].wait()
    z_flows = scatter_halves(
        "row", lambda d, at: matmul(low[at, :], w_z[:, columns(d, width)]), z_o, z_held, z_left, z_right, z_send, z_recv
    )
    for flow in z_flows:
        next(flow)
    s1 = kept["s1"]
    inner_x = xi_o[...] * s1
    xi_o[...] = inner_x
    u_low = silu(conv_sum(inner_x, place, taps[...], as_row(bias))).astype(bf16)
    u = u_low.astype(f32)
    part_s[...] = matmul(u_low, w_xp[...])

    def mix():
        yield from total_of_sums(part_s, half_own, half_in, low_own, low_in, proj_o, (t_send, t_recv))
        pre = matmul(proj_o[...].astype(bf16), w_step[...]) + as_row(dt_bias)
        step_now = jax.nn.softplus(pre)
        step[...] = step_now
        gone[...] = jnp.where(place > 0.0, step_now, 1e30)
        drive[...] = step_now * u
        yield from scan_forward(proj_o, rank, rank + count, gone, drive, rate[...], bb, cb, yv_o)

    mixing = mix()
    next(mixing)
    plane_wait(c_copies, kept["cot"])
    cg_o[...] = pick_rows(source, c_all[...])
    kept["mates"] = to_mates(cg_o, cg_mates, m_send.at[1], m_recv.at[1])
    next(mixing)
    run(*z_flows, mixing)
    yv = yv_o[...] + as_row(skip) * u
    yv_o[...] = yv
    z = z_o[...] * s1
    z_o[...] = z
    go_all[:, columns(row, width)] = (yv * silu(z)).astype(bf16)

    def during_gather():
        n1_o[...] = (xg * s1 * gain1_now).astype(bf16)
        kept["mates"] += to_mates(n1_o, n1_mates, m_send.at[0], m_recv.at[0])
        yield

    weights[5].wait()
    run(
        *gather_halves("row", go_all, width, go_send, go_recv),
        *scatter_halves(
            "row", lambda d, at: transposed(cg_o[at, :], w_down[columns(d, hidden), :]), dhid, h_held, h_left, h_right,
            h_send, h_recv,
        ),
        during_gather(),
    )
    kept["mates"] += quarters_to_mates(go_all, go_mates, m_send.at[3], m_recv.at[3])
    weights[2].wait()
    own[...] = matmul(go_all[...], w_out[...])
    copy = swap("col", own, other, o_send.at[0], o_recv.at[0])
    weights[3].wait()
    weights[4].wait()
    copy.wait()
    h1 = xg + (own[...] + other[...])
    h1_o[...] = h1
    gain2_now = as_row(gain2)
    low[...] = (h1 * gain2_now).astype(bf16)

    def gate_up_flows(first):
        rows_now, size = rows // 2, rows // 4

        def block_of(d, slot, part):
            side = columns(d, hidden)
            if part == 0:
                left = low[first : first + rows_now, :]
                gu_part[slot, :, 0:hidden] = matmul(left, w_gate[:, side])
                gu_part[slot, :, hidden:] = matmul(left, w_up[:, side])
            return gu_part[slot, part * size : (part + 1) * size, :]

        flows = []
        for part in range(2):
            at = pl.ds(first + part * size, size)
            number = first // size + part
            flows.append(
                line_scatter(
                    "row", functools.partial(block_of, part=part), gu.at[at, :], gu_held.at[:, at, :],
                    gu_left.at[:, at, :], gu_right.at[:, at, :], gu_send.at[number], gu_recv.at[number], slots=True,
                )
            )
        return flows

    def hid_flows(first, count):
        size = rows // 2 // count
        flows = []
        for part in range(count):
            at = pl.ds(first + part * size, size)

            def slot_of(d, at=at):
                return hid_all.at[at, columns(d, hidden)]

            number = first // (rows // 4) + part
            flows.append(line_gather("row", slot_of, hid_send.at[number], hid_recv.at[number]))
        return flows

    def activate(first):
        at = slice(first, first + rows // 2)
        s2 = s2_o[at, :]
        gate, up = gu[at, 0:hidden] * s2, gu[at, hidden:] * s2
        gu[at, 0:hidden], gu[at, hidden:] = gate, up
        sig = jax.nn.sigmoid(gate)
        act = gate * sig
        hid_all[at, columns(row, hidden)] = (act * up).astype(bf16)
        d_hid = dhid[at, :]
        dgu_o[at, 0:hidden] = (d_hid * up * (sig * (1.0 + gate * (1.0 - sig)))).astype(bf16)
        dgu_o[at, hidden:] = (d_hid * act).astype(bf16)

    def during_scatter():
        sum_own[...] = rows_form(h1 * h1)
        sum_copies = spray("row", lambda k: sum_own, sum_in, sum2_send, sum2_recv)
        yield
        wait_all(sum_copies)
        s2 = column_form(lax.rsqrt(line_total(sum_own[...], sum_in) / model_width + epsilon))
        s2_o[...] = s2
        n2_o[...] = (h1 * s2 * gain2_now).astype(bf16)
        leave("n1", "cg", "xi", "z", "proj", "yv", "go_all", "h1", "s2", "n2")
        kept["mates"] += to_mates(n2_o, n2_mates, m_send.at[2], m_recv.at[2])

    def dots():
        yield
        dot_o[...] = rows_form(dgu_o[...].astype(f32) * gu[...])

    run(*gate_up_flows(0), during_scatter())
    activate(0)
    run(*gate_up_flows(rows // 2), *hid_flows(0, 1))
    activate(rows // 2)
    top, bottom = pl.ds(0, rows // 2), pl.ds(rows // 2, rows // 2)
    kept["mates"] += quarters_to_mates(hid_all, hid_mates, m_send.at[4], m_recv.at[4], top)
    run(*hid_flows(rows // 2, 2), dots())
    kept["mates"] += quarters_to_mates(hid_all, hid_mates, m_send.at[5], m_recv.at[5], bottom)
    leave("hid_all", "dgu", "dot")
    wait_all(kept["mates"])
    leave("hid_mates", "n1_mates", "n2_mates", "cg_mates", "go_mates")
    leave.finish()


def dp_bits():
    me = lax.axis_index("dp")
    return lax.rem(me, 2), me // 2


def dp_mates():
    me = lax.axis_index("dp")
    along_x, along_y = dp_bits()
    return {"dp": me + 1 - 2 * along_x}, {"dp": me + 2 - 4 * along_y}


def to_mates(src, dst, send, recv):
    copies = [remote(src, dst.at[h], send.at[h], recv.at[h], mate) for h, mate in enumerate(dp_mates())]
    for copy in copies:
        copy.start()
    return copies


def quarters_to_mates(ref, dst, send, recv, rows=None):
    size = ref.shape[1] // 4
    at = pl.ds(0, ref.shape[0]) if rows is None else rows
    copies = []
    for h, (near, mate) in enumerate(zip(dp_bits(), dp_mates())):
        side = pl.ds(pl.multiple_of((2 * h + 1 - near) * size, size), size)
        copies.append(remote(ref.at[at, side], dst.at[h, at, :], send.at[h], recv.at[h], mate))
        copies[-1].start()
    return copies


def pair_sum(grad, sent, fixed, fixed_mates, by_rows, sent_in, second_in, third_in, send, recv, swapped="sent"):
    quarter = sent.shape[1] // 4
    eighth = (quarter if by_rows else grad.shape[0]) // 2
    bits, mates = dp_bits(), dp_mates()

    def side(h, near):
        return pl.ds(pl.multiple_of((2 * h + near) * quarter, quarter), quarter)

    def view(h, near, far):
        if by_rows:
            return grad.at[pl.ds(pl.multiple_of((2 * h + near) * quarter + far * eighth, eighth), eighth), :]
        return grad.at[pl.ds(pl.multiple_of(far * eighth, eighth), eighth), side(h, near)]

    class Half:
        def __init__(self, h):
            near, far = bits[h], bits[1 - h]
            mate, other = mates[h], mates[1 - h]

            def copy(stage, src, dst, to):
                return remote(src, dst, send.at[stage, h], recv.at[stage, h], to)

            self.h, self.near = h, near
            self.own, self.rest = view(h, near, far), view(h, near, 1 - far)
            there = view(h, 1 - near, far), view(h, 1 - near, 1 - far)
            first = None
            if swapped == "fixed":
                first = copy(0, fixed, fixed_mates.at[h], mate)
            elif swapped == "sent":
                first = copy(0, sent.at[:, side(h, 1 - near)], sent_in.at[h], mate)
            self.out = (
                first,
                copy(1, self.rest, second_in.at[h], other),
                copy(2, self.own, third_in.at[h], other),
                copy(3, self.own, self.own, mate),
                copy(4, self.rest, self.rest, mate),
            )
            self.back = (copy(3, there[0], there[0], mate), copy(4, there[1], there[1], mate))

    def products():
        def one(h, _):
            near = jnp.where(h == 0, bits[0], bits[1])
            here = side(h, near)
            mine, mates_part, mates_fixed = sent[:, here], sent_in[h], fixed_mates[h]
            if by_rows:
                grad[here, :] = (over_rows(mine, fixed[...]) + over_rows(mates_part, mates_fixed)).astype(bf16)
            else:
                grad[:, here] = (over_rows(fixed[...], mine) + over_rows(mates_fixed, mates_part)).astype(bf16)
            return 0

        lax.fori_loop(0, 2, one, 0)

    both_halves = (Half(0), Half(1))
    if swapped:
        for half in both_halves:
            half.out[0].start()
        yield
    for half in both_halves:
        if swapped:
            half.out[0].wait_recv()
    products()
    for half in both_halves:
        half.out[1].start()
    yield
    for half in both_halves:
        half.out[1].wait_recv()
        add_view(half.own, second_in.at[half.h], eighth)
        half.out[2].start()
        half.out[3].start()
    yield
    for half in both_halves:
        half.out[2].wait_recv()
        half.out[1].wait_send()
        half.rest[...] = third_in[half.h]
        half.out[4].start()
    yield
    for half in both_halves:
        for copy in half.back:
            copy.wait_recv()
        for stage in (0, 2, 3, 4) if swapped else (2, 3, 4):
            half.out[stage].wait_send()


def add_view(target, source, rows):
    def piece(j, _):
        at = pl.ds(pl.multiple_of(j * 16, 16), 16)
        target[at, :] = (target[at, :].astype(f32) + source[at, :].astype(f32)).astype(bf16)
        return 0

    lax.fori_loop(0, rows // 16, piece, 0)


def add_rows(target, base, source, rows):
    def piece(j, _):
        at = pl.ds(pl.multiple_of(base + j * 16, 16), 16)
        found = target[at, :].astype(f32) + source[pl.ds(pl.multiple_of(j * 16, 16), 16), :].astype(f32)
        target[at, :] = found.astype(target.dtype)
        return 0

    lax.fori_loop(0, rows // 16, piece, 0)


def plane_sum(grad, first_in, second_in, send, recv, free):
    quarter = grad.shape[0] // 4
    eighth = quarter // 2
    bits, partners = dp_bits(), dp_mates()

    def rows(ref, start, count):
        return ref.at[pl.ds(pl.multiple_of(start, 16), count), :]

    class Half:
        def __init__(self, h):
            near, far = bits[h], bits[1 - h]
            self.free, self.mate, self.first = free.at[h], partners[h], first_in.at[h]
            base = h * 2 * quarter
            self.kept = base + near * quarter
            self.own = self.kept + far * eighth
            self.rest = self.kept + (1 - far) * eighth
            self.rest_in = (1 - far) * eighth
            across = base + (1 - near) * quarter
            self.second = second_in.at[h]

            def copy(stage, src, dst, to):
                return remote(src, dst, send.at[stage, h], recv.at[stage, h], to)

            mate, other = partners[h], partners[1 - h]
            own, rest = rows(grad, self.own, eighth), rows(grad, self.rest, eighth)
            there = (rows(grad, across + far * eighth, eighth), rows(grad, across + (1 - far) * eighth, eighth))
            back = rows(self.first, self.rest_in, eighth)
            self.out = (
                copy(0, rows(grad, across, quarter), self.first, mate),
                copy(1, rest, self.second, other),
                copy(2, own, rows(self.first, far * eighth, eighth), other),
                copy(3, own, own, mate),
                copy(4, rest, rest, mate),
            )
            self.back = (
                None,
                None,
                copy(2, back, back, other),
                copy(3, there[0], there[0], mate),
                copy(4, there[1], there[1], mate),
            )

    halves = (Half(0), Half(1))
    for half in halves:
        half.out[0].start()
    yield
    for half in halves:
        half.out[0].wait_recv()
        add_rows(grad, half.kept, half.first, quarter)
        half.out[1].start()
        half.out[0].wait_send()
        pl.semaphore_signal(half.free, inc=1, device_id=half.mate, device_id_type=MESH)
    yield
    for half in halves:
        half.out[1].wait_recv()
        add_rows(grad, half.own, half.second, eighth)
        half.out[2].start()
        pl.semaphore_wait(half.free, 1)
        half.out[3].start()
    yield
    for half in halves:
        half.back[2].wait_recv()
        half.out[1].wait_send()
        grad[pl.ds(pl.multiple_of(half.rest, 16), eighth), :] = half.first[
            pl.ds(pl.multiple_of(half.rest_in, 16), eighth), :
        ]
        half.out[4].start()
    yield
    for half in halves:
        half.back[3].wait_recv()
        half.back[4].wait_recv()
        for copy in half.out[2:]:
            copy.wait_send()


class Sums:
    def __init__(self):
        self.active = []

    def add(self, flow):
        next(flow)
        self.active.append(flow)

    def pump(self, count=1):
        for _ in range(count):
            if self.active:
                flow = self.active.pop(0)
                if next(flow, self) is not self:
                    self.active.append(flow)

    def drain(self):
        while self.active:
            self.pump()


def backward_kernel(
    lens, order, gain2, taps, bias, w_xp, w_dt, dt_bias, a_log, skip, gain1,
    w_gate_h, w_up_h, w_down_h, w_out_h, w_x_h, w_z_h,
    y_o, dx_o, small_o, g_down_o, g_gate_o, g_up_o, g_z_o, g_x_o, g_out_o,
    w_gate, w_up, w_down, w_out, w_x, w_z, w_step, rate,
    dg_all, du_all, dz_all, dxi_all, dh1, dmix, y_own, dx_own, y_all, dx_all,
    own, other, y_part, y_other, dot_in, dot_own, dot_sum, dot_other,
    dgo, d_held, d_left, d_right,
    hs, bb, cb, pb, pc, step, gone, drive, u_s, dy_s, du_s, dstep, dproj,
    half_own, half_in, low_own, low_in, full,
    g_down, g_gate, g_up, g_z, g_x, g_out, small,
    g_gate_1, g_up_1, g_z_1, g_x_1, small_1,
    g_down_2, g_gate_2, g_up_2, g_z_2, g_x_2, g_out_2, small_2,
    g_down_3, g_gate_3, g_up_3, g_z_3, g_x_3, g_out_3, dmix_mates,
    w_sems, g_send, g_recv, u_send, u_recv, o_send, o_recv, dot_send, dot_recv,
    y_send, y_recv, dx_send, dx_recv, d_send, d_recv, z_send, z_recv, t_send, t_recv, x_send, x_recv,
    dot2_send, dot2_recv, sum_send, sum_recv, sum_free, write_sems,
    *, rank, model_width, late
):
    rows, width = dgo.shape
    count = rate.shape[0]
    block = y_o.shape[0]
    tap_count = taps.shape[0]
    group, row, column = lax.axis_index("dp"), lax.axis_index("row"), lax.axis_index("col")
    row_size, col_size = lax.axis_size("row"), lax.axis_size("col")
    weights = fetch(
        (w_down_h, w_gate_h, w_up_h, w_out_h, w_x_h, w_z_h), (w_down, w_gate, w_up, w_out, w_x, w_z), w_sems
    )
    half = columns(column, block)
    sums = Sums()
    writes = []

    def write(number, grad, result):
        copy = pltpu.make_async_copy(grad, result, write_sems.at[number])
        copy.start()
        writes.append(copy)

    def total(number, grad, first_in, second_in, result):
        yield from plane_sum(
            grad, first_in, second_in, sum_send.at[number], sum_recv.at[number], sum_free.at[number]
        )
        write(number, grad, result)

    def pair(number, grad, sent, fixed, fixed_mates, by_rows, ins, result, swapped="sent"):
        yield from pair_sum(
            grad, sent, fixed, fixed_mates, by_rows, *ins, sum_send.at[number], sum_recv.at[number], swapped
        )
        write(number, grad, result)

    met = greet("dp", "row", "col")
    dgu = late("dgu")
    hidden = dgu.shape[1] // 2
    dg_all[:, columns(row, hidden)] = dgu[:, 0:hidden]
    du_all[:, columns(row, hidden)] = dgu[:, hidden:]
    dot, hid_all, cg, cg_mates = late("dot"), late("hid_all"), late("cg"), late("cg_mates")
    hid_mates = late("hid_mates")
    met()
    dot_copies = spray("row", lambda k: dot, dot_in, dot_send, dot_recv)

    def first_work():
        sums.add(pair(0, g_down, hid_all, cg, cg_mates, True, (hid_mates, g_down_2, g_down_3), g_down_o, None))
        yield
        weights[0].wait()
        y_part[...] = matmul(hid_all[...], w_down[...])
        y_copy = swap("col", y_part, y_other, o_send.at[0], o_recv.at[0])
        yield
        wait_all(dot_copies)
        dot_own[...] = line_total(dot[...], dot_in)
        dot_copy = swap("col", dot_own, dot_other, o_send.at[2], o_recv.at[2])
        weights[1].wait()
        weights[2].wait()
        yield
        y_copy.wait()
        dot_copy.wait()
        y_own[...] = (late("h1")[...] + (y_part[...] + y_other[...])).astype(bf16)

    run(*gather_halves("row", dg_all, hidden, g_send, g_recv), first_work(), pump=(sums, PUMPS[0]))
    n2, n2_mates = late("n2"), late("n2_mates")
    sums.add(pair(1, g_gate, dg_all, n2, n2_mates, False, (g_gate_1, g_gate_2, g_gate_3), g_gate_o))

    def second_work():
        own[...] = transposed(dg_all[...], w_gate[...])
        yield

    run(*gather_halves("row", du_all, hidden, u_send, u_recv), second_work(), pump=(sums, PUMPS[1]))
    own[...] += transposed(du_all[...], w_up[...])
    copy = swap("col", own, other, o_send.at[1], o_recv.at[1])
    sums.add(pair(2, g_up, du_all, n2, n2_mates, False, (g_up_1, g_up_2, g_up_3), g_up_o))
    sums.pump(PUMPS[2])
    copy.wait()
    h1_now, s2_now = late("h1")[...], late("s2")[...]
    dn2 = own[...] + other[...]
    dots = column_form(dot_own[...] + dot_other[...])
    dh1_now = (
        cg[...].astype(f32)
        + s2_now * (as_row(gain2) * dn2)
        - h1_now * (s2_now * s2_now * dots / model_width)
    )
    dh1[...] = dh1_now
    dmix[...] = dh1_now.astype(bf16)
    gnorm2 = jnp.sum(dn2 * h1_now * s2_now, axis=0, keepdims=True)

    inner_x = late("xi")[...]
    place_now = late("place")[...]
    proj = late("proj")
    kept = {}

    def states():
        go_all = late("go_all")
        sums.add(
            pair(5, g_out, go_all, dmix, dmix_mates, True, (late("go_mates"), g_out_2, g_out_3), g_out_o, "fixed")
        )
        w_step[...] = jnp.zeros_like(w_step)
        w_step[0:rank, :] = w_dt[...]
        rate[...] = -jnp.exp(a_log[...])
        xc = conv_sum(inner_x, place_now, taps[...], as_row(bias))
        sig_c = jax.nn.sigmoid(xc)
        u_low = (xc * sig_c).astype(bf16)
        u = u_low.astype(f32)
        u_s[...] = u
        step_low = proj[...].astype(bf16)
        pre = matmul(step_low, w_step[...]) + as_row(dt_bias)
        step_now = jax.nn.softplus(pre)
        step[...] = step_now
        gone[...] = jnp.where(place_now > 0.0, step_now, 1e30)
        drive[...] = step_now * u
        kept.update(xc=xc, sig_c=sig_c, u_low=u_low, u=u, step_low=step_low, pre=pre)
        yield from scan_states(proj, rank, gone, drive, rate[...], bb, hs)

    weights[3].wait()
    run(
        *scatter_halves(
            "row", lambda d, at: transposed(dmix[at, :], w_out[columns(d, width), :]), dgo, d_held, d_left, d_right,
            d_send, d_recv,
        ),
        states(),
        pump=(sums, PUMPS[3]),
    )
    xc, sig_c, u_low, u = kept["xc"], kept["sig_c"], kept["u_low"], kept["u"]
    step_low, pre = kept["step_low"], kept["pre"]
    z_now = late("z")[...]
    sig_z = jax.nn.sigmoid(z_now)
    d_z = (dgo[...] * late("yv")[...] * (sig_z * (1.0 + z_now * (1.0 - sig_z)))).astype(bf16)
    mine = dz_all.at[:, columns(row, width)]
    mine[...] = d_z
    z_copies = []
    for k in range(1, row_size):
        copy = remote(mine, mine, z_send.at[k - 1], z_recv.at[k - 1], away("row", k))
        copy.start()
        z_copies.append(copy)
    dy = dgo[...] * (z_now * sig_z)
    dy_s[...] = dy
    dproj[...] = jnp.zeros_like(dproj)

    def adjoint():
        kept["rate"] = yield from scan_backward(
            proj, rank, rank + count, step, gone, drive, u_s, dy_s, rate[...], hs, bb, cb, pb, pc, du_s, dstep, dproj
        )

    run(adjoint(), pump=(sums, PUMPS[4]))
    g_rate = kept["rate"]
    d_pre = dstep[...] * jax.nn.sigmoid(pre)
    d_pre_low = d_pre.astype(bf16)
    dproj[...] += transposed(d_pre_low, w_step[...])

    def during_sums():
        yield
        wait_all(z_copies)
        sums.add(pair(3, g_z, dz_all, late("n1"), late("n1_mates"), False, (g_z_1, g_z_2, g_z_3), g_z_o))

    run(
        total_of_sums(dproj, half_own, half_in, low_own, low_in, full, (t_send, t_recv)),
        during_sums(),
        pump=(sums, PUMPS[5]),
    )
    dproj_low = full[...].astype(bf16)
    du = du_s[...] + as_row(skip) * dy + transposed(dproj_low, w_xp[...])
    dxc = du * (sig_c * (1.0 + xc * (1.0 - sig_c)))
    taps_now = taps[...]
    d_inner = dxc * taps_now[tap_count - 1 : tap_count, :]
    masked = [dxc]
    for shift in range(1, tap_count):
        masked.append(jnp.where(place_now >= shift, dxc, 0.0))
        k = tap_count - 1 - shift
        d_inner = d_inner + pltpu.roll(masked[shift], rows - shift, 0) * taps_now[k : k + 1, :]
    d_inner = d_inner.astype(bf16)
    dxi_all[:, columns(row, width)] = d_inner

    def during():
        dot_own[...] = rows_form(d_inner.astype(f32) * inner_x + d_z.astype(f32) * z_now)
        dot_copies = spray("row", lambda k: dot_own, dot_in, dot2_send, dot2_recv)
        small[0:RANK_LANES, :] = over_rows(dproj_low, u_low).astype(bf16)
        small[RANK_LANES : RANK_LANES + rank, :] = over_rows(step_low, d_pre_low)[0:rank, :].astype(bf16)
        yield
        wait_all(dot_copies)
        dot_sum[...] = line_total(dot_own[...], dot_in)
        dot_copy = swap("col", dot_sum, dot_other, o_send.at[3], o_recv.at[3])
        weights[4].wait()
        weights[5].wait()
        own[...] = transposed(dz_all[...], w_z[...])
        yield
        dot_copy.wait()

    run(*gather_halves("row", dxi_all, width, x_send, x_recv), during(), pump=(sums, PUMPS[6]))
    own[...] += transposed(dxi_all[...], w_x[...])
    copy = swap("col", own, other, o_send.at[4], o_recv.at[4])
    sums.add(pair(4, g_x, dxi_all, late("n1"), late("n1_mates"), False, (g_x_1, g_x_2, g_x_3), g_x_o))
    sums.pump(PUMPS[7])
    copy.wait()
    dn1 = own[...] + other[...]
    s1_now = late("s1")[...]
    xg_now = late("xg")[...].astype(f32)
    dots = column_form(dot_sum[...] + dot_other[...])
    dx = dh1[...] + s1_now * (as_row(gain1) * dn1) - xg_now * (s1_now * s1_now * dots / model_width)
    dx_own[...] = dx.astype(bf16)
    dx_copies = plane_start(dx_own.at[half], dx_all, dx_send, dx_recv)
    y_copies = plane_start(y_own.at[half], y_all, y_send, y_recv)
    g_taps = [None] * tap_count
    for shift in range(tap_count):
        moved = pltpu.roll(inner_x, shift, 0) if shift else inner_x
        g_taps[tap_count - 1 - shift] = jnp.sum(masked[shift] * moved, axis=0, keepdims=True)
    pieces = [
        g_rate,
        *g_taps,
        jnp.sum(dxc, axis=0, keepdims=True),
        jnp.sum(d_pre, axis=0, keepdims=True),
        jnp.sum(dy * u, axis=0, keepdims=True),
        jnp.sum(dn1 * xg_now * s1_now, axis=0, keepdims=True),
        gnorm2,
    ]
    found = sum(piece.shape[0] for piece in pieces)
    pieces.append(jnp.zeros((small.shape[0] - RANK_LANES - rank - found, width), f32))
    small[RANK_LANES + rank :, :] = jnp.concatenate(pieces, axis=0).astype(bf16)
    sums.add(total(6, small, small_1, small_2, small_o))
    first = (group * col_size + column) * block
    wanted = owner_rows(lengths_row(lens), as_row(order), lens.shape[1], rows, block, first)
    sums.pump(PUMPS[8])
    plane_finish(dx_copies, dx_all, dx_send, dx_recv)
    dx_o[...] = pick_rows(wanted, dx_all[...])
    plane_finish(y_copies, y_all, y_send, y_recv)
    y_o[...] = pick_rows(wanted, y_all[...])
    sums.drain()
    for write in writes:
        write.wait()


def finish_kernel(
    y, dx, small, down, gate, up, z, x, out,
    y_o, dx_o, norm1_o, z_o, x_o, taps_o, bias_o, w_xp_o, w_dt_o, dt_bias_o, rate_o, skip_o, out_o, norm2_o, gate_o,
    up_o, down_o,
    *, rank
):
    for source, target in ((z, z_o), (x, x_o), (out, out_o), (gate, gate_o), (up, up_o), (down, down_o)):
        target[...] = source[...].astype(f32)

    @pl.when(pl.program_id(0) == 0)
    def _():
        y_o[...] = y[...]
        dx_o[...] = dx[...]
        values = small[...].astype(f32)
        w_xp_o[...] = jnp.transpose(values[0:RANK_LANES, :])
        w_dt_o[...] = values[RANK_LANES : RANK_LANES + rank, :]
        at = RANK_LANES + rank
        for target in (rate_o, taps_o):
            target[...] = values[at : at + target.shape[0], :]
            at += target.shape[0]
        for target in (bias_o, dt_bias_o, skip_o, norm1_o, norm2_o):
            target[...] = values[at : at + 1, :].reshape(target.shape)
            at += 1


VMEM_BYTES = 60 << 20
DMA = pltpu.SemaphoreType.DMA


def in_vmem(kernel, name, ident, outs, scratch, args, far=(), far_outs=(), late=None, leave=None):
    late, leave = late or {}, leave or {}
    space = pl.BlockSpec(memory_space=pltpu.VMEM)
    anywhere = pl.BlockSpec(memory_space=pl.ANY)
    heads, tails, before, after = len(args) + len(far), len(outs) + len(far_outs), len(late), len(leave)

    def whole(*refs):
        at = [0]

        def take(count):
            at[0] += count
            return refs[at[0] - count : at[0]]

        head, sources, tail, targets = take(heads), take(before), take(tails), take(after)
        middle = take(len(scratch))
        keywords = {}
        if late:
            held = take(before)
            keywords["late"] = Late(list(late), sources, held, take(1)[0])
        held = take(after)
        if leave:
            keywords["leave"] = Leave(list(leave), held, targets, take(1)[0])
        kernel(*head, *tail, *held, *middle, **keywords)

    own = list(scratch)
    if late:
        own += [pltpu.VMEM(value.shape, value.dtype) for value in late.values()] + [DMA((before,))]
    if leave:
        own += [pltpu.VMEM(shape, kind) for shape, kind in leave.values()] + [DMA((after,))]
    return pl.pallas_call(
        whole,
        out_shape=tuple(jax.ShapeDtypeStruct(shape, kind) for shape, kind in [*outs, *far_outs, *leave.values()]),
        in_specs=[space] * len(args) + [anywhere] * (len(far) + before),
        out_specs=tuple([space] * len(outs) + [anywhere] * (len(far_outs) + after)),
        scratch_shapes=own,
        compiler_params=pltpu.CompilerParams(
            collective_id=ident, has_side_effects=ident is not None, vmem_limit_bytes=VMEM_BYTES
        ),
        name=name,
    )(*args, *far, *late.values())


def both(*shape):
    return [DMA(shape), DMA(shape)]


def on_pairs(
    x_in, lengths, seq_order, norm1_gain, w_in_x, w_in_z, conv_w, conv_b, w_xp, w_dt, dt_bias, a_log,
    skip_weight, w_out, norm2_gain, w_gate, w_up, w_down, cotangent,
):
    dp, rs = lax.axis_size("dp"), lax.axis_size("row")
    block, wide_d = x_in.shape
    rows = block * 2
    model_width = wide_d * rs
    width = conv_w.shape[0]
    hidden = w_gate.shape[1] // rs
    rank, count, taps = w_dt.shape[0], a_log.shape[1], conv_w.shape[1]
    conv_taps = conv_w.T
    rates = a_log.T
    vm = pltpu.VMEM
    tile = vm((128, count, 128), f32)
    big = vm((rows, width), f32)
    model = vm((rows, wide_d), f32)
    sums = [vm((8, rows), f32), vm((rs - 1, 8, rows), f32)]
    sums_scratch = [
        vm((rows // 2, RANK_LANES), f32),
        vm((rows // 2, RANK_LANES), f32),
        vm((rows // 2, RANK_LANES), bf16),
        vm((rs - 1, rows // 2, RANK_LANES), bf16),
    ]

    def weight(value):
        return vm(value.shape, value.dtype)

    def line(size, width):
        return [vm((size, rows, width), bf16)] * 3

    leave = {
        "xg": ((rows, wide_d), bf16), "cg": ((rows, wide_d), bf16), "n1": ((rows, wide_d), bf16),
        "s1": ((rows, 1), f32), "place": ((rows, 1), f32), "xi": ((rows, width), f32), "z": ((rows, width), f32),
        "proj": ((rows, RANK_LANES), f32), "yv": ((rows, width), f32), "go_all": ((rows, rs * width), bf16),
        "h1": ((rows, wide_d), f32), "s2": ((rows, 1), f32), "n2": ((rows, wide_d), bf16),
        "hid_all": ((rows, rs * hidden), bf16), "dgu": ((rows, 2 * hidden), bf16), "dot": ((8, rows), f32),
        "n1_mates": ((2, rows, wide_d), bf16), "n2_mates": ((2, rows, wide_d), bf16),
        "cg_mates": ((2, rows, wide_d), bf16), "go_mates": ((2, rows, width), bf16),
        "hid_mates": ((2, rows, hidden), bf16),
    }
    passed = in_vmem(
        functools.partial(forward_kernel, model_width=model_width, rank=rank, count=count),
        "forward",
        0,
        [],
        [
            weight(w_in_x), weight(w_in_z), weight(w_out), weight(w_gate), weight(w_up), weight(w_down),
            vm((RANK_LANES, width), bf16), vm((count, width), f32),
            vm((2, dp, block, wide_d), bf16), vm((2, dp, block, wide_d), bf16), *sums, vm((rows, wide_d), bf16),
            *line(rs, width), *line(rs, width),
            vm((rows, RANK_LANES), f32), *sums_scratch, tile, tile, big, big, big,
            model, model, vm((rows, 2 * hidden), f32), vm((3, rows // 2, 2 * hidden), f32), *line(rs, 2 * hidden), vm((rows, hidden), f32), *line(rs, hidden),
            DMA((6,)), *both(dp), *both(dp), *both(rs - 1), *both(2, 2, rs), *both(2, 2, rs), *both(rs + 1),
            *both(2, 2, rs), *both(1), *both(rs - 1), *both(4, 2, rs), *both(2, 2, rs), *both(4, 2, rs), *both(6, 2),
        ],
        (
            x_in, cotangent, lengths, seq_order, norm1_gain, conv_taps, conv_b, w_xp, w_dt, dt_bias, rates, skip_weight,
            norm2_gain,
        ),
        (w_in_x, w_in_z, w_out, w_gate, w_up, w_down),
        leave=leave,
    )
    passed = dict(zip(leave, passed))
    first = ("dgu", "dot", "hid_all", "hid_mates", "cg", "cg_mates", "n2", "n2_mates")
    late = {name: passed[name] for name in (*first, *(name for name in passed if name not in first))}

    def sizes(value, parts):
        return vm((2, value[0] // parts, value[1]), bf16)

    def eighths(value):
        return vm((2, value[0] // 8, value[1]) if value in (d_cols, grads[5]) else (2, value[0] // 2, value[1] // 4), bf16)

    d_cols, f_cols, e_cols = (rs * hidden, wide_d), (wide_d, rs * hidden), (wide_d, rs * width)
    grads = (d_cols, f_cols, f_cols, e_cols, e_cols, (rs * width, wide_d), (2 * RANK_LANES, width))
    returned = in_vmem(
        functools.partial(backward_kernel, rank=rank, model_width=model_width),
        "backward",
        1,
        [((block, wide_d), bf16), ((block, wide_d), bf16)],
        [
            weight(w_gate), weight(w_up), weight(w_down), weight(w_out), weight(w_in_x), weight(w_in_z),
            vm((RANK_LANES, width), bf16), vm((count, width), f32),
            vm((rows, rs * hidden), bf16), vm((rows, rs * hidden), bf16),
            vm((rows, rs * width), bf16), vm((rows, rs * width), bf16),
            model, vm((rows, wide_d), bf16), vm((rows, wide_d), bf16), vm((rows, wide_d), bf16),
            vm((2, dp, block, wide_d), bf16), vm((2, dp, block, wide_d), bf16),
            model, model, model, model, vm((rs - 1, 8, rows), f32), vm((8, rows), f32), vm((8, rows), f32),
            vm((8, rows), f32), big, *line(rs, width),
            vm((rows + 1, count, width), f32), tile, tile, tile, tile,
            big, big, big, big, big, big, big, vm((rows, RANK_LANES), f32), *sums_scratch, vm((rows, RANK_LANES), f32),
            *[vm(value, bf16) for value in grads],
            *[vm((2, rows, max(value) // 4), bf16) for value in grads[1:5]], sizes(grads[6], 4),
            *[eighths(value) for value in grads[:6]], sizes(grads[6], 8),
            *[eighths(value) for value in grads[:6]], vm((2, rows, wide_d), bf16),
            DMA((6,)), *both(2, 2, rs), *both(2, 2, rs), *both(5), *both(rs - 1), *both(dp), *both(dp), *both(2, 2, rs),
            *both(rs - 1), *both(rs + 1), *both(2, 2, rs), *both(rs - 1), *both(len(grads), 5, 2),
            pltpu.SemaphoreType.REGULAR((len(grads), 2)), DMA((len(grads),)),
        ],
        (
            lengths, seq_order, norm2_gain, conv_taps, conv_b, w_xp, w_dt, dt_bias, rates, skip_weight, norm1_gain,
        ),
        (w_gate, w_up, w_down, w_out, w_in_x, w_in_z),
        [(value, bf16) for value in (grads[-1], *grads[:-1])],
        late,
    )
    steps = 2

    def pieces(value):
        return pl.BlockSpec((value[0] // steps, value[1]), lambda i: (i, 0))

    def whole(*shape):
        return pl.BlockSpec(shape, lambda i: (0,) * len(shape))

    rows_spec = whole(block, wide_d)
    shape = jax.ShapeDtypeStruct
    outs = (
        (rows_spec, (block, wide_d), bf16), (rows_spec, (block, wide_d), bf16), (whole(wide_d), (wide_d,), f32),
        (pieces(e_cols), e_cols, f32), (pieces(e_cols), e_cols, f32), (whole(taps, width), (taps, width), f32),
        (whole(width), (width,), f32), (whole(width, RANK_LANES), (width, RANK_LANES), f32),
        (whole(rank, width), (rank, width), f32), (whole(width), (width,), f32),
        (whole(count, width), (count, width), f32), (whole(width), (width,), f32), (pieces(grads[5]), grads[5], f32),
        (whole(wide_d), (wide_d,), f32), (pieces(f_cols), f_cols, f32), (pieces(f_cols), f_cols, f32),
        (pieces(d_cols), d_cols, f32),
    )
    results = pl.pallas_call(
        functools.partial(finish_kernel, rank=rank),
        grid=(steps,),
        in_specs=[rows_spec, rows_spec, whole(2 * RANK_LANES, width), *[pieces(value) for value in grads[:-1]]],
        out_specs=tuple(spec for spec, _, _ in outs),
        out_shape=tuple(shape(size, kind) for _, size, kind in outs),
        compiler_params=pltpu.CompilerParams(vmem_limit_bytes=VMEM_BYTES),
        name="finish",
    )(*returned)
    (y_out, dx_out, norm1, g_z, g_x, g_taps, g_bias, g_xp, g_dt, g_dt_bias, g_rate, g_skip, g_out, norm2, g_gate, g_up,
     g_down) = results
    return (
        y_out, dx_out, norm1, g_x, g_z, g_taps.T, g_bias, g_xp, g_dt, g_dt_bias, g_rate.T, g_skip, g_out, norm2,
        g_gate, g_up, g_down,
    )


def on_device(
    x_in,
    lengths,
    seq_order,
    norm1_gain,
    w_in_x,
    w_in_z,
    conv_w,
    conv_b,
    w_xp,
    w_dt,
    dt_bias,
    a_log,
    skip_weight,
    w_out,
    norm2_gain,
    w_gate,
    w_up,
    w_down,
    cotangent,
):
    rows_in, width_row = x_in.shape
    row_devices = lax.axis_size("row")
    col_devices = lax.axis_size("col")
    group_rows = rows_in * col_devices
    model_width = width_row * row_devices
    rank_cols = w_dt.shape[0]
    state_count = a_log.shape[1]
    channels = conv_w.shape[0]
    ff_cols = w_gate.shape[1]
    my_group = lax.axis_index("dp")
    my_column = lax.axis_index("col")
    source, position_all = layout(lengths, seq_order, group_rows)
    my_source = lax.dynamic_index_in_dim(source, my_group, 0, keepdims=False)
    position = lax.dynamic_index_in_dim(position_all, my_group, 0, keepdims=False)
    slice_source = lax.dynamic_slice_in_dim(my_source, my_column * rows_in, rows_in, 0)

    def row_total(values):
        return lax.psum(values, "row")

    def token_rows(values):
        return lax.all_gather(values, "col", axis=0, tiled=True)

    def row_pieces(values):
        return lax.all_gather(values, "row", axis=0, tiled=True)

    def col_reduce(term_fn):
        return lax.psum_scatter(
            term_fn(jnp.int32(0), lax.axis_size("col") * rows_in),
            "col",
            scatter_dimension=0,
            tiled=True,
        )

    def row_reduce(term_fn, keep_rows):
        return lax.psum_scatter(
            term_fn(jnp.int32(0), lax.axis_size("row") * keep_rows),
            "row",
            scatter_dimension=0,
            tiled=True,
        )

    def projection_total(values):
        return lax.psum(values, ("row", "col"))

    blank_rows = jnp.zeros((rows_in, width_row), jnp.bfloat16)
    pieces = (
        lax.all_gather(x_in, ("dp", "col"), axis=0, tiled=True),
        lax.all_gather(cotangent, ("dp", "col"), axis=0, tiled=True),
    )
    row_count = pieces[0].shape[0]
    offset = slice_source
    inside = ((offset >= 0) & (offset < row_count))[:, None]
    index = jnp.clip(offset, 0, row_count - 1)
    x_rows = jnp.where(inside, jnp.take(pieces[0], index, axis=0), blank_rows)
    cot_rows = jnp.where(inside, jnp.take(pieces[1], index, axis=0), blank_rows)
    x_val = x_rows.astype(jnp.float32)
    scale_one = lax.rsqrt(row_total(jnp.sum(x_val * x_val, axis=1)) / model_width + epsilon)
    normed_one = (x_val * scale_one[:, None] * norm1_gain[None, :]).astype(jnp.bfloat16)
    normed_all = token_rows(normed_one)

    def inner_term(begin_row, row_count):
        return jnp.concatenate(
            [contract(w_in_x, normed_all, 0, 1), contract(w_in_z, normed_all, 0, 1)], axis=1
        )

    inner = row_reduce(inner_term, channels)
    inner_x = inner[:, :group_rows]
    inner_z = inner[:, group_rows:]

    def conv_part(values, kernel, kernel_bias):
        return convolve(values, kernel, kernel_bias, position)

    conv_out, conv_pull = jax.vjp(conv_part, inner_x, conv_w, conv_b)
    u_low = conv_out.astype(jnp.bfloat16)
    u_val = u_low.astype(jnp.float32)
    projected = projection_total(contract(w_xp, u_low, 0, 0))
    step_low = projected[:rank_cols].astype(jnp.bfloat16)
    pre_step = contract(w_dt, step_low, 0, 0) + dt_bias[:, None]
    step_size = jax.nn.softplus(pre_step)

    decay_rate = -jnp.exp(a_log).T
    proj_rows = projected.T
    u_rows = u_val.T
    step_rows = step_size.T
    gone_rows = jnp.where(position[:, None] > 0, step_rows, 1e30)
    drive_rows = step_rows * u_rows
    at_b, at_c = rank_cols, rank_cols + state_count
    scanned = scan_alone(proj_rows, gone_rows, drive_rows, decay_rate, at_b, at_c)
    mixer_y = scanned.T + skip_weight[:, None] * u_val
    gated = mixer_y * jax.nn.silu(inner_z)
    gated_low = gated.astype(jnp.bfloat16)
    gated_all = row_pieces(gated_low)

    def mix_term(begin_row, row_count):
        return contract(gated_all, w_out, 0, 0)

    first_sum = x_val + col_reduce(mix_term)
    scale_two = lax.rsqrt(row_total(jnp.sum(first_sum * first_sum, axis=1)) / model_width + epsilon)
    normed_two = (first_sum * scale_two[:, None] * norm2_gain[None, :]).astype(jnp.bfloat16)
    normed_rows = token_rows(normed_two)

    def ffn_term(begin_row, row_count):
        return jnp.concatenate(
            [
                jnp.dot(normed_rows, w_gate, preferred_element_type=jnp.float32),
                jnp.dot(normed_rows, w_up, preferred_element_type=jnp.float32),
            ],
            axis=1,
        )

    gate_up = row_reduce(ffn_term, group_rows // row_devices)
    gate_val = gate_up[:, :ff_cols]
    up_val = gate_up[:, ff_cols:]
    hidden = (jax.nn.silu(gate_val) * up_val).astype(jnp.bfloat16)
    hidden_all = row_pieces(hidden)

    def down_term(begin_row, row_count):
        return jnp.dot(hidden_all, w_down, preferred_element_type=jnp.float32)

    second_sum = first_sum + col_reduce(down_term)
    out_low = second_sum.astype(jnp.bfloat16)
    back_down_all = token_rows(cot_rows)
    grad_down = contract(hidden_all, back_down_all, 0, 0)

    def hidden_term(begin_row, row_count):
        return contract(back_down_all, w_down, 1, 1)

    d_hidden = row_reduce(hidden_term, group_rows // row_devices)
    d_gate = (d_hidden * up_val * silu_slope(gate_val)).astype(jnp.bfloat16)
    d_up = (d_hidden * jax.nn.silu(gate_val)).astype(jnp.bfloat16)
    d_gate_up_all = row_pieces(jnp.concatenate([d_gate, d_up], axis=1))
    grad_gate = contract(normed_rows, d_gate_up_all[:, :ff_cols], 0, 0)
    grad_up = contract(normed_rows, d_gate_up_all[:, ff_cols:], 0, 0)

    def norm_two_term(begin_row, row_count):
        return contract(d_gate_up_all[:, :ff_cols], w_gate, 1, 1) + contract(
            d_gate_up_all[:, ff_cols:], w_up, 1, 1
        )

    d_normed_two = col_reduce(norm_two_term)
    cot_val = cot_rows.astype(jnp.float32)
    weighted_two = d_normed_two * norm2_gain[None, :]
    grad_norm_two = jnp.sum(d_normed_two * first_sum * scale_two[:, None], axis=0)
    dot_two = row_total(jnp.sum(weighted_two * first_sum, axis=1))
    d_first = (
        cot_val
        + scale_two[:, None] * weighted_two
        - first_sum * (scale_two**3 * dot_two / model_width)[:, None]
    )
    d_mix_all = token_rows(d_first.astype(jnp.bfloat16))
    grad_out = contract(gated_all, d_mix_all, 1, 0)

    def gated_term(begin_row, row_count):
        return contract(w_out, d_mix_all, 1, 1)

    d_gated = row_reduce(gated_term, channels)
    d_inner_z = d_gated * mixer_y * silu_slope(inner_z)
    d_mixer = d_gated * jax.nn.silu(inner_z)
    d_u_rows, d_step_rows, d_proj_rows, grad_rate_rows = adjoint_alone(
        proj_rows, step_rows, gone_rows, drive_rows, u_rows, d_mixer.T, decay_rate, at_b, at_c
    )
    d_u_mix = d_u_rows.T + skip_weight[:, None] * d_mixer
    d_step = d_step_rows.T
    d_enter = d_proj_rows.T[at_b:at_c]
    d_leave = d_proj_rows.T[at_c:]
    grad_rate = grad_rate_rows.T
    grad_skip = jnp.sum(d_mixer * u_val, axis=1)
    d_pre = d_step * jax.nn.sigmoid(pre_step)
    grad_step_bias = jnp.sum(d_pre, axis=1)
    d_pre_low = d_pre.astype(jnp.bfloat16)
    grad_step_w = contract(step_low, d_pre_low, 1, 1)
    d_projected = projection_total(
        jnp.concatenate(
            [jnp.dot(w_dt, d_pre_low, preferred_element_type=jnp.float32), d_enter, d_leave], axis=0
        )
    )
    d_proj_low = d_projected.astype(jnp.bfloat16)
    grad_proj_w = contract(u_low, d_proj_low, 1, 1)
    d_u_all = d_u_mix + jnp.dot(w_xp, d_proj_low, preferred_element_type=jnp.float32)
    d_inner_x, grad_kernel, grad_kernel_bias = conv_pull(d_u_all)
    d_inner_all = row_pieces(
        jnp.concatenate([d_inner_x.astype(jnp.bfloat16), d_inner_z.astype(jnp.bfloat16)], axis=1)
    )
    grad_in_x = contract(normed_all, d_inner_all[:, :group_rows], 0, 1)
    grad_in_z = contract(normed_all, d_inner_all[:, group_rows:], 0, 1)

    def norm_one_term(begin_row, row_count):
        piece_x = lax.dynamic_slice_in_dim(d_inner_all, begin_row, row_count, 1)
        piece_z = lax.dynamic_slice_in_dim(d_inner_all, group_rows, row_count, 1)
        return contract(piece_x, w_in_x, 0, 1) + contract(piece_z, w_in_z, 0, 1)

    d_normed_one = col_reduce(norm_one_term)
    weighted_one = d_normed_one * norm1_gain[None, :]
    grad_norm_one = jnp.sum(d_normed_one * x_val * scale_one[:, None], axis=0)
    dot_one = row_total(jnp.sum(weighted_one * x_val, axis=1))
    d_input = (
        d_first
        + scale_one[:, None] * weighted_one
        - x_val * (scale_one**3 * dot_one / model_width)[:, None]
    )
    d_input_low = d_input.astype(jnp.bfloat16)
    grad_norm_one, grad_norm_two = lax.psum((grad_norm_one, grad_norm_two), ("dp", "col"))
    (
        grad_in_x,
        grad_in_z,
        grad_kernel,
        grad_kernel_bias,
        grad_proj_w,
        grad_step_w,
        grad_step_bias,
        grad_rate,
        grad_skip,
        grad_out,
        grad_gate,
        grad_up,
        grad_down,
    ) = (
        lax.psum(grad_in_x.astype(jnp.bfloat16), "dp").astype(jnp.float32),
        lax.psum(grad_in_z.astype(jnp.bfloat16), "dp").astype(jnp.float32),
        lax.psum(grad_kernel.astype(jnp.bfloat16), "dp").astype(jnp.float32),
        lax.psum(grad_kernel_bias.astype(jnp.bfloat16), "dp").astype(jnp.float32),
        lax.psum(grad_proj_w.astype(jnp.bfloat16), "dp").astype(jnp.float32),
        lax.psum(grad_step_w.astype(jnp.bfloat16), "dp").astype(jnp.float32),
        lax.psum(grad_step_bias.astype(jnp.bfloat16), "dp").astype(jnp.float32),
        lax.psum(grad_rate.astype(jnp.bfloat16), "dp").astype(jnp.float32),
        lax.psum(grad_skip.astype(jnp.bfloat16), "dp").astype(jnp.float32),
        lax.psum(grad_out.astype(jnp.bfloat16), "dp").astype(jnp.float32),
        lax.psum(grad_gate.astype(jnp.bfloat16), "dp").astype(jnp.float32),
        lax.psum(grad_up.astype(jnp.bfloat16), "dp").astype(jnp.float32),
        lax.psum(grad_down.astype(jnp.bfloat16), "dp").astype(jnp.float32),
    )
    payload = jnp.concatenate([out_low, d_input_low], axis=1)
    tokens_all = lengths.shape[0] * group_rows
    owner = (
        jnp.zeros((tokens_all,), jnp.int32)
        .at[source.reshape(-1)]
        .set(jnp.arange(tokens_all, dtype=jnp.int32))
    )
    my_rows = lax.dynamic_slice_in_dim(
        owner, (my_group * col_devices + my_column) * rows_in, rows_in, 0
    )
    pieces = lax.all_gather(payload, ("dp", "col"), axis=0, tiled=True)
    row_count = pieces.shape[0]
    offset = my_rows
    inside = ((offset >= 0) & (offset < row_count))[:, None]
    returned = jnp.where(
        inside,
        jnp.take(pieces, jnp.clip(offset, 0, row_count - 1), axis=0),
        jnp.zeros_like(payload),
    )
    y_out = returned[:, :width_row]
    dx_out = returned[:, width_row:]
    return (
        y_out,
        dx_out,
        grad_norm_one,
        grad_in_x,
        grad_in_z,
        grad_kernel,
        grad_kernel_bias,
        grad_proj_w,
        grad_step_w,
        grad_step_bias,
        grad_rate,
        grad_skip,
        grad_out,
        grad_norm_two,
        grad_gate,
        grad_up,
        grad_down,
    )


def solution(mesh):
    placed = (
        P(("dp", "col"), "row"),
        P(),
        P(),
        P("row"),
        P("row", "col"),
        P("row", "col"),
        P(("col", "row"), None),
        P(("col", "row")),
        P(("col", "row"), None),
        P(None, ("col", "row")),
        P(("col", "row")),
        P(("col", "row"), None),
        P(("col", "row")),
        P("col", "row"),
        P("row"),
        P("row", "col"),
        P("row", "col"),
        P("col", "row"),
        P(("dp", "col"), "row"),
    )
    paired = mesh.shape["col"] == 2 and mesh.shape["dp"] == 4
    return jax.shard_map(
        on_pairs if paired else on_device,
        mesh=mesh,
        in_specs=placed,
        out_specs=(
            P(("dp", "col"), "row"),
            P(("dp", "col"), "row"),
            P("row"),
            P("row", "col"),
            P("row", "col"),
            P(("col", "row"), None),
            P(("col", "row")),
            P(("col", "row"), None),
            P(None, ("col", "row")),
            P(("col", "row")),
            P(("col", "row"), None),
            P(("col", "row")),
            P("col", "row"),
            P("row"),
            P("row", "col"),
            P("row", "col"),
            P("col", "row"),
        ),
        check_vma=False,
    )
```
